128 devices in a mesh: seq: 32 (over x, y, core), head: 4 (over z).
Axes of the slice: x: 4, y: 4, z: 4, core: 2. Of those that a mesh axis runs over, the one named last changes fastest.
Arguments:
- tokens: bfloat16 [16384, 1152], P('seq'), may hold values from -6 to 6
- cotangent: bfloat16 [16384, 1152], P('seq'), may hold values from -6 to 6
- doc_starts: int32 [7], replicated, may hold values from 0 to 16256, as said below
- query_weight: bfloat16 [1152, 1024], P(None, 'head'), may hold values from -0.1875 to 0.1875
- key_weight: bfloat16 [1152, 256], replicated, may hold values from -0.1875 to 0.1875
- value_weight: bfloat16 [1152, 256], replicated, may hold values from -0.1875 to 0.1875
- out_weight: bfloat16 [1024, 1152], P('head'), may hold values from -0.1875 to 0.1875
- gate_weight: bfloat16 [1152, 6912], P(None, 'head'), may hold values from -0.1875 to 0.1875
- up_weight: bfloat16 [1152, 6912], P(None, 'head'), may hold values from -0.1875 to 0.1875
- down_weight: bfloat16 [6912, 1152], P('head'), may hold values from -0.078125 to 0.078125
- input_gain: float32 [1152], replicated, may hold values from 0.5 to 1.5
- attn_gain: float32 [1152], replicated, may hold values from 0.5 to 1.5
- prenorm_gain: float32 [1152], replicated, may hold values from 0.5 to 1.5
- post_gain: float32 [1152], replicated, may hold values from 0.5 to 1.5
- query_gain: float32 [256], replicated, may hold values from 0.5 to 1.5
- key_gain: float32 [256], replicated, may hold values from 0.5 to 1.5
Outputs:
- mixed: bfloat16 [16384, 1152], P('seq')
- tokens_grad: float32 [16384, 1152], P('seq')
- query_weight_grad: float32 [1152, 1024], P(None, 'head')
- key_weight_grad: float32 [1152, 256], replicated
- value_weight_grad: float32 [1152, 256], replicated
- out_weight_grad: float32 [1024, 1152], P('head')
- gate_weight_grad: float32 [1152, 6912], P(None, 'head')
- up_weight_grad: float32 [1152, 6912], P(None, 'head')
- down_weight_grad: float32 [6912, 1152], P('head')
- input_gain_grad: float32 [1152], replicated
- attn_gain_grad: float32 [1152], replicated
- prenorm_gain_grad: float32 [1152], replicated
- post_gain_grad: float32 [1152], replicated
- query_gain_grad: float32 [256], replicated
- key_gain_grad: float32 [256], replicated
The draws below stay inside these ranges and needn't reach their ends.
Inputs may be any that keep to these rules, and one draw needn't show every extreme that they name: doc_starts[0] is 0 and the starts rise strictly. Each of the first 3 and the last 3 sequences has at most 128 tokens, and the last sequence has exactly 128, so sequence number 3 begins among the first 512 tokens and ends among the last 512.
All inputs are finite; a program needn't handle non-finite values.
Results may differ from the reference program's by a relative error of at most 0.025.
Values may be sent and summed in bfloat16 or wider, within the bound.
A program may use at most 256 MiB of HBM per device.

```python
import math
from functools import partial
import jax
import jax.numpy as jnp
from jax import lax

D = 1152
HEADS = 4
HD = 256
FF = 6912
TOK_DEV = 512
SHORT = 3
TOKENS = 16384


def draw_doc_starts(key, part):
    key = jax.random.fold_in(key, 11)
    lead_key, behind = jax.random.split(key)
    lead_lengths = jax.random.randint(lead_key, (SHORT,), 1, TOK_DEV // 4 + 1)
    tail_random = jax.random.randint(behind, (SHORT - 1,), 1, TOK_DEV // 4 + 1)
    tail_lengths = jnp.concatenate([tail_random, jnp.full((1,), TOK_DEV // 4, jnp.int32)]).astype(jnp.int32)
    lead_starts = jnp.concatenate([jnp.zeros((1,), jnp.int32), jnp.cumsum(lead_lengths).astype(jnp.int32)])
    tail_starts = TOKENS - jnp.cumsum(tail_lengths[::-1])[::-1]
    return jnp.concatenate([lead_starts, tail_starts.astype(jnp.int32)]).astype(jnp.int32)


def steps_of(key, dims, shards, low, largest):
    loudness, own = 1.0, jax.random.fold_in(key, 6)
    for dim, shards_of in shards:
        heights = jnp.exp(jax.random.uniform(jax.random.fold_in(own, dim), (shards_of,), jnp.float32, low / len(shards), largest / len(shards)))
        loudness = loudness * jnp.repeat(heights, dims[dim] // shards_of).reshape([-1 if axis == dim else 1 for axis in range(len(dims))])
    return loudness


def gaussian(stream_key, dims, spread, reach, cuts=(), kind=jnp.bfloat16):
    entries = jax.random.normal(stream_key, dims, jnp.float32) * spread
    if len(cuts) > 0:
        entries = steps_of(stream_key, dims, cuts, -0.22, 0.18) * entries
    return jnp.clip(entries, min=-reach, max=reach).astype(kind)


def setup_inputs(seed: int = 0) -> dict:
    streams_of = jax.random.split(jax.random.key(seed), 17)
    return {
        "tokens": gaussian(streams_of[0], (TOKENS, D), 1.0, 6.0, ((0, 32),)),
        "cotangent": gaussian(streams_of[1], (TOKENS, D), 1.0, 6.0, ((0, 32),)),
        "doc_starts": draw_doc_starts(jax.random.fold_in(streams_of[16], 71), 0),
        "query_weight": gaussian(streams_of[3], (D, HEADS * HD), D ** -0.5, 0.1875, ((1, 4),)),
        "key_weight": gaussian(streams_of[4], (D, HD), D ** -0.5, 0.1875),
        "value_weight": gaussian(streams_of[5], (D, HD), D ** -0.5, 0.1875),
        "out_weight": gaussian(streams_of[6], (HEADS * HD, D), (HEADS * HD) ** -0.5, 0.1875, ((0, 4),)),
        "gate_weight": gaussian(streams_of[7], (D, FF), D ** -0.5, 0.1875, ((1, 4),)),
        "up_weight": gaussian(streams_of[8], (D, FF), D ** -0.5, 0.1875, ((1, 4),)),
        "down_weight": gaussian(streams_of[9], (FF, D), FF ** -0.5, 0.078125, ((0, 4),)),
        "input_gain": jnp.clip(1.0 + 0.1 * jax.random.normal(streams_of[10], (D,), jnp.float32), 0.5, 1.5),
        "attn_gain": jnp.clip(1.0 + 0.1 * jax.random.normal(streams_of[11], (D,), jnp.float32), 0.5, 1.5),
        "prenorm_gain": jnp.clip(1.0 + 0.1 * jax.random.normal(streams_of[12], (D,), jnp.float32), 0.5, 1.5),
        "post_gain": jnp.clip(1.0 + 0.1 * jax.random.normal(streams_of[13], (D,), jnp.float32), 0.5, 1.5),
        "query_gain": jnp.clip(1.0 + 0.1 * jax.random.normal(streams_of[14], (HD,), jnp.float32), 0.5, 1.5),
        "key_gain": jnp.clip(1.0 + 0.1 * jax.random.normal(streams_of[15], (HD,), jnp.float32), 0.5, 1.5),
    }


EPS = 1e-06
THETA = 1000000.0
NEG = -1e+30
HIGH = lax.Precision.HIGHEST

@jax.custom_vjp
def low(v):
    return lax.optimization_barrier(v.astype(jnp.bfloat16)).astype(jnp.float32)

@jax.custom_vjp
def low_back(v):
    return v

def low_keep(v):
    return (low(v), None)

def low_pass(kept, grad):
    return (grad,)

def back_keep(v):
    return (v, None)

def back_low(kept, grad):
    return (low(grad),)
low.defvjp(low_keep, low_pass)
low_back.defvjp(back_keep, back_low)

def rms_norm(values, scaling):
    return values * lax.rsqrt(lax.optimization_barrier(jnp.mean(values * values, axis=-1, keepdims=True)) + EPS) * scaling

def doc_layout(doc_starts, token_index):
    before = doc_starts[None, :] <= token_index[:, None]
    segment = lax.optimization_barrier(jnp.sum(before.astype(jnp.int32), axis=1)).astype(jnp.int32)
    doc_begin = lax.optimization_barrier(jnp.max(jnp.where(before, doc_starts[None, :], 0), axis=1))
    return (segment, (token_index - doc_begin).astype(jnp.int32))

def rope_tables(position, head_width):
    half_width = head_width // 2
    inverse = jnp.exp(-math.log(THETA) * 2.0 * jnp.arange(half_width, dtype=jnp.float32) / head_width)
    angles = position.astype(jnp.float32)[:, None] * inverse[None, :]
    angles = jnp.concatenate([angles, angles], axis=1)
    return (jnp.cos(angles), jnp.sin(angles))

def rotate(values, cos_table, sine_table):
    half_width = values.shape[-1] // 2
    turned = jnp.concatenate([-values[..., half_width:], values[..., :half_width]], axis=-1)
    return values * cos_table + turned * sine_table

def attend_block(key_rows, value_rows, key_segment, query_block):
    queries, query_index, query_segment = query_block
    scores = low_back(jnp.einsum('qhd,kd->hqk', queries, key_rows, precision=HIGH))
    key_index = jnp.arange(key_rows.shape[0], dtype=jnp.int32)
    allowed = (key_index[None, :] <= query_index[:, None]) & (key_segment[None, :] == query_segment[:, None])
    scores = jnp.where(allowed[None], scores, NEG)
    row_max = lax.optimization_barrier(jnp.max(scores, axis=-1, keepdims=True))
    exp_scores = jnp.exp(scores - row_max)
    attn_probs = low(exp_scores / lax.optimization_barrier(jnp.sum(exp_scores, axis=-1, keepdims=True)))
    return jnp.einsum('hqk,kd->qhd', attn_probs, value_rows, precision=HIGH)

def block_layer(tokens, query_weight, key_weight, value_weight, out_weight, gate_weight, up_weight, down_weight, input_gain, attn_gain, prenorm_gain, post_gain, query_gain, key_gain, segment, cos_table, sine_table):
    token_count = tokens.shape[0]
    normed = low(rms_norm(tokens, input_gain))
    query_raw = low_back(jnp.dot(normed, query_weight, precision=HIGH))
    key_raw = low_back(jnp.dot(normed, key_weight, precision=HIGH))
    value_rows = low(low_back(jnp.dot(normed, value_weight, precision=HIGH)))
    query_heads = rms_norm(query_raw.reshape(token_count, HEADS, HD), query_gain)
    query_rows = low(rotate(query_heads, cos_table[:, None, :], sine_table[:, None, :]) * HD ** (-0.5))
    key_rows = low(rotate(rms_norm(key_raw, key_gain), cos_table, sine_table))
    block_rows = math.gcd(token_count, 512)
    block_count = token_count // block_rows
    token_index = jnp.arange(token_count, dtype=jnp.int32)
    attend_all = jax.checkpoint(partial(attend_block, key_rows, value_rows, segment))
    mixed_heads = lax.map(attend_all, (query_rows.reshape(block_count, block_rows, HEADS, HD), token_index.reshape(block_count, block_rows), segment.reshape(block_count, block_rows)))
    attn_mix = low(low_back(mixed_heads.reshape(token_count, HEADS * HD)))
    attn_out = low_back(jnp.dot(attn_mix, out_weight, precision=HIGH))
    hidden_state = tokens + rms_norm(attn_out, attn_gain)
    ffn_in = low(rms_norm(hidden_state, prenorm_gain))
    gate_rows = low_back(jnp.dot(ffn_in, gate_weight, precision=HIGH))
    up_rows = low_back(jnp.dot(ffn_in, up_weight, precision=HIGH))
    act_rows = low(jax.nn.gelu(gate_rows, approximate=True) * up_rows)
    ffn_out = low_back(jnp.dot(act_rows, down_weight, precision=HIGH))
    return hidden_state + rms_norm(ffn_out, post_gain)

def reference(tokens, cotangent, doc_starts, query_weight, key_weight, value_weight, out_weight, gate_weight, up_weight, down_weight, input_gain, attn_gain, prenorm_gain, post_gain, query_gain, key_gain):
    token_count = tokens.shape[0]
    segment, position = doc_layout(doc_starts, jnp.arange(token_count, dtype=jnp.int32))
    cos_table, sine_table = rope_tables(position, HD)
    primals = tuple((operand.astype(jnp.float32) for operand in (tokens, query_weight, key_weight, value_weight, out_weight, gate_weight, up_weight, down_weight, input_gain, attn_gain, prenorm_gain, post_gain, query_gain, key_gain)))

    def forward(*operands):
        return block_layer(*operands, segment, cos_table, sine_table)
    mixed, pullback = jax.vjp(forward, *primals)
    gradients = pullback(cotangent.astype(jnp.float32))
    return (mixed.astype(jnp.bfloat16), gradients[0], gradients[1], gradients[2], gradients[3], gradients[4], gradients[5], gradients[6], gradients[7], gradients[8], gradients[9], gradients[10], gradients[11], gradients[12], gradients[13])
```

```python
import functools
import math

import jax
import jax.numpy as jnp
from jax import lax
from jax.experimental import pallas as pl
from jax.experimental.pallas import tpu as pltpu
from jax.sharding import PartitionSpec as P

HD = 256


EPS = 1e-06
THETA = 1000000.0
NEG = -1e30


def rms_norm(values, scaling):
    return values * lax.rsqrt(jnp.mean(values * values, axis=-1, keepdims=True) + EPS) * scaling


def doc_layout(doc_starts, token_index):
    before = doc_starts[None, :] <= token_index[:, None]
    segment = jnp.sum(before.astype(jnp.int32), axis=1)
    doc_begin = jnp.max(jnp.where(before, doc_starts[None, :], 0), axis=1)
    return (segment, token_index - doc_begin)


def rope_tables(position, head_width):
    half_width = head_width // 2
    inverse = jnp.exp(
        -math.log(THETA) * 2.0 * jnp.arange(half_width, dtype=jnp.float32) / head_width
    )
    angles = position.astype(jnp.float32)[:, None] * inverse[None, :]
    angles = jnp.concatenate([angles, angles], axis=1)
    return (jnp.cos(angles), jnp.sin(angles))


def rotate(values, cos_table, sine_table):
    half_width = values.shape[-1] // 2
    turned = jnp.concatenate([-values[..., half_width:], values[..., :half_width]], axis=-1)
    return values * cos_table + turned * sine_table


def dot_last(left_side, right_side):
    return lax.dot_general(
        left_side, right_side, (((1,), (1,)), ((), ())), preferred_element_type=jnp.float32
    )


def dot_first(left_side, right_side):
    return lax.dot_general(
        left_side, right_side, (((0,), (0,)), ((), ())), preferred_element_type=jnp.float32
    )


def residual_norm(residual, branch, scaling):
    return residual + rms_norm(branch, scaling)


def gated_act(gate_vals, up_vals):
    return jax.nn.gelu(gate_vals, approximate=True) * up_vals


MESH_ID = pl.DeviceIdType.MESH
HALF = 256
BLK = 512
X_SIZE, Y_SIZE = 4, 4
STEPS = (0, 1, 3, 2)


def place():
    s = lax.axis_index("seq")
    return s // 8, (s // 2) % 4, s % 2, lax.axis_index("head")


def at(x, y, c, z):
    return ((x % 4) * 8 + (y % 4) * 2 + c, z % 4)


def greet(peers):
    barrier = pltpu.get_barrier_semaphore()
    for peer in peers:
        pl.semaphore_signal(barrier, inc=1, device_id=peer, device_id_type=MESH_ID)
    pl.semaphore_wait(barrier, len(peers))


def remote(src, dst, send_sem, recv_sem, peer):
    return pltpu.make_async_remote_copy(
        src_ref=src,
        dst_ref=dst,
        send_sem=send_sem,
        recv_sem=recv_sem,
        device_id=peer,
        device_id_type=MESH_ID,
    )


def plane_peers(x, y, c, z):
    along_x = [at(x + j, y, c, z) for j in (1, 3, 2)]
    along_y = [at(x, y + j, c, z) for j in (1, 3, 2)]
    mirror = [at(3 - x, y + j, 1 - c, z) for j in range(4)]
    sibling = at(x, y, 1 - c, z)
    along_z = [at(x, y, c, z + j) for j in (1, 3, 2)]
    return along_x, along_y, mirror, sibling, along_z


def half_token(x, y_slot, c, upper):
    d = 8 * x + 2 * y_slot + c
    return HALF * (63 - 2 * d) if upper else HALF * 2 * d


def tile_first(i, x, c):
    d = 8 * x + 2 * (i // 2) + c
    return jnp.where(i % 2 == 1, HALF * (63 - 2 * d), HALF * 2 * d)


def begin_of(token, starts_ref):
    begin = jnp.zeros_like(token)
    for n in range(starts_ref.shape[0]):
        start = starts_ref[n]
        begin = jnp.where(start <= token, start, begin)
    return begin


def attn_forward(
    starts_ref, q_ref, k_ref, v_ref,
    mix_ref, lse_ref, qg_ref, kg_ref, vg_ref,
    acc, lacc, osend, lsend, orecv, lrecv,
    q_ssem, q_rsem, kv_ssem, kv_rsem, fw_ssem, o_ssem, o_rsem, l_ssem, l_rsem, z_ssem, z_rsem,
):
    x, y, c, z = place()
    along_x, along_y, mirror, sibling, along_z = plane_peers(x, y, c, z)
    greet(along_x + along_y + mirror + [sibling] + along_z)

    own_low = y * 2
    own_high = (3 - y) * 2 + 1
    own_slot = x * 2 + c
    q_low, q_high = q_ref.at[pl.ds(0, HALF)], q_ref.at[pl.ds(HALF, HALF)]
    sends = []
    kv_peers = [sibling] + along_x
    for n, peer in enumerate(kv_peers):
        for m, (src, dst) in enumerate(((k_ref, kg_ref), (v_ref, vg_ref))):
            sends.append(remote(src, dst.at[own_slot], kv_ssem.at[n, m], kv_rsem.at[own_slot, m], peer))
    for n, peer in enumerate(along_y):
        sends.append(remote(q_low, qg_ref.at[own_low], q_ssem.at[n], q_rsem.at[own_low], peer))
    for n, peer in enumerate(mirror):
        sends.append(remote(q_high, qg_ref.at[own_high], q_ssem.at[3 + n], q_rsem.at[own_high], peer))
    for copy in sends:
        copy.start()
    qg_ref[own_low] = q_ref[0:HALF, :]
    kg_ref[own_slot] = k_ref[...]
    vg_ref[own_slot] = v_ref[...]
    acc[...] = jnp.zeros_like(acc)
    lacc[...] = jnp.zeros_like(lacc)

    def q_arrival(slot):
        remote(q_low, qg_ref.at[slot], q_ssem.at[0], q_rsem.at[slot], sibling).wait_recv()

    def kv_arrival(slot):
        for m, (src, dst) in enumerate(((k_ref, kg_ref), (v_ref, vg_ref))):
            remote(src, dst.at[slot], kv_ssem.at[0, m], kv_rsem.at[slot, m], sibling).wait_recv()

    for j in (1, 3, 2):
        q_arrival(((y + j) % 4) * 2)
    for j in range(4):
        q_arrival(j * 2 + 1)

    def chunk(i, first_q, pair, first_k, masked):
        queries = qg_ref[i]
        if masked:
            token = first_q + lax.broadcasted_iota(jnp.int32, (HALF, 1), 0)
            begin = begin_of(token, starts_ref)
        total = None
        sums = None
        for cc in range(2):
            keys, values = kg_ref[pair * 2 + cc], vg_ref[pair * 2 + cc]
            scores = lax.dot_general(
                queries, keys, (((1,), (1,)), ((), ())), preferred_element_type=jnp.float32
            )
            exps = jnp.exp(scores)
            if masked:
                key_index = first_k + cc * BLK + lax.broadcasted_iota(jnp.int32, (1, BLK), 1)
                exps = jnp.where((key_index <= token) & (key_index >= begin), exps, 0.0)
            part = jnp.dot(exps.astype(jnp.bfloat16), values, preferred_element_type=jnp.float32)
            total = part if total is None else total + part
            for n in range(BLK // 128):
                piece = exps[:, n * 128 : (n + 1) * 128]
                sums = piece if sums is None else sums + piece
        acc[i] = acc[i] + total
        lacc[i] = lacc[i] + sums

    forwards = []
    for step, j in enumerate(STEPS):
        pair = (x + j) % 4
        if step > 0:
            kv_arrival(pair * 2 + c)
            for m, ref in enumerate((kg_ref, vg_ref)):
                slot = pair * 2 + c
                copy = remote(ref.at[slot], ref.at[slot], fw_ssem.at[step - 1, m], kv_rsem.at[slot, m], sibling)
                copy.start()
                forwards.append(copy)
        kv_arrival(pair * 2 + 1 - c)
        first_k = 4096 * pair + 1024 * y

        def visit(i, carry):
            first_q = tile_first(i, x, c)
            some = first_k <= first_q + (HALF - 1)
            full = (first_k + 1023 <= first_q) & (first_k > 0) & (first_q < 31 * BLK)

            @pl.when(full)
            def _():
                chunk(i, first_q, pair, first_k, False)

            @pl.when(some & jnp.logical_not(full))
            def _():
                chunk(i, first_q, pair, first_k, True)

            return carry

        lax.fori_loop(0, 8, visit, 0)

    out_copies = []
    for slot_y in range(4):
        for upper in range(2):
            i = slot_y * 2 + upper
            osend[i] = acc[i].astype(jnp.bfloat16)
            row = jnp.sum(jnp.transpose(lacc[i]), axis=0, keepdims=True)
            lsend[i] = jnp.broadcast_to(row, (8, HALF))
    for j in (1, 3, 2):
        i = ((y + j) % 4) * 2
        peer = at(x, y + j, c, z)
        out_copies.append(remote(osend.at[i], orecv.at[y], o_ssem.at[j - 1], o_rsem.at[y], peer))
        out_copies.append(remote(lsend.at[i], lrecv.at[y], l_ssem.at[j - 1], l_rsem.at[y], peer))
    for j in range(4):
        i = j * 2 + 1
        peer = at(3 - x, 3 - j, 1 - c, z)
        out_copies.append(remote(osend.at[i], orecv.at[4 + y], o_ssem.at[3 + j], o_rsem.at[4 + y], peer))
        out_copies.append(remote(lsend.at[i], lrecv.at[4 + y], l_ssem.at[3 + j], l_rsem.at[4 + y], peer))
    for copy in out_copies:
        copy.start()
    orecv[y] = osend[own_low]
    lrecv[y] = lsend[own_low]

    def o_arrival(slot):
        remote(osend.at[0], orecv.at[slot], o_ssem.at[0], o_rsem.at[slot], sibling).wait_recv()
        remote(lsend.at[0], lrecv.at[slot], l_ssem.at[0], l_rsem.at[slot], sibling).wait_recv()

    for j in (1, 3, 2):
        o_arrival((y + j) % 4)
    for j in range(4):
        o_arrival(4 + j)
    mine = mix_ref.at[:, pl.ds(pl.multiple_of(z * HD, HD), HD)]
    for upper in range(2):
        numer = sum(orecv[4 * upper + n].astype(jnp.float32) for n in range(4))
        denom = sum(lrecv[4 * upper + n] for n in range(4))[0:1, :]
        lse_ref[:, upper * HALF : (upper + 1) * HALF] = jnp.broadcast_to(jnp.log(denom), (8, HALF))
        inverse = jnp.transpose(jnp.broadcast_to(1.0 / denom, (128, HALF)))
        scaled = numer * jnp.concatenate([inverse, inverse], axis=1)
        mix_ref[pl.ds(upper * HALF, HALF), pl.ds(pl.multiple_of(z * HD, HD), HD)] = scaled.astype(jnp.bfloat16)
    z_copies = []
    for j in (1, 3, 2):
        z_copies.append(remote(mine, mine, z_ssem.at[j - 1], z_rsem.at[z], at(x, y, c, z + j)))
    for copy in z_copies:
        copy.start()
    for j in (1, 3, 2):
        other = (z + j) % 4
        theirs = mix_ref.at[:, pl.ds(pl.multiple_of(other * HD, HD), HD)]
        remote(mine, theirs, z_ssem.at[0], z_rsem.at[other], sibling).wait_recv()
    for copy in sends + forwards + out_copies + z_copies:
        copy.wait_send()


def forward_attention(doc_starts, query, key, value):
    vmem = pl.BlockSpec(memory_space=pltpu.VMEM)
    dma = pltpu.SemaphoreType.DMA
    return pl.pallas_call(
        attn_forward,
        name="attn_forward",
        out_shape=[
            jax.ShapeDtypeStruct((BLK, 4 * HD), jnp.bfloat16),
            jax.ShapeDtypeStruct((8, BLK), jnp.float32),
            jax.ShapeDtypeStruct((8, HALF, HD), jnp.bfloat16),
            jax.ShapeDtypeStruct((8, BLK, HD), jnp.bfloat16),
            jax.ShapeDtypeStruct((8, BLK, HD), jnp.bfloat16),
        ],
        in_specs=[pl.BlockSpec(memory_space=pltpu.SMEM)] + [vmem] * 3,
        out_specs=[vmem] * 5,
        scratch_shapes=[
            pltpu.VMEM((8, HALF, HD), jnp.float32),
            pltpu.VMEM((8, HALF, 128), jnp.float32),
            pltpu.VMEM((8, HALF, HD), jnp.bfloat16),
            pltpu.VMEM((8, 8, HALF), jnp.float32),
            pltpu.VMEM((8, HALF, HD), jnp.bfloat16),
            pltpu.VMEM((8, 8, HALF), jnp.float32),
            dma((7,)), dma((8,)), dma((4, 2)), dma((8, 2)), dma((3, 2)),
            dma((7,)), dma((8,)), dma((7,)), dma((8,)), dma((3,)), dma((4,)),
        ],
        compiler_params=pltpu.CompilerParams(
            collective_id=1, has_side_effects=True, vmem_limit_bytes=40 << 20
        ),
        cost_estimate=pl.CostEstimate(flops=6 * 10**9, bytes_accessed=20 * 2**20, transcendentals=5 * 10**6),
    )(doc_starts, query, key, value)


def attn_backward(
    starts_ref, do_ref, stat_ref, q_in, k_in, v_in,
    dq_ref, dkv_ref,
    dog, statg, dqacc, dkacc, dvacc, ktbuf, sibsend, sibrecv, ringsend, ringrecv,
    dqsend, dqrecv, zpart, zsend, zrecv,
    do_ssem, do_rsem, st_ssem, st_rsem, sib_ssem, sib_rsem, ring_ssem, ring_rsem,
    dq_ssem, dq_rsem, z_ssem, z_rsem, g_ssem, g_rsem,
):
    x, y, c, z = place()
    along_x, along_y, mirror, sibling, along_z = plane_peers(x, y, c, z)
    greet(along_x + along_y + mirror + [sibling] + along_z)
    own_low = y * 2
    own_high = (3 - y) * 2 + 1
    sends = []
    for part, (own, peers, base) in enumerate(((own_low, along_y, 0), (own_high, mirror, 3))):
        do_half = do_ref.at[pl.ds(part * HALF, HALF)]
        st_half = stat_ref.at[part]
        for n, peer in enumerate(peers):
            sends.append(remote(do_half, dog.at[own], do_ssem.at[base + n], do_rsem.at[own], peer))
            sends.append(remote(st_half, statg.at[own], st_ssem.at[base + n], st_rsem.at[own], peer))
    for copy in sends:
        copy.start()
    dog[own_low] = do_ref[0:HALF, :]
    statg[own_low] = stat_ref[0]
    dqacc[...] = jnp.zeros_like(dqacc)

    def arrival(slot):
        remote(do_ref.at[pl.ds(0, HALF)], dog.at[slot], do_ssem.at[0], do_rsem.at[slot], sibling).wait_recv()
        remote(stat_ref.at[0], statg.at[slot], st_ssem.at[0], st_rsem.at[slot], sibling).wait_recv()

    for j in (1, 3, 2):
        arrival(((y + j) % 4) * 2)
    for j in range(4):
        arrival(j * 2 + 1)

    def tile(i, first_q, slot, first_k, masked):
        queries, out_grads = q_in[i], dog[i]
        lse, delta = statg[i, 0:1, :], statg[i, 1:2, :]
        if masked:
            token = first_q + lax.broadcasted_iota(jnp.int32, (1, HALF), 1)
            begin = begin_of(token, starts_ref)
        dq_part = None
        for n in range(2):
            rows = pl.ds(n * 256, 256)
            keys, values = k_in[slot, rows], v_in[slot, rows]
            nt = (((1,), (1,)), ((), ()))
            scores = lax.dot_general(keys, queries, nt, preferred_element_type=jnp.float32)
            prob_grad = lax.dot_general(values, out_grads, nt, preferred_element_type=jnp.float32)
            soft = jnp.exp(scores - lse)
            if masked:
                key_index = first_k + n * 256 + lax.broadcasted_iota(jnp.int32, (256, 1), 0)
                soft = jnp.where((key_index <= token) & (key_index >= begin), soft, 0.0)
            score_grad = (soft * (prob_grad - delta)).astype(jnp.bfloat16)
            dvacc[rows, :] += jnp.dot(soft.astype(jnp.bfloat16), out_grads, preferred_element_type=jnp.float32)
            dkacc[rows, :] += jnp.dot(score_grad, queries, preferred_element_type=jnp.float32)
            part = jnp.dot(ktbuf[:, n * 256 : (n + 1) * 256], score_grad, preferred_element_type=jnp.float32)
            dq_part = part if dq_part is None else dq_part + part
        dqacc[i] = dqacc[i] + dq_part

    copies = []
    for step, j in enumerate((2, 1, 3, 0)):
        pair = (x + j) % 4
        for turn in range(2):
            cc = 1 - c if turn == 0 else c
            slot = pair * 2 + cc
            first_k = 4096 * pair + 1024 * y + BLK * cc
            dkacc[...] = jnp.zeros_like(dkacc)
            dvacc[...] = jnp.zeros_like(dvacc)
            ktbuf[...] = jnp.transpose(k_in[slot])

            def visit(i, carry):
                first_q = tile_first(i, x, c)
                some = first_k <= first_q + (HALF - 1)
                full = (first_k + BLK - 1 <= first_q) & (first_k > 0) & (first_q < 31 * BLK)

                @pl.when(full)
                def _():
                    tile(i, first_q, slot, first_k, False)

                @pl.when(some & jnp.logical_not(full))
                def _():
                    tile(i, first_q, slot, first_k, True)

                return carry

            lax.fori_loop(0, 8, visit, 0)
            if turn == 0:
                sibsend[step, 0] = dkacc[...].astype(jnp.bfloat16)
                sibsend[step, 1] = dvacc[...].astype(jnp.bfloat16)
                copy = remote(sibsend.at[step], sibrecv.at[step], sib_ssem.at[step], sib_rsem.at[step], sibling)
                copy.start()
                copies.append(copy)
            else:
                remote(sibsend.at[step], sibrecv.at[step], sib_ssem.at[step], sib_rsem.at[step], sibling).wait_recv()
                dk = dkacc[...] + sibrecv[step, 0].astype(jnp.float32)
                dv = dvacc[...] + sibrecv[step, 1].astype(jnp.float32)
                if step < 3:
                    ringsend[step, 0] = dk.astype(jnp.bfloat16)
                    ringsend[step, 1] = dv.astype(jnp.bfloat16)
                    for m in range(2):
                        copy = remote(
                            ringsend.at[step, m], ringrecv.at[step, m], ring_ssem.at[step, m], ring_rsem.at[step, m],
                            at(x + j, y, c, z),
                        )
                        copy.start()
                        copies.append(copy)
                else:
                    dkacc[...] = dk
                    dvacc[...] = dv

    for i in range(8):
        dqsend[i] = jnp.transpose(dqacc[i]).astype(jnp.bfloat16)
    for j in (1, 3, 2):
        i = ((y + j) % 4) * 2
        copies.append(remote(dqsend.at[i], dqrecv.at[y], dq_ssem.at[j - 1], dq_rsem.at[y], at(x, y + j, c, z)))
        copies[-1].start()
    for j in range(4):
        i = j * 2 + 1
        copies.append(
            remote(dqsend.at[i], dqrecv.at[4 + y], dq_ssem.at[3 + j], dq_rsem.at[4 + y], at(3 - x, 3 - j, 1 - c, z))
        )
        copies[-1].start()
    dqrecv[y] = dqsend[own_low]

    for step in range(3):
        for m in range(2):
            remote(
                ringsend.at[step, m], ringrecv.at[step, m], ring_ssem.at[step, m], ring_rsem.at[step, m], sibling
            ).wait_recv()
    for n in range(4):
        rows = pl.ds(n * 128, 128)
        for m, ref in enumerate((dkacc, dvacc)):
            whole = ref[rows, :] + sum(ringrecv[step, m, rows, :].astype(jnp.float32) for step in range(3))
            zpart[n, m * 128 : (m + 1) * 128, :] = whole.astype(jnp.bfloat16)
    for j in (1, 3, 2):
        other = (z + j) % 4
        copies.append(remote(zpart.at[other], zrecv.at[z], z_ssem.at[j - 1], z_rsem.at[z], at(x, y, c, other)))
        copies[-1].start()
    zrecv[z] = zpart[z]

    def dq_arrival(slot):
        remote(dqsend.at[0], dqrecv.at[slot], dq_ssem.at[0], dq_rsem.at[slot], sibling).wait_recv()

    for j in (1, 3, 2):
        dq_arrival((y + j) % 4)
    for j in range(4):
        dq_arrival(4 + j)
    for upper in range(2):
        dq_ref[pl.ds(upper * HALF, HALF), :] = sum(dqrecv[4 * upper + n].astype(jnp.float32) for n in range(4))

    for j in (1, 3, 2):
        other = (z + j) % 4
        remote(zpart.at[0], zrecv.at[other], z_ssem.at[0], z_rsem.at[other], sibling).wait_recv()
    dkv_ref[z] = sum(zrecv[n].astype(jnp.float32) for n in range(4)).astype(jnp.bfloat16)
    for j in (1, 3, 2):
        copies.append(remote(dkv_ref.at[z], dkv_ref.at[z], g_ssem.at[j - 1], g_rsem.at[z], at(x, y, c, z + j)))
        copies[-1].start()
    for j in (1, 3, 2):
        other = (z + j) % 4
        remote(zpart.at[0], dkv_ref.at[other], g_ssem.at[0], g_rsem.at[other], sibling).wait_recv()
    for copy in sends + copies:
        copy.wait_send()


def backward_attention(doc_starts, out_grad, stats, q_all, k_all, v_all):
    vmem = pl.BlockSpec(memory_space=pltpu.VMEM)
    dma = pltpu.SemaphoreType.DMA
    low, full = jnp.bfloat16, jnp.float32
    return pl.pallas_call(
        attn_backward,
        name="attn_backward",
        out_shape=[
            jax.ShapeDtypeStruct((BLK, HD), full),
            jax.ShapeDtypeStruct((4, 256, HD), low),
        ],
        in_specs=[pl.BlockSpec(memory_space=pltpu.SMEM)] + [vmem] * 5,
        out_specs=[vmem] * 2,
        scratch_shapes=[
            pltpu.VMEM((8, HALF, HD), low),
            pltpu.VMEM((8, 8, HALF), full),
            pltpu.VMEM((8, HD, HALF), full),
            pltpu.VMEM((BLK, HD), full),
            pltpu.VMEM((BLK, HD), full),
            pltpu.VMEM((HD, BLK), low),
            pltpu.VMEM((4, 2, BLK, HD), low),
            pltpu.VMEM((4, 2, BLK, HD), low),
            pltpu.VMEM((3, 2, BLK, HD), low),
            pltpu.VMEM((3, 2, BLK, HD), low),
            pltpu.VMEM((8, HALF, HD), low),
            pltpu.VMEM((8, HALF, HD), low),
            pltpu.VMEM((4, 256, HD), low),
            pltpu.VMEM((8, 128), low),
            pltpu.VMEM((4, 256, HD), low),
            dma((7,)), dma((8,)), dma((7,)), dma((8,)), dma((4,)), dma((4,)), dma((3, 2)), dma((3, 2)),
            dma((7,)), dma((8,)), dma((3,)), dma((4,)), dma((3,)), dma((4,)),
        ],
        compiler_params=pltpu.CompilerParams(
            collective_id=2, has_side_effects=True, vmem_limit_bytes=48 << 20
        ),
        cost_estimate=pl.CostEstimate(flops=60 * 10**9, bytes_accessed=20 * 2**20, transcendentals=5 * 10**6),
    )(doc_starts, out_grad, stats, q_all, k_all, v_all)


def head_sum_kernel(part_ref, out_ref, recv, s_ssem, s_rsem, g_ssem, g_rsem):
    x, y, c, z = place()
    peers = [at(x, y, c, z + j) for j in (1, 3, 2)]
    greet(peers)
    rows = part_ref.shape[0] // 4

    def block(ref, n):
        return ref.at[pl.ds(pl.multiple_of(n * rows, rows), rows)]

    copies = []
    for n, j in enumerate((1, 3, 2)):
        copies.append(remote(block(part_ref, (z + j) % 4), recv.at[z], s_ssem.at[n], s_rsem.at[z], peers[n]))
        copies[-1].start()
    for j in (1, 3, 2):
        other = (z + j) % 4
        remote(block(part_ref, 0), recv.at[other], s_ssem.at[0], s_rsem.at[other], peers[0]).wait_recv()
    own = pl.ds(pl.multiple_of(z * rows, rows), rows)
    total = part_ref[own, :].astype(jnp.float32)
    for j in (1, 3, 2):
        total = total + recv[(z + j) % 4].astype(jnp.float32)
    out_ref[own, :] = total.astype(out_ref.dtype)
    for n, j in enumerate((1, 3, 2)):
        copies.append(remote(block(out_ref, z), block(out_ref, z), g_ssem.at[n], g_rsem.at[z], peers[n]))
        copies[-1].start()
    for j in (1, 3, 2):
        other = (z + j) % 4
        remote(block(part_ref, 0), block(out_ref, other), g_ssem.at[0], g_rsem.at[other], peers[0]).wait_recv()
    for copy in copies:
        copy.wait_send()


def head_sum(part, number):
    vmem = pl.BlockSpec(memory_space=pltpu.VMEM)
    dma = pltpu.SemaphoreType.DMA
    rows, columns = part.shape
    return pl.pallas_call(
        head_sum_kernel,
        name=f"head_sum_{number}",
        out_shape=jax.ShapeDtypeStruct(part.shape, part.dtype),
        in_specs=[vmem],
        out_specs=vmem,
        scratch_shapes=[
            pltpu.VMEM((4, rows // 4, columns), part.dtype),
            dma((3,)), dma((4,)), dma((3,)), dma((4,)),
        ],
        compiler_params=pltpu.CompilerParams(
            collective_id=3 + number, has_side_effects=True, vmem_limit_bytes=32 << 20
        ),
        cost_estimate=pl.CostEstimate(flops=10**7, bytes_accessed=10 * 2**20, transcendentals=0),
    )(part)


def head_gather_kernel(part_ref, out_ref, g_ssem, g_rsem):
    x, y, c, z = place()
    peers = [at(x, y, c, z + j) for j in (1, 3, 2)]
    greet(peers)
    width = part_ref.shape[1]

    def block(n):
        return out_ref.at[:, pl.ds(pl.multiple_of(n * width, width), width)]

    copies = []
    for n, j in enumerate((1, 3, 2)):
        copies.append(remote(part_ref, block(z), g_ssem.at[n], g_rsem.at[z], peers[n]))
        copies[-1].start()
    out_ref[:, pl.ds(pl.multiple_of(z * width, width), width)] = part_ref[...]
    for j in (1, 3, 2):
        other = (z + j) % 4
        remote(part_ref, block(other), g_ssem.at[0], g_rsem.at[other], peers[0]).wait_recv()
    for copy in copies:
        copy.wait_send()


def head_gather(part):
    vmem = pl.BlockSpec(memory_space=pltpu.VMEM)
    dma = pltpu.SemaphoreType.DMA
    rows, columns = part.shape
    return pl.pallas_call(
        head_gather_kernel,
        name="head_gather",
        out_shape=jax.ShapeDtypeStruct((rows, 4 * columns), part.dtype),
        in_specs=[vmem],
        out_specs=vmem,
        scratch_shapes=[dma((3,)), dma((4,))],
        compiler_params=pltpu.CompilerParams(
            collective_id=8, has_side_effects=True, vmem_limit_bytes=32 << 20
        ),
        cost_estimate=pl.CostEstimate(flops=10**7, bytes_accessed=10 * 2**20, transcendentals=0),
    )(part)


def per_device(
    tokens,
    cotangent,
    doc_starts,
    query_weight,
    key_weight,
    value_weight,
    out_weight,
    gate_weight,
    up_weight,
    down_weight,
    input_gain,
    attn_gain,
    prenorm_gain,
    post_gain,
    query_gain,
    key_gain,
):
    row_count = tokens.shape[0]
    first_row = lax.axis_index("seq") * row_count
    own_index = first_row + jnp.arange(row_count, dtype=jnp.int32)
    own_position = doc_layout(doc_starts, own_index)[1]
    cos_table, sine_table = rope_tables(own_position, HD)
    query_scale = HD ** (-0.5)
    inputs = tokens.astype(jnp.float32)
    query_weight_all = lax.all_gather(query_weight, "head", axis=1, tiled=True)
    out_weight_all = lax.all_gather(out_weight, "head", axis=0, tiled=True)
    normed, input_back = jax.vjp(rms_norm, inputs, input_gain)
    normed_low = normed.astype(jnp.bfloat16)
    query_raw = jnp.dot(normed_low, query_weight, preferred_element_type=jnp.float32)
    key_raw = jnp.dot(normed_low, key_weight, preferred_element_type=jnp.float32)
    value_low = jnp.dot(normed_low, value_weight, preferred_element_type=jnp.float32).astype(
        jnp.bfloat16
    )

    def query_piece(source, scaling):
        return rotate(rms_norm(source, scaling), cos_table, sine_table) * query_scale

    def key_piece(source, scaling):
        return rotate(rms_norm(source, scaling), cos_table, sine_table)

    query_rows, query_back = jax.vjp(query_piece, query_raw, query_gain)
    query_low = query_rows.astype(jnp.bfloat16)
    key_rows, key_back = jax.vjp(key_piece, key_raw, key_gain)
    key_low = key_rows.astype(jnp.bfloat16)
    mix_all, lse_rows, q_all, k_all, v_all = forward_attention(
        doc_starts, query_low, key_low, value_low
    )
    attn_mix = lax.dynamic_slice_in_dim(mix_all, lax.axis_index("head") * HD, HD, 1)
    attn_out = jnp.dot(mix_all, out_weight_all, preferred_element_type=jnp.float32)
    hidden_state, attn_back = jax.vjp(residual_norm, inputs, attn_out, attn_gain)
    ffn_in, prenorm_back = jax.vjp(rms_norm, hidden_state, prenorm_gain)
    ffn_low = ffn_in.astype(jnp.bfloat16)
    gate_rows = jnp.dot(ffn_low, gate_weight, preferred_element_type=jnp.float32)
    up_rows = jnp.dot(ffn_low, up_weight, preferred_element_type=jnp.float32)
    act_rows, act_back = jax.vjp(gated_act, gate_rows, up_rows)
    act_low = act_rows.astype(jnp.bfloat16)
    ffn_out = head_sum(
        jnp.dot(act_low, down_weight, preferred_element_type=jnp.float32).astype(jnp.bfloat16), 0
    ).astype(jnp.float32)
    mixed, post_back = jax.vjp(residual_norm, hidden_state, ffn_out, post_gain)
    upstream = cotangent.astype(jnp.float32)
    hidden_grad, ffn_out_grad, post_gain_grad = post_back(upstream)
    ffn_out_low = ffn_out_grad.astype(jnp.bfloat16)
    down_weight_grad = dot_first(act_low, ffn_out_low).astype(jnp.bfloat16)
    act_grad = dot_last(ffn_out_low, down_weight)
    gate_grad, up_grad = act_back(act_grad)
    gate_low = gate_grad.astype(jnp.bfloat16)
    up_low = up_grad.astype(jnp.bfloat16)
    gate_weight_grad = dot_first(ffn_low, gate_low).astype(jnp.bfloat16)
    up_weight_grad = dot_first(ffn_low, up_low).astype(jnp.bfloat16)
    ffn_in_grad = head_sum(
        (dot_last(gate_low, gate_weight) + dot_last(up_low, up_weight)).astype(jnp.bfloat16), 1
    ).astype(jnp.float32)
    hidden_more, prenorm_gain_grad = prenorm_back(ffn_in_grad)
    hidden_grad = hidden_grad + hidden_more
    input_grad, attn_out_grad, attn_gain_grad = attn_back(hidden_grad)
    attn_out_low = attn_out_grad.astype(jnp.bfloat16)
    out_weight_grad = dot_first(attn_mix, attn_out_low)
    mix_grad = dot_last(attn_out_low, out_weight).astype(jnp.bfloat16)
    delta = jnp.sum(mix_grad.astype(jnp.float32) * attn_mix.astype(jnp.float32), axis=1)
    stats = jnp.stack([lse_rows[0], delta] + [jnp.zeros_like(delta)] * 6)
    stats = jnp.transpose(stats.reshape(8, 2, HALF), (1, 0, 2))
    down_weight_grad, gate_weight_grad, up_weight_grad, mix_grad = lax.optimization_barrier(
        (down_weight_grad, gate_weight_grad, up_weight_grad, mix_grad)
    )
    down_weight_grad, gate_weight_grad, up_weight_grad = lax.psum(
        (down_weight_grad, gate_weight_grad, up_weight_grad), "seq"
    )
    query_grad, key_value_grad = backward_attention(
        doc_starts, mix_grad, stats, q_all, k_all, v_all
    )
    key_value_grad = key_value_grad.reshape(4, 2, 128, HD)
    key_grad = key_value_grad[:, 0].reshape(row_count, HD).astype(jnp.float32)
    value_grad_low = key_value_grad[:, 1].reshape(row_count, HD)
    query_raw_grad, query_gain_part = query_back(query_grad)
    query_raw_low = query_raw_grad.astype(jnp.bfloat16)
    query_weight_grad = dot_first(normed_low, query_raw_low)
    query_raw_all = head_gather(query_raw_low)
    key_raw_grad, key_gain_grad = key_back(key_grad)
    key_raw_low = key_raw_grad.astype(jnp.bfloat16)
    key_weight_grad = dot_first(normed_low, key_raw_low)
    value_weight_grad = dot_first(normed_low, value_grad_low)
    normed_grad = (
        dot_last(query_raw_all, query_weight_all)
        + dot_last(key_raw_low, key_weight)
        + dot_last(value_grad_low, value_weight)
    )
    input_more, input_gain_grad = input_back(normed_grad)
    tokens_grad = input_grad + input_more
    query_gain_part = lax.psum(query_gain_part, "head")
    late = (
        query_weight_grad,
        key_weight_grad,
        value_weight_grad,
        out_weight_grad,
        input_gain_grad,
        attn_gain_grad,
        prenorm_gain_grad,
        post_gain_grad,
        query_gain_part,
        key_gain_grad,
    )
    late = tuple(piece.astype(jnp.bfloat16) for piece in late)
    late, down_weight_grad, gate_weight_grad, up_weight_grad = lax.optimization_barrier(
        (late, down_weight_grad, gate_weight_grad, up_weight_grad)
    )
    (
        query_weight_grad,
        key_weight_grad,
        value_weight_grad,
        out_weight_grad,
        input_gain_grad,
        attn_gain_grad,
        prenorm_gain_grad,
        post_gain_grad,
        query_gain_grad,
        key_gain_grad,
    ) = (piece.astype(jnp.float32) for piece in lax.psum(late, "seq"))
    gate_weight_grad = gate_weight_grad.astype(jnp.float32)
    up_weight_grad = up_weight_grad.astype(jnp.float32)
    down_weight_grad = down_weight_grad.astype(jnp.float32)
    return (
        mixed.astype(jnp.bfloat16),
        tokens_grad,
        query_weight_grad,
        key_weight_grad,
        value_weight_grad,
        out_weight_grad,
        gate_weight_grad,
        up_weight_grad,
        down_weight_grad,
        input_gain_grad,
        attn_gain_grad,
        prenorm_gain_grad,
        post_gain_grad,
        query_gain_grad,
        key_gain_grad,
    )


def solution(mesh):
    placed = (
        P("seq", None),
        P("seq", None),
        P(),
        P(None, "head"),
        P(),
        P(),
        P("head", None),
        P(None, "head"),
        P(None, "head"),
        P("head", None),
        P(),
        P(),
        P(),
        P(),
        P(),
        P(),
    )
    return jax.shard_map(
        per_device,
        mesh=mesh,
        in_specs=placed,
        out_specs=(
            P("seq", None),
            P("seq", None),
            P(None, "head"),
            P(),
            P(),
            P("head", None),
            P(None, "head"),
            P(None, "head"),
            P("head", None),
            P(),
            P(),
            P(),
            P(),
            P(),
            P(),
        ),
        check_vma=False,
    )
```

```python
import functools
import math

import jax
import jax.numpy as jnp
from jax import lax
from jax.experimental import pallas as pl
from jax.experimental.pallas import tpu as pltpu
from jax.sharding import PartitionSpec as P

HD = 256


EPS = 1e-06
THETA = 1000000.0
NEG = -1e30


def rms_norm(values, scaling):
    return values * lax.rsqrt(jnp.mean(values * values, axis=-1, keepdims=True) + EPS) * scaling


def doc_layout(doc_starts, token_index):
    before = doc_starts[None, :] <= token_index[:, None]
    segment = jnp.sum(before.astype(jnp.int32), axis=1)
    doc_begin = jnp.max(jnp.where(before, doc_starts[None, :], 0), axis=1)
    return (segment, token_index - doc_begin)


def rope_tables(position, head_width):
    half_width = head_width // 2
    inverse = jnp.exp(
        -math.log(THETA) * 2.0 * jnp.arange(half_width, dtype=jnp.float32) / head_width
    )
    angles = position.astype(jnp.float32)[:, None] * inverse[None, :]
    angles = jnp.concatenate([angles, angles], axis=1)
    return (jnp.cos(angles), jnp.sin(angles))


def rotate(values, cos_table, sine_table):
    half_width = values.shape[-1] // 2
    turned = jnp.concatenate([-values[..., half_width:], values[..., :half_width]], axis=-1)
    return values * cos_table + turned * sine_table


def dot_last(left_side, right_side):
    return lax.dot_general(
        left_side, right_side, (((1,), (1,)), ((), ())), preferred_element_type=jnp.float32
    )


def dot_first(left_side, right_side):
    return lax.dot_general(
        left_side, right_side, (((0,), (0,)), ((), ())), preferred_element_type=jnp.float32
    )


def residual_norm(residual, branch, scaling):
    return residual + rms_norm(branch, scaling)


def gated_act(gate_vals, up_vals):
    return jax.nn.gelu(gate_vals, approximate=True) * up_vals


MESH_ID = pl.DeviceIdType.MESH
HALF = 256
BLK = 512
LOW = jnp.bfloat16
FULL = jnp.float32
NT = (((1,), (1,)), ((), ()))


def place():
    s = lax.axis_index("seq")
    return s // 8, (s // 2) % 4, s % 2, lax.axis_index("head")


def at(x, y, c, z):
    return ((x % 4) * 8 + (y % 4) * 2 + c, z % 4)


def greet(peers):
    barrier = pltpu.get_barrier_semaphore()
    for peer in peers:
        pl.semaphore_signal(barrier, inc=1, device_id=peer, device_id_type=MESH_ID)
    pl.semaphore_wait(barrier, len(peers))


def remote(src, dst, send_sem, recv_sem, peer):
    return pltpu.make_async_remote_copy(
        src_ref=src,
        dst_ref=dst,
        send_sem=send_sem,
        recv_sem=recv_sem,
        device_id=peer,
        device_id_type=MESH_ID,
    )


def rows_at(ref, start, size):
    return ref.at[pl.ds(pl.multiple_of(start, 16), size)]


class RingGather:
    def __init__(self, view, me, plus, minus, sems, ring, source=None):
        send, recv = sems

        def near(rel, half):
            return view((me + rel) % 4, half)

        own = source or (lambda half: near(0, half))
        plan = (
            (own(0), near(0, 0), plus),
            (own(1), near(0, 1), plus),
            (near(3, 0), near(3, 0), plus),
            (own(0), near(0, 0), minus),
            (own(1), near(0, 1), minus),
            (near(1, 1), near(1, 1), minus),
        )
        self.copies = [
            remote(src, dst, send.at[ring, k], recv.at[ring, k], peer) for k, (src, dst, peer) in enumerate(plan)
        ]

    def own(self, half):
        self.copies[half].start()
        self.copies[3 + half].start()

    def forward(self):
        self.copies[0].wait_recv()
        self.copies[2].start()
        self.copies[4].wait_recv()
        self.copies[5].start()

    def near(self):
        self.copies[1].wait_recv()
        self.copies[3].wait_recv()

    def far(self):
        self.copies[2].wait_recv()
        self.copies[5].wait_recv()

    def drain(self):
        for copy in self.copies:
            copy.wait_send()


class RingReduce:
    def __init__(self, view, passing, got, plus, minus, sems, ring):
        send, recv = sems
        self.view, self.passing, self.got = view, passing, got
        plan = (
            (view(2, 0), passing(0), minus),
            (view(2, 1), passing(1), plus),
            (view(3, 1), got(0, 1), minus),
            (view(1, 0), got(1, 0), plus),
            (passing(0), got(0, 0), minus),
            (passing(1), got(1, 1), plus),
        )
        self.copies = [
            remote(src, dst, send.at[ring, k], recv.at[ring, k], peer) for k, (src, dst, peer) in enumerate(plan)
        ]

    def start(self, *numbers):
        for k in numbers or (0, 1, 2, 3):
            self.copies[k].start()

    def relay(self):
        for half, rel in ((0, 3), (1, 1)):
            self.copies[half].wait_recv()
            land, term = self.passing(half), self.view(rel, half)
            land[...] = (land[...].astype(FULL) + term[...].astype(FULL)).astype(LOW)
            self.copies[4 + half].start()

    def finish(self):
        for k in (2, 3, 4, 5):
            self.copies[k].wait_recv()

    def arrived(self, half):
        return self.got(0, half)[...].astype(FULL) + self.got(1, half)[...].astype(FULL)

    def drain(self):
        for copy in self.copies:
            copy.wait_send()


def tile_first(i, x, c):
    column = jnp.where(i % 2 == 1, 3 - x, x)
    return BLK * (8 * column + 2 * (i // 2) + c) + HALF * (i % 2)


def begin_of(token, starts_ref):
    begin = jnp.zeros_like(token)
    for n in range(starts_ref.shape[0]):
        start = starts_ref[n]
        begin = jnp.where(start <= token, start, begin)
    return begin


def attn_forward(
    starts_ref, q_ref, k_ref, v_ref,
    mix_ref, lse_ref, qg_ref, kg_ref, vg_ref,
    acc, lacc, osend, opass, ogot, lsend, lrecv, hsend, lhsend,
    rs, rr, sib_s, sib_r, l_s, l_r, sw_s, sw_r,
):
    x, y, c, z = place()
    xp, xm, yp, ym = at(x + 1, y, c, z), at(x + 3, y, c, z), at(x, y + 1, c, z), at(x, y + 3, c, z)
    zp, zm, y2 = at(x, y, c, z + 1), at(x, y, c, z + 3), at(x, y + 2, c, z)
    sibling, partner = at(x, y, 1 - c, z), at(3 - x, y, c, z)
    greet([partner, sibling, xp, xm, yp, ym, y2, zp, zm])
    copies = []

    def go(copy):
        copy.start()
        copies.append(copy)

    q_low, q_high = q_ref.at[pl.ds(0, HALF)], q_ref.at[pl.ds(HALF, HALF)]
    swap = remote(q_high, qg_ref.at[2 * y + 1], sw_s.at[0], sw_r.at[0], partner)
    go(swap)

    def kv_view(index, half):
        return (kg_ref, vg_ref)[half].at[2 * index + c]

    kv = RingGather(kv_view, x, xp, xm, (rs, rr), 0, lambda half: (k_ref, v_ref)[half])
    kv.own(0)
    kv.own(1)
    qs = RingGather(
        lambda index, half: qg_ref.at[2 * index + half], y, yp, ym, (rs, rr), 1,
        lambda half: q_low if half == 0 else qg_ref.at[2 * y + 1],
    )
    qs.own(0)

    def pass_on(index, half, source=None):
        block = kv_view(index, half)
        return remote(block if source is None else source, block, sib_s.at[index, half], sib_r.at[index, half], sibling)

    for half, source in enumerate((k_ref, v_ref)):
        go(pass_on(x, half, source))
    qg_ref[2 * y] = q_ref[0:HALF, :]
    kg_ref[2 * x + c] = k_ref[...]
    vg_ref[2 * x + c] = v_ref[...]
    acc[...] = jnp.zeros_like(acc)
    lacc[...] = jnp.zeros_like(lacc)
    swap.wait_recv()
    qs.own(1)
    kv.forward()
    qs.forward()
    kv.near()
    for rel in (1, 3):
        for half in range(2):
            go(pass_on((x + rel) % 4, half))
    qs.near()
    qs.far()

    def chunk(i, first_q, pair, first_k, masked):
        queries = qg_ref[i]
        if masked:
            token = first_q + lax.broadcasted_iota(jnp.int32, (HALF, 1), 0)
            begin = begin_of(token, starts_ref)
        total = None
        sums = None
        for cc in range(2):
            keys, values = kg_ref[pair * 2 + cc], vg_ref[pair * 2 + cc]
            scores = lax.dot_general(queries, keys, NT, preferred_element_type=FULL)
            exps = jnp.exp(scores)
            if masked:
                key_index = first_k + cc * BLK + lax.broadcasted_iota(jnp.int32, (1, BLK), 1)
                exps = jnp.where((key_index <= token) & (key_index >= begin), exps, 0.0)
            part = jnp.dot(exps.astype(LOW), values, preferred_element_type=FULL)
            total = part if total is None else total + part
            for n in range(BLK // 128):
                piece = exps[:, n * 128 : (n + 1) * 128]
                sums = piece if sums is None else sums + piece
        acc[i] = acc[i] + total
        lacc[i] = lacc[i] + sums

    for rel in (0, 1, 3, 2):
        pair = (x + rel) % 4
        if rel == 2:
            kv.far()
            for half in range(2):
                go(pass_on(pair, half))
        for half in range(2):
            pass_on(pair, half).wait_recv()
        first_k = 4096 * pair + 1024 * y

        def visit(i, carry):
            first_q = tile_first(i, x, c)
            some = first_k <= first_q + (HALF - 1)
            full = (first_k + 1023 <= first_q) & (first_k > 0) & (first_q < 31 * BLK)

            @pl.when(full)
            def _():
                chunk(i, first_q, pair, first_k, False)

            @pl.when(some & jnp.logical_not(full))
            def _():
                chunk(i, first_q, pair, first_k, True)

            return carry

        lax.fori_loop(0, 8, visit, 0)

    def cast(i, carry):
        osend[i] = acc[i].astype(LOW)
        row = jnp.sum(jnp.transpose(lacc[i]), axis=0, keepdims=True)
        lsend[i] = jnp.broadcast_to(row, (8, HALF))
        return carry

    lax.fori_loop(0, 8, cast, 0)
    numer = RingReduce(
        lambda rel, half: osend.at[2 * ((y + rel) % 4) + half],
        lambda half: opass.at[half],
        lambda side, half: ogot.at[side, half],
        yp, ym, (rs, rr), 2,
    )
    numer.start()

    def sums_to(rel, peer):
        index = (y + rel) % 4
        return remote(lsend.at[pl.ds(2 * index, 2)], lrecv.at[y], l_s.at[rel - 1], l_r.at[y], peer)

    for rel, peer in ((1, yp), (3, ym), (2, y2)):
        go(sums_to(rel, peer))
    lrecv[y] = lsend[pl.ds(2 * y, 2)]
    numer.relay()
    for rel in (1, 3, 2):
        remote(lsend.at[pl.ds(0, 2)], lrecv.at[(y + rel) % 4], l_s.at[0], l_r.at[(y + rel) % 4], sibling).wait_recv()
    numer.finish()

    def mix_view(index, half):
        return mix_ref.at[pl.ds(half * HALF, HALF), pl.ds(pl.multiple_of(index * HD, HD), HD)]

    mixes = RingGather(mix_view, z, zp, zm, (rs, rr), 3)
    returns = (
        remote(hsend, mix_view(z, 1), sw_s.at[1], sw_r.at[1], partner),
        remote(lhsend, lse_ref.at[1], sw_s.at[2], sw_r.at[2], partner),
    )
    for half in (1, 0):
        denom = sum(lrecv[n, half] for n in range(4))
        total = osend[2 * y + half].astype(FULL) + numer.arrived(half)
        inverse = jnp.transpose(jnp.broadcast_to(1.0 / denom[0:1, :], (128, HALF)))
        scaled = (total * jnp.concatenate([inverse, inverse], axis=1)).astype(LOW)
        if half == 1:
            hsend[...] = scaled
            lhsend[...] = jnp.log(denom)
            for copy in returns:
                go(copy)
        else:
            mix_view(z, 0)[...] = scaled
            lse_ref[0] = jnp.log(denom)
    mixes.own(0)
    for copy in returns:
        copy.wait_recv()
    mixes.own(1)
    mixes.forward()
    mixes.near()
    mixes.far()
    for ring in (kv, qs, numer, mixes):
        ring.drain()
    for copy in copies:
        copy.wait_send()


VMEM = pl.BlockSpec(memory_space=pltpu.VMEM)
SMEM = pl.BlockSpec(memory_space=pltpu.SMEM)
ANY = pl.BlockSpec(memory_space=pl.ANY)


def dma(*shape):
    return pltpu.SemaphoreType.DMA(shape)


def shape(dtype, *dims):
    return jax.ShapeDtypeStruct(dims, dtype)


def vmem(dtype, *dims):
    return pltpu.VMEM(dims, dtype)


def params(number, mebibytes):
    return pltpu.CompilerParams(collective_id=number, has_side_effects=True, vmem_limit_bytes=mebibytes << 20)


def cost(gflops):
    return pl.CostEstimate(flops=gflops * 10**9, bytes_accessed=20 * 2**20, transcendentals=0)


def forward_attention(doc_starts, query, key, value):
    return pl.pallas_call(
        attn_forward,
        name="attn_forward",
        out_shape=[
            shape(LOW, BLK, 4 * HD),
            shape(FULL, 2, 8, HALF),
            shape(LOW, 8, HALF, HD),
            shape(LOW, 8, BLK, HD),
            shape(LOW, 8, BLK, HD),
        ],
        in_specs=[SMEM] + [VMEM] * 3,
        out_specs=[VMEM] * 5,
        scratch_shapes=[
            vmem(FULL, 8, HALF, HD),
            vmem(FULL, 8, HALF, 128),
            vmem(LOW, 8, HALF, HD),
            vmem(LOW, 2, HALF, HD),
            vmem(LOW, 2, 2, HALF, HD),
            vmem(FULL, 8, 8, HALF),
            vmem(FULL, 4, 2, 8, HALF),
            vmem(LOW, HALF, HD),
            vmem(FULL, 8, HALF),
            dma(4, 6), dma(4, 6), dma(4, 2), dma(4, 2), dma(3), dma(4), dma(3), dma(3),
        ],
        compiler_params=params(1, 40),
        cost_estimate=cost(6),
    )(doc_starts, query, key, value)


ROWS = 2560
SIDE = ROWS // 2
PIECE = SIDE // 4
WINDOW = PIECE // 4
CUTS = (0, 448, 896, 1280, 1728, 2144, 2560)


def ffn_grads_kernel(
    part_ref, ffn_ref, out_grad_ref, gate_ref, up_ref, act_ref,
    sum_ref, piece_a_ref, piece_b_ref, rest_ref,
    left, right, sib_send, sib_recv, mine, pass_ab, got_ab, z_pass, z_got,
    in_sem, sib_s, sib_r, rs, rr,
):
    x, y, c, z = place()
    xp, xm, yp, ym = at(x + 1, y, c, z), at(x + 3, y, c, z), at(x, y + 1, c, z), at(x, y + 3, c, z)
    zp, zm, sibling = at(x, y, c, z + 1), at(x, y, c, z + 3), at(x, y, 1 - c, z)
    hidden = gate_ref.shape[0]
    loads = [pltpu.make_async_copy(out_grad_ref, right.at[1], in_sem.at[0])]
    loads.append(pltpu.make_async_copy(ffn_ref, right.at[0], in_sem.at[1]))
    for n, ref in enumerate((gate_ref, up_ref, act_ref)):
        loads.append(pltpu.make_async_copy(ref, left.at[pl.ds(n * hidden, hidden)], in_sem.at[2 + n]))
    for load in loads:
        load.start()
    greet([xp, xm, yp, ym, zp, zm, sibling])
    rows = part_ref.shape[0] // 4

    zs = RingReduce(
        lambda rel, half: rows_at(part_ref, ((z + rel) % 4) * rows + half * (rows // 2), rows // 2),
        lambda half: z_pass.at[half],
        lambda side, half: z_got.at[side, half],
        zp, zm, (rs, rr), 0,
    )
    zg = RingGather(
        lambda index, half: rows_at(sum_ref, index * rows + half * (rows // 2), rows // 2),
        z, zp, zm, (rs, rr), 1,
    )
    zs.start()
    for load in loads:
        load.wait()

    def product(core, n, target, added):
        first, size = CUTS[n], CUTS[n + 1] - CUTS[n]
        lhs = left[pl.ds(pl.multiple_of(ROWS * core + first, 16), size), :]
        which = jnp.where(n >= 2, core, 0)
        width = right.shape[2] // 3
        for k in range(3):
            columns = pl.ds(k * width, width)
            tile = jnp.dot(lhs, right[which, :, columns], preferred_element_type=FULL)
            if added is not None:
                tile = tile + added[pl.ds(first, size), columns].astype(FULL)
            target[pl.ds(first, size), columns] = tile.astype(LOW)

    def to_sibling(n):
        span = pl.ds(CUTS[n], CUTS[n + 1] - CUTS[n])
        return remote(sib_send.at[span], sib_recv.at[span], sib_s.at[n], sib_r.at[n], sibling)

    count = len(CUTS) - 1
    for n in range(count):
        product(1 - c, n, sib_send, None)
        to_sibling(n).start()
        if n == count // 2 - 1:
            zs.relay()
    zs.finish()
    for half in range(2):
        own = pl.ds(pl.multiple_of(z * rows + half * (rows // 2), 16), rows // 2)
        sum_ref[own, :] = (part_ref[own, :].astype(FULL) + zs.arrived(half)).astype(LOW)
        zg.own(half)

    def side_ring(h, me, plus, minus):
        return RingReduce(
            lambda rel, half: rows_at(mine, SIDE * h + PIECE * ((me + rel) % 4) + half * (PIECE // 2), PIECE // 2),
            lambda half: pass_ab.at[h, half],
            lambda side, half: got_ab.at[h, side, half],
            plus, minus, (rs, rr), 2 + h,
        )

    rings = (side_ring(0, x, xp, xm), side_ring(1, y, yp, ym))
    for n in range(count):
        to_sibling(n).wait_recv()
        product(c, n, mine, sib_recv)
        if n == count // 2 - 1:
            rings[0].start()
            zg.forward()
    rings[1].start()
    rest = jnp.dot(left[2 * ROWS :, :], right[1], preferred_element_type=FULL)
    rest_ref[...] = rest.astype(LOW)
    for ring in rings:
        ring.relay()
    zg.near()
    zg.far()
    for h, (ring, me, out) in enumerate(((rings[0], x, piece_a_ref), (rings[1], y, piece_b_ref))):
        ring.finish()
        for half in range(2):
            size = PIECE // 2
            own = mine[pl.ds(pl.multiple_of(SIDE * h + PIECE * me + half * size, 16), size), :]
            out[pl.ds(half * size, size), :] = (own.astype(FULL) + ring.arrived(half)).astype(LOW)
    for ring in (zs, zg) + rings:
        ring.drain()
    for n in range(count):
        to_sibling(n).wait_send()


def ffn_grads(part, ffn_low, ffn_out_low, gate_t, up_t, act_t):
    rows, width = part.shape
    hidden = gate_t.shape[0]
    return pl.pallas_call(
        ffn_grads_kernel,
        name="ffn_grads",
        out_shape=[
            shape(LOW, rows, width),
            shape(LOW, PIECE, width),
            shape(LOW, PIECE, width),
            shape(LOW, 3 * hidden - 2 * ROWS, width),
        ],
        in_specs=[VMEM] + [ANY] * 5,
        out_specs=[VMEM] * 4,
        scratch_shapes=[
            vmem(LOW, 3 * hidden, rows),
            vmem(LOW, 2, rows, width),
            vmem(LOW, ROWS, width),
            vmem(LOW, ROWS, width),
            vmem(LOW, ROWS, width),
            vmem(LOW, 2, 2, PIECE // 2, width),
            vmem(LOW, 2, 2, 2, PIECE // 2, width),
            vmem(LOW, 2, rows // 8, width),
            vmem(LOW, 2, 2, rows // 8, width),
            dma(5), dma(6), dma(6), dma(4, 6), dma(4, 6),
        ],
        compiler_params=params(4, 56),
        cost_estimate=cost(6),
    )(part, ffn_low, ffn_out_low, gate_t, up_t, act_t)


def attn_backward(
    starts_ref, do_ref, stat_ref, q_in, k_in, v_in, piece_a_ref, piece_b_ref, raw_ref, cos_ref, sin_ref, gain_ref,
    draw_ref, dgain_ref, dkv_ref, big_ref,
    dog, statg, dqacc, dkacc, dvacc, ktbuf, sibsend, sibrecv, kvsrc, kvpass, kvgot,
    dqsend, dqpass, dqgot, dqback, dqhigh, zpart, zpass, zgot, gaing, winpass, wingot, full_a, full_b,
    rs, rr, st_s, st_r, sw_s, sw_r, sib_s, sib_r, gn_s, gn_r, sf_s, sf_r, own_sem,
):
    x, y, c, z = place()
    xp, xm, yp, ym = at(x + 1, y, c, z), at(x + 3, y, c, z), at(x, y + 1, c, z), at(x, y + 3, c, z)
    zp, zm, y2, z2 = at(x, y, c, z + 1), at(x, y, c, z + 3), at(x, y + 2, c, z), at(x, y, c, z + 2)
    sibling, partner = at(x, y, 1 - c, z), at(3 - x, y, c, z)
    greet([partner, sibling, xp, xm, yp, ym, y2, zp, zm, z2])
    copies = []

    def go(copy):
        copy.start()
        copies.append(copy)

    sems = (rs, rr)
    do_low, do_high = do_ref.at[pl.ds(0, HALF)], do_ref.at[pl.ds(HALF, HALF)]
    swaps = (
        remote(do_high, dog.at[2 * y + 1], sw_s.at[0], sw_r.at[0], partner),
        remote(stat_ref.at[1], statg.at[2 * y + 1], sw_s.at[1], sw_r.at[1], partner),
    )
    for copy in swaps:
        go(copy)
    dos = RingGather(
        lambda index, half: dog.at[2 * index + half], y, yp, ym, sems, 0,
        lambda half: do_low if half == 0 else dog.at[2 * y + 1],
    )
    dos.own(0)

    def stats_to(upper, rel, peer):
        slot = 2 * y + upper
        source = statg.at[slot] if upper else stat_ref.at[0]
        return remote(source, statg.at[slot], st_s.at[upper, rel - 1], st_r.at[slot], peer)

    y_peers = ((1, yp), (3, ym), (2, y2))
    for rel, peer in y_peers:
        go(stats_to(0, rel, peer))

    cut = (48, WINDOW - 48)

    def window(ref, index, half):
        return rows_at(ref, WINDOW * index + 48 * half, cut[half])

    sides = ((piece_a_ref, full_a, y, yp, ym), (piece_b_ref, full_b, x, xp, xm))
    reduces, gathers = [], []
    for h, (piece, full, me, plus, minus) in enumerate(sides):
        reduces.append(
            RingReduce(
                lambda rel, half, piece=piece, me=me: window(piece, (me + rel) % 4, half),
                lambda half, h=h: winpass.at[h, pl.ds(48 * half, cut[half])],
                lambda side, half, h=h: wingot.at[h, side, pl.ds(48 * half, cut[half])],
                plus, minus, sems, 1 + h,
            )
        )
        gathers.append(
            RingGather(lambda index, half, full=full: window(full, index, half), me, plus, minus, sems, 3 + h)
        )
        reduces[h].start()

    def big_view(core, h, index, half):
        return rows_at(big_ref, ROWS * core + SIDE * h + PIECE * index + half * (PIECE // 2), PIECE // 2)

    owners = ((x, xp, xm), (y, yp, ym))
    pieces = [
        RingGather(
            lambda index, half, h=h: big_view(c, h, index, half), me, plus, minus, sems, 5 + h,
            lambda half, h=h: sides[h][1].at[pl.ds(half * (PIECE // 2), PIECE // 2)],
        )
        for h, (me, plus, minus) in enumerate(owners)
    ]

    def piece_to_sibling(h, index, half, source=None):
        block = big_view(c, h, index, half)
        return remote(block if source is None else source, block, sf_s.at[h, index, half], sf_r.at[h, index, half], sibling)

    def keep(h, half):
        source = sides[h][1].at[pl.ds(half * (PIECE // 2), PIECE // 2)]
        return pltpu.make_async_copy(source, big_view(c, h, owners[h][0], half), own_sem.at[h, half])

    dog[2 * y] = do_ref[0:HALF, :]
    statg[2 * y] = stat_ref[0]
    dqacc[...] = jnp.zeros_like(dqacc)
    for copy in swaps:
        copy.wait_recv()
    dos.own(1)
    for rel, peer in y_peers:
        go(stats_to(1, rel, peer))
    dos.forward()
    dos.near()
    dos.far()
    for upper in range(2):
        for rel, peer in y_peers:
            slot = 2 * ((y + rel) % 4) + upper
            remote(stat_ref.at[0], statg.at[slot], st_s.at[0, 0], st_r.at[slot], sibling).wait_recv()

    def windows_relayed():
        for ring in reduces:
            ring.relay()

    def windows_summed():
        for ring, gather, (piece, full, me, _, _) in zip(reduces, gathers, sides):
            ring.finish()
            for half in range(2):
                total = window(piece, me, half)[...].astype(FULL) + ring.arrived(half)
                window(full, me, half)[...] = total.astype(LOW)
                gather.own(half)

    def windows_forwarded():
        for gather in gathers:
            gather.forward()

    def pieces_sent():
        for h, gather in enumerate(gathers):
            gather.near()
            gather.far()
            for half in range(2):
                pieces[h].own(half)
                source = sides[h][1].at[pl.ds(half * (PIECE // 2), PIECE // 2)]
                go(piece_to_sibling(h, owners[h][0], half, source))
                keep(h, half).start()

    def pieces_forwarded():
        for ring in pieces:
            ring.forward()

    def pieces_near():
        for h, ring in enumerate(pieces):
            ring.near()
            for rel in (1, 3):
                for half in range(2):
                    go(piece_to_sibling(h, (owners[h][0] + rel) % 4, half))

    def pieces_far():
        for h, ring in enumerate(pieces):
            ring.far()
            for half in range(2):
                go(piece_to_sibling(h, (owners[h][0] + 2) % 4, half))

    def tile(i, first_q, slot, first_k, masked):
        queries, out_grads = q_in[i], dog[i]
        lse, delta = statg[i, 0:1, :], statg[i, 1:2, :]
        if masked:
            token = first_q + lax.broadcasted_iota(jnp.int32, (1, HALF), 1)
            begin = begin_of(token, starts_ref)
        dq_part = None
        for n in range(2):
            rows = pl.ds(n * 256, 256)
            keys, values = k_in[slot, rows], v_in[slot, rows]
            scores = lax.dot_general(keys, queries, NT, preferred_element_type=FULL)
            prob_grad = lax.dot_general(values, out_grads, NT, preferred_element_type=FULL)
            soft = jnp.exp(scores - lse)
            if masked:
                key_index = first_k + n * 256 + lax.broadcasted_iota(jnp.int32, (256, 1), 0)
                soft = jnp.where((key_index <= token) & (key_index >= begin), soft, 0.0)
            score_grad = (soft * (prob_grad - delta)).astype(LOW)
            dvacc[rows, :] += jnp.dot(soft.astype(LOW), out_grads, preferred_element_type=FULL)
            dkacc[rows, :] += jnp.dot(score_grad, queries, preferred_element_type=FULL)
            part = jnp.dot(ktbuf[:, n * 256 : (n + 1) * 256], score_grad, preferred_element_type=FULL)
            dq_part = part if dq_part is None else dq_part + part
        dqacc[i] = dqacc[i] + dq_part

    place_of = {2: 0, 1: 1, 3: 2}
    kvs = RingReduce(
        lambda rel, half: kvsrc.at[place_of[rel], half],
        lambda half: kvpass.at[half],
        lambda side, half: kvgot.at[side, half],
        xp, xm, sems, 7,
    )
    between = {
        (0, 0): windows_relayed,
        (0, 1): windows_summed,
        (1, 0): windows_forwarded,
        (1, 1): pieces_sent,
        (2, 1): pieces_forwarded,
        (3, 0): pieces_near,
    }
    for step, rel in enumerate((2, 1, 3, 0)):
        pair = (x + rel) % 4
        for turn in range(2):
            if (step, turn) in between:
                between[step, turn]()
            cc = 1 - c if turn == 0 else c
            slot = pair * 2 + cc
            first_k = 4096 * pair + 1024 * y + BLK * cc
            dkacc[...] = jnp.zeros_like(dkacc)
            dvacc[...] = jnp.zeros_like(dvacc)
            ktbuf[...] = jnp.transpose(k_in[slot])

            def visit(i, carry):
                first_q = tile_first(i, x, c)
                some = first_k <= first_q + (HALF - 1)
                full = (first_k + BLK - 1 <= first_q) & (first_k > 0) & (first_q < 31 * BLK)

                @pl.when(full)
                def _():
                    tile(i, first_q, slot, first_k, False)

                @pl.when(some & jnp.logical_not(full))
                def _():
                    tile(i, first_q, slot, first_k, True)

                return carry

            lax.fori_loop(0, 8, visit, 0)
            to_sibling = remote(sibsend.at[step], sibrecv.at[step], sib_s.at[step], sib_r.at[step], sibling)
            if turn == 0:
                sibsend[step, 0] = dkacc[...].astype(LOW)
                sibsend[step, 1] = dvacc[...].astype(LOW)
                go(to_sibling)
            else:
                to_sibling.wait_recv()
                for half, ref in enumerate((dkacc, dvacc)):
                    both = ref[...] + sibrecv[step, half].astype(FULL)
                    if rel == 0:
                        ref[...] = both
                    else:
                        kvsrc[place_of[rel], half] = both.astype(LOW)
                if rel == 2:
                    kvs.start(0, 1)
                elif rel == 1:
                    kvs.start(3)
                elif rel == 3:
                    kvs.start(2)
                    kvs.relay()

    def cast(i, carry):
        dqsend[i] = jnp.transpose(dqacc[i]).astype(LOW)
        return carry

    lax.fori_loop(0, 8, cast, 0)
    dqs = RingReduce(
        lambda rel, half: dqsend.at[2 * ((y + rel) % 4) + half],
        lambda half: dqpass.at[half],
        lambda side, half: dqgot.at[side, half],
        yp, ym, sems, 8,
    )
    dqs.start()
    kvs.finish()
    zrows = BLK // 4
    for n in range(4):
        for half, ref in enumerate((dkacc, dvacc)):
            rows = pl.ds(n * zrows, zrows)
            whole = ref[rows, :] + kvgot[0, half, rows, :].astype(FULL) + kvgot[1, half, rows, :].astype(FULL)
            zpart[n, half] = whole.astype(LOW)
    zs = RingReduce(
        lambda rel, half: zpart.at[(z + rel) % 4, half],
        lambda half: zpass.at[half],
        lambda side, half: zgot.at[side, half],
        zp, zm, sems, 9,
    )
    zg = RingGather(lambda index, half: dkv_ref.at[index, half], z, zp, zm, sems, 10)
    zs.start()
    dqs.relay()
    zs.relay()
    dqs.finish()
    back = remote(dqback, dqhigh, sw_s.at[2], sw_r.at[2], partner)
    dqback[...] = (dqsend[2 * y + 1].astype(FULL) + dqs.arrived(1)).astype(LOW)
    go(back)

    draws = RingGather(
        lambda index, half: draw_ref.at[pl.ds(half * HALF, HALF), pl.ds(pl.multiple_of(index * HD, HD), HD)],
        z, zp, zm, sems, 11,
    )
    gain = gain_ref[...]
    gain_grad = None
    for half in range(2):
        if half == 0:
            grad = dqsend[2 * y].astype(FULL) + dqs.arrived(0)
        else:
            back.wait_recv()
            grad = dqhigh[...].astype(FULL)
        grad = grad * (HD**-0.5)
        rows = pl.ds(half * HALF, HALF)
        cosine, sine = cos_ref[rows, :], sin_ref[rows, :]
        first, second = grad[:, : HD // 2], grad[:, HD // 2 :]
        turned = jnp.concatenate([first * cosine + second * sine, second * cosine - first * sine], axis=1)
        raw = raw_ref[rows, :]
        inverse = lax.rsqrt(jnp.mean(raw * raw, axis=1, keepdims=True) + EPS)
        unit = raw * inverse
        scaled = gain * turned
        raw_grad = inverse * (scaled - unit * jnp.mean(unit * scaled, axis=1, keepdims=True))
        draw_ref[rows, pl.ds(pl.multiple_of(z * HD, HD), HD)] = raw_grad.astype(LOW)
        draws.own(half)
        part = jnp.sum(unit * turned, axis=0, keepdims=True)
        gain_grad = part if gain_grad is None else gain_grad + part
    gaing[z] = jnp.broadcast_to(gain_grad, (8, HD))
    for n, peer in enumerate((zp, zm, z2)):
        go(remote(gaing.at[z], gaing.at[z], gn_s.at[n], gn_r.at[z], peer))

    zs.finish()
    for half in range(2):
        dkv_ref[z, half] = (zpart[z, half].astype(FULL) + zs.arrived(half)).astype(LOW)
        zg.own(half)
    pieces_far()
    draws.forward()
    zg.forward()
    draws.near()
    zg.near()
    draws.far()
    zg.far()
    for rel in (1, 3, 2):
        other = (z + rel) % 4
        remote(gaing.at[z], gaing.at[other], gn_s.at[0], gn_r.at[other], sibling).wait_recv()
    dgain_ref[...] = sum(gaing[n] for n in range(4))
    for h in range(2):
        for half in range(2):
            keep(h, half).wait()
            for n in range(4):
                piece_to_sibling(h, n, half).wait_recv()
    for ring in [dos, kvs, dqs, zs, zg, draws] + reduces + gathers + pieces:
        ring.drain()
    for copy in copies:
        copy.wait_send()


def backward_attention(
    doc_starts, out_grad, stats, q_all, k_all, v_all, piece_a, piece_b, query_raw, cosine, sine, query_gain
):
    width = piece_a.shape[1]
    return pl.pallas_call(
        attn_backward,
        name="attn_backward",
        out_shape=[
            shape(LOW, BLK, 4 * HD),
            shape(FULL, 8, HD),
            shape(LOW, 4, 2, BLK // 4, HD),
            shape(LOW, 2 * ROWS + 64, width),
        ],
        in_specs=[SMEM] + [VMEM] * 11,
        out_specs=[VMEM] * 3 + [ANY],
        scratch_shapes=[
            vmem(LOW, 8, HALF, HD),
            vmem(FULL, 8, 8, HALF),
            vmem(FULL, 8, HD, HALF),
            vmem(FULL, BLK, HD),
            vmem(FULL, BLK, HD),
            vmem(LOW, HD, BLK),
            vmem(LOW, 4, 2, BLK, HD),
            vmem(LOW, 4, 2, BLK, HD),
            vmem(LOW, 3, 2, BLK, HD),
            vmem(LOW, 2, BLK, HD),
            vmem(LOW, 2, 2, BLK, HD),
            vmem(LOW, 8, HALF, HD),
            vmem(LOW, 2, HALF, HD),
            vmem(LOW, 2, 2, HALF, HD),
            vmem(LOW, HALF, HD),
            vmem(LOW, HALF, HD),
            vmem(LOW, 4, 2, BLK // 4, HD),
            vmem(LOW, 2, BLK // 4, HD),
            vmem(LOW, 2, 2, BLK // 4, HD),
            vmem(FULL, 4, 8, HD),
            vmem(LOW, 2, WINDOW, width),
            vmem(LOW, 2, 2, WINDOW, width),
            vmem(LOW, PIECE, width),
            vmem(LOW, PIECE, width),
            dma(12, 6), dma(12, 6), dma(2, 3), dma(8), dma(3), dma(3), dma(4), dma(4), dma(3), dma(4),
            dma(2, 4, 2), dma(2, 4, 2), dma(2, 2),
        ],
        compiler_params=params(2, 48),
        cost_estimate=cost(15),
    )(doc_starts, out_grad, stats, q_all, k_all, v_all, piece_a, piece_b, query_raw, cosine, sine, query_gain)


def head_sum_kernel(part_ref, out_ref, passing, got, rs, rr):
    x, y, c, z = place()
    zp, zm = at(x, y, c, z + 1), at(x, y, c, z + 3)
    greet([zp, zm])
    rows = part_ref.shape[0] // 4
    zs = RingReduce(
        lambda rel, half: rows_at(part_ref, ((z + rel) % 4) * rows + half * (rows // 2), rows // 2),
        lambda half: passing.at[half],
        lambda side, half: got.at[side, half],
        zp, zm, (rs, rr), 0,
    )
    zg = RingGather(
        lambda index, half: rows_at(out_ref, index * rows + half * (rows // 2), rows // 2),
        z, zp, zm, (rs, rr), 1,
    )
    zs.start()
    zs.relay()
    zs.finish()
    for half in range(2):
        own = pl.ds(pl.multiple_of(z * rows + half * (rows // 2), 16), rows // 2)
        out_ref[own, :] = (part_ref[own, :].astype(FULL) + zs.arrived(half)).astype(LOW)
        zg.own(half)
    zg.forward()
    zg.near()
    zg.far()
    zs.drain()
    zg.drain()


def head_sum(part):
    rows, columns = part.shape
    return pl.pallas_call(
        head_sum_kernel,
        name="head_sum",
        out_shape=shape(LOW, rows, columns),
        in_specs=[VMEM],
        out_specs=VMEM,
        scratch_shapes=[vmem(LOW, 2, rows // 8, columns), vmem(LOW, 2, 2, rows // 8, columns), dma(2, 6), dma(2, 6)],
        compiler_params=params(3, 32),
        cost_estimate=cost(1),
    )(part)


def late_sum_kernel(part_ref, out_ref, core_recv, half, plane_recv, c_ssem, c_rsem, p_ssem, p_rsem, g_ssem, g_rsem, f_ssem, f_rsem):
    x, y, c, z = place()
    sibling = at(x, y, 1 - c, z)
    shifts = [(a, b) for a in range(4) for b in range(4) if (a, b) != (0, 0)]
    peers = [at(x + a, y + b, c, z) for a, b in shifts]
    greet(peers + [sibling])
    first = pl.multiple_of(2 * c, 2)
    copies = []

    def core_copy(m):
        return remote(part_ref.at[2 * (1 - c) + m], core_recv.at[m], c_ssem.at[m], c_rsem.at[m], sibling)

    for m in range(2):
        copies.append(core_copy(m))
        copies[-1].start()
    for m in range(2):
        core_copy(m).wait_recv()

        def add(r, carry):
            both = part_ref[first + m, r].astype(jnp.float32) + core_recv[m, r].astype(jnp.float32)
            half[m * 8 + r] = both.astype(jnp.bfloat16)
            return carry

        lax.fori_loop(0, 8, add, 0)
    me = x * 4 + y
    for n, (a, b) in enumerate(shifts):
        target = ((x + a) % 4) * 4 + (y + b) % 4
        copies.append(remote(half.at[target], plane_recv.at[me], p_ssem.at[n], p_rsem.at[me], peers[n]))
        copies[-1].start()
    total = half[me].astype(jnp.float32)
    for n, (a, b) in enumerate(shifts):
        source = ((x + a) % 4) * 4 + (y + b) % 4
        remote(half.at[0], plane_recv.at[source], p_ssem.at[0], p_rsem.at[source], sibling).wait_recv()
        total = total + plane_recv[source].astype(jnp.float32)

    def piece(owner):
        return out_ref.at[first + owner // 8, owner % 8]

    out_ref[first + me // 8, me % 8] = total.astype(jnp.bfloat16)
    for n in range(15):
        copies.append(remote(piece(me), piece(me), g_ssem.at[n], g_rsem.at[me], peers[n]))
        copies[-1].start()
    copies.append(remote(piece(me), piece(me), f_ssem.at[me], f_rsem.at[me], sibling))
    copies[-1].start()
    for a, b in shifts:
        source = ((x + a) % 4) * 4 + (y + b) % 4
        remote(half.at[0], piece(source), g_ssem.at[0], g_rsem.at[source], sibling).wait_recv()
        copies.append(remote(piece(source), piece(source), f_ssem.at[source], f_rsem.at[source], sibling))
        copies[-1].start()
    for n in range(16):
        theirs = out_ref.at[2 * (1 - c) + n // 8, n % 8]
        remote(half.at[0], theirs, f_ssem.at[0], f_rsem.at[n], sibling).wait_recv()
    for copy in copies:
        copy.wait_send()


def late_sum(part):
    _, _, rows, columns = part.shape
    return pl.pallas_call(
        late_sum_kernel,
        name="late_sum",
        out_shape=shape(LOW, *part.shape),
        in_specs=[VMEM],
        out_specs=VMEM,
        scratch_shapes=[
            vmem(LOW, 2, 8, rows, columns),
            vmem(LOW, 16, rows, columns),
            vmem(LOW, 16, rows, columns),
            dma(2), dma(2), dma(15), dma(16), dma(15), dma(16), dma(16), dma(16),
        ],
        compiler_params=pltpu.CompilerParams(
            collective_id=9, has_side_effects=True, vmem_limit_bytes=40 << 20
        ),
        cost_estimate=pl.CostEstimate(flops=10**8, bytes_accessed=10 * 2**20, transcendentals=0),
    )(part)


def per_device(
    tokens,
    cotangent,
    doc_starts,
    query_weight,
    key_weight,
    value_weight,
    out_weight,
    gate_weight,
    up_weight,
    down_weight,
    input_gain,
    attn_gain,
    prenorm_gain,
    post_gain,
    query_gain,
    key_gain,
):
    row_count = tokens.shape[0]
    first_row = lax.axis_index("seq") * row_count
    own_index = first_row + jnp.arange(row_count, dtype=jnp.int32)
    own_position = doc_layout(doc_starts, own_index)[1]
    cos_table, sine_table = rope_tables(own_position, HD)
    query_scale = HD ** (-0.5)
    inputs = tokens.astype(jnp.float32)
    query_weight_all = lax.all_gather(query_weight, "head", axis=1, tiled=True)
    out_weight_all = lax.all_gather(out_weight, "head", axis=0, tiled=True)
    normed, input_back = jax.vjp(rms_norm, inputs, input_gain)
    normed_low = normed.astype(jnp.bfloat16)
    query_raw = jnp.dot(normed_low, query_weight, preferred_element_type=jnp.float32)
    key_raw = jnp.dot(normed_low, key_weight, preferred_element_type=jnp.float32)
    value_low = jnp.dot(normed_low, value_weight, preferred_element_type=jnp.float32).astype(
        jnp.bfloat16
    )

    def query_piece(source, scaling):
        return rotate(rms_norm(source, scaling), cos_table, sine_table) * query_scale

    def key_piece(source, scaling):
        return rotate(rms_norm(source, scaling), cos_table, sine_table)

    query_rows = query_piece(query_raw, query_gain)
    query_low = query_rows.astype(jnp.bfloat16)
    key_rows, key_back = jax.vjp(key_piece, key_raw, key_gain)
    key_low = key_rows.astype(jnp.bfloat16)
    mix_all, lse_rows, q_all, k_all, v_all = forward_attention(
        doc_starts, query_low, key_low, value_low
    )
    lse_row = lse_rows[:, 0].reshape(-1)
    attn_mix = lax.dynamic_slice_in_dim(mix_all, lax.axis_index("head") * HD, HD, 1)
    attn_out = jnp.dot(mix_all, out_weight_all, preferred_element_type=jnp.float32)
    hidden_state, attn_back = jax.vjp(residual_norm, inputs, attn_out, attn_gain)
    ffn_in, prenorm_back = jax.vjp(rms_norm, hidden_state, prenorm_gain)
    ffn_low = ffn_in.astype(jnp.bfloat16)
    gate_rows = jnp.dot(ffn_low, gate_weight, preferred_element_type=jnp.float32)
    up_rows = jnp.dot(ffn_low, up_weight, preferred_element_type=jnp.float32)
    act_rows, act_back = jax.vjp(gated_act, gate_rows, up_rows)
    act_low = act_rows.astype(jnp.bfloat16)
    ffn_out = head_sum(
        jnp.dot(act_low, down_weight, preferred_element_type=jnp.float32).astype(jnp.bfloat16)
    ).astype(jnp.float32)
    mixed, post_back = jax.vjp(residual_norm, hidden_state, ffn_out, post_gain)
    upstream = cotangent.astype(jnp.float32)
    hidden_grad, ffn_out_grad, post_gain_grad = post_back(upstream)
    ffn_out_low = ffn_out_grad.astype(jnp.bfloat16)
    act_grad = dot_last(ffn_out_low, down_weight)
    gate_grad, up_grad = act_back(act_grad)
    gate_low = gate_grad.astype(jnp.bfloat16)
    up_low = up_grad.astype(jnp.bfloat16)
    ffn_in_sum, piece_a, piece_b, rest = ffn_grads(
        (dot_last(gate_low, gate_weight) + dot_last(up_low, up_weight)).astype(jnp.bfloat16),
        ffn_low,
        ffn_out_low,
        jnp.transpose(gate_low),
        jnp.transpose(up_low),
        jnp.transpose(act_low),
    )
    ffn_in_grad = ffn_in_sum.astype(jnp.float32)
    hidden_more, prenorm_gain_grad = prenorm_back(ffn_in_grad)
    hidden_grad = hidden_grad + hidden_more
    input_grad, attn_out_grad, attn_gain_grad = attn_back(hidden_grad)
    attn_out_low = attn_out_grad.astype(jnp.bfloat16)
    out_weight_grad_t = dot_first(attn_out_low, attn_mix)
    mix_grad = dot_last(attn_out_low, out_weight).astype(jnp.bfloat16)
    delta = jnp.sum(mix_grad.astype(jnp.float32) * attn_mix.astype(jnp.float32), axis=1)
    stats = jnp.stack([lse_row, delta] + [jnp.zeros_like(delta)] * 6)
    stats = jnp.transpose(stats.reshape(8, 2, HALF), (1, 0, 2))
    query_raw_all, query_gain_rows, key_value_grad, big = backward_attention(
        doc_starts,
        mix_grad,
        stats,
        q_all,
        k_all,
        v_all,
        piece_a,
        piece_b,
        query_raw,
        cos_table[:, : HD // 2],
        sine_table[:, : HD // 2],
        query_gain.reshape(1, HD),
    )
    query_gain_part = query_gain_rows[0]
    key_grad = key_value_grad[:, 0].reshape(row_count, HD).astype(jnp.float32)
    value_grad_low = key_value_grad[:, 1].reshape(row_count, HD)
    query_raw_low = lax.dynamic_slice_in_dim(query_raw_all, lax.axis_index("head") * HD, HD, 1)
    query_weight_grad = dot_first(normed_low, query_raw_low)
    key_raw_grad, key_gain_grad = key_back(key_grad)
    key_raw_low = key_raw_grad.astype(jnp.bfloat16)
    key_weight_grad = dot_first(normed_low, key_raw_low)
    value_weight_grad = dot_first(normed_low, value_grad_low)
    normed_grad = (
        dot_last(query_raw_all, query_weight_all)
        + dot_last(key_raw_low, key_weight)
        + dot_last(value_grad_low, value_weight)
    )
    input_more, input_gain_grad = input_back(normed_grad)
    tokens_grad = input_grad + input_more
    width = tokens.shape[1]
    rest_rows = rest.size // HD
    gains = jnp.concatenate(
        [
            input_gain_grad,
            attn_gain_grad,
            prenorm_gain_grad,
            post_gain_grad,
            query_gain_part,
            key_gain_grad,
        ]
    ).astype(jnp.bfloat16)
    gain_rows = gains.size // HD
    extra = jnp.concatenate(
        [
            gains.reshape(gain_rows, HD),
            rest.reshape(rest_rows, HD),
            jnp.zeros((4 * 128 - gain_rows - rest_rows, HD), jnp.bfloat16),
        ]
    ).reshape(4, 128, HD)
    late = jnp.stack(
        [query_weight_grad, key_weight_grad, value_weight_grad, out_weight_grad_t]
    ).astype(jnp.bfloat16)
    late = jnp.concatenate([late, extra], axis=1).reshape(4, 8, (width + 128) // 8, HD)
    late = late_sum(late).reshape(4, width + 128, HD)
    query_weight_grad = late[0, :width].astype(jnp.float32)
    key_weight_grad = late[1, :width].astype(jnp.float32)
    value_weight_grad = late[2, :width].astype(jnp.float32)
    out_weight_grad = jnp.transpose(late[3, :width].astype(jnp.float32))
    extra = late[:, width:].reshape(4 * 128, HD)
    gains = extra[:gain_rows].reshape(-1).astype(jnp.float32)
    rest = extra[gain_rows : gain_rows + rest_rows].reshape(rest.shape)
    input_gain_grad = gains[:width]
    attn_gain_grad = gains[width : 2 * width]
    prenorm_gain_grad = gains[2 * width : 3 * width]
    post_gain_grad = gains[3 * width : 4 * width]
    query_gain_grad = gains[4 * width : 4 * width + HD]
    key_gain_grad = gains[4 * width + HD : 4 * width + 2 * HD]
    hidden = gate_weight.shape[1]
    gate_weight_grad = jnp.transpose(big[:hidden].astype(jnp.float32))
    up_weight_grad = jnp.transpose(big[hidden : 2 * hidden].astype(jnp.float32))
    down_weight_grad = big[2 * hidden :].astype(jnp.float32)
    down_weight_grad = lax.dynamic_update_slice(
        down_weight_grad, rest.astype(jnp.float32), (hidden - rest.shape[0], 0)
    )
    return (
        mixed.astype(jnp.bfloat16),
        tokens_grad,
        query_weight_grad,
        key_weight_grad,
        value_weight_grad,
        out_weight_grad,
        gate_weight_grad,
        up_weight_grad,
        down_weight_grad,
        input_gain_grad,
        attn_gain_grad,
        prenorm_gain_grad,
        post_gain_grad,
        query_gain_grad,
        key_gain_grad,
    )


def solution(mesh):
    placed = (
        P("seq", None),
        P("seq", None),
        P(),
        P(None, "head"),
        P(),
        P(),
        P("head", None),
        P(None, "head"),
        P(None, "head"),
        P("head", None),
        P(),
        P(),
        P(),
        P(),
        P(),
        P(),
    )
    return jax.shard_map(
        per_device,
        mesh=mesh,
        in_specs=placed,
        out_specs=(
            P("seq", None),
            P("seq", None),
            P(None, "head"),
            P(),
            P(),
            P("head", None),
            P(None, "head"),
            P(None, "head"),
            P("head", None),
            P(),
            P(),
            P(),
            P(),
            P(),
            P(),
        ),
        check_vma=False,
    )
```

```python
import functools
import math

import jax
import jax.numpy as jnp
from jax import lax
from jax.experimental import pallas as pl
from jax.experimental.pallas import tpu as pltpu
from jax.sharding import PartitionSpec as P

HD = 256


EPS = 1e-06
THETA = 1000000.0
NEG = -1e30


def rms_norm(values, scaling):
    return values * lax.rsqrt(jnp.mean(values * values, axis=-1, keepdims=True) + EPS) * scaling


def doc_layout(doc_starts, token_index):
    before = doc_starts[None, :] <= token_index[:, None]
    segment = jnp.sum(before.astype(jnp.int32), axis=1)
    doc_begin = jnp.max(jnp.where(before, doc_starts[None, :], 0), axis=1)
    return (segment, token_index - doc_begin)


def rope_tables(position, head_width):
    half_width = head_width // 2
    inverse = jnp.exp(
        -math.log(THETA) * 2.0 * jnp.arange(half_width, dtype=jnp.float32) / head_width
    )
    angles = position.astype(jnp.float32)[:, None] * inverse[None, :]
    angles = jnp.concatenate([angles, angles], axis=1)
    return (jnp.cos(angles), jnp.sin(angles))


def rotate(values, cos_table, sine_table):
    half_width = values.shape[-1] // 2
    turned = jnp.concatenate([-values[..., half_width:], values[..., :half_width]], axis=-1)
    return values * cos_table + turned * sine_table


MESH_ID = pl.DeviceIdType.MESH
HALF = 256
BLK = 512
LOW = jnp.bfloat16
FULL = jnp.float32
NT = (((1,), (1,)), ((), ()))


def place():
    s = lax.axis_index("seq")
    return s // 8, (s // 2) % 4, s % 2, lax.axis_index("head")


def at(x, y, c, z):
    return ((x % 4) * 8 + (y % 4) * 2 + c, z % 4)


def greet(peers):
    barrier = pltpu.get_barrier_semaphore()
    for peer in peers:
        pl.semaphore_signal(barrier, inc=1, device_id=peer, device_id_type=MESH_ID)
    pl.semaphore_wait(barrier, len(peers))


def remote(src, dst, send_sem, recv_sem, peer):
    return pltpu.make_async_remote_copy(
        src_ref=src,
        dst_ref=dst,
        send_sem=send_sem,
        recv_sem=recv_sem,
        device_id=peer,
        device_id_type=MESH_ID,
    )


def rows_at(ref, start, size):
    return ref.at[pl.ds(pl.multiple_of(start, 16), size)]


class RingGather:
    def __init__(self, view, me, plus, minus, sems, ring, source=None):
        send, recv = sems

        def near(rel, half):
            return view((me + rel) % 4, half)

        own = source or (lambda half: near(0, half))
        plan = (
            (own(0), near(0, 0), plus),
            (own(1), near(0, 1), plus),
            (near(3, 0), near(3, 0), plus),
            (own(0), near(0, 0), minus),
            (own(1), near(0, 1), minus),
            (near(1, 1), near(1, 1), minus),
        )
        self.copies = [
            remote(src, dst, send.at[ring, k], recv.at[ring, k], peer) for k, (src, dst, peer) in enumerate(plan)
        ]

    def own(self, half):
        self.copies[half].start()
        self.copies[3 + half].start()

    def forward(self):
        self.copies[0].wait_recv()
        self.copies[2].start()
        self.copies[4].wait_recv()
        self.copies[5].start()

    def near(self):
        self.copies[1].wait_recv()
        self.copies[3].wait_recv()

    def far(self):
        self.copies[2].wait_recv()
        self.copies[5].wait_recv()

    def drain(self):
        for copy in self.copies:
            copy.wait_send()


class RingReduce:
    def __init__(self, view, passing, got, plus, minus, sems, ring):
        send, recv = sems
        self.view, self.passing, self.got = view, passing, got
        plan = (
            (view(2, 0), passing(0), minus),
            (view(2, 1), passing(1), plus),
            (view(3, 1), got(0, 1), minus),
            (view(1, 0), got(1, 0), plus),
            (passing(0), got(0, 0), minus),
            (passing(1), got(1, 1), plus),
        )
        self.copies = [
            remote(src, dst, send.at[ring, k], recv.at[ring, k], peer) for k, (src, dst, peer) in enumerate(plan)
        ]

    def start(self, *numbers):
        for k in numbers or (0, 1, 2, 3):
            self.copies[k].start()

    def relay(self):
        for half, rel in ((0, 3), (1, 1)):
            self.copies[half].wait_recv()
            land, term = self.passing(half), self.view(rel, half)
            land[...] = (land[...].astype(FULL) + term[...].astype(FULL)).astype(LOW)
            self.copies[4 + half].start()

    def finish(self):
        for k in (2, 3, 4, 5):
            self.copies[k].wait_recv()

    def arrived(self, half):
        return self.got(0, half)[...].astype(FULL) + self.got(1, half)[...].astype(FULL)

    def drain(self):
        for copy in self.copies:
            copy.wait_send()


def tile_first(i, x, c):
    column = jnp.where(i % 2 == 1, 3 - x, x)
    return BLK * (8 * column + 2 * (i // 2) + c) + HALF * (i % 2)


def begin_of(token, starts_ref):
    begin = jnp.zeros_like(token)
    for n in range(starts_ref.shape[0]):
        start = starts_ref[n]
        begin = jnp.where(start <= token, start, begin)
    return begin


def attn_forward(
    starts_ref, q_ref, k_ref, v_ref,
    mix_ref, lse_ref, qg_ref, kg_ref, vg_ref,
    acc, lacc, osend, opass, ogot, lsend, lrecv, hsend, lhsend,
    rs, rr, sib_s, sib_r, l_s, l_r, sw_s, sw_r,
):
    x, y, c, z = place()
    xp, xm, yp, ym = at(x + 1, y, c, z), at(x + 3, y, c, z), at(x, y + 1, c, z), at(x, y + 3, c, z)
    zp, zm, y2 = at(x, y, c, z + 1), at(x, y, c, z + 3), at(x, y + 2, c, z)
    sibling, partner = at(x, y, 1 - c, z), at(3 - x, y, c, z)
    greet([partner, sibling, xp, xm, yp, ym, y2, zp, zm])
    copies = []

    def go(copy):
        copy.start()
        copies.append(copy)

    q_low, q_high = q_ref.at[pl.ds(0, HALF)], q_ref.at[pl.ds(HALF, HALF)]
    swap = remote(q_high, qg_ref.at[2 * y + 1], sw_s.at[0], sw_r.at[0], partner)
    go(swap)

    def kv_view(index, half):
        return (kg_ref, vg_ref)[half].at[2 * index + c]

    kv = RingGather(kv_view, x, xp, xm, (rs, rr), 0, lambda half: (k_ref, v_ref)[half])
    kv.own(0)
    kv.own(1)
    qs = RingGather(
        lambda index, half: qg_ref.at[2 * index + half], y, yp, ym, (rs, rr), 1,
        lambda half: q_low if half == 0 else qg_ref.at[2 * y + 1],
    )
    qs.own(0)

    def pass_on(index, half, source=None):
        block = kv_view(index, half)
        return remote(block if source is None else source, block, sib_s.at[index, half], sib_r.at[index, half], sibling)

    for half, source in enumerate((k_ref, v_ref)):
        go(pass_on(x, half, source))
    qg_ref[2 * y] = q_ref[0:HALF, :]
    kg_ref[2 * x + c] = k_ref[...]
    vg_ref[2 * x + c] = v_ref[...]
    acc[...] = jnp.zeros_like(acc)
    lacc[...] = jnp.zeros_like(lacc)
    swap.wait_recv()
    qs.own(1)
    kv.forward()
    qs.forward()
    kv.near()
    for rel in (1, 3):
        for half in range(2):
            go(pass_on((x + rel) % 4, half))
    qs.near()
    qs.far()

    def chunk(i, first_q, pair, first_k, masked):
        queries = qg_ref[i]
        if masked:
            token = first_q + lax.broadcasted_iota(jnp.int32, (HALF, 1), 0)
            begin = begin_of(token, starts_ref)
        total = None
        sums = None
        for cc in range(2):
            keys, values = kg_ref[pair * 2 + cc], vg_ref[pair * 2 + cc]
            scores = lax.dot_general(queries, keys, NT, preferred_element_type=FULL)
            exps = jnp.exp(scores)
            if masked:
                key_index = first_k + cc * BLK + lax.broadcasted_iota(jnp.int32, (1, BLK), 1)
                exps = jnp.where((key_index <= token) & (key_index >= begin), exps, 0.0)
            part = jnp.dot(exps.astype(LOW), values, preferred_element_type=FULL)
            total = part if total is None else total + part
            for n in range(BLK // 128):
                piece = exps[:, n * 128 : (n + 1) * 128]
                sums = piece if sums is None else sums + piece
        acc[i] = acc[i] + total
        lacc[i] = lacc[i] + sums

    for rel in (0, 1, 3, 2):
        pair = (x + rel) % 4
        if rel == 2:
            kv.far()
            for half in range(2):
                go(pass_on(pair, half))
        for half in range(2):
            pass_on(pair, half).wait_recv()
        first_k = 4096 * pair + 1024 * y

        def visit(i, carry):
            first_q = tile_first(i, x, c)
            some = first_k <= first_q + (HALF - 1)
            full = (first_k + 1023 <= first_q) & (first_k > 0) & (first_q < 31 * BLK)

            @pl.when(full)
            def _():
                chunk(i, first_q, pair, first_k, False)

            @pl.when(some & jnp.logical_not(full))
            def _():
                chunk(i, first_q, pair, first_k, True)

            return carry

        lax.fori_loop(0, 8, visit, 0)

    def cast(i, carry):
        osend[i] = acc[i].astype(LOW)
        row = jnp.sum(jnp.transpose(lacc[i]), axis=0, keepdims=True)
        lsend[i] = jnp.broadcast_to(row, (8, HALF))
        return carry

    lax.fori_loop(0, 8, cast, 0)
    numer = RingReduce(
        lambda rel, half: osend.at[2 * ((y + rel) % 4) + half],
        lambda half: opass.at[half],
        lambda side, half: ogot.at[side, half],
        yp, ym, (rs, rr), 2,
    )
    numer.start()

    def sums_to(rel, peer):
        index = (y + rel) % 4
        return remote(lsend.at[pl.ds(2 * index, 2)], lrecv.at[y], l_s.at[rel - 1], l_r.at[y], peer)

    for rel, peer in ((1, yp), (3, ym), (2, y2)):
        go(sums_to(rel, peer))
    lrecv[y] = lsend[pl.ds(2 * y, 2)]
    numer.relay()
    for rel in (1, 3, 2):
        remote(lsend.at[pl.ds(0, 2)], lrecv.at[(y + rel) % 4], l_s.at[0], l_r.at[(y + rel) % 4], sibling).wait_recv()
    numer.finish()

    def mix_view(index, half):
        return mix_ref.at[pl.ds(half * HALF, HALF), pl.ds(pl.multiple_of(index * HD, HD), HD)]

    mixes = RingGather(mix_view, z, zp, zm, (rs, rr), 3)
    returns = (
        remote(hsend, mix_view(z, 1), sw_s.at[1], sw_r.at[1], partner),
        remote(lhsend, lse_ref.at[1], sw_s.at[2], sw_r.at[2], partner),
    )
    for half in (1, 0):
        denom = sum(lrecv[n, half] for n in range(4))
        total = osend[2 * y + half].astype(FULL) + numer.arrived(half)
        inverse = jnp.transpose(jnp.broadcast_to(1.0 / denom[0:1, :], (128, HALF)))
        scaled = (total * jnp.concatenate([inverse, inverse], axis=1)).astype(LOW)
        if half == 1:
            hsend[...] = scaled
            lhsend[...] = jnp.log(denom)
            for copy in returns:
                go(copy)
        else:
            mix_view(z, 0)[...] = scaled
            lse_ref[0] = jnp.log(denom)
    mixes.own(0)
    for copy in returns:
        copy.wait_recv()
    mixes.own(1)
    mixes.forward()
    mixes.near()
    mixes.far()
    for ring in (kv, qs, numer, mixes):
        ring.drain()
    for copy in copies:
        copy.wait_send()


VMEM = pl.BlockSpec(memory_space=pltpu.VMEM)
SMEM = pl.BlockSpec(memory_space=pltpu.SMEM)
ANY = pl.BlockSpec(memory_space=pl.ANY)


def dma(*shape):
    return pltpu.SemaphoreType.DMA(shape)


def shape(dtype, *dims):
    return jax.ShapeDtypeStruct(dims, dtype)


def vmem(dtype, *dims):
    return pltpu.VMEM(dims, dtype)


def params(number, mebibytes):
    return pltpu.CompilerParams(collective_id=number, has_side_effects=True, vmem_limit_bytes=mebibytes << 20)


def cost(gflops):
    return pl.CostEstimate(flops=gflops * 10**9, bytes_accessed=20 * 2**20, transcendentals=0)


def forward_attention(doc_starts, query, key, value):
    return pl.pallas_call(
        attn_forward,
        name="attn_forward",
        out_shape=[
            shape(LOW, BLK, 4 * HD),
            shape(FULL, 2, 8, HALF),
            shape(LOW, 8, HALF, HD),
            shape(LOW, 8, BLK, HD),
            shape(LOW, 8, BLK, HD),
        ],
        in_specs=[SMEM] + [VMEM] * 3,
        out_specs=[VMEM] * 5,
        scratch_shapes=[
            vmem(FULL, 8, HALF, HD),
            vmem(FULL, 8, HALF, 128),
            vmem(LOW, 8, HALF, HD),
            vmem(LOW, 2, HALF, HD),
            vmem(LOW, 2, 2, HALF, HD),
            vmem(FULL, 8, 8, HALF),
            vmem(FULL, 4, 2, 8, HALF),
            vmem(LOW, HALF, HD),
            vmem(FULL, 8, HALF),
            dma(4, 6), dma(4, 6), dma(4, 2), dma(4, 2), dma(3), dma(4), dma(3), dma(3),
        ],
        compiler_params=params(1, 40),
        cost_estimate=cost(6),
    )(doc_starts, query, key, value)


ROWS = 2560
SIDE = ROWS // 2
PIECE = SIDE // 4
WINDOW = PIECE // 4
CUTS = (0, 448, 896, 1280, 1728, 2144, 2560)


BLOCKS = ((0, 384), (384, 384), (768, 384), (1152, 384), (1536, 192))
THIRD = 384
CORNER = 0.7978845608028654


def unit_of(values):
    inverse = lax.rsqrt(jnp.mean(values * values, axis=1, keepdims=True) + EPS)
    return inverse, values * inverse


def norm_back(inverse, unit, scaled):
    return inverse * (scaled - unit * jnp.mean(unit * scaled, axis=1, keepdims=True))


def middle_kernel(
    again_ref, pgain_ref, fgain_ref, lse_ref,
    mix_hbm, wout_hbm, tokens_hbm, cot_hbm, gate_hbm, up_hbm, down_hbm,
    mixed_ref, mgrad_ref, stat_ref, resid_ref, early_ref, piece_a_ref, piece_b_ref,
    weights, wout, mix, tokens, cot, attn_out, left, right, turned, turned_up, aol,
    part_f, part_b, sum_f, sum_b, z_pass, z_got, sib_recv, pass_ab, got_ab, grows,
    in_sem, sib_s, sib_r, rs, rr,
):
    x, y, c, z = place()
    xp, xm, yp, ym = at(x + 1, y, c, z), at(x + 3, y, c, z), at(x, y + 1, c, z), at(x, y + 3, c, z)
    zp, zm, sibling = at(x, y, c, z + 1), at(x, y, c, z + 3), at(x, y, 1 - c, z)
    hidden = gate_hbm.shape[0]
    width = weights.shape[1]
    loads = [
        pltpu.make_async_copy(src, dst, in_sem.at[n])
        for n, (src, dst) in enumerate(
            (
                (mix_hbm, mix),
                (wout_hbm, wout),
                (tokens_hbm, tokens),
                (gate_hbm, weights.at[pl.ds(0, hidden)]),
                (up_hbm, weights.at[pl.ds(hidden, hidden)]),
                (down_hbm, weights.at[pl.ds(2 * hidden, hidden)]),
                (cot_hbm, cot),
            )
        )
    ]
    for load in loads:
        load.start()
    greet([xp, xm, yp, ym, zp, zm, sibling])
    sems = (rs, rr)
    thirds = [pl.ds(k * THIRD, THIRD) for k in range(width // THIRD)]

    def rows_of(r):
        return pl.ds(r * HALF, HALF)

    def head_sum(r, number, part, whole):
        quarter = HALF // 4
        first = r * HALF

        def span(ref, index, half):
            return rows_at(ref, first + quarter * index + half * (quarter // 2), quarter // 2)

        reduce = RingReduce(
            lambda rel, half: span(part, (z + rel) % 4, half),
            lambda half: z_pass.at[number, half],
            lambda side, half: z_got.at[number, side, half],
            zp, zm, sems, 2 * number,
        )
        gather = RingGather(lambda index, half: span(whole, index, half), z, zp, zm, sems, 2 * number + 1)

        def summed():
            reduce.finish()
            for half in range(2):
                own = span(part, z, half)[...].astype(FULL) + reduce.arrived(half)
                span(whole, z, half)[...] = own.astype(LOW)
                gather.own(half)

        def gathered():
            gather.near()
            gather.far()

        return reduce, gather, summed, gathered

    sums = [head_sum(0, 0, part_f, sum_f), head_sum(1, 1, part_f, sum_f)]
    sums += [head_sum(0, 2, part_b, sum_b), head_sum(1, 3, part_b, sum_b)]

    def forward(r, hooks):
        rows, columns = rows_of(r), pl.ds(r * HALF, HALF)
        if r == 0:
            for load in loads[:3]:
                load.wait()
        for third in thirds:
            attn_out[rows, third] = jnp.dot(mix[rows, :], wout[:, third], preferred_element_type=FULL)
        _, unit = unit_of(attn_out[rows, :])
        state = tokens[rows, :].astype(FULL) + unit * again_ref[...]
        resid_ref[rows, :] = state
        _, unit = unit_of(state)
        right[0, rows, :] = (unit * pgain_ref[...]).astype(LOW)
        if r == 0:
            for load in loads[3:5]:
                load.wait()
        for n, (start, size) in enumerate(BLOCKS):
            low = right[0, rows, :]
            gate = lax.dot_general(weights[pl.ds(start, size), :], low, NT, preferred_element_type=FULL)
            up = lax.dot_general(weights[pl.ds(hidden + start, size), :], low, NT, preferred_element_type=FULL)
            square = gate * gate
            bend = jnp.tanh(CORNER * gate * (1.0 + 0.044715 * square))
            share = 0.5 * (1.0 + bend)
            gelu = gate * share
            slope = share + 0.5 * gate * (1.0 - bend * bend) * (CORNER * (1.0 + 3.0 * 0.044715 * square))
            act = (gelu * up).astype(LOW)
            left[pl.ds(start, size), columns] = (up * slope).astype(LOW)
            left[pl.ds(hidden + start, size), columns] = gelu.astype(LOW)
            left[pl.ds(2 * hidden + start, size), columns] = act
            turned[:, start : start + size] = jnp.transpose(act)
            if n in hooks:
                hooks[n]()
        if r == 0:
            loads[5].wait()
        for third in thirds:
            part = jnp.dot(
                turned[:, :hidden], weights[pl.ds(2 * hidden, hidden), third], preferred_element_type=FULL
            )
            part_f[rows, third] = part.astype(LOW)

    def backward(r, hooks):
        rows, columns = rows_of(r), pl.ds(r * HALF, HALF)
        if r == 0:
            loads[6].wait()
        inverse, unit = unit_of(sum_f[rows, :].astype(FULL))
        mixed_ref[rows, :] = (resid_ref[rows, :] + unit * fgain_ref[...]).astype(LOW)
        grad = cot[rows, :].astype(FULL)
        grows[2, r : r + 1, :] = jnp.sum(unit * grad, axis=0, keepdims=True)
        right[1, rows, :] = norm_back(inverse, unit, fgain_ref[...] * grad).astype(LOW)
        for n, (start, size) in enumerate(BLOCKS):
            act_grad = lax.dot_general(
                weights[pl.ds(2 * hidden + start, size), :], right[1, rows, :], NT, preferred_element_type=FULL
            )
            for first, turn in ((start, turned), (hidden + start, turned_up)):
                span = pl.ds(first, size)
                grads = (act_grad * left[span, columns].astype(FULL)).astype(LOW)
                left[span, columns] = grads
                turn[:, start : start + size] = jnp.transpose(grads)
            if n in hooks:
                hooks[n]()
        for third in thirds:
            part = jnp.dot(turned[:, :hidden], weights[pl.ds(0, hidden), third], preferred_element_type=FULL)
            part = part + jnp.dot(
                turned_up[:, :hidden], weights[pl.ds(hidden, hidden), third], preferred_element_type=FULL
            )
            part_b[rows, third] = part.astype(LOW)

    own_head = pl.ds(pl.multiple_of(z * HD, HD), HD)

    def finish(r):
        rows = rows_of(r)
        grad = sum_b[rows, :].astype(FULL)
        inverse, unit = unit_of(resid_ref[rows, :])
        grows[1, r : r + 1, :] = jnp.sum(unit * grad, axis=0, keepdims=True)
        grad = cot[rows, :].astype(FULL) + norm_back(inverse, unit, pgain_ref[...] * grad)
        resid_ref[rows, :] = grad
        inverse, unit = unit_of(attn_out[rows, :])
        grows[0, r : r + 1, :] = jnp.sum(unit * grad, axis=0, keepdims=True)
        aol[rows, :] = norm_back(inverse, unit, again_ref[...] * grad).astype(LOW)
        grads = lax.dot_general(aol[rows, :], wout[own_head, :], NT, preferred_element_type=FULL).astype(LOW)
        mgrad_ref[rows, :] = grads
        products = grads.astype(FULL) * mix[rows, own_head].astype(FULL)
        delta = jnp.sum(jnp.transpose(products), axis=0, keepdims=True)
        number = lax.broadcasted_iota(jnp.int32, (8, HALF), 0)
        stat_ref[r] = jnp.where(number == 1, delta, lse_ref[r])

    sib_send, mine = weights.at[pl.ds(0, ROWS)], weights.at[pl.ds(ROWS, ROWS)]

    def product(core, n, target, added):
        first, size = CUTS[n], CUTS[n + 1] - CUTS[n]
        lhs = left[pl.ds(pl.multiple_of(ROWS * core + first, 16), size), :]
        which = jnp.where(n >= 2, core, 0)
        for third in thirds:
            tile = jnp.dot(lhs, right[which, :, third], preferred_element_type=FULL)
            if added is not None:
                tile = tile + added[pl.ds(first, size), third].astype(FULL)
            target[pl.ds(first, size), third] = tile.astype(LOW)

    def to_sibling(n):
        span = pl.ds(CUTS[n], CUTS[n + 1] - CUTS[n])
        return remote(sib_send.at[span], sib_recv.at[span], sib_s.at[n], sib_r.at[n], sibling)

    def side_ring(h, me, plus, minus):
        return RingReduce(
            lambda rel, half: rows_at(
                weights, ROWS + SIDE * h + PIECE * ((me + rel) % 4) + half * (PIECE // 2), PIECE // 2
            ),
            lambda half: pass_ab.at[h, half],
            lambda side, half: got_ab.at[h, side, half],
            plus, minus, sems, 8 + h,
        )

    rings = (side_ring(0, x, xp, xm), side_ring(1, y, yp, ym))
    forward(0, {})
    sums[0][0].start()
    forward(1, {3: sums[0][0].relay})
    sums[0][2]()
    sums[1][0].start()
    sums[0][1].forward()
    sums[1][0].relay()
    sums[0][3]()
    backward(0, {1: sums[1][2], 4: sums[1][1].forward})
    sums[2][0].start()
    sums[1][3]()
    backward(1, {2: sums[2][0].relay, 4: sums[2][2]})
    sums[3][0].start()
    rest = jnp.dot(left[2 * ROWS :, :], right[1], preferred_element_type=FULL)
    early_ref[pl.ds(HD, 64), :] = rest.astype(LOW)
    count = len(CUTS) - 1
    for n in range(count):
        product(1 - c, n, sib_send, None)
        to_sibling(n).start()
        if n == 0:
            sums[2][1].forward()
            sums[3][0].relay()
        if n == 2:
            sums[3][2]()
    sums[2][3]()
    for n in range(count):
        to_sibling(n).wait_recv()
        product(c, n, mine, sib_recv)
        if n == 0:
            sums[3][1].forward()
        if n == count // 2 - 1:
            rings[0].start()
    rings[1].start()
    finish(0)
    sums[3][3]()
    rings[0].relay()
    finish(1)
    rings[1].relay()
    lhs = jnp.transpose(mix[:, own_head])
    for third in thirds:
        early_ref[0:HD, third] = jnp.dot(lhs, aol[:, third], preferred_element_type=FULL).astype(LOW)
    number = lax.broadcasted_iota(jnp.int32, (32, width), 0)
    gains = jnp.zeros((32, width), FULL)
    for n in range(3):
        gains = jnp.where(number == n, grows[n, 0:1, :] + grows[n, 1:2, :], gains)
    early_ref[pl.ds(HD + 64, 32), :] = gains.astype(LOW)
    for h, (ring, me, out) in enumerate(((rings[0], x, piece_a_ref), (rings[1], y, piece_b_ref))):
        ring.finish()
        for half in range(2):
            size = PIECE // 2
            own = rows_at(weights, ROWS + SIDE * h + PIECE * me + half * size, size)[...]
            out[pl.ds(half * size, size), :] = (own.astype(FULL) + ring.arrived(half)).astype(LOW)
    for reduce, gather, _, _ in sums:
        reduce.drain()
        gather.drain()
    for ring in rings:
        ring.drain()
    for n in range(count):
        to_sibling(n).wait_send()


def middle(again, pgain, fgain, lse, mix, wout, tokens, cot, gate_t, up_t, down):
    rows, width = tokens.shape
    hidden = gate_t.shape[0]
    stacked = 3 * hidden
    return pl.pallas_call(
        middle_kernel,
        name="middle",
        out_shape=[
            shape(LOW, rows, width),
            shape(LOW, rows, HD),
            shape(FULL, 2, 8, HALF),
            shape(FULL, rows, width),
            shape(LOW, HD + 96, width),
            shape(LOW, PIECE, width),
            shape(LOW, PIECE, width),
        ],
        in_specs=[VMEM] * 4 + [ANY] * 7,
        out_specs=[VMEM] * 7,
        scratch_shapes=[
            vmem(LOW, stacked, width),
            vmem(LOW, 4 * HD, width),
            vmem(LOW, rows, 4 * HD),
            vmem(LOW, rows, width),
            vmem(LOW, rows, width),
            vmem(FULL, rows, width),
            vmem(LOW, stacked, rows),
            vmem(LOW, 2, rows, width),
            vmem(LOW, HALF, 1792),
            vmem(LOW, HALF, 1792),
            vmem(LOW, rows, width),
            *[vmem(LOW, rows, width)] * 4,
            vmem(LOW, 4, 2, HALF // 8, width),
            vmem(LOW, 4, 2, 2, HALF // 8, width),
            vmem(LOW, ROWS, width),
            vmem(LOW, 2, 2, PIECE // 2, width),
            vmem(LOW, 2, 2, 2, PIECE // 2, width),
            vmem(FULL, 3, 8, width),
            dma(7), dma(6), dma(6), dma(10, 6), dma(10, 6),
        ],
        compiler_params=params(4, 60),
        cost_estimate=cost(20),
    )(again, pgain, fgain, lse, mix, wout, tokens, cot, gate_t, up_t, down)


LATE = 112
EARLY = 176
KEEPERS = 11


def attn_backward(
    starts_ref, do_ref, stat_ref, piece_a_ref, piece_b_ref, qgain_ref, kgain_ref, igain_ref, early_ref,
    q_hbm, k_hbm, v_hbm, raw_hbm, kraw_hbm, cos_hbm, sin_hbm, wk_hbm, wv_hbm, normed_hbm, wq_hbm, tokens_hbm, resid_hbm,
    late_ref, esum_ref, tgrad_ref, dgain_ref, big_ref,
    dog, statg, dqacc, dkacc, dvacc, ktbuf, sibsend, sibrecv, kvsrc, kvpass, kvgot,
    dqsend, dqpass, dqgot, dqback, dqhigh, zpart, zpass, zgot, gaing, winpass, wingot, full_a, full_b,
    draw_ref, dkv_ref, dkraw, dvrow, part, core_recv, half_sum, plane_recv, grow, grecv,
    e_core, e_half, e_plane,
    q_in, k_in, v_in, raw_ref, kraw_ref, cos_ref, sin_ref, wk_ref, wv_ref, normed_t, wq_ref, tok_ref, resid_ref,
    rs, rr, st_s, st_r, sw_s, sw_r, sib_s, sib_r, gn_s, gn_r, sf_s, sf_r, own_sem,
    load_sem, c_s, c_r, p_s, p_r, g_s, g_r, f_s, f_r, i_s, i_r,
    ep_s, ep_r, eg_s, eg_r, ef_s, ef_r,
):
    x, y, c, z = place()
    xp, xm, yp, ym = at(x + 1, y, c, z), at(x + 3, y, c, z), at(x, y + 1, c, z), at(x, y + 3, c, z)
    zp, zm, y2, z2 = at(x, y, c, z + 1), at(x, y, c, z + 3), at(x, y + 2, c, z), at(x, y, c, z + 2)
    sibling, partner = at(x, y, 1 - c, z), at(3 - x, y, c, z)
    shifts = [(a, b) for a in range(4) for b in range(4) if (a, b) != (0, 0)]
    plane = [at(x + a, y + b, c, z) for a, b in shifts]
    loads = [
        pltpu.make_async_copy(src, dst, load_sem.at[n])
        for n, (src, dst) in enumerate(
            (
                (q_hbm, q_in), (k_hbm, k_in), (v_hbm, v_in), (raw_hbm, raw_ref), (kraw_hbm, kraw_ref),
                (cos_hbm, cos_ref), (sin_hbm, sin_ref), (wk_hbm, wk_ref), (wv_hbm, wv_ref),
                (normed_hbm, normed_t), (wq_hbm, wq_ref), (tokens_hbm, tok_ref), (resid_hbm, resid_ref),
            )
        )
    ]
    for load in loads:
        load.start()
    greet(plane + [sibling, zp, zm, z2])
    copies = []

    def go(copy):
        copy.start()
        copies.append(copy)

    sems = (rs, rr)
    do_low, do_high = do_ref.at[pl.ds(0, HALF)], do_ref.at[pl.ds(HALF, HALF)]
    swaps = (
        remote(do_high, dog.at[2 * y + 1], sw_s.at[0], sw_r.at[0], partner),
        remote(stat_ref.at[1], statg.at[2 * y + 1], sw_s.at[1], sw_r.at[1], partner),
    )
    for copy in swaps:
        go(copy)
    dos = RingGather(
        lambda index, half: dog.at[2 * index + half], y, yp, ym, sems, 0,
        lambda half: do_low if half == 0 else dog.at[2 * y + 1],
    )
    dos.own(0)
    chip = x * 4 + y
    e_cross = remote(rows_at(early_ref, EARLY * (1 - c), EARLY), e_core, c_s.at[1], c_r.at[1], sibling)
    go(e_cross)

    def early_part(owner):
        return remote(
            rows_at(e_half, 16 * owner, 16), e_plane.at[chip], ep_s.at[owner], ep_r.at[chip],
            at(owner // 4, owner % 4, c, z),
        )

    def early_spread():
        e_cross.wait_recv()
        own = early_ref[pl.ds(pl.multiple_of(EARLY * c, 16), EARLY), :]
        e_half[...] = (own.astype(FULL) + e_core[...].astype(FULL)).astype(LOW)
        for owner in range(KEEPERS):
            pl.when(chip != owner)(early_part(owner).start)

    def early_piece(core, owner):
        return rows_at(esum_ref, EARLY * core + 16 * owner, 16)

    def early_out(n):
        return remote(early_piece(c, chip), early_piece(c, chip), eg_s.at[n], eg_r.at[chip], plane[n])

    def early_across(owner):
        block = early_piece(c, owner)
        return remote(block, block, ef_s.at[owner], ef_r.at[owner], sibling)

    def early_summed():
        @pl.when(chip < KEEPERS)
        def _():
            total = rows_at(e_half, 16 * chip, 16)[...].astype(FULL)
            for a, b in shifts:
                source = ((x + a) % 4) * 4 + (y + b) % 4
                block = rows_at(e_half, 0, 16)
                remote(block, e_plane.at[source], ep_s.at[0], ep_r.at[source], sibling).wait_recv()
                total = total + e_plane[source].astype(FULL)
            early_piece(c, chip)[...] = total.astype(LOW)
            for n in range(15):
                early_out(n).start()
            early_across(chip).start()

    def early_passed():
        for owner in range(KEEPERS):

            @pl.when(chip != owner)
            def _():
                block = early_piece(c, owner)
                remote(rows_at(e_half, 0, 16), block, eg_s.at[0], eg_r.at[owner], sibling).wait_recv()
                early_across(owner).start()

    def early_done():
        for owner in range(KEEPERS):
            block = early_piece(1 - c, owner)
            remote(rows_at(e_half, 0, 16), block, ef_s.at[0], ef_r.at[owner], sibling).wait_recv()
            early_across(owner).wait_send()
            pl.when(chip != owner)(early_part(owner).wait_send)

        @pl.when(chip < KEEPERS)
        def _():
            for n in range(15):
                early_out(n).wait_send()

    def stats_to(upper, rel, peer):
        slot = 2 * y + upper
        source = statg.at[slot] if upper else stat_ref.at[0]
        return remote(source, statg.at[slot], st_s.at[upper, rel - 1], st_r.at[slot], peer)

    y_peers = ((1, yp), (3, ym), (2, y2))
    for rel, peer in y_peers:
        go(stats_to(0, rel, peer))

    cut = (48, WINDOW - 48)

    def window(ref, index, half):
        return rows_at(ref, WINDOW * index + 48 * half, cut[half])

    sides = ((piece_a_ref, full_a, y, yp, ym), (piece_b_ref, full_b, x, xp, xm))
    reduces, gathers = [], []
    for h, (piece, full, me, plus, minus) in enumerate(sides):
        reduces.append(
            RingReduce(
                lambda rel, half, piece=piece, me=me: window(piece, (me + rel) % 4, half),
                lambda half, h=h: winpass.at[h, pl.ds(48 * half, cut[half])],
                lambda side, half, h=h: wingot.at[h, side, pl.ds(48 * half, cut[half])],
                plus, minus, sems, 1 + h,
            )
        )
        gathers.append(
            RingGather(lambda index, half, full=full: window(full, index, half), me, plus, minus, sems, 3 + h)
        )
        reduces[h].start()

    def big_view(core, h, index, half):
        return rows_at(big_ref, ROWS * core + SIDE * h + PIECE * index + half * (PIECE // 2), PIECE // 2)

    owners = ((x, xp, xm), (y, yp, ym))
    pieces = [
        RingGather(
            lambda index, half, h=h: big_view(c, h, index, half), me, plus, minus, sems, 5 + h,
            lambda half, h=h: sides[h][1].at[pl.ds(half * (PIECE // 2), PIECE // 2)],
        )
        for h, (me, plus, minus) in enumerate(owners)
    ]

    def piece_to_sibling(h, index, half, source=None):
        block = big_view(c, h, index, half)
        return remote(block if source is None else source, block, sf_s.at[h, index, half], sf_r.at[h, index, half], sibling)

    def keep(h, half):
        source = sides[h][1].at[pl.ds(half * (PIECE // 2), PIECE // 2)]
        return pltpu.make_async_copy(source, big_view(c, h, owners[h][0], half), own_sem.at[h, half])

    dog[2 * y] = do_ref[0:HALF, :]
    statg[2 * y] = stat_ref[0]
    dqacc[...] = jnp.zeros_like(dqacc)
    for copy in swaps:
        copy.wait_recv()
    dos.own(1)
    for rel, peer in y_peers:
        go(stats_to(1, rel, peer))
    dos.forward()
    dos.near()
    dos.far()
    for upper in range(2):
        for rel, peer in y_peers:
            slot = 2 * ((y + rel) % 4) + upper
            remote(stat_ref.at[0], statg.at[slot], st_s.at[0, 0], st_r.at[slot], sibling).wait_recv()

    def windows_relayed():
        for load in loads[:3]:
            load.wait()
        early_spread()
        for ring in reduces:
            ring.relay()

    def windows_summed():
        for ring, gather, (piece, full, me, _, _) in zip(reduces, gathers, sides):
            ring.finish()
            for half in range(2):
                total = window(piece, me, half)[...].astype(FULL) + ring.arrived(half)
                window(full, me, half)[...] = total.astype(LOW)
                gather.own(half)

    def windows_forwarded():
        early_summed()
        for gather in gathers:
            gather.forward()

    def pieces_sent(h):
        for half in range(2):
            pieces[h].own(half)
            source = sides[h][1].at[pl.ds(half * (PIECE // 2), PIECE // 2)]
            go(piece_to_sibling(h, owners[h][0], half, source))
            keep(h, half).start()

    def windows_gathered():
        for gather in gathers:
            gather.near()
            gather.far()
        pieces_sent(1)

    def pieces_near(h):
        pieces[h].near()
        for rel in (1, 3):
            for half in range(2):
                go(piece_to_sibling(h, (owners[h][0] + rel) % 4, half))

    def pieces_far(h):
        pieces[h].far()
        for half in range(2):
            go(piece_to_sibling(h, (owners[h][0] + 2) % 4, half))

    def tile(i, first_q, slot, first_k, masked):
        queries, out_grads = q_in[i], dog[i]
        lse, delta = statg[i, 0:1, :], statg[i, 1:2, :]
        if masked:
            token = first_q + lax.broadcasted_iota(jnp.int32, (1, HALF), 1)
            begin = begin_of(token, starts_ref)
        dq_part = None
        for n in range(2):
            rows = pl.ds(n * 256, 256)
            keys, values = k_in[slot, rows], v_in[slot, rows]
            scores = lax.dot_general(keys, queries, NT, preferred_element_type=FULL)
            prob_grad = lax.dot_general(values, out_grads, NT, preferred_element_type=FULL)
            soft = jnp.exp(scores - lse)
            if masked:
                key_index = first_k + n * 256 + lax.broadcasted_iota(jnp.int32, (256, 1), 0)
                soft = jnp.where((key_index <= token) & (key_index >= begin), soft, 0.0)
            score_grad = (soft * (prob_grad - delta)).astype(LOW)
            dvacc[rows, :] += jnp.dot(soft.astype(LOW), out_grads, preferred_element_type=FULL)
            dkacc[rows, :] += jnp.dot(score_grad, queries, preferred_element_type=FULL)
            part = jnp.dot(ktbuf[:, n * 256 : (n + 1) * 256], score_grad, preferred_element_type=FULL)
            dq_part = part if dq_part is None else dq_part + part
        dqacc[i] = dqacc[i] + dq_part

    place_of = {2: 0, 1: 1, 3: 2}
    kvs = RingReduce(
        lambda rel, half: kvsrc.at[place_of[rel], half],
        lambda half: kvpass.at[half],
        lambda side, half: kvgot.at[side, half],
        xp, xm, sems, 7,
    )
    between = {
        (0, 0): windows_relayed,
        (0, 1): windows_summed,
        (1, 0): windows_forwarded,
        (1, 1): windows_gathered,
        (2, 1): pieces[1].forward,
        (2, 0): early_passed,
        (3, 0): lambda: pieces_sent(0),
        (3, 1): lambda: pieces_near(1),
    }
    for step, rel in enumerate((2, 1, 3, 0)):
        pair = (x + rel) % 4
        for turn in range(2):
            if (step, turn) in between:
                between[step, turn]()
            cc = 1 - c if turn == 0 else c
            slot = pair * 2 + cc
            first_k = 4096 * pair + 1024 * y + BLK * cc
            dkacc[...] = jnp.zeros_like(dkacc)
            dvacc[...] = jnp.zeros_like(dvacc)
            ktbuf[...] = jnp.transpose(k_in[slot])

            def visit(i, carry):
                first_q = tile_first(i, x, c)
                some = first_k <= first_q + (HALF - 1)
                full = (first_k + BLK - 1 <= first_q) & (first_k > 0) & (first_q < 31 * BLK)

                @pl.when(full)
                def _():
                    tile(i, first_q, slot, first_k, False)

                @pl.when(some & jnp.logical_not(full))
                def _():
                    tile(i, first_q, slot, first_k, True)

                return carry

            lax.fori_loop(0, 8, visit, 0)
            to_sibling = remote(sibsend.at[step], sibrecv.at[step], sib_s.at[step], sib_r.at[step], sibling)
            if turn == 0:
                sibsend[step, 0] = dkacc[...].astype(LOW)
                sibsend[step, 1] = dvacc[...].astype(LOW)
                go(to_sibling)
            else:
                to_sibling.wait_recv()
                for half, ref in enumerate((dkacc, dvacc)):
                    both = ref[...] + sibrecv[step, half].astype(FULL)
                    if rel == 0:
                        ref[...] = both
                    else:
                        kvsrc[place_of[rel], half] = both.astype(LOW)
                if rel == 2:
                    kvs.start(0, 1)
                elif rel == 1:
                    kvs.start(3)
                elif rel == 3:
                    kvs.start(2)
                    kvs.relay()

    kvs.finish()
    zrows = BLK // 4
    for n in range(4):
        for half, ref in enumerate((dkacc, dvacc)):
            rows = pl.ds(n * zrows, zrows)
            whole = ref[rows, :] + kvgot[0, half, rows, :].astype(FULL) + kvgot[1, half, rows, :].astype(FULL)
            zpart[n, half] = whole.astype(LOW)
    zs = RingReduce(
        lambda rel, half: zpart.at[(z + rel) % 4, half],
        lambda half: zpass.at[half],
        lambda side, half: zgot.at[side, half],
        zp, zm, sems, 9,
    )
    zg = RingGather(lambda index, half: dkv_ref.at[index, half], z, zp, zm, sems, 10)
    zs.start()

    def cast(i, carry):
        dqsend[i] = jnp.transpose(dqacc[i]).astype(LOW)
        return carry

    lax.fori_loop(0, 8, cast, 0)
    dqs = RingReduce(
        lambda rel, half: dqsend.at[2 * ((y + rel) % 4) + half],
        lambda half: dqpass.at[half],
        lambda side, half: dqgot.at[side, half],
        yp, ym, sems, 8,
    )
    dqs.start()
    zs.relay()
    dqs.relay()
    zs.finish()
    for half in range(2):
        dkv_ref[z, half] = (zpart[z, half].astype(FULL) + zs.arrived(half)).astype(LOW)
        zg.own(half)
    for load in loads[3:]:
        load.wait()
    dqs.finish()
    back = remote(dqback, dqhigh, sw_s.at[2], sw_r.at[2], partner)
    dqback[...] = (dqsend[2 * y + 1].astype(FULL) + dqs.arrived(1)).astype(LOW)
    go(back)

    draws = RingGather(
        lambda index, half: draw_ref.at[pl.ds(half * HALF, HALF), pl.ds(pl.multiple_of(index * HD, HD), HD)],
        z, zp, zm, sems, 11,
    )

    def unrotated(grad, raw, gain, rows):
        cosine, sine = cos_ref[rows, :], sin_ref[rows, :]
        first, second = grad[:, : HD // 2], grad[:, HD // 2 :]
        turned = jnp.concatenate([first * cosine + second * sine, second * cosine - first * sine], axis=1)
        inverse = lax.rsqrt(jnp.mean(raw * raw, axis=1, keepdims=True) + EPS)
        unit = raw * inverse
        scaled = gain * turned
        raw_grad = inverse * (scaled - unit * jnp.mean(unit * scaled, axis=1, keepdims=True))
        return raw_grad.astype(LOW), jnp.sum(unit * turned, axis=0, keepdims=True)

    gain_grad = None
    for half in range(2):
        if half == 0:
            grad = dqsend[2 * y].astype(FULL) + dqs.arrived(0)
        else:
            back.wait_recv()
            grad = dqhigh[...].astype(FULL)
        rows = pl.ds(half * HALF, HALF)
        raw_grad, piece = unrotated(grad * (HD**-0.5), raw_ref[rows, :], qgain_ref[...], rows)
        draw_ref[rows, pl.ds(pl.multiple_of(z * HD, HD), HD)] = raw_grad
        draws.own(half)
        gain_grad = piece if gain_grad is None else gain_grad + piece
    gaing[z] = jnp.broadcast_to(gain_grad, (8, HD))
    for n, peer in enumerate((zp, zm, z2)):
        go(remote(gaing.at[z], gaing.at[z], gn_s.at[n], gn_r.at[z], peer))

    chunk_rows = normed_t.shape[0] // 8

    def weight_grad(m, rhs):
        def block(r, carry):
            lhs = normed_t[pl.ds(pl.multiple_of(r * chunk_rows, 16), chunk_rows), :]
            tile = jnp.dot(lhs, rhs[...], preferred_element_type=FULL).astype(LOW)
            part[pl.ds(pl.multiple_of((8 * m + r) * chunk_rows, 16), chunk_rows), :] = tile
            return carry

        lax.fori_loop(0, 8, block, 0)

    zg.forward()
    weight_grad(0, draw_ref.at[:, pl.ds(pl.multiple_of(z * HD, HD), HD)])
    draws.forward()
    zg.near()
    zg.far()
    key_gain_grad = None
    for n in range(4):
        rows = pl.ds(n * zrows, zrows)
        raw_grad, piece = unrotated(dkv_ref[n, 0].astype(FULL), kraw_ref[rows, :], kgain_ref[...], rows)
        dkraw[rows, :] = raw_grad
        dvrow[rows, :] = dkv_ref[n, 1]
        key_gain_grad = piece if key_gain_grad is None else key_gain_grad + piece
    for rel in (1, 3, 2):
        other = (z + rel) % 4
        remote(gaing.at[z], gaing.at[other], gn_s.at[0], gn_r.at[other], sibling).wait_recv()
    query_gain_grad = sum(gaing[n, 0:1, :] for n in range(4))
    number = lax.broadcasted_iota(jnp.int32, (16, HD), 0)
    both = jnp.where(number == 0, query_gain_grad, jnp.where(number == 1, key_gain_grad, 0.0))
    part[pl.ds(24 * chunk_rows, 16), :] = both.astype(LOW)
    part[pl.ds(24 * chunk_rows + 16, LATE), :] = jnp.zeros((LATE, HD), LOW)
    weight_grad(1, dkraw)
    weight_grad(2, dvrow)

    side = 16 * LATE

    def late_piece(ref, core, owner):
        return rows_at(ref, side * core + LATE * owner, LATE)

    cross = remote(rows_at(part, side * (1 - c), side), core_recv, c_s.at[0], c_r.at[0], sibling)
    go(cross)
    cross.wait_recv()

    def add(r, carry):
        both = part[pl.ds(pl.multiple_of(side * c + 2 * LATE * r, 16), 2 * LATE), :].astype(FULL)
        rows = pl.ds(pl.multiple_of(2 * LATE * r, 16), 2 * LATE)
        half_sum[rows, :] = (both + core_recv[rows, :].astype(FULL)).astype(LOW)
        return carry

    lax.fori_loop(0, 8, add, 0)
    for n, (a, b) in enumerate(shifts):
        target = ((x + a) % 4) * 4 + (y + b) % 4
        go(remote(late_piece(half_sum, 0, target), plane_recv.at[chip], p_s.at[n], p_r.at[chip], plane[n]))

    pieces[0].forward()
    pieces_far(1)
    draws.near()
    draws.far()
    gain_row = None
    for half in range(2):
        rows = pl.ds(half * HALF, HALF)
        grad = lax.dot_general(draw_ref[rows, :], wq_ref[...], NT, preferred_element_type=FULL)
        grad = grad + lax.dot_general(dkraw[rows, :], wk_ref[...], NT, preferred_element_type=FULL)
        grad = grad + lax.dot_general(dvrow[rows, :], wv_ref[...], NT, preferred_element_type=FULL)
        value = tok_ref[rows, :].astype(FULL)
        inverse = lax.rsqrt(jnp.mean(value * value, axis=1, keepdims=True) + EPS)
        unit = value * inverse
        scaled = igain_ref[...] * grad
        back_grad = inverse * (scaled - unit * jnp.mean(unit * scaled, axis=1, keepdims=True))
        tgrad_ref[rows, :] = resid_ref[rows, :] + back_grad
        piece = jnp.sum(unit * grad, axis=0, keepdims=True)
        gain_row = piece if gain_row is None else gain_row + piece
    grow[0] = jnp.broadcast_to(gain_row, grow.shape[1:])
    to_core = remote(grow.at[0], grow.at[1], i_s.at[15], i_r.at[16], sibling)
    go(to_core)

    total = late_piece(half_sum, 0, chip)[...].astype(FULL)
    for a, b in shifts:
        source = ((x + a) % 4) * 4 + (y + b) % 4
        remote(late_piece(half_sum, 0, 0), plane_recv.at[source], p_s.at[0], p_r.at[source], sibling).wait_recv()
        total = total + plane_recv[source].astype(FULL)

    def piece_of(owner):
        return late_piece(late_ref, c, owner)

    piece_of(chip)[...] = total.astype(LOW)
    for n in range(15):
        go(remote(piece_of(chip), piece_of(chip), g_s.at[n], g_r.at[chip], plane[n]))
    go(remote(piece_of(chip), piece_of(chip), f_s.at[chip], f_r.at[chip], sibling))
    to_core.wait_recv()
    grecv[chip] = grow[0] + grow[1]
    for n in range(15):
        go(remote(grecv.at[chip], grecv.at[chip], i_s.at[n], i_r.at[chip], plane[n]))
    pieces_near(0)
    pieces_far(0)
    for a, b in shifts:
        source = ((x + a) % 4) * 4 + (y + b) % 4
        remote(late_piece(half_sum, 0, 0), piece_of(source), g_s.at[0], g_r.at[source], sibling).wait_recv()
        go(remote(piece_of(source), piece_of(source), f_s.at[source], f_r.at[source], sibling))
    for a, b in shifts:
        source = ((x + a) % 4) * 4 + (y + b) % 4
        remote(grecv.at[chip], grecv.at[source], i_s.at[0], i_r.at[source], sibling).wait_recv()
    dgain_ref[...] = sum(grecv[n] for n in range(16))
    for n in range(16):
        theirs = late_piece(late_ref, 1 - c, n)
        remote(late_piece(half_sum, 0, 0), theirs, f_s.at[0], f_r.at[n], sibling).wait_recv()
    early_done()
    for h in range(2):
        for half in range(2):
            keep(h, half).wait()
            for n in range(4):
                piece_to_sibling(h, n, half).wait_recv()
    for ring in [dos, kvs, dqs, zs, zg, draws] + reduces + gathers + pieces:
        ring.drain()
    for copy in copies:
        copy.wait_send()


def backward_attention(doc_starts, *operands):
    width = operands[2].shape[1]
    streamed = operands[8:]
    return pl.pallas_call(
        attn_backward,
        name="attn_backward",
        out_shape=[
            shape(LOW, 32 * LATE, HD),
            shape(LOW, 2 * EARLY, width),
            shape(FULL, BLK, width),
            shape(FULL, 8, width),
            shape(LOW, 2 * ROWS + 64, width),
        ],
        in_specs=[SMEM] + [VMEM] * 8 + [ANY] * 13,
        out_specs=[VMEM] * 4 + [ANY],
        scratch_shapes=[
            vmem(LOW, 8, HALF, HD),
            vmem(FULL, 8, 8, HALF),
            vmem(FULL, 8, HD, HALF),
            vmem(FULL, BLK, HD),
            vmem(FULL, BLK, HD),
            vmem(LOW, HD, BLK),
            vmem(LOW, 4, 2, BLK, HD),
            vmem(LOW, 4, 2, BLK, HD),
            vmem(LOW, 3, 2, BLK, HD),
            vmem(LOW, 2, BLK, HD),
            vmem(LOW, 2, 2, BLK, HD),
            vmem(LOW, 8, HALF, HD),
            vmem(LOW, 2, HALF, HD),
            vmem(LOW, 2, 2, HALF, HD),
            vmem(LOW, HALF, HD),
            vmem(LOW, HALF, HD),
            vmem(LOW, 4, 2, BLK // 4, HD),
            vmem(LOW, 2, BLK // 4, HD),
            vmem(LOW, 2, 2, BLK // 4, HD),
            vmem(FULL, 4, 8, HD),
            vmem(LOW, 2, WINDOW, width),
            vmem(LOW, 2, 2, WINDOW, width),
            vmem(LOW, PIECE, width),
            vmem(LOW, PIECE, width),
            vmem(LOW, BLK, 4 * HD),
            vmem(LOW, 4, 2, BLK // 4, HD),
            vmem(LOW, BLK, HD),
            vmem(LOW, BLK, HD),
            vmem(LOW, 32 * LATE, HD),
            vmem(LOW, 16 * LATE, HD),
            vmem(LOW, 16 * LATE, HD),
            vmem(LOW, 16, LATE, HD),
            vmem(FULL, 2, 8, width),
            vmem(FULL, 16, 8, width),
            vmem(LOW, EARLY, width),
            vmem(LOW, EARLY, width),
            vmem(LOW, 16, 16, width),
            *[vmem(operand.dtype, *operand.shape) for operand in streamed],
            dma(12, 6), dma(12, 6), dma(2, 3), dma(8), dma(3), dma(3), dma(4), dma(4), dma(3), dma(4),
            dma(2, 4, 2), dma(2, 4, 2), dma(2, 2),
            dma(13), dma(2), dma(2), dma(15), dma(16), dma(15), dma(16), dma(16), dma(16), dma(16), dma(17),
            dma(KEEPERS), dma(16), dma(15), dma(16), dma(KEEPERS), dma(KEEPERS),
        ],
        compiler_params=params(2, 58),
        cost_estimate=cost(15),
    )(doc_starts, *operands)


def per_device(
    tokens,
    cotangent,
    doc_starts,
    query_weight,
    key_weight,
    value_weight,
    out_weight,
    gate_weight,
    up_weight,
    down_weight,
    input_gain,
    attn_gain,
    prenorm_gain,
    post_gain,
    query_gain,
    key_gain,
):
    row_count = tokens.shape[0]
    first_row = lax.axis_index("seq") * row_count
    own_index = first_row + jnp.arange(row_count, dtype=jnp.int32)
    own_position = doc_layout(doc_starts, own_index)[1]
    cos_table, sine_table = rope_tables(own_position, HD)
    query_scale = HD ** (-0.5)
    inputs = tokens.astype(jnp.float32)
    query_weight_all = lax.all_gather(query_weight, "head", axis=1, tiled=True)
    out_weight_all = lax.all_gather(out_weight, "head", axis=0, tiled=True)
    normed = rms_norm(inputs, input_gain)
    normed_low = normed.astype(jnp.bfloat16)
    query_raw = jnp.dot(normed_low, query_weight, preferred_element_type=jnp.float32)
    key_raw = jnp.dot(normed_low, key_weight, preferred_element_type=jnp.float32)
    value_low = jnp.dot(normed_low, value_weight, preferred_element_type=jnp.float32).astype(
        jnp.bfloat16
    )

    def query_piece(source, scaling):
        return rotate(rms_norm(source, scaling), cos_table, sine_table) * query_scale

    def key_piece(source, scaling):
        return rotate(rms_norm(source, scaling), cos_table, sine_table)

    query_rows = query_piece(query_raw, query_gain)
    query_low = query_rows.astype(jnp.bfloat16)
    key_rows = key_piece(key_raw, key_gain)
    key_low = key_rows.astype(jnp.bfloat16)
    mix_all, lse_rows, q_all, k_all, v_all = forward_attention(
        doc_starts, query_low, key_low, value_low
    )
    width = tokens.shape[1]
    mixed, mix_grad, stats, resid, early, piece_a, piece_b = middle(
        attn_gain.reshape(1, width),
        prenorm_gain.reshape(1, width),
        post_gain.reshape(1, width),
        lse_rows,
        mix_all,
        out_weight_all,
        tokens,
        cotangent,
        jnp.transpose(gate_weight),
        jnp.transpose(up_weight),
        down_weight,
    )
    late, early, tokens_grad, input_gain_rows, big = backward_attention(
        doc_starts,
        mix_grad,
        stats,
        piece_a,
        piece_b,
        query_gain.reshape(1, HD),
        key_gain.reshape(1, HD),
        input_gain.reshape(1, width),
        early,
        q_all,
        k_all,
        v_all,
        query_raw,
        key_raw,
        cos_table[:, : HD // 2],
        sine_table[:, : HD // 2],
        key_weight,
        value_weight,
        jnp.transpose(normed_low),
        query_weight_all,
        tokens,
        resid,
    )
    input_gain_grad = input_gain_rows[0]
    query_weight_grad = late[:width].astype(jnp.float32)
    key_weight_grad = late[width : 2 * width].astype(jnp.float32)
    value_weight_grad = late[2 * width : 3 * width].astype(jnp.float32)
    query_gain_grad = late[3 * width].astype(jnp.float32)
    key_gain_grad = late[3 * width + 1].astype(jnp.float32)
    out_weight_grad = early[:HD].astype(jnp.float32)
    rest = early[HD : HD + 64]
    gains = early[HD + 64 : HD + 67].astype(jnp.float32)
    attn_gain_grad, prenorm_gain_grad, post_gain_grad = gains[0], gains[1], gains[2]
    hidden = gate_weight.shape[1]
    gate_weight_grad = jnp.transpose(big[:hidden].astype(jnp.float32))
    up_weight_grad = jnp.transpose(big[hidden : 2 * hidden].astype(jnp.float32))
    down_weight_grad = big[2 * hidden :].astype(jnp.float32)
    down_weight_grad = lax.dynamic_update_slice(
        down_weight_grad, rest.astype(jnp.float32), (hidden - rest.shape[0], 0)
    )
    return (
        mixed,
        tokens_grad,
        query_weight_grad,
        key_weight_grad,
        value_weight_grad,
        out_weight_grad,
        gate_weight_grad,
        up_weight_grad,
        down_weight_grad,
        input_gain_grad,
        attn_gain_grad,
        prenorm_gain_grad,
        post_gain_grad,
        query_gain_grad,
        key_gain_grad,
    )


def solution(mesh):
    placed = (
        P("seq", None),
        P("seq", None),
        P(),
        P(None, "head"),
        P(),
        P(),
        P("head", None),
        P(None, "head"),
        P(None, "head"),
        P("head", None),
        P(),
        P(),
        P(),
        P(),
        P(),
        P(),
    )
    return jax.shard_map(
        per_device,
        mesh=mesh,
        in_specs=placed,
        out_specs=(
            P("seq", None),
            P("seq", None),
            P(None, "head"),
            P(),
            P(),
            P("head", None),
            P(None, "head"),
            P(None, "head"),
            P("head", None),
            P(),
            P(),
            P(),
            P(),
            P(),
            P(),
        ),
        check_vma=False,
    )
```

```python
import functools
import math

import jax
import jax.numpy as jnp
from jax import lax
from jax.experimental import pallas as pl
from jax.experimental.pallas import tpu as pltpu
from jax.sharding import PartitionSpec as P

HD = 256


EPS = 1e-06
THETA = 1000000.0
NEG = -1e30


def rms_norm(values, scaling):
    return values * lax.rsqrt(jnp.mean(values * values, axis=-1, keepdims=True) + EPS) * scaling


def doc_layout(doc_starts, token_index):
    before = doc_starts[None, :] <= token_index[:, None]
    segment = jnp.sum(before.astype(jnp.int32), axis=1)
    doc_begin = jnp.max(jnp.where(before, doc_starts[None, :], 0), axis=1)
    return (segment, token_index - doc_begin)


def rope_tables(position, head_width):
    half_width = head_width // 2
    inverse = jnp.exp(
        -math.log(THETA) * 2.0 * jnp.arange(half_width, dtype=jnp.float32) / head_width
    )
    angles = position.astype(jnp.float32)[:, None] * inverse[None, :]
    return (jnp.cos(angles), jnp.sin(angles))


def rotate(values, cos_table, sine_table):
    half_width = values.shape[-1] // 2
    first, second = values[..., :half_width], values[..., half_width:]
    return jnp.concatenate(
        [first * cos_table - second * sine_table, second * cos_table + first * sine_table], axis=-1
    )


MESH_ID = pl.DeviceIdType.MESH
HALF = 256
BLK = 512
LOW = jnp.bfloat16
FULL = jnp.float32
NT = (((1,), (1,)), ((), ()))


def place():
    s = lax.axis_index("seq")
    return s // 8, (s // 2) % 4, s % 2, lax.axis_index("head")


def at(x, y, c, z):
    return ((x % 4) * 8 + (y % 4) * 2 + c, z % 4)


def greet(peers):
    barrier = pltpu.get_barrier_semaphore()
    for peer in peers:
        pl.semaphore_signal(barrier, inc=1, device_id=peer, device_id_type=MESH_ID)
    pl.semaphore_wait(barrier, len(peers))


def remote(src, dst, send_sem, recv_sem, peer):
    return pltpu.make_async_remote_copy(
        src_ref=src,
        dst_ref=dst,
        send_sem=send_sem,
        recv_sem=recv_sem,
        device_id=peer,
        device_id_type=MESH_ID,
    )


def rows_at(ref, start, size):
    return ref.at[pl.ds(pl.multiple_of(start, 16), size)]


class RingGather:
    def __init__(self, view, me, plus, minus, sems, ring, source=None):
        send, recv = sems

        def near(rel, half):
            return view((me + rel) % 4, half)

        own = source or (lambda half: near(0, half))
        plan = (
            (own(0), near(0, 0), plus),
            (own(1), near(0, 1), plus),
            (near(3, 0), near(3, 0), plus),
            (own(0), near(0, 0), minus),
            (own(1), near(0, 1), minus),
            (near(1, 1), near(1, 1), minus),
        )
        self.copies = [
            remote(src, dst, send.at[ring, k], recv.at[ring, k], peer) for k, (src, dst, peer) in enumerate(plan)
        ]

    def own(self, half):
        self.copies[half].start()
        self.copies[3 + half].start()

    def forward(self):
        self.copies[0].wait_recv()
        self.copies[2].start()
        self.copies[4].wait_recv()
        self.copies[5].start()

    def near(self):
        self.copies[1].wait_recv()
        self.copies[3].wait_recv()

    def far(self):
        self.copies[2].wait_recv()
        self.copies[5].wait_recv()

    def drain(self):
        for copy in self.copies:
            copy.wait_send()


class RingReduce:
    def __init__(self, view, passing, got, plus, minus, sems, ring):
        send, recv = sems
        self.view, self.passing, self.got = view, passing, got
        plan = (
            (view(2, 0), passing(0), minus),
            (view(2, 1), passing(1), plus),
            (view(3, 1), got(0, 1), minus),
            (view(1, 0), got(1, 0), plus),
            (passing(0), got(0, 0), minus),
            (passing(1), got(1, 1), plus),
        )
        self.copies = [
            remote(src, dst, send.at[ring, k], recv.at[ring, k], peer) for k, (src, dst, peer) in enumerate(plan)
        ]

    def start(self, *numbers):
        for k in numbers or (0, 1, 2, 3):
            self.copies[k].start()

    def relay(self):
        for half, rel in ((0, 3), (1, 1)):
            self.copies[half].wait_recv()
            land, term = self.passing(half), self.view(rel, half)
            land[...] = (land[...].astype(FULL) + term[...].astype(FULL)).astype(LOW)
            self.copies[4 + half].start()

    def finish(self):
        for k in (2, 3, 4, 5):
            self.copies[k].wait_recv()

    def arrived(self, half):
        return self.got(0, half)[...].astype(FULL) + self.got(1, half)[...].astype(FULL)

    def drain(self):
        for copy in self.copies:
            copy.wait_send()


def tile_first(i, x, c):
    column = jnp.where(i % 2 == 1, 3 - x, x)
    return BLK * (8 * column + 2 * (i // 2) + c) + HALF * (i % 2)


def begin_of(token, starts_ref):
    begin = jnp.zeros_like(token)
    for n in range(starts_ref.shape[0]):
        start = starts_ref[n]
        begin = jnp.where(start <= token, start, begin)
    return begin


def attn_forward(
    starts_ref, q_ref, k_ref, v_ref, wout_hbm,
    mix_ref, lse_ref, q_out, k_out, v_out, wout_all,
    qg_ref, kg_ref, vg_ref, acc, lacc, osend, opass, ogot, lsend, lrecv, hsend, lhsend,
    rs, rr, sib_s, sib_r, l_s, l_r, sw_s, sw_r, keep_sem,
):
    x, y, c, z = place()
    xp, xm, yp, ym = at(x + 1, y, c, z), at(x + 3, y, c, z), at(x, y + 1, c, z), at(x, y + 3, c, z)
    zp, zm, y2 = at(x, y, c, z + 1), at(x, y, c, z + 3), at(x, y + 2, c, z)
    sibling, partner = at(x, y, 1 - c, z), at(3 - x, y, c, z)
    greet([partner, sibling, xp, xm, yp, ym, y2, zp, zm])
    copies = []

    def go(copy):
        copy.start()
        copies.append(copy)

    q_low, q_high = q_ref.at[pl.ds(0, HALF)], q_ref.at[pl.ds(HALF, HALF)]
    swap = remote(q_high, qg_ref.at[2 * y + 1], sw_s.at[0], sw_r.at[0], partner)
    go(swap)

    def kv_view(index, half):
        return (kg_ref, vg_ref)[half].at[2 * index + c]

    kv = RingGather(kv_view, x, xp, xm, (rs, rr), 0, lambda half: (k_ref, v_ref)[half])
    kv.own(0)
    kv.own(1)
    qs = RingGather(
        lambda index, half: qg_ref.at[2 * index + half], y, yp, ym, (rs, rr), 1,
        lambda half: q_low if half == 0 else qg_ref.at[2 * y + 1],
    )
    qs.own(0)

    def pass_on(index, half, source=None):
        block = kv_view(index, half)
        return remote(block if source is None else source, block, sib_s.at[index, half], sib_r.at[index, half], sibling)

    for half, source in enumerate((k_ref, v_ref)):
        go(pass_on(x, half, source))
    wide = wout_hbm.shape[0]

    def wout_view(index, half):
        return rows_at(wout_all, wide * index + half * (wide // 2), wide // 2)

    wouts = RingGather(
        wout_view, z, zp, zm, (rs, rr), 4, lambda half: wout_hbm.at[pl.ds(half * (wide // 2), wide // 2)]
    )
    wouts.own(0)
    wouts.own(1)
    wout_keep = pltpu.make_async_copy(wout_hbm, rows_at(wout_all, wide * z, wide), keep_sem.at[3])
    wout_keep.start()
    qg_ref[2 * y] = q_ref[0:HALF, :]
    kg_ref[2 * x + c] = k_ref[...]
    vg_ref[2 * x + c] = v_ref[...]
    acc[...] = jnp.zeros_like(acc)
    lacc[...] = jnp.zeros_like(lacc)
    swap.wait_recv()
    qs.own(1)
    kv.forward()
    qs.forward()
    kv.near()
    for rel in (1, 3):
        for half in range(2):
            go(pass_on((x + rel) % 4, half))
    qs.near()
    qs.far()
    wouts.forward()

    def chunk(i, first_q, pair, first_k, masked):
        queries = qg_ref[i]
        if masked:
            token = first_q + lax.broadcasted_iota(jnp.int32, (HALF, 1), 0)
            begin = begin_of(token, starts_ref)
        total = None
        sums = None
        for cc in range(2):
            keys, values = kg_ref[pair * 2 + cc], vg_ref[pair * 2 + cc]
            scores = lax.dot_general(queries, keys, NT, preferred_element_type=FULL)
            exps = jnp.exp(scores)
            if masked:
                key_index = first_k + cc * BLK + lax.broadcasted_iota(jnp.int32, (1, BLK), 1)
                exps = jnp.where((key_index <= token) & (key_index >= begin), exps, 0.0)
            part = jnp.dot(exps.astype(LOW), values, preferred_element_type=FULL)
            total = part if total is None else total + part
            for n in range(BLK // 128):
                piece = exps[:, n * 128 : (n + 1) * 128]
                sums = piece if sums is None else sums + piece
        acc[i] = acc[i] + total
        lacc[i] = lacc[i] + sums

    def visit(i, pair):
        first_q, first_k = tile_first(i, x, c), 4096 * pair + 1024 * y
        some = first_k <= first_q + (HALF - 1)
        full = (first_k + 1023 <= first_q) & (first_k > 0) & (first_q < 31 * BLK)

        @pl.when(full)
        def _():
            chunk(i, first_q, pair, first_k, False)

        @pl.when(some & jnp.logical_not(full))
        def _():
            chunk(i, first_q, pair, first_k, True)

    numer = RingReduce(
        lambda rel, half: osend.at[2 * ((y + rel) % 4) + half],
        lambda half: opass.at[half],
        lambda side, half: ogot.at[side, half],
        yp, ym, (rs, rr), 2,
    )

    def sums_to(rel, peer):
        index = (y + rel) % 4
        return remote(lsend.at[pl.ds(2 * index, 2)], lrecv.at[y], l_s.at[rel - 1], l_r.at[y], peer)

    keeps = [
        pltpu.make_async_copy(src, dst, keep_sem.at[n])
        for n, (src, dst) in enumerate(((qg_ref, q_out), (kg_ref, k_out), (vg_ref, v_out)))
    ]
    for rel, peer in ((2, y2), (1, yp), (3, ym), (0, None)):
        first = 2 * ((y + rel) % 4)
        if rel == 2:
            for turn in (0, 1, 3, 2):
                pair = (x + turn) % 4
                if turn == 2:
                    kv.far()
                    for half in range(2):
                        go(pass_on(pair, half))
                for half in range(2):
                    pass_on(pair, half).wait_recv()
                for upper in range(2):
                    visit(first + upper, pair)
            for keep in keeps:
                keep.start()
        else:

            def one(n, carry):
                visit(first + n // 4, n % 4)
                return carry

            lax.fori_loop(0, 8, one, 0)

        for upper in range(2):
            i = first + upper
            osend[i] = acc[i].astype(LOW)
            row = jnp.sum(jnp.transpose(lacc[i]), axis=0, keepdims=True)
            lsend[i] = jnp.broadcast_to(row, (8, HALF))
        if rel == 2:
            numer.start(0, 1)
        elif rel == 1:
            numer.start(3)
        elif rel == 3:
            numer.start(2)
            numer.relay()
        if rel > 0:
            go(sums_to(rel, peer))
    lrecv[y] = lsend[pl.ds(2 * y, 2)]
    for rel in (1, 3, 2):
        remote(lsend.at[pl.ds(0, 2)], lrecv.at[(y + rel) % 4], l_s.at[0], l_r.at[(y + rel) % 4], sibling).wait_recv()
    numer.finish()

    def mix_view(index, half):
        return mix_ref.at[pl.ds(half * HALF, HALF), pl.ds(pl.multiple_of(index * HD, HD), HD)]

    mixes = RingGather(mix_view, z, zp, zm, (rs, rr), 3)
    returns = (
        remote(hsend, mix_view(z, 1), sw_s.at[1], sw_r.at[1], partner),
        remote(lhsend, lse_ref.at[1], sw_s.at[2], sw_r.at[2], partner),
    )
    for half in (1, 0):
        denom = sum(lrecv[n, half] for n in range(4))
        total = osend[2 * y + half].astype(FULL) + numer.arrived(half)
        inverse = jnp.transpose(jnp.broadcast_to(1.0 / denom[0:1, :], (128, HALF)))
        scaled = (total * jnp.concatenate([inverse, inverse], axis=1)).astype(LOW)
        if half == 1:
            hsend[...] = scaled
            lhsend[...] = jnp.log(denom)
            for copy in returns:
                go(copy)
        else:
            mix_view(z, 0)[...] = scaled
            lse_ref[0] = jnp.log(denom)
    mixes.own(0)
    for copy in returns:
        copy.wait_recv()
    mixes.own(1)
    wouts.near()
    wouts.far()
    wout_keep.wait()
    mixes.forward()
    mixes.near()
    mixes.far()
    for ring in (kv, qs, numer, mixes, wouts):
        ring.drain()
    for keep in keeps:
        keep.wait()
    for copy in copies:
        copy.wait_send()


VMEM = pl.BlockSpec(memory_space=pltpu.VMEM)
SMEM = pl.BlockSpec(memory_space=pltpu.SMEM)
ANY = pl.BlockSpec(memory_space=pl.ANY)


def dma(*shape):
    return pltpu.SemaphoreType.DMA(shape)


def shape(dtype, *dims):
    return jax.ShapeDtypeStruct(dims, dtype)


def vmem(dtype, *dims):
    return pltpu.VMEM(dims, dtype)


def params(number, mebibytes):
    return pltpu.CompilerParams(collective_id=number, has_side_effects=True, vmem_limit_bytes=mebibytes << 20)


def cost(gflops):
    return pl.CostEstimate(flops=gflops * 10**9, bytes_accessed=20 * 2**20, transcendentals=0)


def forward_attention(doc_starts, query, key, value, wout):
    return pl.pallas_call(
        attn_forward,
        name="attn_forward",
        out_shape=[
            shape(LOW, BLK, 4 * HD),
            shape(FULL, 2, 8, HALF),
            shape(LOW, 8, HALF, HD),
            shape(LOW, 8, BLK, HD),
            shape(LOW, 8, BLK, HD),
            shape(LOW, 4 * HD, wout.shape[1]),
        ],
        in_specs=[SMEM] + [VMEM] * 3 + [ANY],
        out_specs=[VMEM] * 2 + [ANY] * 4,
        scratch_shapes=[
            vmem(LOW, 8, HALF, HD),
            vmem(LOW, 8, BLK, HD),
            vmem(LOW, 8, BLK, HD),
            vmem(FULL, 8, HALF, HD),
            vmem(FULL, 8, HALF, 128),
            vmem(LOW, 8, HALF, HD),
            vmem(LOW, 2, HALF, HD),
            vmem(LOW, 2, 2, HALF, HD),
            vmem(FULL, 8, 8, HALF),
            vmem(FULL, 4, 2, 8, HALF),
            vmem(LOW, HALF, HD),
            vmem(FULL, 8, HALF),
            dma(5, 6), dma(5, 6), dma(4, 2), dma(4, 2), dma(3), dma(4), dma(3), dma(3), dma(4),
        ],
        compiler_params=params(1, 60),
        cost_estimate=cost(6),
    )(doc_starts, query, key, value, wout)


ROWS = 2560
SIDE = ROWS // 2
PIECE = SIDE // 4
WINDOW = PIECE // 4
CUTS = (0, 448, 896, 1280, 1728, 2144, 2560)


BLOCKS = ((0, 384), (384, 384), (768, 384), (1152, 384), (1536, 192))
PARTS = ((0, 512), (512, 640))
CORNER = 0.7978845608028654


def unit_of(values):
    inverse = lax.rsqrt(jnp.mean(values * values, axis=1, keepdims=True) + EPS)
    return inverse, values * inverse


def norm_back(inverse, unit, scaled):
    return inverse * (scaled - unit * jnp.mean(unit * scaled, axis=1, keepdims=True))


def middle_kernel(
    again_ref, pgain_ref, fgain_ref, lse_ref,
    mix_hbm, wout_hbm, tokens_hbm, cot_hbm, gate_hbm, up_hbm, down_hbm,
    mgrad_ref, stat_ref, early_ref, piece_a_ref, piece_b_ref, mixed_hbm, resid_hbm,
    mixed_ref, resid_ref, weights, wout, mix, tokens, cot, attn_out, left, right, turned, turned_up, aol,
    part_f, part_b, sum_f, sum_b, z_pass, z_got, sib_recv, pass_ab, got_ab, grows,
    in_sem, sib_s, sib_r, rs, rr, out_sem,
):
    x, y, c, z = place()
    xp, xm, yp, ym = at(x + 1, y, c, z), at(x + 3, y, c, z), at(x, y + 1, c, z), at(x, y + 3, c, z)
    zp, zm, sibling = at(x, y, c, z + 1), at(x, y, c, z + 3), at(x, y, 1 - c, z)
    hidden = gate_hbm.shape[0]
    width = weights.shape[1]
    loads = [
        pltpu.make_async_copy(src, dst, in_sem.at[n])
        for n, (src, dst) in enumerate(
            (
                (mix_hbm, mix),
                (wout_hbm, wout),
                (tokens_hbm, tokens),
                (gate_hbm, weights.at[pl.ds(0, hidden)]),
                (up_hbm, weights.at[pl.ds(hidden, hidden)]),
                (down_hbm, weights.at[pl.ds(2 * hidden, hidden)]),
                (cot_hbm, cot),
            )
        )
    ]
    for load in loads:
        load.start()
    greet([xp, xm, yp, ym, zp, zm, sibling])
    sems = (rs, rr)
    thirds = [pl.ds(start, size) for start, size in PARTS]

    def rows_of(r):
        return pl.ds(r * HALF, HALF)

    def head_sum(r, number, part, whole):
        quarter = HALF // 4
        first = r * HALF

        def span(ref, index, half):
            return rows_at(ref, first + quarter * index + half * (quarter // 2), quarter // 2)

        reduce = RingReduce(
            lambda rel, half: span(part, (z + rel) % 4, half),
            lambda half: z_pass.at[number, half],
            lambda side, half: z_got.at[number, side, half],
            zp, zm, sems, 2 * number,
        )
        gather = RingGather(lambda index, half: span(whole, index, half), z, zp, zm, sems, 2 * number + 1)

        def summed():
            reduce.finish()
            for half in range(2):
                own = span(part, z, half)[...].astype(FULL) + reduce.arrived(half)
                span(whole, z, half)[...] = own.astype(LOW)
                gather.own(half)

        def gathered():
            gather.near()
            gather.far()

        return reduce, gather, summed, gathered

    sums = [head_sum(0, 0, part_f, sum_f), head_sum(1, 1, part_f, sum_f)]
    sums += [head_sum(0, 2, part_b, sum_b), head_sum(1, 3, part_b, sum_b)]

    def forward(r, hooks):
        rows, columns = rows_of(r), pl.ds(r * HALF, HALF)
        if r == 0:
            for load in loads[:3]:
                load.wait()
        for third in thirds:
            attn_out[rows, third] = jnp.dot(mix[rows, :], wout[:, third], preferred_element_type=FULL)
        _, unit = unit_of(attn_out[rows, :])
        state = tokens[rows, :].astype(FULL) + unit * again_ref[0:1, :]
        resid_ref[rows, :] = state
        _, unit = unit_of(state)
        right[0, rows, :] = (unit * pgain_ref[0:1, :]).astype(LOW)
        if r == 0:
            for load in loads[3:5]:
                load.wait()
        for n, (start, size) in enumerate(BLOCKS):
            low = right[0, rows, :]
            gate = lax.dot_general(weights[pl.ds(start, size), :], low, NT, preferred_element_type=FULL)
            up = lax.dot_general(weights[pl.ds(hidden + start, size), :], low, NT, preferred_element_type=FULL)
            square = gate * gate
            bend = jnp.tanh(CORNER * gate * (1.0 + 0.044715 * square))
            share = 0.5 * (1.0 + bend)
            gelu = gate * share
            slope = share + 0.5 * gate * (1.0 - bend * bend) * (CORNER * (1.0 + 3.0 * 0.044715 * square))
            act = (gelu * up).astype(LOW)
            left[pl.ds(start, size), columns] = (up * slope).astype(LOW)
            left[pl.ds(hidden + start, size), columns] = gelu.astype(LOW)
            left[pl.ds(2 * hidden + start, size), columns] = act
            turned[:, start : start + size] = jnp.transpose(act)
            if n in hooks:
                hooks[n]()
        if r == 0:
            loads[5].wait()
        for third in thirds:
            part = jnp.dot(
                turned[:, :hidden], weights[pl.ds(2 * hidden, hidden), third], preferred_element_type=FULL
            )
            part_f[rows, third] = part.astype(LOW)

    def backward(r, hooks):
        rows, columns = rows_of(r), pl.ds(r * HALF, HALF)
        if r == 0:
            loads[6].wait()
        inverse, unit = unit_of(sum_f[rows, :].astype(FULL))
        mixed_ref[rows, :] = (resid_ref[rows, :] + unit * fgain_ref[0:1, :]).astype(LOW)
        grad = cot[rows, :].astype(FULL)
        grows[2, r : r + 1, :] = jnp.sum(unit * grad, axis=0, keepdims=True)
        right[1, rows, :] = norm_back(inverse, unit, fgain_ref[0:1, :] * grad).astype(LOW)
        for n, (start, size) in enumerate(BLOCKS):
            act_grad = lax.dot_general(
                weights[pl.ds(2 * hidden + start, size), :], right[1, rows, :], NT, preferred_element_type=FULL
            )
            for first, turn in ((start, turned), (hidden + start, turned_up)):
                span = pl.ds(first, size)
                grads = (act_grad * left[span, columns].astype(FULL)).astype(LOW)
                left[span, columns] = grads
                turn[:, start : start + size] = jnp.transpose(grads)
            if n in hooks:
                hooks[n]()
        for third in thirds:
            part = jnp.dot(turned[:, :hidden], weights[pl.ds(0, hidden), third], preferred_element_type=FULL)
            part = part + jnp.dot(
                turned_up[:, :hidden], weights[pl.ds(hidden, hidden), third], preferred_element_type=FULL
            )
            part_b[rows, third] = part.astype(LOW)

    own_head = pl.ds(pl.multiple_of(z * HD, HD), HD)

    def finish(r):
        rows = rows_of(r)
        grad = sum_b[rows, :].astype(FULL)
        inverse, unit = unit_of(resid_ref[rows, :])
        grows[1, r : r + 1, :] = jnp.sum(unit * grad, axis=0, keepdims=True)
        grad = cot[rows, :].astype(FULL) + norm_back(inverse, unit, pgain_ref[0:1, :] * grad)
        resid_ref[rows, :] = grad
        inverse, unit = unit_of(attn_out[rows, :])
        grows[0, r : r + 1, :] = jnp.sum(unit * grad, axis=0, keepdims=True)
        aol[rows, :] = norm_back(inverse, unit, again_ref[0:1, :] * grad).astype(LOW)
        grads = lax.dot_general(aol[rows, :], wout[own_head, :], NT, preferred_element_type=FULL).astype(LOW)
        mgrad_ref[rows, :] = grads
        products = grads.astype(FULL) * mix[rows, own_head].astype(FULL)
        delta = jnp.sum(jnp.transpose(products), axis=0, keepdims=True)
        number = lax.broadcasted_iota(jnp.int32, (8, HALF), 0)
        stat_ref[r] = jnp.where(number == 1, delta, lse_ref[r])

    sib_send, mine = weights.at[pl.ds(0, ROWS)], weights.at[pl.ds(ROWS, ROWS)]

    def product(core, n, target, added):
        first, size = CUTS[n], CUTS[n + 1] - CUTS[n]
        lhs = left[pl.ds(pl.multiple_of(ROWS * core + first, 16), size), :]
        which = jnp.where(n >= 2, core, 0)
        for third in thirds:
            tile = jnp.dot(lhs, right[which, :, third], preferred_element_type=FULL)
            if added is not None:
                tile = tile + added[pl.ds(first, size), third].astype(FULL)
            target[pl.ds(first, size), third] = tile.astype(LOW)

    def to_sibling(n):
        span = pl.ds(CUTS[n], CUTS[n + 1] - CUTS[n])
        return remote(sib_send.at[span], sib_recv.at[span], sib_s.at[n], sib_r.at[n], sibling)

    def side_ring(h, me, plus, minus):
        return RingReduce(
            lambda rel, half: rows_at(
                weights, ROWS + SIDE * h + PIECE * ((me + rel) % 4) + half * (PIECE // 2), PIECE // 2
            ),
            lambda half: pass_ab.at[h, half],
            lambda side, half: got_ab.at[h, side, half],
            plus, minus, sems, 8 + h,
        )

    rings = (side_ring(0, x, xp, xm), side_ring(1, y, yp, ym))
    outs = [
        pltpu.make_async_copy(src, dst, out_sem.at[n])
        for n, (src, dst) in enumerate(
            ((mixed_ref, mixed_hbm), (resid_ref, resid_hbm))
        )
    ]
    forward(0, {})
    sums[0][0].start()
    forward(1, {3: sums[0][0].relay})
    sums[0][2]()
    sums[1][0].start()
    sums[0][1].forward()
    sums[1][0].relay()
    sums[0][3]()
    backward(0, {1: sums[1][2], 4: sums[1][1].forward})
    sums[2][0].start()
    sums[1][3]()
    backward(1, {2: sums[2][0].relay, 4: sums[2][2]})
    sums[3][0].start()
    outs[0].start()
    count = len(CUTS) - 1
    for part in (range(count // 2), range(count // 2, count)):
        for n in part:
            product(1 - c, n, sib_send, None)
            to_sibling(n).start()
        if part[0] > 0:
            sums[2][1].forward()
            sums[3][0].relay()
        for n in part:
            to_sibling(n).wait_recv()
            product(c, n, mine, sib_recv)
        rings[int(part[0] > 0)].start()
    sums[3][2]()
    sums[2][3]()
    finish(0)
    rings[0].relay()
    sums[3][1].forward()
    rest = jnp.dot(left[2 * ROWS :, :], right[1], preferred_element_type=FULL)
    early_ref[pl.ds(HD, 64), :] = rest.astype(LOW)
    sums[3][3]()
    finish(1)
    outs[1].start()
    rings[1].relay()
    lhs = jnp.transpose(mix[:, own_head])
    for third in thirds:
        early_ref[0:HD, third] = jnp.dot(lhs, aol[:, third], preferred_element_type=FULL).astype(LOW)
    number = lax.broadcasted_iota(jnp.int32, (32, width), 0)
    gains = jnp.zeros((32, width), FULL)
    for n in range(3):
        gains = jnp.where(number == n, grows[n, 0:1, :] + grows[n, 1:2, :], gains)
    early_ref[pl.ds(HD + 64, 32), :] = gains.astype(LOW)
    for h, (ring, me, out) in enumerate(((rings[0], x, piece_a_ref), (rings[1], y, piece_b_ref))):
        ring.finish()
        for half in range(2):
            size = PIECE // 2
            own = rows_at(weights, ROWS + SIDE * h + PIECE * me + half * size, size)[...]
            out[pl.ds(half * size, size), :] = (own.astype(FULL) + ring.arrived(half)).astype(LOW)
    for out in outs:
        out.wait()
    for reduce, gather, _, _ in sums:
        reduce.drain()
        gather.drain()
    for ring in rings:
        ring.drain()
    for n in range(count):
        to_sibling(n).wait_send()


def middle(again, pgain, fgain, lse, mix, wout, tokens, cot, gate_t, up_t, down):
    rows, width = tokens.shape
    hidden = gate_t.shape[0]
    stacked = 3 * hidden
    return pl.pallas_call(
        middle_kernel,
        name="middle",
        out_shape=[
            shape(LOW, rows, HD),
            shape(FULL, 2, 8, HALF),
            shape(LOW, HD + 96, width),
            shape(LOW, PIECE, width),
            shape(LOW, PIECE, width),
            shape(LOW, rows, width),
            shape(FULL, rows, width),
        ],
        in_specs=[VMEM] * 4 + [ANY] * 7,
        out_specs=[VMEM] * 5 + [ANY] * 2,
        scratch_shapes=[
            vmem(LOW, rows, width),
            vmem(FULL, rows, width),
            vmem(LOW, stacked, width),
            vmem(LOW, 4 * HD, width),
            vmem(LOW, rows, 4 * HD),
            vmem(LOW, rows, width),
            vmem(LOW, rows, width),
            vmem(FULL, rows, width),
            vmem(LOW, stacked, rows),
            vmem(LOW, 2, rows, width),
            vmem(LOW, HALF, 1792),
            vmem(LOW, HALF, 1792),
            vmem(LOW, rows, width),
            *[vmem(LOW, rows, width)] * 4,
            vmem(LOW, 4, 2, HALF // 8, width),
            vmem(LOW, 4, 2, 2, HALF // 8, width),
            vmem(LOW, ROWS, width),
            vmem(LOW, 2, 2, PIECE // 2, width),
            vmem(LOW, 2, 2, 2, PIECE // 2, width),
            vmem(FULL, 3, 8, width),
            dma(7), dma(6), dma(6), dma(10, 6), dma(10, 6), dma(2),
        ],
        compiler_params=params(4, 60),
        cost_estimate=cost(20),
    )(again, pgain, fgain, lse, mix, wout, tokens, cot, gate_t, up_t, down)


LATE = 112
EARLY = 176
KEEPERS = 11


def attn_backward(
    starts_ref, do_ref, stat_ref, piece_a_ref, piece_b_ref, qgain_ref, kgain_ref, igain_ref, early_ref,
    q_hbm, k_hbm, v_hbm, raw_hbm, kraw_hbm, cos_hbm, sin_hbm, wk_hbm, wv_hbm, normed_hbm, wq_hbm, tokens_hbm, resid_hbm,
    late_ref, esum_ref, tgrad_ref, dgain_ref, big_ref,
    dog, statg, dqacc, dkacc, dvacc, ktbuf, sibsend, sibrecv, kvsrc, kvpass, kvgot,
    dqsend, dqpass, dqgot, dqback, dqhigh, zpart, zpass, zgot, gaing, winpass, wingot, full_a, full_b,
    draw_ref, dkv_ref, dkraw, dvrow, part, core_recv, half_sum, plane_recv, grow, grecv,
    e_core, e_half, e_plane,
    q_in, k_in, v_in, raw_ref, kraw_ref, cos_ref, sin_ref, wk_ref, wv_ref, normed_t, wq_ref, tok_ref, resid_ref,
    rs, rr, st_s, st_r, sw_s, sw_r, sib_s, sib_r, gn_s, gn_r, sf_s, sf_r, own_sem,
    load_sem, c_s, c_r, p_s, p_r, g_s, g_r, f_s, f_r, i_s, i_r,
    ep_s, ep_r, eg_s, eg_r, ef_s, ef_r,
):
    x, y, c, z = place()
    xp, xm, yp, ym = at(x + 1, y, c, z), at(x + 3, y, c, z), at(x, y + 1, c, z), at(x, y + 3, c, z)
    zp, zm, y2, z2 = at(x, y, c, z + 1), at(x, y, c, z + 3), at(x, y + 2, c, z), at(x, y, c, z + 2)
    sibling, partner = at(x, y, 1 - c, z), at(3 - x, y, c, z)
    shifts = [(a, b) for a in range(4) for b in range(4) if (a, b) != (0, 0)]
    plane = [at(x + a, y + b, c, z) for a, b in shifts]
    loads = [
        pltpu.make_async_copy(src, dst, load_sem.at[n])
        for n, (src, dst) in enumerate(
            (
                (q_hbm, q_in), (k_hbm, k_in), (v_hbm, v_in), (raw_hbm, raw_ref), (kraw_hbm, kraw_ref),
                (cos_hbm, cos_ref), (sin_hbm, sin_ref), (wk_hbm, wk_ref), (wv_hbm, wv_ref),
                (normed_hbm, normed_t), (wq_hbm, wq_ref.at[:, pl.ds(pl.multiple_of(z * HD, HD), HD)]), (tokens_hbm, tok_ref), (resid_hbm, resid_ref),
            )
        )
    ]
    for load in loads:
        load.start()
    greet(plane + [sibling, zp, zm, z2])
    copies = []

    def go(copy):
        copy.start()
        copies.append(copy)

    sems = (rs, rr)
    do_low, do_high = do_ref.at[pl.ds(0, HALF)], do_ref.at[pl.ds(HALF, HALF)]
    swaps = (
        remote(do_high, dog.at[2 * y + 1], sw_s.at[0], sw_r.at[0], partner),
        remote(stat_ref.at[1], statg.at[2 * y + 1], sw_s.at[1], sw_r.at[1], partner),
    )
    for copy in swaps:
        go(copy)
    dos = RingGather(
        lambda index, half: dog.at[2 * index + half], y, yp, ym, sems, 0,
        lambda half: do_low if half == 0 else dog.at[2 * y + 1],
    )
    dos.own(0)
    tall = wq_hbm.shape[0] // 2

    def wq_view(index, half):
        return wq_ref.at[pl.ds(half * tall, tall), pl.ds(pl.multiple_of(index * HD, HD), HD)]

    wqs = RingGather(
        wq_view, z, zp, zm, sems, 12, lambda half: wq_hbm.at[pl.ds(half * tall, tall)]
    )
    wqs.own(0)
    wqs.own(1)
    chip = x * 4 + y
    e_cross = remote(rows_at(early_ref, EARLY * (1 - c), EARLY), e_core, c_s.at[1], c_r.at[1], sibling)
    go(e_cross)

    def early_part(owner):
        return remote(
            rows_at(e_half, 16 * owner, 16), e_plane.at[chip], ep_s.at[owner], ep_r.at[chip],
            at(owner // 4, owner % 4, c, z),
        )

    def early_spread():
        e_cross.wait_recv()
        own = early_ref[pl.ds(pl.multiple_of(EARLY * c, 16), EARLY), :]
        e_half[...] = (own.astype(FULL) + e_core[...].astype(FULL)).astype(LOW)
        for owner in range(KEEPERS):
            pl.when(chip != owner)(early_part(owner).start)

    def early_piece(core, owner):
        return rows_at(esum_ref, EARLY * core + 16 * owner, 16)

    def early_out(n):
        return remote(early_piece(c, chip), early_piece(c, chip), eg_s.at[n], eg_r.at[chip], plane[n])

    def early_across(owner):
        block = early_piece(c, owner)
        return remote(block, block, ef_s.at[owner], ef_r.at[owner], sibling)

    def early_summed():
        @pl.when(chip < KEEPERS)
        def _():
            total = rows_at(e_half, 16 * chip, 16)[...].astype(FULL)
            for a, b in shifts:
                source = ((x + a) % 4) * 4 + (y + b) % 4
                block = rows_at(e_half, 0, 16)
                remote(block, e_plane.at[source], ep_s.at[0], ep_r.at[source], sibling).wait_recv()
                total = total + e_plane[source].astype(FULL)
            early_piece(c, chip)[...] = total.astype(LOW)
            for n in range(15):
                early_out(n).start()
            early_across(chip).start()

    def early_passed():
        for owner in range(KEEPERS):

            @pl.when(chip != owner)
            def _():
                block = early_piece(c, owner)
                remote(rows_at(e_half, 0, 16), block, eg_s.at[0], eg_r.at[owner], sibling).wait_recv()
                early_across(owner).start()

    def early_done():
        for owner in range(KEEPERS):
            block = early_piece(1 - c, owner)
            remote(rows_at(e_half, 0, 16), block, ef_s.at[0], ef_r.at[owner], sibling).wait_recv()
            early_across(owner).wait_send()
            pl.when(chip != owner)(early_part(owner).wait_send)

        @pl.when(chip < KEEPERS)
        def _():
            for n in range(15):
                early_out(n).wait_send()

    def stats_to(upper, rel, peer):
        slot = 2 * y + upper
        source = statg.at[slot] if upper else stat_ref.at[0]
        return remote(source, statg.at[slot], st_s.at[upper, rel - 1], st_r.at[slot], peer)

    y_peers = ((1, yp), (3, ym), (2, y2))
    for rel, peer in y_peers:
        go(stats_to(0, rel, peer))

    cut = (48, WINDOW - 48)

    def window(ref, index, half):
        return rows_at(ref, WINDOW * index + 48 * half, cut[half])

    sides = ((piece_a_ref, full_a, y, yp, ym), (piece_b_ref, full_b, x, xp, xm))
    reduces, gathers = [], []
    for h, (piece, full, me, plus, minus) in enumerate(sides):
        reduces.append(
            RingReduce(
                lambda rel, half, piece=piece, me=me: window(piece, (me + rel) % 4, half),
                lambda half, h=h: winpass.at[h, pl.ds(48 * half, cut[half])],
                lambda side, half, h=h: wingot.at[h, side, pl.ds(48 * half, cut[half])],
                plus, minus, sems, 1 + h,
            )
        )
        gathers.append(
            RingGather(lambda index, half, full=full: window(full, index, half), me, plus, minus, sems, 3 + h)
        )
        reduces[h].start()

    def big_view(core, h, index, half):
        return rows_at(big_ref, ROWS * core + SIDE * h + PIECE * index + half * (PIECE // 2), PIECE // 2)

    owners = ((x, xp, xm), (y, yp, ym))
    pieces = [
        RingGather(
            lambda index, half, h=h: big_view(c, h, index, half), me, plus, minus, sems, 5 + h,
            lambda half, h=h: sides[h][1].at[pl.ds(half * (PIECE // 2), PIECE // 2)],
        )
        for h, (me, plus, minus) in enumerate(owners)
    ]

    def piece_to_sibling(h, index, half, source=None):
        block = big_view(c, h, index, half)
        return remote(block if source is None else source, block, sf_s.at[h, index, half], sf_r.at[h, index, half], sibling)

    def keep(h, half):
        source = sides[h][1].at[pl.ds(half * (PIECE // 2), PIECE // 2)]
        return pltpu.make_async_copy(source, big_view(c, h, owners[h][0], half), own_sem.at[h, half])

    dog[2 * y] = do_ref[0:HALF, :]
    statg[2 * y] = stat_ref[0]
    dqacc[...] = jnp.zeros_like(dqacc)
    for copy in swaps:
        copy.wait_recv()
    dos.own(1)
    for rel, peer in y_peers:
        go(stats_to(1, rel, peer))
    dos.forward()
    dos.near()
    dos.far()
    for upper in range(2):
        for rel, peer in y_peers:
            slot = 2 * ((y + rel) % 4) + upper
            remote(stat_ref.at[0], statg.at[slot], st_s.at[0, 0], st_r.at[slot], sibling).wait_recv()

    def window_summed(h):
        ring, gather = reduces[h], gathers[h]
        piece, full, me, _, _ = sides[h]
        ring.finish()
        for half in range(2):
            total = window(piece, me, half)[...].astype(FULL) + ring.arrived(half)
            window(full, me, half)[...] = total.astype(LOW)
            gather.own(half)

    def window_gathered(h):
        gathers[h].near()
        gathers[h].far()

    def pieces_sent(h):
        for half in range(2):
            pieces[h].own(half)
            source = sides[h][1].at[pl.ds(half * (PIECE // 2), PIECE // 2)]
            go(piece_to_sibling(h, owners[h][0], half, source))
            keep(h, half).start()

    def pieces_near(h):
        pieces[h].near()
        for rel in (1, 3):
            for half in range(2):
                go(piece_to_sibling(h, (owners[h][0] + rel) % 4, half))

    def pieces_far(h):
        pieces[h].far()
        for half in range(2):
            go(piece_to_sibling(h, (owners[h][0] + 2) % 4, half))

    def tile(i, first_q, slot, first_k, masked):
        queries, out_grads = q_in[i], dog[i]
        lse, delta = statg[i, 0:1, :], statg[i, 1:2, :]
        if masked:
            token = first_q + lax.broadcasted_iota(jnp.int32, (1, HALF), 1)
            begin = begin_of(token, starts_ref)
        dq_part = None
        for n in range(2):
            rows = pl.ds(n * 256, 256)
            keys, values = k_in[slot, rows], v_in[slot, rows]
            scores = lax.dot_general(keys, queries, NT, preferred_element_type=FULL)
            prob_grad = lax.dot_general(values, out_grads, NT, preferred_element_type=FULL)
            soft = jnp.exp(scores - lse)
            if masked:
                key_index = first_k + n * 256 + lax.broadcasted_iota(jnp.int32, (256, 1), 0)
                soft = jnp.where((key_index <= token) & (key_index >= begin), soft, 0.0)
            score_grad = (soft * (prob_grad - delta)).astype(LOW)
            dvacc[rows, :] += jnp.dot(soft.astype(LOW), out_grads, preferred_element_type=FULL)
            dkacc[rows, :] += jnp.dot(score_grad, queries, preferred_element_type=FULL)
            part = jnp.dot(ktbuf[:, n * 256 : (n + 1) * 256], score_grad, preferred_element_type=FULL)
            dq_part = part if dq_part is None else dq_part + part
        dqacc[i] = dqacc[i] + dq_part

    place_of = {2: 0, 1: 1, 3: 2}
    kvs = RingReduce(
        lambda rel, half: kvsrc.at[place_of[rel], half],
        lambda half: kvpass.at[half],
        lambda side, half: kvgot.at[side, half],
        xp, xm, sems, 7,
    )
    between = {
        (0, 0): (early_spread,),
        (0, 1): (reduces[0].relay, reduces[1].relay),
        (1, 0): (lambda: window_summed(0), lambda: window_summed(1)),
        (2, 0): (early_summed, wqs.forward, gathers[0].forward, gathers[1].forward),
        (3, 0): (wqs.near, wqs.far, lambda: window_gathered(0), lambda: window_gathered(1)),
    }
    for load in loads[:3]:
        load.wait()
    for step, rel in enumerate((2, 1, 3, 0)):
        pair = (x + rel) % 4
        for turn in range(2):
            if (step, turn) in between:
                for hook in between[step, turn]:
                    hook()
            cc = 1 - c if turn == 0 else c
            slot = pair * 2 + cc
            first_k = 4096 * pair + 1024 * y + BLK * cc
            dkacc[...] = jnp.zeros_like(dkacc)
            dvacc[...] = jnp.zeros_like(dvacc)
            ktbuf[...] = jnp.transpose(k_in[slot])

            def visit(i, carry):
                first_q = tile_first(i, x, c)
                some = first_k <= first_q + (HALF - 1)
                full = (first_k + BLK - 1 <= first_q) & (first_k > 0) & (first_q < 31 * BLK)

                @pl.when(full)
                def _():
                    tile(i, first_q, slot, first_k, False)

                @pl.when(some & jnp.logical_not(full))
                def _():
                    tile(i, first_q, slot, first_k, True)

                return carry

            lax.fori_loop(0, 8, visit, 0)
            to_sibling = remote(sibsend.at[step], sibrecv.at[step], sib_s.at[step], sib_r.at[step], sibling)
            if turn == 0:
                sibsend[step, 0] = dkacc[...].astype(LOW)
                sibsend[step, 1] = dvacc[...].astype(LOW)
                go(to_sibling)
            else:
                to_sibling.wait_recv()
                for half, ref in enumerate((dkacc, dvacc)):
                    both = ref[...] + sibrecv[step, half].astype(FULL)
                    if rel == 0:
                        ref[...] = both
                    else:
                        kvsrc[place_of[rel], half] = both.astype(LOW)
                if rel == 2:
                    kvs.start(0, 1)
                elif rel == 1:
                    kvs.start(3)
                elif rel == 3:
                    kvs.start(2)
                    kvs.relay()

    kvs.finish()
    pieces_sent(0)
    zrows = BLK // 4
    for n in range(4):
        for half, ref in enumerate((dkacc, dvacc)):
            rows = pl.ds(n * zrows, zrows)
            whole = ref[rows, :] + kvgot[0, half, rows, :].astype(FULL) + kvgot[1, half, rows, :].astype(FULL)
            zpart[n, half] = whole.astype(LOW)
    zs = RingReduce(
        lambda rel, half: zpart.at[(z + rel) % 4, half],
        lambda half: zpass.at[half],
        lambda side, half: zgot.at[side, half],
        zp, zm, sems, 9,
    )
    zg = RingGather(lambda index, half: dkv_ref.at[index, half], z, zp, zm, sems, 10)
    zs.start()

    def cast(i, carry):
        dqsend[i] = jnp.transpose(dqacc[i]).astype(LOW)
        return carry

    lax.fori_loop(0, 8, cast, 0)
    dqs = RingReduce(
        lambda rel, half: dqsend.at[2 * ((y + rel) % 4) + half],
        lambda half: dqpass.at[half],
        lambda side, half: dqgot.at[side, half],
        yp, ym, sems, 8,
    )
    dqs.start()
    zs.relay()
    dqs.relay()
    zs.finish()
    for half in range(2):
        dkv_ref[z, half] = (zpart[z, half].astype(FULL) + zs.arrived(half)).astype(LOW)
        zg.own(half)
    early_passed()
    for load in loads[3:]:
        load.wait()
    dqs.finish()
    pieces_sent(1)
    back = remote(dqback, dqhigh, sw_s.at[2], sw_r.at[2], partner)
    dqback[...] = (dqsend[2 * y + 1].astype(FULL) + dqs.arrived(1)).astype(LOW)
    go(back)

    draws = RingGather(
        lambda index, half: draw_ref.at[pl.ds(half * HALF, HALF), pl.ds(pl.multiple_of(index * HD, HD), HD)],
        z, zp, zm, sems, 11,
    )

    def unrotated(grad, raw, gain, rows):
        cosine, sine = cos_ref[rows, :], sin_ref[rows, :]
        first, second = grad[:, : HD // 2], grad[:, HD // 2 :]
        turned = jnp.concatenate([first * cosine + second * sine, second * cosine - first * sine], axis=1)
        inverse = lax.rsqrt(jnp.mean(raw * raw, axis=1, keepdims=True) + EPS)
        unit = raw * inverse
        scaled = gain * turned
        raw_grad = inverse * (scaled - unit * jnp.mean(unit * scaled, axis=1, keepdims=True))
        return raw_grad.astype(LOW), jnp.sum(unit * turned, axis=0, keepdims=True)

    gain_grad = None
    for half in range(2):
        if half == 0:
            grad = dqsend[2 * y].astype(FULL) + dqs.arrived(0)
        else:
            back.wait_recv()
            grad = dqhigh[...].astype(FULL)
        rows = pl.ds(half * HALF, HALF)
        raw_grad, piece = unrotated(grad * (HD**-0.5), raw_ref[rows, :], qgain_ref[0:1, :], rows)
        draw_ref[rows, pl.ds(pl.multiple_of(z * HD, HD), HD)] = raw_grad
        draws.own(half)
        gain_grad = piece if gain_grad is None else gain_grad + piece
    gaing[z] = jnp.broadcast_to(gain_grad, (8, HD))
    for n, peer in enumerate((zp, zm, z2)):
        go(remote(gaing.at[z], gaing.at[z], gn_s.at[n], gn_r.at[z], peer))

    chunk_rows = normed_t.shape[0] // 8

    def weight_grad(m, rhs):
        def block(r, carry):
            lhs = normed_t[pl.ds(pl.multiple_of(r * chunk_rows, 16), chunk_rows), :]
            tile = jnp.dot(lhs, rhs[...], preferred_element_type=FULL).astype(LOW)
            part[pl.ds(pl.multiple_of((8 * m + r) * chunk_rows, 16), chunk_rows), :] = tile
            return carry

        lax.fori_loop(0, 8, block, 0)

    zg.forward()
    weight_grad(0, draw_ref.at[:, pl.ds(pl.multiple_of(z * HD, HD), HD)])
    draws.forward()
    pieces[0].forward()
    zg.near()
    zg.far()
    key_gain_grad = None
    for n in range(4):
        rows = pl.ds(n * zrows, zrows)
        raw_grad, piece = unrotated(dkv_ref[n, 0].astype(FULL), kraw_ref[rows, :], kgain_ref[0:1, :], rows)
        dkraw[rows, :] = raw_grad
        dvrow[rows, :] = dkv_ref[n, 1]
        key_gain_grad = piece if key_gain_grad is None else key_gain_grad + piece
    for rel in (1, 3, 2):
        other = (z + rel) % 4
        remote(gaing.at[z], gaing.at[other], gn_s.at[0], gn_r.at[other], sibling).wait_recv()
    query_gain_grad = sum(gaing[n, 0:1, :] for n in range(4))
    number = lax.broadcasted_iota(jnp.int32, (16, HD), 0)
    both = jnp.where(number == 0, query_gain_grad, jnp.where(number == 1, key_gain_grad, 0.0))
    part[pl.ds(24 * chunk_rows, 16), :] = both.astype(LOW)
    part[pl.ds(24 * chunk_rows + 16, LATE), :] = jnp.zeros((LATE, HD), LOW)
    weight_grad(1, dkraw)
    weight_grad(2, dvrow)

    side = 16 * LATE

    def late_piece(ref, core, owner):
        return rows_at(ref, side * core + LATE * owner, LATE)

    cross = remote(rows_at(part, side * (1 - c), side), core_recv, c_s.at[0], c_r.at[0], sibling)
    go(cross)
    cross.wait_recv()

    def add(r, carry):
        both = part[pl.ds(pl.multiple_of(side * c + 2 * LATE * r, 16), 2 * LATE), :].astype(FULL)
        rows = pl.ds(pl.multiple_of(2 * LATE * r, 16), 2 * LATE)
        half_sum[rows, :] = (both + core_recv[rows, :].astype(FULL)).astype(LOW)
        return carry

    lax.fori_loop(0, 8, add, 0)
    for n, (a, b) in enumerate(shifts):
        target = ((x + a) % 4) * 4 + (y + b) % 4
        go(remote(late_piece(half_sum, 0, target), plane_recv.at[chip], p_s.at[n], p_r.at[chip], plane[n]))

    pieces_near(0)
    pieces_far(0)
    pieces[1].forward()
    draws.near()
    draws.far()
    gain_row = None
    for half in range(2):
        rows = pl.ds(half * HALF, HALF)
        grad = lax.dot_general(draw_ref[rows, :], wq_ref[...], NT, preferred_element_type=FULL)
        grad = grad + lax.dot_general(dkraw[rows, :], wk_ref[...], NT, preferred_element_type=FULL)
        grad = grad + lax.dot_general(dvrow[rows, :], wv_ref[...], NT, preferred_element_type=FULL)
        value = tok_ref[rows, :].astype(FULL)
        inverse = lax.rsqrt(jnp.mean(value * value, axis=1, keepdims=True) + EPS)
        unit = value * inverse
        scaled = igain_ref[0:1, :] * grad
        back_grad = inverse * (scaled - unit * jnp.mean(unit * scaled, axis=1, keepdims=True))
        tgrad_ref[rows, :] = resid_ref[rows, :] + back_grad
        piece = jnp.sum(unit * grad, axis=0, keepdims=True)
        gain_row = piece if gain_row is None else gain_row + piece
    grow[0] = jnp.broadcast_to(gain_row, grow.shape[1:])
    to_core = remote(grow.at[0], grow.at[1], i_s.at[15], i_r.at[16], sibling)
    go(to_core)

    total = late_piece(half_sum, 0, chip)[...].astype(FULL)
    for a, b in shifts:
        source = ((x + a) % 4) * 4 + (y + b) % 4
        remote(late_piece(half_sum, 0, 0), plane_recv.at[source], p_s.at[0], p_r.at[source], sibling).wait_recv()
        total = total + plane_recv[source].astype(FULL)

    def piece_of(owner):
        return late_piece(late_ref, c, owner)

    piece_of(chip)[...] = total.astype(LOW)
    for n in range(15):
        go(remote(piece_of(chip), piece_of(chip), g_s.at[n], g_r.at[chip], plane[n]))
    go(remote(piece_of(chip), piece_of(chip), f_s.at[chip], f_r.at[chip], sibling))
    to_core.wait_recv()
    grecv[chip] = grow[0] + grow[1]
    for n in range(15):
        go(remote(grecv.at[chip], grecv.at[chip], i_s.at[n], i_r.at[chip], plane[n]))
    pieces_near(1)
    for a, b in shifts:
        source = ((x + a) % 4) * 4 + (y + b) % 4
        remote(late_piece(half_sum, 0, 0), piece_of(source), g_s.at[0], g_r.at[source], sibling).wait_recv()
        go(remote(piece_of(source), piece_of(source), f_s.at[source], f_r.at[source], sibling))
    for a, b in shifts:
        source = ((x + a) % 4) * 4 + (y + b) % 4
        remote(grecv.at[chip], grecv.at[source], i_s.at[0], i_r.at[source], sibling).wait_recv()
    pieces_far(1)
    dgain_ref[...] = sum(grecv[n] for n in range(16))
    for n in range(16):
        theirs = late_piece(late_ref, 1 - c, n)
        remote(late_piece(half_sum, 0, 0), theirs, f_s.at[0], f_r.at[n], sibling).wait_recv()
    early_done()
    for h in range(2):
        for half in range(2):
            keep(h, half).wait()
            for n in range(4):
                piece_to_sibling(h, n, half).wait_recv()
    for ring in [dos, kvs, dqs, zs, zg, draws, wqs] + reduces + gathers + pieces:
        ring.drain()
    for copy in copies:
        copy.wait_send()


def backward_attention(doc_starts, *operands):
    width = operands[2].shape[1]
    streamed = operands[8:]
    return pl.pallas_call(
        attn_backward,
        name="attn_backward",
        out_shape=[
            shape(LOW, 32 * LATE, HD),
            shape(LOW, 2 * EARLY, width),
            shape(FULL, BLK, width),
            shape(FULL, 8, width),
            shape(LOW, 2 * ROWS + 64, width),
        ],
        in_specs=[SMEM] + [VMEM] * 8 + [ANY] * 13,
        out_specs=[VMEM] * 4 + [ANY],
        scratch_shapes=[
            vmem(LOW, 8, HALF, HD),
            vmem(FULL, 8, 8, HALF),
            vmem(FULL, 8, HD, HALF),
            vmem(FULL, BLK, HD),
            vmem(FULL, BLK, HD),
            vmem(LOW, HD, BLK),
            vmem(LOW, 4, 2, BLK, HD),
            vmem(LOW, 4, 2, BLK, HD),
            vmem(LOW, 3, 2, BLK, HD),
            vmem(LOW, 2, BLK, HD),
            vmem(LOW, 2, 2, BLK, HD),
            vmem(LOW, 8, HALF, HD),
            vmem(LOW, 2, HALF, HD),
            vmem(LOW, 2, 2, HALF, HD),
            vmem(LOW, HALF, HD),
            vmem(LOW, HALF, HD),
            vmem(LOW, 4, 2, BLK // 4, HD),
            vmem(LOW, 2, BLK // 4, HD),
            vmem(LOW, 2, 2, BLK // 4, HD),
            vmem(FULL, 4, 8, HD),
            vmem(LOW, 2, WINDOW, width),
            vmem(LOW, 2, 2, WINDOW, width),
            vmem(LOW, PIECE, width),
            vmem(LOW, PIECE, width),
            vmem(LOW, BLK, 4 * HD),
            vmem(LOW, 4, 2, BLK // 4, HD),
            vmem(LOW, BLK, HD),
            vmem(LOW, BLK, HD),
            vmem(LOW, 32 * LATE, HD),
            vmem(LOW, 16 * LATE, HD),
            vmem(LOW, 16 * LATE, HD),
            vmem(LOW, 16, LATE, HD),
            vmem(FULL, 2, 8, width),
            vmem(FULL, 16, 8, width),
            vmem(LOW, EARLY, width),
            vmem(LOW, EARLY, width),
            vmem(LOW, 16, 16, width),
            *[vmem(operand.dtype, *operand.shape) for operand in streamed[:10]],
            vmem(LOW, width, 4 * HD),
            *[vmem(operand.dtype, *operand.shape) for operand in streamed[11:]],
            dma(13, 6), dma(13, 6), dma(2, 3), dma(8), dma(3), dma(3), dma(4), dma(4), dma(3), dma(4),
            dma(2, 4, 2), dma(2, 4, 2), dma(2, 2),
            dma(13), dma(2), dma(2), dma(15), dma(16), dma(15), dma(16), dma(16), dma(16), dma(16), dma(17),
            dma(KEEPERS), dma(16), dma(15), dma(16), dma(KEEPERS), dma(KEEPERS),
        ],
        compiler_params=params(2, 60),
        cost_estimate=cost(15),
    )(doc_starts, *operands)


def wide(gain):
    return lax.broadcast_in_dim(gain, (8, gain.shape[0]), (1,))


def per_device(
    tokens,
    cotangent,
    doc_starts,
    query_weight,
    key_weight,
    value_weight,
    out_weight,
    gate_weight,
    up_weight,
    down_weight,
    input_gain,
    attn_gain,
    prenorm_gain,
    post_gain,
    query_gain,
    key_gain,
):
    row_count = tokens.shape[0]
    first_row = lax.axis_index("seq") * row_count
    own_index = first_row + jnp.arange(row_count, dtype=jnp.int32)
    own_position = doc_layout(doc_starts, own_index)[1]
    cos_table, sine_table = rope_tables(own_position, HD)
    query_scale = HD ** (-0.5)
    inputs = tokens.astype(jnp.float32)
    normed = rms_norm(inputs, input_gain)
    normed_low = normed.astype(jnp.bfloat16)
    query_raw = jnp.dot(normed_low, query_weight, preferred_element_type=jnp.float32)
    key_raw = jnp.dot(normed_low, key_weight, preferred_element_type=jnp.float32)
    value_low = jnp.dot(normed_low, value_weight, preferred_element_type=jnp.float32).astype(
        jnp.bfloat16
    )

    def query_piece(source, scaling):
        return rotate(rms_norm(source, scaling), cos_table, sine_table) * query_scale

    def key_piece(source, scaling):
        return rotate(rms_norm(source, scaling), cos_table, sine_table)

    query_rows = query_piece(query_raw, query_gain)
    query_low = query_rows.astype(jnp.bfloat16)
    key_rows = key_piece(key_raw, key_gain)
    key_low = key_rows.astype(jnp.bfloat16)
    mix_all, lse_rows, q_all, k_all, v_all, out_weight_all = forward_attention(
        doc_starts, query_low, key_low, value_low, out_weight
    )
    width = tokens.shape[1]
    mix_grad, stats, early, piece_a, piece_b, mixed, resid = middle(
        wide(attn_gain),
        wide(prenorm_gain),
        wide(post_gain),
        lse_rows,
        mix_all,
        out_weight_all,
        tokens,
        cotangent,
        jnp.transpose(gate_weight),
        jnp.transpose(up_weight),
        down_weight,
    )
    late, early, tokens_grad, input_gain_rows, big = backward_attention(
        doc_starts,
        mix_grad,
        stats,
        piece_a,
        piece_b,
        wide(query_gain),
        wide(key_gain),
        wide(input_gain),
        early,
        q_all,
        k_all,
        v_all,
        query_raw,
        key_raw,
        cos_table,
        sine_table,
        key_weight,
        value_weight,
        jnp.transpose(normed_low),
        query_weight,
        tokens,
        resid,
    )
    input_gain_grad = input_gain_rows[0]
    query_weight_grad = late[:width].astype(jnp.float32)
    key_weight_grad = late[width : 2 * width].astype(jnp.float32)
    value_weight_grad = late[2 * width : 3 * width].astype(jnp.float32)
    query_gain_grad = late[3 * width].astype(jnp.float32)
    key_gain_grad = late[3 * width + 1].astype(jnp.float32)
    out_weight_grad = early[:HD].astype(jnp.float32)
    rest = early[HD : HD + 64]
    gains = early[HD + 64 : HD + 67].astype(jnp.float32)
    attn_gain_grad, prenorm_gain_grad, post_gain_grad = gains[0], gains[1], gains[2]
    hidden = gate_weight.shape[1]
    gate_weight_grad = jnp.transpose(big[:hidden].astype(jnp.float32))
    up_weight_grad = jnp.transpose(big[hidden : 2 * hidden].astype(jnp.float32))
    down_weight_grad = big[2 * hidden :].astype(jnp.float32)
    down_weight_grad = lax.dynamic_update_slice(
        down_weight_grad, rest.astype(jnp.float32), (hidden - rest.shape[0], 0)
    )
    return (
        mixed,
        tokens_grad,
        query_weight_grad,
        key_weight_grad,
        value_weight_grad,
        out_weight_grad,
        gate_weight_grad,
        up_weight_grad,
        down_weight_grad,
        input_gain_grad,
        attn_gain_grad,
        prenorm_gain_grad,
        post_gain_grad,
        query_gain_grad,
        key_gain_grad,
    )


def solution(mesh):
    placed = (
        P("seq", None),
        P("seq", None),
        P(),
        P(None, "head"),
        P(),
        P(),
        P("head", None),
        P(None, "head"),
        P(None, "head"),
        P("head", None),
        P(),
        P(),
        P(),
        P(),
        P(),
        P(),
    )
    return jax.shard_map(
        per_device,
        mesh=mesh,
        in_specs=placed,
        out_specs=(
            P("seq", None),
            P("seq", None),
            P(None, "head"),
            P(),
            P(),
            P("head", None),
            P(None, "head"),
            P(None, "head"),
            P("head", None),
            P(),
            P(),
            P(),
            P(),
            P(),
            P(),
        ),
        check_vma=False,
    )
```

```python
import functools
import math

import jax
import jax.numpy as jnp
from jax import lax
from jax.experimental import pallas as pl
from jax.experimental.pallas import tpu as pltpu
from jax.sharding import PartitionSpec as P

HD = 256


EPS = 1e-06
THETA = 1000000.0
NEG = -1e30


def rms_norm(values, scaling):
    return values * lax.rsqrt(jnp.mean(values * values, axis=-1, keepdims=True) + EPS) * scaling


def doc_layout(doc_starts, token_index):
    before = doc_starts[None, :] <= token_index[:, None]
    segment = jnp.sum(before.astype(jnp.int32), axis=1)
    doc_begin = jnp.max(jnp.where(before, doc_starts[None, :], 0), axis=1)
    return (segment, token_index - doc_begin)


def rope_tables(position, head_width):
    half_width = head_width // 2
    inverse = jnp.exp(
        -math.log(THETA) * 2.0 * jnp.arange(half_width, dtype=jnp.float32) / head_width
    )
    angles = position.astype(jnp.float32)[:, None] * inverse[None, :]
    return (jnp.cos(angles), jnp.sin(angles))


def rotate(values, cos_table, sine_table):
    half_width = values.shape[-1] // 2
    first, second = values[..., :half_width], values[..., half_width:]
    return jnp.concatenate(
        [first * cos_table - second * sine_table, second * cos_table + first * sine_table], axis=-1
    )


MESH_ID = pl.DeviceIdType.MESH
HALF = 256
BLK = 512
LOW = jnp.bfloat16
FULL = jnp.float32
NT = (((1,), (1,)), ((), ()))


def place():
    s = lax.axis_index("seq")
    return s // 8, (s // 2) % 4, s % 2, lax.axis_index("head")


def at(x, y, c, z):
    return ((x % 4) * 8 + (y % 4) * 2 + c, z % 4)


def greet(peers):
    barrier = pltpu.get_barrier_semaphore()
    for peer in peers:
        pl.semaphore_signal(barrier, inc=1, device_id=peer, device_id_type=MESH_ID)
    pl.semaphore_wait(barrier, len(peers))


def remote(src, dst, send_sem, recv_sem, peer):
    return pltpu.make_async_remote_copy(
        src_ref=src,
        dst_ref=dst,
        send_sem=send_sem,
        recv_sem=recv_sem,
        device_id=peer,
        device_id_type=MESH_ID,
    )


def rows_at(ref, start, size):
    return ref.at[pl.ds(pl.multiple_of(start, 16), size)]


class RingGather:
    def __init__(self, view, me, plus, minus, sems, ring, source=None):
        send, recv = sems

        def near(rel, half):
            return view((me + rel) % 4, half)

        own = source or (lambda half: near(0, half))
        plan = (
            (own(0), near(0, 0), plus),
            (own(1), near(0, 1), plus),
            (near(3, 0), near(3, 0), plus),
            (own(0), near(0, 0), minus),
            (own(1), near(0, 1), minus),
            (near(1, 1), near(1, 1), minus),
        )
        self.copies = [
            remote(src, dst, send.at[ring, k], recv.at[ring, k], peer) for k, (src, dst, peer) in enumerate(plan)
        ]

    def own(self, half):
        self.copies[half].start()
        self.copies[3 + half].start()

    def whole(self):
        for k in (0, 4, 1, 3):
            self.copies[k].start()

    def forward(self):
        self.copies[0].wait_recv()
        self.copies[2].start()
        self.copies[4].wait_recv()
        self.copies[5].start()

    def near(self):
        self.copies[1].wait_recv()
        self.copies[3].wait_recv()

    def far(self):
        self.copies[2].wait_recv()
        self.copies[5].wait_recv()

    def drain(self):
        for copy in self.copies:
            copy.wait_send()


class RingReduce:
    def __init__(self, view, passing, got, plus, minus, sems, ring):
        send, recv = sems
        self.view, self.passing, self.got = view, passing, got
        plan = (
            (view(2, 0), passing(0), minus),
            (view(2, 1), passing(1), plus),
            (view(3, 1), got(0, 1), minus),
            (view(1, 0), got(1, 0), plus),
            (passing(0), got(0, 0), minus),
            (passing(1), got(1, 1), plus),
        )
        self.copies = [
            remote(src, dst, send.at[ring, k], recv.at[ring, k], peer) for k, (src, dst, peer) in enumerate(plan)
        ]

    def start(self, *numbers):
        for k in numbers or (0, 1, 2, 3):
            self.copies[k].start()

    def relay(self):
        for half, rel in ((0, 3), (1, 1)):
            self.copies[half].wait_recv()
            land, term = self.passing(half), self.view(rel, half)
            land[...] = (land[...].astype(FULL) + term[...].astype(FULL)).astype(LOW)
            self.copies[4 + half].start()

    def finish(self):
        for k in (2, 3, 4, 5):
            self.copies[k].wait_recv()

    def arrived(self, half):
        return self.got(0, half)[...].astype(FULL) + self.got(1, half)[...].astype(FULL)

    def drain(self):
        for copy in self.copies:
            copy.wait_send()


def tile_first(i, x, c):
    column = jnp.where(i % 2 == 1, 3 - x, x)
    return BLK * (8 * column + 2 * (i // 2) + c) + HALF * (i % 2)


def begin_of(token, starts_ref):
    begin = jnp.zeros_like(token)
    for n in range(starts_ref.shape[0]):
        start = starts_ref[n]
        begin = jnp.where(start <= token, start, begin)
    return begin


def attn_forward(
    starts_ref, q_ref, k_ref, v_ref, wout_hbm,
    mix_ref, lse_ref, q_out, k_out, v_out, wout_all,
    qg_ref, kg_ref, vg_ref, acc, lacc, osend, opass, ogot, lsend, lrecv, hsend, lhsend,
    rs, rr, sib_s, sib_r, l_s, l_r, sw_s, sw_r, keep_sem,
):
    x, y, c, z = place()
    xp, xm, yp, ym = at(x + 1, y, c, z), at(x + 3, y, c, z), at(x, y + 1, c, z), at(x, y + 3, c, z)
    zp, zm, y2 = at(x, y, c, z + 1), at(x, y, c, z + 3), at(x, y + 2, c, z)
    sibling, partner = at(x, y, 1 - c, z), at(3 - x, y, c, z)
    greet([partner, sibling, xp, xm, yp, ym, y2, zp, zm])
    copies = []

    def go(copy):
        copy.start()
        copies.append(copy)

    q_low, q_high = q_ref.at[pl.ds(0, HALF)], q_ref.at[pl.ds(HALF, HALF)]
    swap = remote(q_high, qg_ref.at[2 * y + 1], sw_s.at[0], sw_r.at[0], partner)
    go(swap)

    def kv_view(index, half):
        return (kg_ref, vg_ref)[half].at[2 * index + c]

    kv = RingGather(kv_view, x, xp, xm, (rs, rr), 0, lambda half: (k_ref, v_ref)[half])
    kv.whole()
    qs = RingGather(
        lambda index, half: qg_ref.at[2 * index + half], y, yp, ym, (rs, rr), 1,
        lambda half: q_low if half == 0 else qg_ref.at[2 * y + 1],
    )
    qs.own(0)

    def pass_on(index, half, source=None):
        block = kv_view(index, half)
        return remote(block if source is None else source, block, sib_s.at[index, half], sib_r.at[index, half], sibling)

    for half, source in enumerate((k_ref, v_ref)):
        go(pass_on(x, half, source))
    wide = wout_hbm.shape[0]

    def wout_view(index, half):
        return rows_at(wout_all, wide * index + half * (wide // 2), wide // 2)

    wouts = RingGather(
        wout_view, z, zp, zm, (rs, rr), 4, lambda half: wout_hbm.at[pl.ds(half * (wide // 2), wide // 2)]
    )
    wouts.whole()
    wout_keep = pltpu.make_async_copy(wout_hbm, rows_at(wout_all, wide * z, wide), keep_sem.at[3])
    wout_keep.start()
    qg_ref[2 * y] = q_ref[0:HALF, :]
    kg_ref[2 * x + c] = k_ref[...]
    vg_ref[2 * x + c] = v_ref[...]
    acc[...] = jnp.zeros_like(acc)
    lacc[...] = jnp.zeros_like(lacc)
    swap.wait_recv()
    qs.own(1)
    kv.forward()
    qs.forward()
    kv.near()
    for rel in (1, 3):
        for half in range(2):
            go(pass_on((x + rel) % 4, half))
    qs.near()
    qs.far()
    wouts.forward()

    def chunk(i, first_q, pair, first_k, masked):
        queries = qg_ref[i]
        if masked:
            token = first_q + lax.broadcasted_iota(jnp.int32, (HALF, 1), 0)
            begin = begin_of(token, starts_ref)
        total = None
        sums = None
        for cc in range(2):
            keys, values = kg_ref[pair * 2 + cc], vg_ref[pair * 2 + cc]
            scores = lax.dot_general(queries, keys, NT, preferred_element_type=FULL)
            exps = jnp.exp(scores)
            if masked:
                key_index = first_k + cc * BLK + lax.broadcasted_iota(jnp.int32, (1, BLK), 1)
                exps = jnp.where((key_index <= token) & (key_index >= begin), exps, 0.0)
            part = jnp.dot(exps.astype(LOW), values, preferred_element_type=FULL)
            total = part if total is None else total + part
            for n in range(BLK // 128):
                piece = exps[:, n * 128 : (n + 1) * 128]
                sums = piece if sums is None else sums + piece
        acc[i] = acc[i] + total
        lacc[i] = lacc[i] + sums

    def visit(i, pair):
        first_q, first_k = tile_first(i, x, c), 4096 * pair + 1024 * y
        some = first_k <= first_q + (HALF - 1)
        full = (first_k + 1023 <= first_q) & (first_k > 0) & (first_q < 31 * BLK)

        @pl.when(full)
        def _():
            chunk(i, first_q, pair, first_k, False)

        @pl.when(some & jnp.logical_not(full))
        def _():
            chunk(i, first_q, pair, first_k, True)

    numer = RingReduce(
        lambda rel, half: osend.at[2 * ((y + rel) % 4) + half],
        lambda half: opass.at[half],
        lambda side, half: ogot.at[side, half],
        yp, ym, (rs, rr), 2,
    )

    def sums_to(rel, peer):
        index = (y + rel) % 4
        return remote(lsend.at[pl.ds(2 * index, 2)], lrecv.at[y], l_s.at[rel - 1], l_r.at[y], peer)

    keeps = [
        pltpu.make_async_copy(src, dst, keep_sem.at[n])
        for n, (src, dst) in enumerate(((qg_ref, q_out), (kg_ref, k_out), (vg_ref, v_out)))
    ]
    for rel, peer in ((2, y2), (1, yp), (3, ym), (0, None)):
        first = 2 * ((y + rel) % 4)
        if rel == 2:
            for turn in (0, 1, 3, 2):
                pair = (x + turn) % 4
                if turn == 2:
                    kv.far()
                    for half in range(2):
                        go(pass_on(pair, half))
                for half in range(2):
                    pass_on(pair, half).wait_recv()
                for upper in range(2):
                    visit(first + upper, pair)
            for keep in keeps:
                keep.start()
        else:

            def one(n, carry):
                visit(first + n // 4, n % 4)
                return carry

            lax.fori_loop(0, 8, one, 0)

        for upper in range(2):
            i = first + upper
            osend[i] = acc[i].astype(LOW)
            row = jnp.sum(jnp.transpose(lacc[i]), axis=0, keepdims=True)
            lsend[i] = jnp.broadcast_to(row, (8, HALF))
        if rel == 2:
            numer.start(0, 1)
        elif rel == 1:
            numer.start(3)
        elif rel == 3:
            numer.start(2)
            numer.relay()
        if rel > 0:
            go(sums_to(rel, peer))
    lrecv[y] = lsend[pl.ds(2 * y, 2)]
    for rel in (1, 3, 2):
        remote(lsend.at[pl.ds(0, 2)], lrecv.at[(y + rel) % 4], l_s.at[0], l_r.at[(y + rel) % 4], sibling).wait_recv()
    numer.finish()

    def mix_view(index, half):
        return mix_ref.at[pl.ds(half * HALF, HALF), pl.ds(pl.multiple_of(index * HD, HD), HD)]

    mixes = RingGather(mix_view, z, zp, zm, (rs, rr), 3)
    returns = (
        remote(hsend, mix_view(z, 1), sw_s.at[1], sw_r.at[1], partner),
        remote(lhsend, lse_ref.at[1], sw_s.at[2], sw_r.at[2], partner),
    )
    for half in (1, 0):
        denom = sum(lrecv[n, half] for n in range(4))
        total = osend[2 * y + half].astype(FULL) + numer.arrived(half)
        inverse = jnp.transpose(jnp.broadcast_to(1.0 / denom[0:1, :], (128, HALF)))
        scaled = (total * jnp.concatenate([inverse, inverse], axis=1)).astype(LOW)
        if half == 1:
            hsend[...] = scaled
            lhsend[...] = jnp.log(denom)
            for copy in returns:
                go(copy)
        else:
            mix_view(z, 0)[...] = scaled
            lse_ref[0] = jnp.log(denom)
    mixes.own(0)
    for copy in returns:
        copy.wait_recv()
    mixes.own(1)
    wouts.near()
    wouts.far()
    wout_keep.wait()
    mixes.forward()
    mixes.near()
    mixes.far()
    for ring in (kv, qs, numer, mixes, wouts):
        ring.drain()
    for keep in keeps:
        keep.wait()
    for copy in copies:
        copy.wait_send()


VMEM = pl.BlockSpec(memory_space=pltpu.VMEM)
SMEM = pl.BlockSpec(memory_space=pltpu.SMEM)
ANY = pl.BlockSpec(memory_space=pl.ANY)


def dma(*shape):
    return pltpu.SemaphoreType.DMA(shape)


def shape(dtype, *dims):
    return jax.ShapeDtypeStruct(dims, dtype)


def vmem(dtype, *dims):
    return pltpu.VMEM(dims, dtype)


def params(number, mebibytes):
    return pltpu.CompilerParams(collective_id=number, has_side_effects=True, vmem_limit_bytes=mebibytes << 20)


def cost(gflops):
    return pl.CostEstimate(flops=gflops * 10**9, bytes_accessed=20 * 2**20, transcendentals=0)


def forward_attention(doc_starts, query, key, value, wout):
    return pl.pallas_call(
        attn_forward,
        name="attn_forward",
        out_shape=[
            shape(LOW, BLK, 4 * HD),
            shape(FULL, 2, 8, HALF),
            shape(LOW, 8, HALF, HD),
            shape(LOW, 8, BLK, HD),
            shape(LOW, 8, BLK, HD),
            shape(LOW, 4 * HD, wout.shape[1]),
        ],
        in_specs=[SMEM] + [VMEM] * 3 + [ANY],
        out_specs=[VMEM] * 2 + [ANY] * 4,
        scratch_shapes=[
            vmem(LOW, 8, HALF, HD),
            vmem(LOW, 8, BLK, HD),
            vmem(LOW, 8, BLK, HD),
            vmem(FULL, 8, HALF, HD),
            vmem(FULL, 8, HALF, 128),
            vmem(LOW, 8, HALF, HD),
            vmem(LOW, 2, HALF, HD),
            vmem(LOW, 2, 2, HALF, HD),
            vmem(FULL, 8, 8, HALF),
            vmem(FULL, 4, 2, 8, HALF),
            vmem(LOW, HALF, HD),
            vmem(FULL, 8, HALF),
            dma(5, 6), dma(5, 6), dma(4, 2), dma(4, 2), dma(3), dma(4), dma(3), dma(3), dma(4),
        ],
        compiler_params=params(1, 60),
        cost_estimate=cost(6),
    )(doc_starts, query, key, value, wout)


ROWS = 2560
SIDE = ROWS // 2
PIECE = SIDE // 4
WINDOW = PIECE // 4
CUTS = (0, 448, 896, 1280, 1728, 2144, 2560)


BLOCKS = ((0, 384), (384, 384), (768, 384), (1152, 384), (1536, 192))
PARTS = ((0, 512), (512, 640))
CORNER = 0.7978845608028654


def unit_of(values):
    inverse = lax.rsqrt(jnp.mean(values * values, axis=1, keepdims=True) + EPS)
    return inverse, values * inverse


def norm_back(inverse, unit, scaled):
    return inverse * (scaled - unit * jnp.mean(unit * scaled, axis=1, keepdims=True))


def middle_kernel(
    again_ref, pgain_ref, fgain_ref, lse_ref,
    mix_hbm, wout_hbm, tokens_hbm, cot_hbm, gate_hbm, up_hbm, down_hbm,
    mgrad_ref, stat_ref, early_ref, piece_a_ref, piece_b_ref, mixed_hbm, resid_hbm,
    mixed_ref, resid_ref, weights, wout, mix, tokens, cot, attn_out, left, right, turned, turned_up, aol,
    part_f, part_b, sum_f, sum_b, z_pass, z_got, sib_recv, pass_ab, got_ab, grows,
    in_sem, sib_s, sib_r, rs, rr, out_sem,
):
    x, y, c, z = place()
    xp, xm, yp, ym = at(x + 1, y, c, z), at(x + 3, y, c, z), at(x, y + 1, c, z), at(x, y + 3, c, z)
    zp, zm, sibling = at(x, y, c, z + 1), at(x, y, c, z + 3), at(x, y, 1 - c, z)
    hidden = gate_hbm.shape[0]
    width = weights.shape[1]
    loads = [
        pltpu.make_async_copy(src, dst, in_sem.at[n])
        for n, (src, dst) in enumerate(
            (
                (mix_hbm, mix),
                (wout_hbm, wout),
                (tokens_hbm, tokens),
                (gate_hbm, weights.at[pl.ds(0, hidden)]),
                (up_hbm, weights.at[pl.ds(hidden, hidden)]),
                (down_hbm, weights.at[pl.ds(2 * hidden, hidden)]),
                (cot_hbm, cot),
            )
        )
    ]
    for load in loads:
        load.start()
    greet([xp, xm, yp, ym, zp, zm, sibling])
    sems = (rs, rr)
    thirds = [pl.ds(start, size) for start, size in PARTS]

    def rows_of(r):
        return pl.ds(r * HALF, HALF)

    def head_sum(r, number, part, whole):
        quarter = HALF // 4
        first = r * HALF

        def span(ref, index, half):
            return rows_at(ref, first + quarter * index + half * (quarter // 2), quarter // 2)

        reduce = RingReduce(
            lambda rel, half: span(part, (z + rel) % 4, half),
            lambda half: z_pass.at[number, half],
            lambda side, half: z_got.at[number, side, half],
            zp, zm, sems, 2 * number,
        )
        gather = RingGather(lambda index, half: span(whole, index, half), z, zp, zm, sems, 2 * number + 1)

        def summed():
            reduce.finish()
            for half in range(2):
                own = span(part, z, half)[...].astype(FULL) + reduce.arrived(half)
                span(whole, z, half)[...] = own.astype(LOW)
            gather.whole()

        def gathered():
            gather.near()
            gather.far()

        return reduce, gather, summed, gathered

    sums = [head_sum(0, 0, part_f, sum_f), head_sum(1, 1, part_f, sum_f)]
    sums += [head_sum(0, 2, part_b, sum_b), head_sum(1, 3, part_b, sum_b)]

    def forward(r, hooks):
        rows, columns = rows_of(r), pl.ds(r * HALF, HALF)
        if r == 0:
            for load in loads[:3]:
                load.wait()
        for third in thirds:
            attn_out[rows, third] = jnp.dot(mix[rows, :], wout[:, third], preferred_element_type=FULL)
        _, unit = unit_of(attn_out[rows, :])
        state = tokens[rows, :].astype(FULL) + unit * again_ref[0:1, :]
        resid_ref[rows, :] = state
        _, unit = unit_of(state)
        right[0, rows, :] = (unit * pgain_ref[0:1, :]).astype(LOW)
        if r == 0:
            for load in loads[3:5]:
                load.wait()
        for n, (start, size) in enumerate(BLOCKS):
            low = right[0, rows, :]
            gate = lax.dot_general(weights[pl.ds(start, size), :], low, NT, preferred_element_type=FULL)
            up = lax.dot_general(weights[pl.ds(hidden + start, size), :], low, NT, preferred_element_type=FULL)
            square = gate * gate
            bend = jnp.tanh(CORNER * gate * (1.0 + 0.044715 * square))
            share = 0.5 * (1.0 + bend)
            gelu = gate * share
            slope = share + 0.5 * gate * (1.0 - bend * bend) * (CORNER * (1.0 + 3.0 * 0.044715 * square))
            act = (gelu * up).astype(LOW)
            left[pl.ds(start, size), columns] = (up * slope).astype(LOW)
            left[pl.ds(hidden + start, size), columns] = gelu.astype(LOW)
            left[pl.ds(2 * hidden + start, size), columns] = act
            turned[:, start : start + size] = jnp.transpose(act)
            if n in hooks:
                hooks[n]()
        if r == 0:
            loads[5].wait()
        for third in thirds:
            part = jnp.dot(
                turned[:, :hidden], weights[pl.ds(2 * hidden, hidden), third], preferred_element_type=FULL
            )
            part_f[rows, third] = part.astype(LOW)

    def backward(r, hooks):
        rows, columns = rows_of(r), pl.ds(r * HALF, HALF)
        if r == 0:
            loads[6].wait()
        inverse, unit = unit_of(sum_f[rows, :].astype(FULL))
        mixed_ref[rows, :] = (resid_ref[rows, :] + unit * fgain_ref[0:1, :]).astype(LOW)
        grad = cot[rows, :].astype(FULL)
        grows[2, r : r + 1, :] = jnp.sum(unit * grad, axis=0, keepdims=True)
        right[1, rows, :] = norm_back(inverse, unit, fgain_ref[0:1, :] * grad).astype(LOW)
        for n, (start, size) in enumerate(BLOCKS):
            act_grad = lax.dot_general(
                weights[pl.ds(2 * hidden + start, size), :], right[1, rows, :], NT, preferred_element_type=FULL
            )
            for first, turn in ((start, turned), (hidden + start, turned_up)):
                span = pl.ds(first, size)
                grads = (act_grad * left[span, columns].astype(FULL)).astype(LOW)
                left[span, columns] = grads
                turn[:, start : start + size] = jnp.transpose(grads)
            if n in hooks:
                hooks[n]()
        for third in thirds:
            part = jnp.dot(turned[:, :hidden], weights[pl.ds(0, hidden), third], preferred_element_type=FULL)
            part = part + jnp.dot(
                turned_up[:, :hidden], weights[pl.ds(hidden, hidden), third], preferred_element_type=FULL
            )
            part_b[rows, third] = part.astype(LOW)

    own_head = pl.ds(pl.multiple_of(z * HD, HD), HD)

    def finish(r):
        rows = rows_of(r)
        grad = sum_b[rows, :].astype(FULL)
        inverse, unit = unit_of(resid_ref[rows, :])
        grows[1, r : r + 1, :] = jnp.sum(unit * grad, axis=0, keepdims=True)
        grad = cot[rows, :].astype(FULL) + norm_back(inverse, unit, pgain_ref[0:1, :] * grad)
        resid_ref[rows, :] = grad
        inverse, unit = unit_of(attn_out[rows, :])
        grows[0, r : r + 1, :] = jnp.sum(unit * grad, axis=0, keepdims=True)
        aol[rows, :] = norm_back(inverse, unit, again_ref[0:1, :] * grad).astype(LOW)
        grads = lax.dot_general(aol[rows, :], wout[own_head, :], NT, preferred_element_type=FULL).astype(LOW)
        mgrad_ref[rows, :] = grads
        products = grads.astype(FULL) * mix[rows, own_head].astype(FULL)
        delta = jnp.sum(jnp.transpose(products), axis=0, keepdims=True)
        number = lax.broadcasted_iota(jnp.int32, (8, HALF), 0)
        stat_ref[r] = jnp.where(number == 1, delta, lse_ref[r])

    sib_send, mine = weights.at[pl.ds(0, ROWS)], weights.at[pl.ds(ROWS, ROWS)]

    def product(core, n, target, added):
        first, size = CUTS[n], CUTS[n + 1] - CUTS[n]
        lhs = left[pl.ds(pl.multiple_of(ROWS * core + first, 16), size), :]
        which = jnp.where(n >= 2, core, 0)
        for third in thirds:
            tile = jnp.dot(lhs, right[which, :, third], preferred_element_type=FULL)
            if added is not None:
                tile = tile + added[pl.ds(first, size), third].astype(FULL)
            target[pl.ds(first, size), third] = tile.astype(LOW)

    def to_sibling(n):
        span = pl.ds(CUTS[n], CUTS[n + 1] - CUTS[n])
        return remote(sib_send.at[span], sib_recv.at[span], sib_s.at[n], sib_r.at[n], sibling)

    def side_ring(h, me, plus, minus):
        return RingReduce(
            lambda rel, half: rows_at(
                weights, ROWS + SIDE * h + PIECE * ((me + rel) % 4) + half * (PIECE // 2), PIECE // 2
            ),
            lambda half: pass_ab.at[h, half],
            lambda side, half: got_ab.at[h, side, half],
            plus, minus, sems, 8 + h,
        )

    rings = (side_ring(0, x, xp, xm), side_ring(1, y, yp, ym))
    outs = [
        pltpu.make_async_copy(src, dst, out_sem.at[n])
        for n, (src, dst) in enumerate(
            ((mixed_ref, mixed_hbm), (resid_ref, resid_hbm))
        )
    ]
    forward(0, {})
    sums[0][0].start()
    forward(1, {3: sums[0][0].relay})
    sums[1][0].start()
    sums[0][2]()
    sums[1][0].relay()
    sums[0][1].forward()
    sums[0][3]()
    sums[1][2]()
    backward(0, {2: sums[1][1].forward})
    sums[2][0].start()
    sums[1][3]()
    backward(1, {2: sums[2][0].relay, 4: sums[2][2]})
    sums[3][0].start()
    outs[0].start()
    count = len(CUTS) - 1

    def for_sibling(chunks):
        for n in chunks:
            product(1 - c, n, sib_send, None)
            to_sibling(n).start()

    def for_self(chunks):
        for n in chunks:
            to_sibling(n).wait_recv()
            product(c, n, mine, sib_recv)

    side_a, side_b = range(count // 2), range(count // 2, count)
    for_sibling(side_a)
    sums[2][1].forward()
    sums[3][0].relay()
    for_self(side_a)
    rings[0].start()
    sums[3][2]()
    for_sibling(side_b)
    sums[3][1].forward()
    for_self(side_b)
    rings[1].start()
    sums[2][3]()
    finish(0)
    rings[0].relay()
    sums[3][3]()
    finish(1)
    rest = jnp.dot(left[2 * ROWS :, :], right[1], preferred_element_type=FULL)
    early_ref[pl.ds(HD, 64), :] = rest.astype(LOW)
    outs[1].start()
    lhs = jnp.transpose(mix[:, own_head])
    for third in thirds:
        early_ref[0:HD, third] = jnp.dot(lhs, aol[:, third], preferred_element_type=FULL).astype(LOW)
    number = lax.broadcasted_iota(jnp.int32, (32, width), 0)
    gains = jnp.zeros((32, width), FULL)
    for n in range(3):
        gains = jnp.where(number == n, grows[n, 0:1, :] + grows[n, 1:2, :], gains)
    early_ref[pl.ds(HD + 64, 32), :] = gains.astype(LOW)
    rings[1].relay()
    for h, (ring, me, out) in enumerate(((rings[0], x, piece_a_ref), (rings[1], y, piece_b_ref))):
        ring.finish()
        for half in range(2):
            size = PIECE // 2
            own = rows_at(weights, ROWS + SIDE * h + PIECE * me + half * size, size)[...]
            out[pl.ds(half * size, size), :] = (own.astype(FULL) + ring.arrived(half)).astype(LOW)
    for out in outs:
        out.wait()
    for reduce, gather, _, _ in sums:
        reduce.drain()
        gather.drain()
    for ring in rings:
        ring.drain()
    for n in range(count):
        to_sibling(n).wait_send()


def middle(again, pgain, fgain, lse, mix, wout, tokens, cot, gate_t, up_t, down):
    rows, width = tokens.shape
    hidden = gate_t.shape[0]
    stacked = 3 * hidden
    return pl.pallas_call(
        middle_kernel,
        name="middle",
        out_shape=[
            shape(LOW, rows, HD),
            shape(FULL, 2, 8, HALF),
            shape(LOW, HD + 96, width),
            shape(LOW, PIECE, width),
            shape(LOW, PIECE, width),
            shape(LOW, rows, width),
            shape(FULL, rows, width),
        ],
        in_specs=[VMEM] * 4 + [ANY] * 7,
        out_specs=[VMEM] * 5 + [ANY] * 2,
        scratch_shapes=[
            vmem(LOW, rows, width),
            vmem(FULL, rows, width),
            vmem(LOW, stacked, width),
            vmem(LOW, 4 * HD, width),
            vmem(LOW, rows, 4 * HD),
            vmem(LOW, rows, width),
            vmem(LOW, rows, width),
            vmem(FULL, rows, width),
            vmem(LOW, stacked, rows),
            vmem(LOW, 2, rows, width),
            vmem(LOW, HALF, 1792),
            vmem(LOW, HALF, 1792),
            vmem(LOW, rows, width),
            *[vmem(LOW, rows, width)] * 4,
            vmem(LOW, 4, 2, HALF // 8, width),
            vmem(LOW, 4, 2, 2, HALF // 8, width),
            vmem(LOW, ROWS, width),
            vmem(LOW, 2, 2, PIECE // 2, width),
            vmem(LOW, 2, 2, 2, PIECE // 2, width),
            vmem(FULL, 3, 8, width),
            dma(7), dma(6), dma(6), dma(10, 6), dma(10, 6), dma(2),
        ],
        compiler_params=params(4, 60),
        cost_estimate=cost(20),
    )(again, pgain, fgain, lse, mix, wout, tokens, cot, gate_t, up_t, down)


LATE = 112
EARLY = 176
KEEPERS = 11


def attn_backward(
    starts_ref, do_ref, stat_ref, piece_a_ref, piece_b_ref, qgain_ref, kgain_ref, igain_ref, early_ref,
    q_hbm, k_hbm, v_hbm, raw_hbm, kraw_hbm, cos_hbm, sin_hbm, wk_hbm, wv_hbm, normed_hbm, wq_hbm, tokens_hbm, resid_hbm,
    late_ref, esum_ref, tgrad_ref, dgain_ref, big_ref,
    dog, statg, dqacc, dkall, dvall, ktall, sibsend, sibrecv, kvsrc, kvpass, kvgot,
    dqsend, dqpass, dqgot, dqback, dqhigh, zpart, zpass, zgot, own_sum, gaing, winpass, wingot, full_a, full_b,
    draw_ref, dkv_ref, dkraw, dvrow, part, core_recv, half_sum, plane_recv, grow, grecv,
    e_core, e_half, e_plane,
    q_in, k_in, v_in, raw_ref, kraw_ref, cos_ref, sin_ref, wk_ref, wv_ref, normed_t, wq_ref, tok_ref,
    rs, rr, st_s, st_r, sw_s, sw_r, sib_s, sib_r, gn_s, gn_r, sf_s, sf_r, own_sem,
    load_sem, c_s, c_r, p_s, p_r, g_s, g_r, f_s, f_r, i_s, i_r,
    ep_s, ep_r, eg_s, eg_r, ef_s, ef_r,
):
    x, y, c, z = place()
    xp, xm, yp, ym = at(x + 1, y, c, z), at(x + 3, y, c, z), at(x, y + 1, c, z), at(x, y + 3, c, z)
    zp, zm, y2, z2 = at(x, y, c, z + 1), at(x, y, c, z + 3), at(x, y + 2, c, z), at(x, y, c, z + 2)
    sibling, partner = at(x, y, 1 - c, z), at(3 - x, y, c, z)
    shifts = [(a, b) for a in range(4) for b in range(4) if (a, b) != (0, 0)]
    plane = [at(x + a, y + b, c, z) for a, b in shifts]
    loads = [
        pltpu.make_async_copy(src, dst, load_sem.at[n])
        for n, (src, dst) in enumerate(
            (
                (q_hbm, q_in), (k_hbm, k_in), (v_hbm, v_in), (raw_hbm, raw_ref), (kraw_hbm, kraw_ref),
                (cos_hbm, cos_ref), (sin_hbm, sin_ref), (wk_hbm, wk_ref), (wv_hbm, wv_ref),
                (normed_hbm, normed_t), (wq_hbm, wq_ref.at[:, pl.ds(pl.multiple_of(z * HD, HD), HD)]), (tokens_hbm, tok_ref), (resid_hbm, tgrad_ref),
            )
        )
    ]
    for load in loads:
        load.start()
    greet(plane + [sibling, zp, zm, z2])
    copies = []

    def go(copy):
        copy.start()
        copies.append(copy)

    sems = (rs, rr)
    do_low, do_high = do_ref.at[pl.ds(0, HALF)], do_ref.at[pl.ds(HALF, HALF)]
    swaps = (
        remote(do_high, dog.at[2 * y + 1], sw_s.at[0], sw_r.at[0], partner),
        remote(stat_ref.at[1], statg.at[2 * y + 1], sw_s.at[1], sw_r.at[1], partner),
    )
    for copy in swaps:
        go(copy)
    dos = RingGather(
        lambda index, half: dog.at[2 * index + half], y, yp, ym, sems, 0,
        lambda half: do_low if half == 0 else dog.at[2 * y + 1],
    )
    dos.own(0)
    tall = wq_hbm.shape[0] // 2

    def wq_view(index, half):
        return wq_ref.at[pl.ds(half * tall, tall), pl.ds(pl.multiple_of(index * HD, HD), HD)]

    wqs = RingGather(
        wq_view, z, zp, zm, sems, 12, lambda half: wq_hbm.at[pl.ds(half * tall, tall)]
    )
    wqs.whole()
    chip = x * 4 + y
    e_cross = remote(rows_at(early_ref, EARLY * (1 - c), EARLY), e_core, c_s.at[1], c_r.at[1], sibling)
    go(e_cross)

    def early_part(owner):
        return remote(
            rows_at(e_half, 16 * owner, 16), e_plane.at[chip], ep_s.at[owner], ep_r.at[chip],
            at(owner // 4, owner % 4, c, z),
        )

    def early_spread():
        e_cross.wait_recv()
        own = early_ref[pl.ds(pl.multiple_of(EARLY * c, 16), EARLY), :]
        e_half[...] = (own.astype(FULL) + e_core[...].astype(FULL)).astype(LOW)
        for owner in range(KEEPERS):
            pl.when(chip != owner)(early_part(owner).start)

    def early_piece(core, owner):
        return rows_at(esum_ref, EARLY * core + 16 * owner, 16)

    def early_out(n):
        return remote(early_piece(c, chip), early_piece(c, chip), eg_s.at[n], eg_r.at[chip], plane[n])

    def early_across(owner):
        block = early_piece(c, owner)
        return remote(block, block, ef_s.at[owner], ef_r.at[owner], sibling)

    def early_summed():
        @pl.when(chip < KEEPERS)
        def _():
            total = rows_at(e_half, 16 * chip, 16)[...].astype(FULL)
            for a, b in shifts:
                source = ((x + a) % 4) * 4 + (y + b) % 4
                block = rows_at(e_half, 0, 16)
                remote(block, e_plane.at[source], ep_s.at[0], ep_r.at[source], sibling).wait_recv()
                total = total + e_plane[source].astype(FULL)
            early_piece(c, chip)[...] = total.astype(LOW)
            for n in range(15):
                early_out(n).start()
            early_across(chip).start()

    def early_passed():
        for owner in range(KEEPERS):

            @pl.when(chip != owner)
            def _():
                block = early_piece(c, owner)
                remote(rows_at(e_half, 0, 16), block, eg_s.at[0], eg_r.at[owner], sibling).wait_recv()
                early_across(owner).start()

    def early_done():
        for owner in range(KEEPERS):
            block = early_piece(1 - c, owner)
            remote(rows_at(e_half, 0, 16), block, ef_s.at[0], ef_r.at[owner], sibling).wait_recv()
            early_across(owner).wait_send()
            pl.when(chip != owner)(early_part(owner).wait_send)

        @pl.when(chip < KEEPERS)
        def _():
            for n in range(15):
                early_out(n).wait_send()

    def stats_to(upper, rel, peer):
        slot = 2 * y + upper
        source = statg.at[slot] if upper else stat_ref.at[0]
        return remote(source, statg.at[slot], st_s.at[upper, rel - 1], st_r.at[slot], peer)

    y_peers = ((1, yp), (3, ym), (2, y2))
    for rel, peer in y_peers:
        go(stats_to(0, rel, peer))

    cut = (48, WINDOW - 48)

    def window(ref, index, half):
        return rows_at(ref, WINDOW * index + 48 * half, cut[half])

    sides = ((piece_a_ref, full_a, y, yp, ym), (piece_b_ref, full_b, x, xp, xm))
    reduces, gathers = [], []
    for h, (piece, full, me, plus, minus) in enumerate(sides):
        reduces.append(
            RingReduce(
                lambda rel, half, piece=piece, me=me: window(piece, (me + rel) % 4, half),
                lambda half, h=h: winpass.at[h, pl.ds(48 * half, cut[half])],
                lambda side, half, h=h: wingot.at[h, side, pl.ds(48 * half, cut[half])],
                plus, minus, sems, 1 + h,
            )
        )
        gathers.append(
            RingGather(lambda index, half, full=full: window(full, index, half), me, plus, minus, sems, 3 + h)
        )
        reduces[h].start()

    def big_view(core, h, index, half):
        return rows_at(big_ref, ROWS * core + SIDE * h + PIECE * index + half * (PIECE // 2), PIECE // 2)

    owners = ((x, xp, xm), (y, yp, ym))
    pieces = [
        RingGather(
            lambda index, half, h=h: big_view(c, h, index, half), me, plus, minus, sems, 5 + h,
            lambda half, h=h: sides[h][1].at[pl.ds(half * (PIECE // 2), PIECE // 2)],
        )
        for h, (me, plus, minus) in enumerate(owners)
    ]

    def piece_to_sibling(h, index, half, source=None):
        block = big_view(c, h, index, half)
        return remote(block if source is None else source, block, sf_s.at[h, index, half], sf_r.at[h, index, half], sibling)

    def keep(h, half):
        source = sides[h][1].at[pl.ds(half * (PIECE // 2), PIECE // 2)]
        return pltpu.make_async_copy(source, big_view(c, h, owners[h][0], half), own_sem.at[h, half])

    def window_summed(h):
        ring, gather = reduces[h], gathers[h]
        piece, full, me, _, _ = sides[h]
        ring.finish()
        for half in range(2):
            total = window(piece, me, half)[...].astype(FULL) + ring.arrived(half)
            window(full, me, half)[...] = total.astype(LOW)
        gather.whole()

    def window_gathered(h):
        gathers[h].near()
        gathers[h].far()

    def pieces_sent(h):
        pieces[h].whole()
        for half in range(2):
            source = sides[h][1].at[pl.ds(half * (PIECE // 2), PIECE // 2)]
            go(piece_to_sibling(h, owners[h][0], half, source))
            keep(h, half).start()

    def pieces_near(h):
        pieces[h].near()
        for rel in (1, 3):
            for half in range(2):
                go(piece_to_sibling(h, (owners[h][0] + rel) % 4, half))

    def pieces_far(h):
        pieces[h].far()
        for half in range(2):
            go(piece_to_sibling(h, (owners[h][0] + 2) % 4, half))

    def tile(i, first_q, slot, first_k, masked):
        queries, out_grads = q_in[i], dog[i]
        lse, delta = statg[i, 0:1, :], statg[i, 1:2, :]
        if masked:
            token = first_q + lax.broadcasted_iota(jnp.int32, (1, HALF), 1)
            begin = begin_of(token, starts_ref)
        dq_part = None
        for n in range(2):
            rows = pl.ds(n * 256, 256)
            keys, values = k_in[slot, rows], v_in[slot, rows]
            scores = lax.dot_general(keys, queries, NT, preferred_element_type=FULL)
            prob_grad = lax.dot_general(values, out_grads, NT, preferred_element_type=FULL)
            soft = jnp.exp(scores - lse)
            if masked:
                key_index = first_k + n * 256 + lax.broadcasted_iota(jnp.int32, (256, 1), 0)
                soft = jnp.where((key_index <= token) & (key_index >= begin), soft, 0.0)
            score_grad = (soft * (prob_grad - delta)).astype(LOW)
            dvall[slot, rows, :] += jnp.dot(soft.astype(LOW), out_grads, preferred_element_type=FULL)
            dkall[slot, rows, :] += jnp.dot(score_grad, queries, preferred_element_type=FULL)
            part = jnp.dot(ktall[slot, :, n * 256 : (n + 1) * 256], score_grad, preferred_element_type=FULL)
            dq_part = part if dq_part is None else dq_part + part
        dqacc[i] = dqacc[i] + dq_part

    def visit(i, slot):
        first_q = tile_first(i, x, c)
        first_k = 4096 * (slot // 2) + 1024 * y + BLK * (slot % 2)
        some = first_k <= first_q + (HALF - 1)
        full = (first_k + BLK - 1 <= first_q) & (first_k > 0) & (first_q < 31 * BLK)

        @pl.when(full)
        def _():
            tile(i, first_q, slot, first_k, False)

        @pl.when(some & jnp.logical_not(full))
        def _():
            tile(i, first_q, slot, first_k, True)

    def own_tile(upper):
        def one(slot, carry):
            visit(2 * y + upper, slot)
            return carry

        lax.fori_loop(0, 8, one, 0)

    dog[2 * y] = do_ref[0:HALF, :]
    statg[2 * y] = stat_ref[0]
    dqacc[...] = jnp.zeros_like(dqacc)
    dkall[...] = jnp.zeros_like(dkall)
    dvall[...] = jnp.zeros_like(dvall)
    for load in loads[:3]:
        load.wait()

    def turn_keys(slot, carry):
        ktall[slot] = jnp.transpose(k_in[slot])
        return carry

    lax.fori_loop(0, 8, turn_keys, 0)
    for copy in swaps:
        copy.wait_recv()
    dos.own(1)
    for rel, peer in y_peers:
        go(stats_to(1, rel, peer))
    own_tile(0)
    dos.forward()
    for ring in reduces:
        ring.relay()
    own_tile(1)
    dos.near()
    dos.far()
    for upper in range(2):
        for rel, peer in y_peers:
            slot = 2 * ((y + rel) % 4) + upper
            remote(stat_ref.at[0], statg.at[slot], st_s.at[0, 0], st_r.at[slot], sibling).wait_recv()

    window_summed(0)
    window_summed(1)

    zrows = BLK // 4
    place_of = {2: 0, 1: 1, 3: 2, 0: 3}
    kvs = RingReduce(
        lambda rel, half: kvsrc.at[place_of[rel], half],
        lambda half: kvpass.at[half],
        lambda side, half: kvgot.at[side, half],
        xp, xm, sems, 7,
    )
    zrings = [
        RingReduce(
            lambda rel, half, step=step: zpart.at[step, (z + rel) % 4, half],
            lambda half, step=step: zpass.at[step, half],
            lambda side, half, step=step: zgot.at[step, side, half],
            zp, zm, sems, number,
        )
        for step, number in enumerate((9, 13, 14, 15))
    ]

    def cores_summed(step, rel):
        slot = ((x + rel) % 4) * 2 + c
        remote(sibsend.at[step], sibrecv.at[step], sib_s.at[step], sib_r.at[step], sibling).wait_recv()
        for half, ref in enumerate((dkall, dvall)):
            for n in range(4):
                rows = pl.ds(n * zrows, zrows)
                both = ref[slot, rows, :] + sibrecv[step, half, rows, :].astype(FULL)
                zpart[step, n, half] = both.astype(LOW)
        zrings[step].start()

    def heads_summed(step):
        zrings[step].finish()
        for half in range(2):
            total = zpart[step, z, half].astype(FULL) + zrings[step].arrived(half)
            if step == 3:
                own_sum[half] = total
            else:
                kvsrc[step, half] = total.astype(LOW)
        if step < 3:
            kvs.start(*((0, 1), (3,), (2,))[step])

    def pieces_start():
        for h in range(2):
            window_gathered(h)
            pieces_sent(h)

    def each_side(method):
        for h in range(2):
            method(h)

    between = {
        (0, 0): (early_spread,),
        (0, 1): (gathers[0].forward, gathers[1].forward),
        (1, 0): (pieces_start,),
        (1, 1): (lambda: cores_summed(0, 2),),
        (2, 0): (zrings[0].relay, early_summed, wqs.forward),
        (2, 1): (lambda: cores_summed(1, 1), lambda: heads_summed(0), pieces[0].forward, pieces[1].forward),
        (3, 0): (zrings[1].relay, wqs.near, wqs.far),
        (3, 1): (lambda: cores_summed(2, 3), lambda: heads_summed(1), lambda: each_side(pieces_near)),
    }
    for step, rel in enumerate((2, 1, 3, 0)):
        pair = (x + rel) % 4
        for turn in range(2):
            if (step, turn) in between:
                for hook in between[step, turn]:
                    hook()
            cc = 1 - c if turn == 0 else c
            slot = pair * 2 + cc

            def one(n, carry):
                visit((2 * y + 2 + n) % 8, slot)
                return carry

            lax.fori_loop(0, 6, one, 0)
            if turn == 0:
                sibsend[step, 0] = dkall[slot].astype(LOW)
                sibsend[step, 1] = dvall[slot].astype(LOW)
                go(remote(sibsend.at[step], sibrecv.at[step], sib_s.at[step], sib_r.at[step], sibling))

    zrings[2].relay()
    cores_summed(3, 0)
    zg = RingGather(lambda index, half: dkv_ref.at[index, half], z, zp, zm, sems, 10)

    def cast(i, carry):
        dqsend[i] = jnp.transpose(dqacc[i]).astype(LOW)
        return carry

    lax.fori_loop(0, 8, cast, 0)
    dqs = RingReduce(
        lambda rel, half: dqsend.at[2 * ((y + rel) % 4) + half],
        lambda half: dqpass.at[half],
        lambda side, half: dqgot.at[side, half],
        yp, ym, sems, 8,
    )
    dqs.start()
    heads_summed(2)
    zrings[3].relay()
    kvs.relay()
    dqs.relay()
    heads_summed(3)
    kvs.finish()
    for half in range(2):
        dkv_ref[z, half] = (own_sum[half] + kvs.arrived(half)).astype(LOW)
    zg.whole()
    early_passed()
    each_side(pieces_far)
    for load in loads[3:]:
        load.wait()
    dqs.finish()
    back = remote(dqback, dqhigh, sw_s.at[2], sw_r.at[2], partner)
    dqback[...] = (dqsend[2 * y + 1].astype(FULL) + dqs.arrived(1)).astype(LOW)
    go(back)

    draws = RingGather(
        lambda index, half: draw_ref.at[pl.ds(half * HALF, HALF), pl.ds(pl.multiple_of(index * HD, HD), HD)],
        z, zp, zm, sems, 11,
    )

    def unrotated(grad, raw, gain, rows):
        cosine, sine = cos_ref[rows, :], sin_ref[rows, :]
        first, second = grad[:, : HD // 2], grad[:, HD // 2 :]
        turned = jnp.concatenate([first * cosine + second * sine, second * cosine - first * sine], axis=1)
        inverse = lax.rsqrt(jnp.mean(raw * raw, axis=1, keepdims=True) + EPS)
        unit = raw * inverse
        scaled = gain * turned
        raw_grad = inverse * (scaled - unit * jnp.mean(unit * scaled, axis=1, keepdims=True))
        return raw_grad.astype(LOW), jnp.sum(unit * turned, axis=0, keepdims=True)

    gain_grad = None
    for half in range(2):
        if half == 0:
            grad = dqsend[2 * y].astype(FULL) + dqs.arrived(0)
        else:
            back.wait_recv()
            grad = dqhigh[...].astype(FULL)
        rows = pl.ds(half * HALF, HALF)
        raw_grad, piece = unrotated(grad * (HD**-0.5), raw_ref[rows, :], qgain_ref[0:1, :], rows)
        draw_ref[rows, pl.ds(pl.multiple_of(z * HD, HD), HD)] = raw_grad
        draws.own(half)
        gain_grad = piece if gain_grad is None else gain_grad + piece
    gaing[z] = jnp.broadcast_to(gain_grad, (8, HD))
    for n, peer in enumerate((zp, zm, z2)):
        go(remote(gaing.at[z], gaing.at[z], gn_s.at[n], gn_r.at[z], peer))

    chunk_rows = normed_t.shape[0] // 4

    def weight_grad(m, rhs):
        def block(r, carry):
            lhs = normed_t[pl.ds(pl.multiple_of(r * chunk_rows, 16), chunk_rows), :]
            tile = jnp.dot(lhs, rhs[...], preferred_element_type=FULL).astype(LOW)
            part[pl.ds(pl.multiple_of((4 * m + r) * chunk_rows, 16), chunk_rows), :] = tile
            return carry

        lax.fori_loop(0, 4, block, 0)

    zg.forward()
    weight_grad(0, draw_ref.at[:, pl.ds(pl.multiple_of(z * HD, HD), HD)])
    draws.forward()
    zg.near()
    zg.far()
    key_gain_grad = None
    for n in range(4):
        rows = pl.ds(n * zrows, zrows)
        raw_grad, piece = unrotated(dkv_ref[n, 0].astype(FULL), kraw_ref[rows, :], kgain_ref[0:1, :], rows)
        dkraw[rows, :] = raw_grad
        dvrow[rows, :] = dkv_ref[n, 1]
        key_gain_grad = piece if key_gain_grad is None else key_gain_grad + piece
    for rel in (1, 3, 2):
        other = (z + rel) % 4
        remote(gaing.at[z], gaing.at[other], gn_s.at[0], gn_r.at[other], sibling).wait_recv()
    query_gain_grad = sum(gaing[n, 0:1, :] for n in range(4))
    number = lax.broadcasted_iota(jnp.int32, (16, HD), 0)
    both = jnp.where(number == 0, query_gain_grad, jnp.where(number == 1, key_gain_grad, 0.0))
    part[pl.ds(12 * chunk_rows, 16), :] = both.astype(LOW)
    part[pl.ds(12 * chunk_rows + 16, LATE), :] = jnp.zeros((LATE, HD), LOW)
    weight_grad(1, dkraw)
    weight_grad(2, dvrow)

    side = 16 * LATE

    def late_piece(ref, core, owner):
        return rows_at(ref, side * core + LATE * owner, LATE)

    cross = remote(rows_at(part, side * (1 - c), side), core_recv, c_s.at[0], c_r.at[0], sibling)
    go(cross)
    cross.wait_recv()

    def add(r, carry):
        both = part[pl.ds(pl.multiple_of(side * c + 2 * LATE * r, 16), 2 * LATE), :].astype(FULL)
        rows = pl.ds(pl.multiple_of(2 * LATE * r, 16), 2 * LATE)
        half_sum[rows, :] = (both + core_recv[rows, :].astype(FULL)).astype(LOW)
        return carry

    lax.fori_loop(0, 8, add, 0)
    for n, (a, b) in enumerate(shifts):
        target = ((x + a) % 4) * 4 + (y + b) % 4
        go(remote(late_piece(half_sum, 0, target), plane_recv.at[chip], p_s.at[n], p_r.at[chip], plane[n]))

    draws.near()
    draws.far()
    gain_row = None
    for half in range(2):
        rows = pl.ds(half * HALF, HALF)
        grad = lax.dot_general(draw_ref[rows, :], wq_ref[...], NT, preferred_element_type=FULL)
        grad = grad + lax.dot_general(dkraw[rows, :], wk_ref[...], NT, preferred_element_type=FULL)
        grad = grad + lax.dot_general(dvrow[rows, :], wv_ref[...], NT, preferred_element_type=FULL)
        value = tok_ref[rows, :].astype(FULL)
        inverse = lax.rsqrt(jnp.mean(value * value, axis=1, keepdims=True) + EPS)
        unit = value * inverse
        scaled = igain_ref[0:1, :] * grad
        back_grad = inverse * (scaled - unit * jnp.mean(unit * scaled, axis=1, keepdims=True))
        tgrad_ref[rows, :] = tgrad_ref[rows, :] + back_grad
        piece = jnp.sum(unit * grad, axis=0, keepdims=True)
        gain_row = piece if gain_row is None else gain_row + piece
    grow[0] = jnp.broadcast_to(gain_row, grow.shape[1:])
    to_core = remote(grow.at[0], grow.at[1], i_s.at[15], i_r.at[16], sibling)
    go(to_core)

    total = late_piece(half_sum, 0, chip)[...].astype(FULL)
    for a, b in shifts:
        source = ((x + a) % 4) * 4 + (y + b) % 4
        remote(late_piece(half_sum, 0, 0), plane_recv.at[source], p_s.at[0], p_r.at[source], sibling).wait_recv()
        total = total + plane_recv[source].astype(FULL)

    def piece_of(owner):
        return late_piece(late_ref, c, owner)

    piece_of(chip)[...] = total.astype(LOW)
    for n in range(15):
        go(remote(piece_of(chip), piece_of(chip), g_s.at[n], g_r.at[chip], plane[n]))
    go(remote(piece_of(chip), piece_of(chip), f_s.at[chip], f_r.at[chip], sibling))
    to_core.wait_recv()
    grecv[chip] = grow[0] + grow[1]
    for n in range(15):
        go(remote(grecv.at[chip], grecv.at[chip], i_s.at[n], i_r.at[chip], plane[n]))
    for a, b in shifts:
        source = ((x + a) % 4) * 4 + (y + b) % 4
        remote(late_piece(half_sum, 0, 0), piece_of(source), g_s.at[0], g_r.at[source], sibling).wait_recv()
        go(remote(piece_of(source), piece_of(source), f_s.at[source], f_r.at[source], sibling))
    for a, b in shifts:
        source = ((x + a) % 4) * 4 + (y + b) % 4
        remote(grecv.at[chip], grecv.at[source], i_s.at[0], i_r.at[source], sibling).wait_recv()
    dgain_ref[...] = sum(grecv[n] for n in range(16))
    for n in range(16):
        theirs = late_piece(late_ref, 1 - c, n)
        remote(late_piece(half_sum, 0, 0), theirs, f_s.at[0], f_r.at[n], sibling).wait_recv()
    early_done()
    for h in range(2):
        for half in range(2):
            keep(h, half).wait()
            for n in range(4):
                piece_to_sibling(h, n, half).wait_recv()
    for ring in [dos, kvs, dqs, zg, draws, wqs] + zrings + reduces + gathers + pieces:
        ring.drain()
    for copy in copies:
        copy.wait_send()


def backward_attention(doc_starts, *operands):
    width = operands[2].shape[1]
    streamed = operands[8:]
    return pl.pallas_call(
        attn_backward,
        name="attn_backward",
        out_shape=[
            shape(LOW, 32 * LATE, HD),
            shape(LOW, 2 * EARLY, width),
            shape(FULL, BLK, width),
            shape(FULL, 8, width),
            shape(LOW, 2 * ROWS + 64, width),
        ],
        in_specs=[SMEM] + [VMEM] * 8 + [ANY] * 13,
        out_specs=[VMEM] * 4 + [ANY],
        scratch_shapes=[
            vmem(LOW, 8, HALF, HD),
            vmem(FULL, 8, 8, HALF),
            vmem(FULL, 8, HD, HALF),
            vmem(FULL, 8, BLK, HD),
            vmem(FULL, 8, BLK, HD),
            vmem(LOW, 8, HD, BLK),
            vmem(LOW, 4, 2, BLK, HD),
            vmem(LOW, 4, 2, BLK, HD),
            vmem(LOW, 3, 2, BLK // 4, HD),
            vmem(LOW, 2, BLK // 4, HD),
            vmem(LOW, 2, 2, BLK // 4, HD),
            vmem(LOW, 8, HALF, HD),
            vmem(LOW, 2, HALF, HD),
            vmem(LOW, 2, 2, HALF, HD),
            vmem(LOW, HALF, HD),
            vmem(LOW, HALF, HD),
            vmem(LOW, 4, 4, 2, BLK // 4, HD),
            vmem(LOW, 4, 2, BLK // 4, HD),
            vmem(LOW, 4, 2, 2, BLK // 4, HD),
            vmem(FULL, 2, BLK // 4, HD),
            vmem(FULL, 4, 8, HD),
            vmem(LOW, 2, WINDOW, width),
            vmem(LOW, 2, 2, WINDOW, width),
            vmem(LOW, PIECE, width),
            vmem(LOW, PIECE, width),
            vmem(LOW, BLK, 4 * HD),
            vmem(LOW, 4, 2, BLK // 4, HD),
            vmem(LOW, BLK, HD),
            vmem(LOW, BLK, HD),
            vmem(LOW, 32 * LATE, HD),
            vmem(LOW, 16 * LATE, HD),
            vmem(LOW, 16 * LATE, HD),
            vmem(LOW, 16, LATE, HD),
            vmem(FULL, 2, 8, width),
            vmem(FULL, 16, 8, width),
            vmem(LOW, EARLY, width),
            vmem(LOW, EARLY, width),
            vmem(LOW, 16, 16, width),
            *[vmem(operand.dtype, *operand.shape) for operand in streamed[:10]],
            vmem(LOW, width, 4 * HD),
            vmem(LOW, *streamed[11].shape),
            dma(16, 6), dma(16, 6), dma(2, 3), dma(8), dma(3), dma(3), dma(4), dma(4), dma(3), dma(4),
            dma(2, 4, 2), dma(2, 4, 2), dma(2, 2),
            dma(13), dma(2), dma(2), dma(15), dma(16), dma(15), dma(16), dma(16), dma(16), dma(16), dma(17),
            dma(KEEPERS), dma(16), dma(15), dma(16), dma(KEEPERS), dma(KEEPERS),
        ],
        compiler_params=params(2, 60),
        cost_estimate=cost(15),
    )(doc_starts, *operands)


def wide(gain):
    return lax.broadcast_in_dim(gain, (8, gain.shape[0]), (1,))


def per_device(
    tokens,
    cotangent,
    doc_starts,
    query_weight,
    key_weight,
    value_weight,
    out_weight,
    gate_weight,
    up_weight,
    down_weight,
    input_gain,
    attn_gain,
    prenorm_gain,
    post_gain,
    query_gain,
    key_gain,
):
    row_count = tokens.shape[0]
    first_row = lax.axis_index("seq") * row_count
    own_index = first_row + jnp.arange(row_count, dtype=jnp.int32)
    own_position = doc_layout(doc_starts, own_index)[1]
    cos_table, sine_table = rope_tables(own_position, HD)
    query_scale = HD ** (-0.5)
    inputs = tokens.astype(jnp.float32)
    normed = rms_norm(inputs, input_gain)
    normed_low = normed.astype(jnp.bfloat16)
    query_raw = jnp.dot(normed_low, query_weight, preferred_element_type=jnp.float32)
    key_raw = jnp.dot(normed_low, key_weight, preferred_element_type=jnp.float32)
    value_low = jnp.dot(normed_low, value_weight, preferred_element_type=jnp.float32).astype(
        jnp.bfloat16
    )

    def query_piece(source, scaling):
        return rotate(rms_norm(source, scaling), cos_table, sine_table) * query_scale

    def key_piece(source, scaling):
        return rotate(rms_norm(source, scaling), cos_table, sine_table)

    query_rows = query_piece(query_raw, query_gain)
    query_low = query_rows.astype(jnp.bfloat16)
    key_rows = key_piece(key_raw, key_gain)
    key_low = key_rows.astype(jnp.bfloat16)
    mix_all, lse_rows, q_all, k_all, v_all, out_weight_all = forward_attention(
        doc_starts, query_low, key_low, value_low, out_weight
    )
    width = tokens.shape[1]
    mix_grad, stats, early, piece_a, piece_b, mixed, resid = middle(
        wide(attn_gain),
        wide(prenorm_gain),
        wide(post_gain),
        lse_rows,
        mix_all,
        out_weight_all,
        tokens,
        cotangent,
        jnp.transpose(gate_weight),
        jnp.transpose(up_weight),
        down_weight,
    )
    late, early, tokens_grad, input_gain_rows, big = backward_attention(
        doc_starts,
        mix_grad,
        stats,
        piece_a,
        piece_b,
        wide(query_gain),
        wide(key_gain),
        wide(input_gain),
        early,
        q_all,
        k_all,
        v_all,
        query_raw,
        key_raw,
        cos_table,
        sine_table,
        key_weight,
        value_weight,
        jnp.transpose(normed_low),
        query_weight,
        tokens,
        resid,
    )
    input_gain_grad = input_gain_rows[0]
    query_weight_grad = late[:width].astype(jnp.float32)
    key_weight_grad = late[width : 2 * width].astype(jnp.float32)
    value_weight_grad = late[2 * width : 3 * width].astype(jnp.float32)
    query_gain_grad = late[3 * width].astype(jnp.float32)
    key_gain_grad = late[3 * width + 1].astype(jnp.float32)
    out_weight_grad = early[:HD].astype(jnp.float32)
    rest = early[HD : HD + 64]
    gains = early[HD + 64 : HD + 67].astype(jnp.float32)
    attn_gain_grad, prenorm_gain_grad, post_gain_grad = gains[0], gains[1], gains[2]
    hidden = gate_weight.shape[1]
    gate_weight_grad = jnp.transpose(big[:hidden].astype(jnp.float32))
    up_weight_grad = jnp.transpose(big[hidden : 2 * hidden].astype(jnp.float32))
    down_weight_grad = big[2 * hidden :].astype(jnp.float32)
    down_weight_grad = lax.dynamic_update_slice(
        down_weight_grad, rest.astype(jnp.float32), (hidden - rest.shape[0], 0)
    )
    return (
        mixed,
        tokens_grad,
        query_weight_grad,
        key_weight_grad,
        value_weight_grad,
        out_weight_grad,
        gate_weight_grad,
        up_weight_grad,
        down_weight_grad,
        input_gain_grad,
        attn_gain_grad,
        prenorm_gain_grad,
        post_gain_grad,
        query_gain_grad,
        key_gain_grad,
    )


def solution(mesh):
    placed = (
        P("seq", None),
        P("seq", None),
        P(),
        P(None, "head"),
        P(),
        P(),
        P("head", None),
        P(None, "head"),
        P(None, "head"),
        P("head", None),
        P(),
        P(),
        P(),
        P(),
        P(),
        P(),
    )
    return jax.shard_map(
        per_device,
        mesh=mesh,
        in_specs=placed,
        out_specs=(
            P("seq", None),
            P("seq", None),
            P(None, "head"),
            P(),
            P(),
            P("head", None),
            P(None, "head"),
            P(None, "head"),
            P("head", None),
            P(),
            P(),
            P(),
            P(),
            P(),
            P(),
        ),
        check_vma=False,
    )
```

```python
import functools
import math

import jax
import jax.numpy as jnp
from jax import lax
from jax.experimental import pallas as pl
from jax.experimental.pallas import tpu as pltpu
from jax.sharding import PartitionSpec as P

HD = 256


EPS = 1e-06
THETA = 1000000.0
NEG = -1e30


def rms_norm(values, scaling):
    return values * lax.rsqrt(jnp.mean(values * values, axis=-1, keepdims=True) + EPS) * scaling


def doc_layout(doc_starts, token_index):
    before = doc_starts[None, :] <= token_index[:, None]
    segment = jnp.sum(before.astype(jnp.int32), axis=1)
    doc_begin = jnp.max(jnp.where(before, doc_starts[None, :], 0), axis=1)
    return (segment, token_index - doc_begin)


def rope_tables(position, head_width):
    half_width = head_width // 2
    inverse = jnp.exp(
        -math.log(THETA) * 2.0 * jnp.arange(half_width, dtype=jnp.float32) / head_width
    )
    angles = position.astype(jnp.float32)[:, None] * inverse[None, :]
    return (jnp.cos(angles), jnp.sin(angles))


def rotate(values, cos_table, sine_table):
    half_width = values.shape[-1] // 2
    first, second = values[..., :half_width], values[..., half_width:]
    return jnp.concatenate(
        [first * cos_table - second * sine_table, second * cos_table + first * sine_table], axis=-1
    )


MESH_ID = pl.DeviceIdType.MESH
HALF = 256
BLK = 512
LOW = jnp.bfloat16
FULL = jnp.float32
NT = (((1,), (1,)), ((), ()))


def place():
    s = lax.axis_index("seq")
    return s // 8, (s // 2) % 4, s % 2, lax.axis_index("head")


def at(x, y, c, z):
    return ((x % 4) * 8 + (y % 4) * 2 + c, z % 4)


def greet(peers):
    barrier = pltpu.get_barrier_semaphore()
    for peer in peers:
        pl.semaphore_signal(barrier, inc=1, device_id=peer, device_id_type=MESH_ID)
    pl.semaphore_wait(barrier, len(peers))


def remote(src, dst, send_sem, recv_sem, peer):
    return pltpu.make_async_remote_copy(
        src_ref=src,
        dst_ref=dst,
        send_sem=send_sem,
        recv_sem=recv_sem,
        device_id=peer,
        device_id_type=MESH_ID,
    )


def rows_at(ref, start, size):
    return ref.at[pl.ds(pl.multiple_of(start, 16), size)]


class RingGather:
    def __init__(self, view, me, plus, minus, sems, ring, source=None):
        send, recv = sems

        def near(rel, half):
            return view((me + rel) % 4, half)

        own = source or (lambda half: near(0, half))
        plan = (
            (own(0), near(0, 0), plus),
            (own(1), near(0, 1), plus),
            (near(3, 0), near(3, 0), plus),
            (own(0), near(0, 0), minus),
            (own(1), near(0, 1), minus),
            (near(1, 1), near(1, 1), minus),
        )
        self.copies = [
            remote(src, dst, send.at[ring, k], recv.at[ring, k], peer) for k, (src, dst, peer) in enumerate(plan)
        ]

    def own(self, half):
        self.copies[half].start()
        self.copies[3 + half].start()

    def whole(self):
        for k in (0, 4, 1, 3):
            self.copies[k].start()

    def forward(self):
        self.copies[0].wait_recv()
        self.copies[2].start()
        self.copies[4].wait_recv()
        self.copies[5].start()

    def near(self):
        self.copies[1].wait_recv()
        self.copies[3].wait_recv()

    def far(self):
        self.copies[2].wait_recv()
        self.copies[5].wait_recv()

    def drain(self):
        for copy in self.copies:
            copy.wait_send()


class RingReduce:
    def __init__(self, view, passing, got, plus, minus, sems, ring):
        send, recv = sems
        self.view, self.passing, self.got = view, passing, got
        plan = (
            (view(2, 0), passing(0), minus),
            (view(2, 1), passing(1), plus),
            (view(3, 1), got(0, 1), minus),
            (view(1, 0), got(1, 0), plus),
            (passing(0), got(0, 0), minus),
            (passing(1), got(1, 1), plus),
        )
        self.copies = [
            remote(src, dst, send.at[ring, k], recv.at[ring, k], peer) for k, (src, dst, peer) in enumerate(plan)
        ]

    def start(self, *numbers):
        for k in numbers or (0, 1, 2, 3):
            self.copies[k].start()

    def relay(self):
        for half, rel in ((0, 3), (1, 1)):
            self.copies[half].wait_recv()
            land, term = self.passing(half), self.view(rel, half)
            land[...] = (land[...].astype(FULL) + term[...].astype(FULL)).astype(LOW)
            self.copies[4 + half].start()

    def finish(self):
        for k in (2, 3, 4, 5):
            self.copies[k].wait_recv()

    def arrived(self, half):
        return self.got(0, half)[...].astype(FULL) + self.got(1, half)[...].astype(FULL)

    def drain(self):
        for copy in self.copies:
            copy.wait_send()


def tile_first(i, x, c):
    column = jnp.where(i % 2 == 1, 3 - x, x)
    return BLK * (8 * column + 2 * (i // 2) + c) + HALF * (i % 2)


def begin_of(token, starts_ref):
    begin = jnp.zeros_like(token)
    for n in range(starts_ref.shape[0]):
        start = starts_ref[n]
        begin = jnp.where(start <= token, start, begin)
    return begin


def attn_forward(
    starts_ref, q_ref, k_ref, v_ref, wout_hbm,
    mix_ref, lse_ref, q_out, k_out, v_out, wout_all,
    qg_ref, kg_ref, vg_ref, acc, lacc, osend, opass, ogot, lsend, lrecv, hsend, lhsend,
    rs, rr, sib_s, sib_r, l_s, l_r, sw_s, sw_r, keep_sem,
):
    x, y, c, z = place()
    xp, xm, yp, ym = at(x + 1, y, c, z), at(x + 3, y, c, z), at(x, y + 1, c, z), at(x, y + 3, c, z)
    zp, zm, y2 = at(x, y, c, z + 1), at(x, y, c, z + 3), at(x, y + 2, c, z)
    sibling, partner = at(x, y, 1 - c, z), at(3 - x, y, c, z)
    greet([partner, sibling, xp, xm, yp, ym, y2, zp, zm])
    copies = []

    def go(copy):
        copy.start()
        copies.append(copy)

    q_low, q_high = q_ref.at[pl.ds(0, HALF)], q_ref.at[pl.ds(HALF, HALF)]
    swap = remote(q_high, qg_ref.at[2 * y + 1], sw_s.at[0], sw_r.at[0], partner)
    go(swap)

    def kv_view(index, half):
        return (kg_ref, vg_ref)[half].at[2 * index + c]

    kv = RingGather(kv_view, x, xp, xm, (rs, rr), 0, lambda half: (k_ref, v_ref)[half])
    kv.whole()
    qs = RingGather(
        lambda index, half: qg_ref.at[2 * index + half], y, yp, ym, (rs, rr), 1,
        lambda half: q_low if half == 0 else qg_ref.at[2 * y + 1],
    )
    qs.own(0)

    def pass_on(index, half, source=None):
        block = kv_view(index, half)
        return remote(block if source is None else source, block, sib_s.at[index, half], sib_r.at[index, half], sibling)

    for half, source in enumerate((k_ref, v_ref)):
        go(pass_on(x, half, source))
    wide = wout_hbm.shape[0]

    def wout_view(index, half):
        return rows_at(wout_all, wide * index + half * (wide // 2), wide // 2)

    wouts = RingGather(
        wout_view, z, zp, zm, (rs, rr), 4, lambda half: wout_hbm.at[pl.ds(half * (wide // 2), wide // 2)]
    )
    wouts.whole()
    wout_keep = pltpu.make_async_copy(wout_hbm, rows_at(wout_all, wide * z, wide), keep_sem.at[3])
    wout_keep.start()
    qg_ref[2 * y] = q_ref[0:HALF, :]
    kg_ref[2 * x + c] = k_ref[...]
    vg_ref[2 * x + c] = v_ref[...]
    acc[...] = jnp.zeros_like(acc)
    lacc[...] = jnp.zeros_like(lacc)
    swap.wait_recv()
    qs.own(1)
    kv.forward()
    qs.forward()
    kv.near()
    for rel in (1, 3):
        for half in range(2):
            go(pass_on((x + rel) % 4, half))
    qs.near()
    qs.far()
    wouts.forward()

    def chunk(i, first_q, pair, first_k, masked):
        queries = qg_ref[i]
        if masked:
            token = first_q + lax.broadcasted_iota(jnp.int32, (HALF, 1), 0)
            begin = begin_of(token, starts_ref)
        total = None
        sums = None
        for cc in range(2):
            keys, values = kg_ref[pair * 2 + cc], vg_ref[pair * 2 + cc]
            scores = lax.dot_general(queries, keys, NT, preferred_element_type=FULL)
            exps = jnp.exp(scores)
            if masked:
                key_index = first_k + cc * BLK + lax.broadcasted_iota(jnp.int32, (1, BLK), 1)
                exps = jnp.where((key_index <= token) & (key_index >= begin), exps, 0.0)
            part = jnp.dot(exps.astype(LOW), values, preferred_element_type=FULL)
            total = part if total is None else total + part
            for n in range(BLK // 128):
                piece = exps[:, n * 128 : (n + 1) * 128]
                sums = piece if sums is None else sums + piece
        acc[i] = acc[i] + total
        lacc[i] = lacc[i] + sums

    def visit(i, pair):
        first_q, first_k = tile_first(i, x, c), 4096 * pair + 1024 * y
        some = first_k <= first_q + (HALF - 1)
        full = (first_k + 1023 <= first_q) & (first_k > 0) & (first_q < 31 * BLK)

        @pl.when(full)
        def _():
            chunk(i, first_q, pair, first_k, False)

        @pl.when(some & jnp.logical_not(full))
        def _():
            chunk(i, first_q, pair, first_k, True)

    numer = RingReduce(
        lambda rel, half: osend.at[2 * ((y + rel) % 4) + half],
        lambda half: opass.at[half],
        lambda side, half: ogot.at[side, half],
        yp, ym, (rs, rr), 2,
    )

    def sums_to(rel, peer):
        index = (y + rel) % 4
        return remote(lsend.at[pl.ds(2 * index, 2)], lrecv.at[y], l_s.at[rel - 1], l_r.at[y], peer)

    keeps = [
        pltpu.make_async_copy(src, dst, keep_sem.at[n])
        for n, (src, dst) in enumerate(((qg_ref, q_out), (kg_ref, k_out), (vg_ref, v_out)))
    ]
    for rel, peer in ((2, y2), (1, yp), (3, ym), (0, None)):
        first = 2 * ((y + rel) % 4)
        if rel == 2:
            for turn in (0, 1, 3, 2):
                pair = (x + turn) % 4
                if turn == 2:
                    kv.far()
                    for half in range(2):
                        go(pass_on(pair, half))
                for half in range(2):
                    pass_on(pair, half).wait_recv()
                for upper in range(2):
                    visit(first + upper, pair)
            for keep in keeps:
                keep.start()
        else:

            def one(n, carry):
                visit(first + n // 4, n % 4)
                return carry

            lax.fori_loop(0, 8, one, 0)

        for upper in range(2):
            i = first + upper
            osend[i] = acc[i].astype(LOW)
            row = jnp.sum(jnp.transpose(lacc[i]), axis=0, keepdims=True)
            lsend[i] = jnp.broadcast_to(row, (8, HALF))
        if rel == 2:
            numer.start(0, 1)
        elif rel == 1:
            numer.start(3)
        elif rel == 3:
            numer.start(2)
            numer.relay()
        if rel > 0:
            go(sums_to(rel, peer))
    lrecv[y] = lsend[pl.ds(2 * y, 2)]
    for rel in (1, 3, 2):
        remote(lsend.at[pl.ds(0, 2)], lrecv.at[(y + rel) % 4], l_s.at[0], l_r.at[(y + rel) % 4], sibling).wait_recv()
    numer.finish()

    def mix_view(index, half):
        return mix_ref.at[pl.ds(half * HALF, HALF), pl.ds(pl.multiple_of(index * HD, HD), HD)]

    mixes = RingGather(mix_view, z, zp, zm, (rs, rr), 3)
    returns = (
        remote(hsend, mix_view(z, 1), sw_s.at[1], sw_r.at[1], partner),
        remote(lhsend, lse_ref.at[1], sw_s.at[2], sw_r.at[2], partner),
    )
    for half in (1, 0):
        denom = sum(lrecv[n, half] for n in range(4))
        total = osend[2 * y + half].astype(FULL) + numer.arrived(half)
        inverse = jnp.transpose(jnp.broadcast_to(1.0 / denom[0:1, :], (128, HALF)))
        scaled = (total * jnp.concatenate([inverse, inverse], axis=1)).astype(LOW)
        if half == 1:
            hsend[...] = scaled
            lhsend[...] = jnp.log(denom)
            for copy in returns:
                go(copy)
        else:
            mix_view(z, 0)[...] = scaled
            lse_ref[0] = jnp.log(denom)
    mixes.own(0)
    for copy in returns:
        copy.wait_recv()
    mixes.own(1)
    wouts.near()
    wouts.far()
    wout_keep.wait()
    mixes.forward()
    mixes.near()
    mixes.far()
    for ring in (kv, qs, numer, mixes, wouts):
        ring.drain()
    for keep in keeps:
        keep.wait()
    for copy in copies:
        copy.wait_send()


VMEM = pl.BlockSpec(memory_space=pltpu.VMEM)
SMEM = pl.BlockSpec(memory_space=pltpu.SMEM)
ANY = pl.BlockSpec(memory_space=pl.ANY)


def dma(*shape):
    return pltpu.SemaphoreType.DMA(shape)


def shape(dtype, *dims):
    return jax.ShapeDtypeStruct(dims, dtype)


def vmem(dtype, *dims):
    return pltpu.VMEM(dims, dtype)


def params(number, mebibytes):
    return pltpu.CompilerParams(collective_id=number, has_side_effects=True, vmem_limit_bytes=mebibytes << 20)


def cost(gflops):
    return pl.CostEstimate(flops=gflops * 10**9, bytes_accessed=20 * 2**20, transcendentals=0)


def forward_attention(doc_starts, query, key, value, wout):
    return pl.pallas_call(
        attn_forward,
        name="attn_forward",
        out_shape=[
            shape(LOW, BLK, 4 * HD),
            shape(FULL, 2, 8, HALF),
            shape(LOW, 8, HALF, HD),
            shape(LOW, 8, BLK, HD),
            shape(LOW, 8, BLK, HD),
            shape(LOW, 4 * HD, wout.shape[1]),
        ],
        in_specs=[SMEM] + [VMEM] * 3 + [ANY],
        out_specs=[VMEM] * 2 + [ANY] * 4,
        scratch_shapes=[
            vmem(LOW, 8, HALF, HD),
            vmem(LOW, 8, BLK, HD),
            vmem(LOW, 8, BLK, HD),
            vmem(FULL, 8, HALF, HD),
            vmem(FULL, 8, HALF, 128),
            vmem(LOW, 8, HALF, HD),
            vmem(LOW, 2, HALF, HD),
            vmem(LOW, 2, 2, HALF, HD),
            vmem(FULL, 8, 8, HALF),
            vmem(FULL, 4, 2, 8, HALF),
            vmem(LOW, HALF, HD),
            vmem(FULL, 8, HALF),
            dma(5, 6), dma(5, 6), dma(4, 2), dma(4, 2), dma(3), dma(4), dma(3), dma(3), dma(4),
        ],
        compiler_params=params(1, 60),
        cost_estimate=cost(6),
    )(doc_starts, query, key, value, wout)


ROWS = 2560
SIDE = ROWS // 2
PIECE = SIDE // 4
WINDOW = PIECE // 4
CUTS = (0, 448, 896, 1280, 1728, 2144, 2560)


BLOCKS = ((0, 384), (384, 384), (768, 384), (1152, 384), (1536, 192))
PARTS = ((0, 512), (512, 640))
CORNER = 0.7978845608028654


def unit_of(values):
    inverse = lax.rsqrt(jnp.mean(values * values, axis=1, keepdims=True) + EPS)
    return inverse, values * inverse


def norm_back(inverse, unit, scaled):
    return inverse * (scaled - unit * jnp.mean(unit * scaled, axis=1, keepdims=True))


def middle_kernel(
    again_ref, pgain_ref, fgain_ref, lse_ref,
    mix_hbm, wout_hbm, tokens_hbm, cot_hbm, gate_hbm, up_hbm, down_hbm,
    mgrad_ref, stat_ref, early_ref, piece_a_ref, piece_b_ref, mixed_hbm, resid_hbm,
    mixed_ref, resid_ref, weights, wout, mix, tokens, cot, attn_out, left, right, turned, turned_up, aol,
    part_f, part_b, sum_f, sum_b, z_pass, z_got, sib_recv, pass_ab, got_ab, grows,
    in_sem, sib_s, sib_r, rs, rr, out_sem,
):
    x, y, c, z = place()
    xp, xm, yp, ym = at(x + 1, y, c, z), at(x + 3, y, c, z), at(x, y + 1, c, z), at(x, y + 3, c, z)
    zp, zm, sibling = at(x, y, c, z + 1), at(x, y, c, z + 3), at(x, y, 1 - c, z)
    hidden = gate_hbm.shape[0]
    width = weights.shape[1]
    loads = [
        pltpu.make_async_copy(src, dst, in_sem.at[n])
        for n, (src, dst) in enumerate(
            (
                (mix_hbm, mix),
                (wout_hbm, wout),
                (tokens_hbm, tokens),
                (gate_hbm, weights.at[pl.ds(0, hidden)]),
                (up_hbm, weights.at[pl.ds(hidden, hidden)]),
                (down_hbm, weights.at[pl.ds(2 * hidden, hidden)]),
                (cot_hbm, cot),
            )
        )
    ]
    for load in loads:
        load.start()
    greet([xp, xm, yp, ym, zp, zm, sibling])
    sems = (rs, rr)
    thirds = [pl.ds(start, size) for start, size in PARTS]

    def rows_of(r):
        return pl.ds(r * HALF, HALF)

    def head_sum(r, number, part, whole):
        quarter = HALF // 4
        first = r * HALF

        def span(ref, index, half):
            return rows_at(ref, first + quarter * index + half * (quarter // 2), quarter // 2)

        reduce = RingReduce(
            lambda rel, half: span(part, (z + rel) % 4, half),
            lambda half: z_pass.at[number, half],
            lambda side, half: z_got.at[number, side, half],
            zp, zm, sems, 2 * number,
        )
        gather = RingGather(lambda index, half: span(whole, index, half), z, zp, zm, sems, 2 * number + 1)

        def summed():
            reduce.finish()
            for half in range(2):
                own = span(part, z, half)[...].astype(FULL) + reduce.arrived(half)
                span(whole, z, half)[...] = own.astype(LOW)
            gather.whole()

        def gathered():
            gather.near()
            gather.far()

        return reduce, gather, summed, gathered

    sums = [head_sum(0, 0, part_f, sum_f), head_sum(1, 1, part_f, sum_f)]
    sums += [head_sum(0, 2, part_b, sum_b), head_sum(1, 3, part_b, sum_b)]

    def forward(r, hooks):
        rows, columns = rows_of(r), pl.ds(r * HALF, HALF)
        if r == 0:
            for load in loads[:3]:
                load.wait()
        for third in thirds:
            attn_out[rows, third] = jnp.dot(mix[rows, :], wout[:, third], preferred_element_type=FULL)
        _, unit = unit_of(attn_out[rows, :])
        state = tokens[rows, :].astype(FULL) + unit * again_ref[...][None, :]
        resid_ref[rows, :] = state
        _, unit = unit_of(state)
        right[0, rows, :] = (unit * pgain_ref[...][None, :]).astype(LOW)
        if r == 0:
            for load in loads[3:5]:
                load.wait()
        for n, (start, size) in enumerate(BLOCKS):
            low = right[0, rows, :]
            gate = lax.dot_general(weights[pl.ds(start, size), :], low, NT, preferred_element_type=FULL)
            up = lax.dot_general(weights[pl.ds(hidden + start, size), :], low, NT, preferred_element_type=FULL)
            square = gate * gate
            bend = jnp.tanh(CORNER * gate * (1.0 + 0.044715 * square))
            share = 0.5 * (1.0 + bend)
            gelu = gate * share
            slope = share + 0.5 * gate * (1.0 - bend * bend) * (CORNER * (1.0 + 3.0 * 0.044715 * square))
            act = (gelu * up).astype(LOW)
            left[pl.ds(start, size), columns] = (up * slope).astype(LOW)
            left[pl.ds(hidden + start, size), columns] = gelu.astype(LOW)
            left[pl.ds(2 * hidden + start, size), columns] = act
            turned[:, start : start + size] = jnp.transpose(act)
            if n in hooks:
                hooks[n]()
        if r == 0:
            loads[5].wait()
        for third in thirds:
            part = jnp.dot(
                turned[:, :hidden], weights[pl.ds(2 * hidden, hidden), third], preferred_element_type=FULL
            )
            part_f[rows, third] = part.astype(LOW)

    def backward(r, hooks):
        rows, columns = rows_of(r), pl.ds(r * HALF, HALF)
        if r == 0:
            loads[6].wait()
        inverse, unit = unit_of(sum_f[rows, :].astype(FULL))
        mixed_ref[rows, :] = (resid_ref[rows, :] + unit * fgain_ref[...][None, :]).astype(LOW)
        grad = cot[rows, :].astype(FULL)
        grows[2, r : r + 1, :] = jnp.sum(unit * grad, axis=0, keepdims=True)
        right[1, rows, :] = norm_back(inverse, unit, fgain_ref[...][None, :] * grad).astype(LOW)
        for n, (start, size) in enumerate(BLOCKS):
            act_grad = lax.dot_general(
                weights[pl.ds(2 * hidden + start, size), :], right[1, rows, :], NT, preferred_element_type=FULL
            )
            for first, turn in ((start, turned), (hidden + start, turned_up)):
                span = pl.ds(first, size)
                grads = (act_grad * left[span, columns].astype(FULL)).astype(LOW)
                left[span, columns] = grads
                turn[:, start : start + size] = jnp.transpose(grads)
            if n in hooks:
                hooks[n]()
        for third in thirds:
            part = jnp.dot(turned[:, :hidden], weights[pl.ds(0, hidden), third], preferred_element_type=FULL)
            part = part + jnp.dot(
                turned_up[:, :hidden], weights[pl.ds(hidden, hidden), third], preferred_element_type=FULL
            )
            part_b[rows, third] = part.astype(LOW)

    own_head = pl.ds(pl.multiple_of(z * HD, HD), HD)

    def finish(r):
        rows = rows_of(r)
        grad = sum_b[rows, :].astype(FULL)
        inverse, unit = unit_of(resid_ref[rows, :])
        grows[1, r : r + 1, :] = jnp.sum(unit * grad, axis=0, keepdims=True)
        grad = cot[rows, :].astype(FULL) + norm_back(inverse, unit, pgain_ref[...][None, :] * grad)
        resid_ref[rows, :] = grad
        inverse, unit = unit_of(attn_out[rows, :])
        grows[0, r : r + 1, :] = jnp.sum(unit * grad, axis=0, keepdims=True)
        aol[rows, :] = norm_back(inverse, unit, again_ref[...][None, :] * grad).astype(LOW)
        grads = lax.dot_general(aol[rows, :], wout[own_head, :], NT, preferred_element_type=FULL).astype(LOW)
        mgrad_ref[rows, :] = grads
        products = grads.astype(FULL) * mix[rows, own_head].astype(FULL)
        delta = jnp.sum(jnp.transpose(products), axis=0, keepdims=True)
        number = lax.broadcasted_iota(jnp.int32, (8, HALF), 0)
        stat_ref[r] = jnp.where(number == 1, delta, lse_ref[r])

    sib_send, mine = weights.at[pl.ds(0, ROWS)], weights.at[pl.ds(ROWS, ROWS)]

    def product(core, n, target, added):
        first, size = CUTS[n], CUTS[n + 1] - CUTS[n]
        lhs = left[pl.ds(pl.multiple_of(ROWS * core + first, 16), size), :]
        which = jnp.where(n >= 2, core, 0)
        for third in thirds:
            tile = jnp.dot(lhs, right[which, :, third], preferred_element_type=FULL)
            if added is not None:
                tile = tile + added[pl.ds(first, size), third].astype(FULL)
            target[pl.ds(first, size), third] = tile.astype(LOW)

    def to_sibling(n):
        span = pl.ds(CUTS[n], CUTS[n + 1] - CUTS[n])
        return remote(sib_send.at[span], sib_recv.at[span], sib_s.at[n], sib_r.at[n], sibling)

    def side_ring(h, me, plus, minus):
        return RingReduce(
            lambda rel, half: rows_at(
                weights, ROWS + SIDE * h + PIECE * ((me + rel) % 4) + half * (PIECE // 2), PIECE // 2
            ),
            lambda half: pass_ab.at[h, half],
            lambda side, half: got_ab.at[h, side, half],
            plus, minus, sems, 8 + h,
        )

    rings = (side_ring(0, x, xp, xm), side_ring(1, y, yp, ym))
    outs = [
        pltpu.make_async_copy(src, dst, out_sem.at[n])
        for n, (src, dst) in enumerate(
            ((mixed_ref, mixed_hbm), (resid_ref, resid_hbm))
        )
    ]
    forward(0, {})
    sums[0][0].start()
    forward(1, {3: sums[0][0].relay})
    sums[1][0].start()
    sums[0][2]()
    sums[1][0].relay()
    sums[0][1].forward()
    sums[0][3]()
    sums[1][2]()
    backward(0, {2: sums[1][1].forward})
    sums[2][0].start()
    sums[1][3]()
    backward(1, {2: sums[2][0].relay, 4: sums[2][2]})
    sums[3][0].start()
    outs[0].start()
    count = len(CUTS) - 1

    def for_sibling(chunks):
        for n in chunks:
            product(1 - c, n, sib_send, None)
            to_sibling(n).start()

    def for_self(chunks):
        for n in chunks:
            to_sibling(n).wait_recv()
            product(c, n, mine, sib_recv)

    side_a, side_b = range(count // 2), range(count // 2, count)
    for_sibling(side_a)
    sums[2][1].forward()
    sums[3][0].relay()
    for_self(side_a)
    rings[0].start()
    sums[3][2]()
    for_sibling(side_b)
    sums[3][1].forward()
    for_self(side_b)
    rings[1].start()
    sums[2][3]()
    finish(0)
    rings[0].relay()
    sums[3][3]()
    finish(1)
    rest = jnp.dot(left[2 * ROWS :, :], right[1], preferred_element_type=FULL)
    early_ref[pl.ds(HD, 64), :] = rest.astype(LOW)
    outs[1].start()
    lhs = jnp.transpose(mix[:, own_head])
    for third in thirds:
        early_ref[0:HD, third] = jnp.dot(lhs, aol[:, third], preferred_element_type=FULL).astype(LOW)
    number = lax.broadcasted_iota(jnp.int32, (32, width), 0)
    gains = jnp.zeros((32, width), FULL)
    for n in range(3):
        gains = jnp.where(number == n, grows[n, 0:1, :] + grows[n, 1:2, :], gains)
    early_ref[pl.ds(HD + 64, 32), :] = gains.astype(LOW)
    rings[1].relay()
    for h, (ring, me, out) in enumerate(((rings[0], x, piece_a_ref), (rings[1], y, piece_b_ref))):
        ring.finish()
        for half in range(2):
            size = PIECE // 2
            own = rows_at(weights, ROWS + SIDE * h + PIECE * me + half * size, size)[...]
            out[pl.ds(half * size, size), :] = (own.astype(FULL) + ring.arrived(half)).astype(LOW)
    for out in outs:
        out.wait()
    for reduce, gather, _, _ in sums:
        reduce.drain()
        gather.drain()
    for ring in rings:
        ring.drain()
    for n in range(count):
        to_sibling(n).wait_send()


def middle(again, pgain, fgain, lse, mix, wout, tokens, cot, gate_t, up_t, down):
    rows, width = tokens.shape
    hidden = gate_t.shape[0]
    stacked = 3 * hidden
    return pl.pallas_call(
        middle_kernel,
        name="middle",
        out_shape=[
            shape(LOW, rows, HD),
            shape(FULL, 2, 8, HALF),
            shape(LOW, HD + 96, width),
            shape(LOW, PIECE, width),
            shape(LOW, PIECE, width),
            shape(LOW, rows, width),
            shape(FULL, rows, width),
        ],
        in_specs=[VMEM] * 4 + [ANY] * 7,
        out_specs=[VMEM] * 5 + [ANY] * 2,
        scratch_shapes=[
            vmem(LOW, rows, width),
            vmem(FULL, rows, width),
            vmem(LOW, stacked, width),
            vmem(LOW, 4 * HD, width),
            vmem(LOW, rows, 4 * HD),
            vmem(LOW, rows, width),
            vmem(LOW, rows, width),
            vmem(FULL, rows, width),
            vmem(LOW, stacked, rows),
            vmem(LOW, 2, rows, width),
            vmem(LOW, HALF, 1792),
            vmem(LOW, HALF, 1792),
            vmem(LOW, rows, width),
            *[vmem(LOW, rows, width)] * 4,
            vmem(LOW, 4, 2, HALF // 8, width),
            vmem(LOW, 4, 2, 2, HALF // 8, width),
            vmem(LOW, ROWS, width),
            vmem(LOW, 2, 2, PIECE // 2, width),
            vmem(LOW, 2, 2, 2, PIECE // 2, width),
            vmem(FULL, 3, 8, width),
            dma(7), dma(6), dma(6), dma(10, 6), dma(10, 6), dma(2),
        ],
        compiler_params=params(4, 60),
        cost_estimate=cost(20),
    )(again, pgain, fgain, lse, mix, wout, tokens, cot, gate_t, up_t, down)


LATE = 112
EARLY = 176
KEEPERS = 11


def attn_backward(
    starts_ref, do_ref, stat_ref, piece_a_ref, piece_b_ref, qgain_ref, kgain_ref, igain_ref, early_ref,
    q_hbm, k_hbm, v_hbm, raw_hbm, kraw_hbm, cos_hbm, sin_hbm, wk_hbm, wv_hbm, normed_hbm, wq_hbm, tokens_hbm, resid_hbm,
    late_ref, esum_ref, tgrad_ref, dgain_ref, big_ref,
    dog, statg, dqacc, dkall, dvall, ktall, sibsend, sibrecv, kvsrc, kvpass, kvgot,
    dqsend, dqpass, dqgot, dqback, dqhigh, zpart, zpass, zgot, own_sum, gaing, winpass, wingot, full_a, full_b,
    draw_ref, dkv_ref, dkraw, dvrow, part, core_recv, half_sum, plane_recv, grow, grecv,
    e_core, e_half, e_plane,
    q_in, k_in, v_in, raw_ref, kraw_ref, cos_ref, sin_ref, wk_ref, wv_ref, normed_t, wq_ref, tok_ref,
    rs, rr, st_s, st_r, sw_s, sw_r, sib_s, sib_r, gn_s, gn_r, sf_s, sf_r, own_sem,
    load_sem, c_s, c_r, p_s, p_r, g_s, g_r, f_s, f_r, i_s, i_r,
    ep_s, ep_r, eg_s, eg_r, ef_s, ef_r,
):
    x, y, c, z = place()
    xp, xm, yp, ym = at(x + 1, y, c, z), at(x + 3, y, c, z), at(x, y + 1, c, z), at(x, y + 3, c, z)
    zp, zm, y2, z2 = at(x, y, c, z + 1), at(x, y, c, z + 3), at(x, y + 2, c, z), at(x, y, c, z + 2)
    sibling, partner = at(x, y, 1 - c, z), at(3 - x, y, c, z)
    shifts = [(a, b) for a in range(4) for b in range(4) if (a, b) != (0, 0)]
    plane = [at(x + a, y + b, c, z) for a, b in shifts]
    loads = [
        pltpu.make_async_copy(src, dst, load_sem.at[n])
        for n, (src, dst) in enumerate(
            (
                (q_hbm, q_in), (k_hbm, k_in), (v_hbm, v_in), (raw_hbm, raw_ref), (kraw_hbm, kraw_ref),
                (cos_hbm, cos_ref), (sin_hbm, sin_ref), (wk_hbm, wk_ref), (wv_hbm, wv_ref),
                (normed_hbm, normed_t), (wq_hbm, wq_ref.at[:, pl.ds(pl.multiple_of(z * HD, HD), HD)]), (tokens_hbm, tok_ref), (resid_hbm, tgrad_ref),
            )
        )
    ]
    for load in loads:
        load.start()
    greet(plane + [sibling, zp, zm, z2])
    copies = []

    def go(copy):
        copy.start()
        copies.append(copy)

    sems = (rs, rr)
    do_low, do_high = do_ref.at[pl.ds(0, HALF)], do_ref.at[pl.ds(HALF, HALF)]
    swaps = (
        remote(do_high, dog.at[2 * y + 1], sw_s.at[0], sw_r.at[0], partner),
        remote(stat_ref.at[1], statg.at[2 * y + 1], sw_s.at[1], sw_r.at[1], partner),
    )
    for copy in swaps:
        go(copy)
    dos = RingGather(
        lambda index, half: dog.at[2 * index + half], y, yp, ym, sems, 0,
        lambda half: do_low if half == 0 else dog.at[2 * y + 1],
    )
    dos.own(0)
    tall = wq_hbm.shape[0] // 2

    def wq_view(index, half):
        return wq_ref.at[pl.ds(half * tall, tall), pl.ds(pl.multiple_of(index * HD, HD), HD)]

    wqs = RingGather(
        wq_view, z, zp, zm, sems, 12, lambda half: wq_hbm.at[pl.ds(half * tall, tall)]
    )
    wqs.whole()
    chip = x * 4 + y
    e_cross = remote(rows_at(early_ref, EARLY * (1 - c), EARLY), e_core, c_s.at[1], c_r.at[1], sibling)
    go(e_cross)

    def early_part(owner):
        return remote(
            rows_at(e_half, 16 * owner, 16), e_plane.at[chip], ep_s.at[owner], ep_r.at[chip],
            at(owner // 4, owner % 4, c, z),
        )

    def early_spread():
        e_cross.wait_recv()
        own = early_ref[pl.ds(pl.multiple_of(EARLY * c, 16), EARLY), :]
        e_half[...] = (own.astype(FULL) + e_core[...].astype(FULL)).astype(LOW)
        for owner in range(KEEPERS):
            pl.when(chip != owner)(early_part(owner).start)

    def early_piece(core, owner):
        return rows_at(esum_ref, EARLY * core + 16 * owner, 16)

    def early_out(n):
        return remote(early_piece(c, chip), early_piece(c, chip), eg_s.at[n], eg_r.at[chip], plane[n])

    def early_across(owner):
        block = early_piece(c, owner)
        return remote(block, block, ef_s.at[owner], ef_r.at[owner], sibling)

    def early_summed():
        @pl.when(chip < KEEPERS)
        def _():
            total = rows_at(e_half, 16 * chip, 16)[...].astype(FULL)
            for a, b in shifts:
                source = ((x + a) % 4) * 4 + (y + b) % 4
                block = rows_at(e_half, 0, 16)
                remote(block, e_plane.at[source], ep_s.at[0], ep_r.at[source], sibling).wait_recv()
                total = total + e_plane[source].astype(FULL)
            early_piece(c, chip)[...] = total.astype(LOW)
            for n in range(15):
                early_out(n).start()
            early_across(chip).start()

    def early_passed():
        for owner in range(KEEPERS):

            @pl.when(chip != owner)
            def _():
                block = early_piece(c, owner)
                remote(rows_at(e_half, 0, 16), block, eg_s.at[0], eg_r.at[owner], sibling).wait_recv()
                early_across(owner).start()

    def early_done():
        for owner in range(KEEPERS):
            block = early_piece(1 - c, owner)
            remote(rows_at(e_half, 0, 16), block, ef_s.at[0], ef_r.at[owner], sibling).wait_recv()
            early_across(owner).wait_send()
            pl.when(chip != owner)(early_part(owner).wait_send)

        @pl.when(chip < KEEPERS)
        def _():
            for n in range(15):
                early_out(n).wait_send()

    def stats_to(upper, rel, peer):
        slot = 2 * y + upper
        source = statg.at[slot] if upper else stat_ref.at[0]
        return remote(source, statg.at[slot], st_s.at[upper, rel - 1], st_r.at[slot], peer)

    y_peers = ((1, yp), (3, ym), (2, y2))
    for rel, peer in y_peers:
        go(stats_to(0, rel, peer))

    cut = (48, WINDOW - 48)

    def window(ref, index, half):
        return rows_at(ref, WINDOW * index + 48 * half, cut[half])

    sides = ((piece_a_ref, full_a, y, yp, ym), (piece_b_ref, full_b, x, xp, xm))
    reduces, gathers = [], []
    for h, (piece, full, me, plus, minus) in enumerate(sides):
        reduces.append(
            RingReduce(
                lambda rel, half, piece=piece, me=me: window(piece, (me + rel) % 4, half),
                lambda half, h=h: winpass.at[h, pl.ds(48 * half, cut[half])],
                lambda side, half, h=h: wingot.at[h, side, pl.ds(48 * half, cut[half])],
                plus, minus, sems, 1 + h,
            )
        )
        gathers.append(
            RingGather(lambda index, half, full=full: window(full, index, half), me, plus, minus, sems, 3 + h)
        )
        reduces[h].start()

    def big_view(core, h, index, half):
        return rows_at(big_ref, ROWS * core + SIDE * h + PIECE * index + half * (PIECE // 2), PIECE // 2)

    owners = ((x, xp, xm), (y, yp, ym))
    pieces = [
        RingGather(
            lambda index, half, h=h: big_view(c, h, index, half), me, plus, minus, sems, 5 + h,
            lambda half, h=h: sides[h][1].at[pl.ds(half * (PIECE // 2), PIECE // 2)],
        )
        for h, (me, plus, minus) in enumerate(owners)
    ]

    def piece_to_sibling(h, index, half, source=None):
        block = big_view(c, h, index, half)
        return remote(block if source is None else source, block, sf_s.at[h, index, half], sf_r.at[h, index, half], sibling)

    def keep(h, half):
        source = sides[h][1].at[pl.ds(half * (PIECE // 2), PIECE // 2)]
        return pltpu.make_async_copy(source, big_view(c, h, owners[h][0], half), own_sem.at[h, half])

    def window_summed(h):
        ring, gather = reduces[h], gathers[h]
        piece, full, me, _, _ = sides[h]
        ring.finish()
        for half in range(2):
            total = window(piece, me, half)[...].astype(FULL) + ring.arrived(half)
            window(full, me, half)[...] = total.astype(LOW)
        gather.whole()

    def window_gathered(h):
        gathers[h].near()
        gathers[h].far()

    def pieces_sent(h):
        pieces[h].whole()
        for half in range(2):
            source = sides[h][1].at[pl.ds(half * (PIECE // 2), PIECE // 2)]
            go(piece_to_sibling(h, owners[h][0], half, source))
            keep(h, half).start()

    def pieces_near(h):
        pieces[h].near()
        for rel in (1, 3):
            for half in range(2):
                go(piece_to_sibling(h, (owners[h][0] + rel) % 4, half))

    def pieces_far(h):
        pieces[h].far()
        for half in range(2):
            go(piece_to_sibling(h, (owners[h][0] + 2) % 4, half))

    def tile(i, first_q, slot, first_k, masked):
        queries, out_grads = q_in[i], dog[i]
        lse, delta = statg[i, 0:1, :], statg[i, 1:2, :]
        if masked:
            token = first_q + lax.broadcasted_iota(jnp.int32, (1, HALF), 1)
            begin = begin_of(token, starts_ref)
        dq_part = None
        for n in range(2):
            rows = pl.ds(n * 256, 256)
            keys, values = k_in[slot, rows], v_in[slot, rows]
            scores = lax.dot_general(keys, queries, NT, preferred_element_type=FULL)
            prob_grad = lax.dot_general(values, out_grads, NT, preferred_element_type=FULL)
            soft = jnp.exp(scores - lse)
            if masked:
                key_index = first_k + n * 256 + lax.broadcasted_iota(jnp.int32, (256, 1), 0)
                soft = jnp.where((key_index <= token) & (key_index >= begin), soft, 0.0)
            score_grad = (soft * (prob_grad - delta)).astype(LOW)
            dvall[slot, rows, :] += jnp.dot(soft.astype(LOW), out_grads, preferred_element_type=FULL)
            dkall[slot, rows, :] += jnp.dot(score_grad, queries, preferred_element_type=FULL)
            part = jnp.dot(ktall[slot, :, n * 256 : (n + 1) * 256], score_grad, preferred_element_type=FULL)
            dq_part = part if dq_part is None else dq_part + part
        dqacc[i] = dqacc[i] + dq_part

    def visit(i, slot):
        first_q = tile_first(i, x, c)
        first_k = 4096 * (slot // 2) + 1024 * y + BLK * (slot % 2)
        some = first_k <= first_q + (HALF - 1)
        full = (first_k + BLK - 1 <= first_q) & (first_k > 0) & (first_q < 31 * BLK)

        @pl.when(full)
        def _():
            tile(i, first_q, slot, first_k, False)

        @pl.when(some & jnp.logical_not(full))
        def _():
            tile(i, first_q, slot, first_k, True)

    def own_tile(upper):
        def one(slot, carry):
            visit(2 * y + upper, slot)
            return carry

        lax.fori_loop(0, 8, one, 0)

    dog[2 * y] = do_ref[0:HALF, :]
    statg[2 * y] = stat_ref[0]
    dqacc[...] = jnp.zeros_like(dqacc)
    dkall[...] = jnp.zeros_like(dkall)
    dvall[...] = jnp.zeros_like(dvall)
    for load in loads[:3]:
        load.wait()

    def turn_keys(slot, carry):
        ktall[slot] = jnp.transpose(k_in[slot])
        return carry

    lax.fori_loop(0, 8, turn_keys, 0)
    for copy in swaps:
        copy.wait_recv()
    dos.own(1)
    for rel, peer in y_peers:
        go(stats_to(1, rel, peer))
    own_tile(0)
    dos.forward()
    for ring in reduces:
        ring.relay()
    own_tile(1)
    dos.near()
    dos.far()
    for upper in range(2):
        for rel, peer in y_peers:
            slot = 2 * ((y + rel) % 4) + upper
            remote(stat_ref.at[0], statg.at[slot], st_s.at[0, 0], st_r.at[slot], sibling).wait_recv()

    window_summed(0)
    window_summed(1)

    zrows = BLK // 4
    place_of = {2: 0, 1: 1, 3: 2, 0: 3}
    kvs = RingReduce(
        lambda rel, half: kvsrc.at[place_of[rel], half],
        lambda half: kvpass.at[half],
        lambda side, half: kvgot.at[side, half],
        xp, xm, sems, 7,
    )
    zrings = [
        RingReduce(
            lambda rel, half, step=step: zpart.at[step, (z + rel) % 4, half],
            lambda half, step=step: zpass.at[step, half],
            lambda side, half, step=step: zgot.at[step, side, half],
            zp, zm, sems, number,
        )
        for step, number in enumerate((9, 13, 14, 15))
    ]

    def cores_summed(step, rel):
        slot = ((x + rel) % 4) * 2 + c
        remote(sibsend.at[step], sibrecv.at[step], sib_s.at[step], sib_r.at[step], sibling).wait_recv()
        for half, ref in enumerate((dkall, dvall)):
            for n in range(4):
                rows = pl.ds(n * zrows, zrows)
                both = ref[slot, rows, :] + sibrecv[step, half, rows, :].astype(FULL)
                zpart[step, n, half] = both.astype(LOW)
        zrings[step].start()

    def heads_summed(step):
        zrings[step].finish()
        for half in range(2):
            total = zpart[step, z, half].astype(FULL) + zrings[step].arrived(half)
            if step == 3:
                own_sum[half] = total
            else:
                kvsrc[step, half] = total.astype(LOW)
        if step < 3:
            kvs.start(*((0, 1), (3,), (2,))[step])

    def pieces_start():
        for h in range(2):
            window_gathered(h)
            pieces_sent(h)

    def each_side(method):
        for h in range(2):
            method(h)

    between = {
        (0, 0): (early_spread,),
        (0, 1): (gathers[0].forward, gathers[1].forward),
        (1, 0): (pieces_start,),
        (1, 1): (lambda: cores_summed(0, 2),),
        (2, 0): (zrings[0].relay, early_summed, wqs.forward),
        (2, 1): (lambda: cores_summed(1, 1), lambda: heads_summed(0), pieces[0].forward, pieces[1].forward),
        (3, 0): (zrings[1].relay, wqs.near, wqs.far),
        (3, 1): (lambda: cores_summed(2, 3), lambda: heads_summed(1), lambda: each_side(pieces_near)),
    }
    for step, rel in enumerate((2, 1, 3, 0)):
        pair = (x + rel) % 4
        for turn in range(2):
            if (step, turn) in between:
                for hook in between[step, turn]:
                    hook()
            cc = 1 - c if turn == 0 else c
            slot = pair * 2 + cc

            def one(n, carry):
                visit((2 * y + 2 + n) % 8, slot)
                return carry

            lax.fori_loop(0, 6, one, 0)
            if turn == 0:
                sibsend[step, 0] = dkall[slot].astype(LOW)
                sibsend[step, 1] = dvall[slot].astype(LOW)
                go(remote(sibsend.at[step], sibrecv.at[step], sib_s.at[step], sib_r.at[step], sibling))

    zrings[2].relay()
    cores_summed(3, 0)
    zg = RingGather(lambda index, half: dkv_ref.at[index, half], z, zp, zm, sems, 10)

    def cast(i, carry):
        dqsend[i] = jnp.transpose(dqacc[i]).astype(LOW)
        return carry

    lax.fori_loop(0, 8, cast, 0)
    dqs = RingReduce(
        lambda rel, half: dqsend.at[2 * ((y + rel) % 4) + half],
        lambda half: dqpass.at[half],
        lambda side, half: dqgot.at[side, half],
        yp, ym, sems, 8,
    )
    dqs.start()
    heads_summed(2)
    zrings[3].relay()
    kvs.relay()
    dqs.relay()
    heads_summed(3)
    kvs.finish()
    for half in range(2):
        dkv_ref[z, half] = (own_sum[half] + kvs.arrived(half)).astype(LOW)
    zg.whole()
    early_passed()
    each_side(pieces_far)
    for load in loads[3:]:
        load.wait()
    dqs.finish()
    back = remote(dqback, dqhigh, sw_s.at[2], sw_r.at[2], partner)
    dqback[...] = (dqsend[2 * y + 1].astype(FULL) + dqs.arrived(1)).astype(LOW)
    go(back)

    draws = RingGather(
        lambda index, half: draw_ref.at[pl.ds(half * HALF, HALF), pl.ds(pl.multiple_of(index * HD, HD), HD)],
        z, zp, zm, sems, 11,
    )

    def unrotated(grad, raw, gain, rows):
        cosine, sine = cos_ref[rows, :], sin_ref[rows, :]
        first, second = grad[:, : HD // 2], grad[:, HD // 2 :]
        turned = jnp.concatenate([first * cosine + second * sine, second * cosine - first * sine], axis=1)
        inverse = lax.rsqrt(jnp.mean(raw * raw, axis=1, keepdims=True) + EPS)
        unit = raw * inverse
        scaled = gain * turned
        raw_grad = inverse * (scaled - unit * jnp.mean(unit * scaled, axis=1, keepdims=True))
        return raw_grad.astype(LOW), jnp.sum(unit * turned, axis=0, keepdims=True)

    gain_grad = None
    for half in range(2):
        if half == 0:
            grad = dqsend[2 * y].astype(FULL) + dqs.arrived(0)
        else:
            back.wait_recv()
            grad = dqhigh[...].astype(FULL)
        rows = pl.ds(half * HALF, HALF)
        raw_grad, piece = unrotated(grad * (HD**-0.5), raw_ref[rows, :], qgain_ref[...][None, :], rows)
        draw_ref[rows, pl.ds(pl.multiple_of(z * HD, HD), HD)] = raw_grad
        draws.own(half)
        gain_grad = piece if gain_grad is None else gain_grad + piece
    gaing[z] = jnp.broadcast_to(gain_grad, (8, HD))
    for n, peer in enumerate((zp, zm, z2)):
        go(remote(gaing.at[z], gaing.at[z], gn_s.at[n], gn_r.at[z], peer))

    chunk_rows = normed_t.shape[0] // 4

    def weight_grad(m, rhs):
        def block(r, carry):
            lhs = normed_t[pl.ds(pl.multiple_of(r * chunk_rows, 16), chunk_rows), :]
            tile = jnp.dot(lhs, rhs[...], preferred_element_type=FULL).astype(LOW)
            part[pl.ds(pl.multiple_of((4 * m + r) * chunk_rows, 16), chunk_rows), :] = tile
            return carry

        lax.fori_loop(0, 4, block, 0)

    zg.forward()
    weight_grad(0, draw_ref.at[:, pl.ds(pl.multiple_of(z * HD, HD), HD)])
    draws.forward()
    zg.near()
    zg.far()
    key_gain_grad = None
    for n in range(4):
        rows = pl.ds(n * zrows, zrows)
        raw_grad, piece = unrotated(dkv_ref[n, 0].astype(FULL), kraw_ref[rows, :], kgain_ref[...][None, :], rows)
        dkraw[rows, :] = raw_grad
        dvrow[rows, :] = dkv_ref[n, 1]
        key_gain_grad = piece if key_gain_grad is None else key_gain_grad + piece
    for rel in (1, 3, 2):
        other = (z + rel) % 4
        remote(gaing.at[z], gaing.at[other], gn_s.at[0], gn_r.at[other], sibling).wait_recv()
    query_gain_grad = sum(gaing[n, 0:1, :] for n in range(4))
    number = lax.broadcasted_iota(jnp.int32, (16, HD), 0)
    both = jnp.where(number == 0, query_gain_grad, jnp.where(number == 1, key_gain_grad, 0.0))
    part[pl.ds(12 * chunk_rows, 16), :] = both.astype(LOW)
    part[pl.ds(12 * chunk_rows + 16, LATE), :] = jnp.zeros((LATE, HD), LOW)
    weight_grad(1, dkraw)
    weight_grad(2, dvrow)

    side = 16 * LATE

    def late_piece(ref, core, owner):
        return rows_at(ref, side * core + LATE * owner, LATE)

    cross = remote(rows_at(part, side * (1 - c), side), core_recv, c_s.at[0], c_r.at[0], sibling)
    go(cross)
    cross.wait_recv()

    def add(r, carry):
        both = part[pl.ds(pl.multiple_of(side * c + 2 * LATE * r, 16), 2 * LATE), :].astype(FULL)
        rows = pl.ds(pl.multiple_of(2 * LATE * r, 16), 2 * LATE)
        half_sum[rows, :] = (both + core_recv[rows, :].astype(FULL)).astype(LOW)
        return carry

    lax.fori_loop(0, 8, add, 0)
    for n, (a, b) in enumerate(shifts):
        target = ((x + a) % 4) * 4 + (y + b) % 4
        go(remote(late_piece(half_sum, 0, target), plane_recv.at[chip], p_s.at[n], p_r.at[chip], plane[n]))

    draws.near()
    draws.far()
    gain_row = None
    for half in range(2):
        rows = pl.ds(half * HALF, HALF)
        grad = lax.dot_general(draw_ref[rows, :], wq_ref[...], NT, preferred_element_type=FULL)
        grad = grad + lax.dot_general(dkraw[rows, :], wk_ref[...], NT, preferred_element_type=FULL)
        grad = grad + lax.dot_general(dvrow[rows, :], wv_ref[...], NT, preferred_element_type=FULL)
        value = tok_ref[rows, :].astype(FULL)
        inverse = lax.rsqrt(jnp.mean(value * value, axis=1, keepdims=True) + EPS)
        unit = value * inverse
        scaled = igain_ref[...][None, :] * grad
        back_grad = inverse * (scaled - unit * jnp.mean(unit * scaled, axis=1, keepdims=True))
        tgrad_ref[rows, :] = tgrad_ref[rows, :] + back_grad
        piece = jnp.sum(unit * grad, axis=0, keepdims=True)
        gain_row = piece if gain_row is None else gain_row + piece
    grow[0] = jnp.broadcast_to(gain_row, grow.shape[1:])
    to_core = remote(grow.at[0], grow.at[1], i_s.at[15], i_r.at[16], sibling)
    go(to_core)

    total = late_piece(half_sum, 0, chip)[...].astype(FULL)
    for a, b in shifts:
        source = ((x + a) % 4) * 4 + (y + b) % 4
        remote(late_piece(half_sum, 0, 0), plane_recv.at[source], p_s.at[0], p_r.at[source], sibling).wait_recv()
        total = total + plane_recv[source].astype(FULL)

    def piece_of(owner):
        return late_piece(late_ref, c, owner)

    piece_of(chip)[...] = total.astype(LOW)
    for n in range(15):
        go(remote(piece_of(chip), piece_of(chip), g_s.at[n], g_r.at[chip], plane[n]))
    go(remote(piece_of(chip), piece_of(chip), f_s.at[chip], f_r.at[chip], sibling))
    to_core.wait_recv()
    grecv[chip] = grow[0] + grow[1]
    for n in range(15):
        go(remote(grecv.at[chip], grecv.at[chip], i_s.at[n], i_r.at[chip], plane[n]))
    for a, b in shifts:
        source = ((x + a) % 4) * 4 + (y + b) % 4
        remote(late_piece(half_sum, 0, 0), piece_of(source), g_s.at[0], g_r.at[source], sibling).wait_recv()
        go(remote(piece_of(source), piece_of(source), f_s.at[source], f_r.at[source], sibling))
    for a, b in shifts:
        source = ((x + a) % 4) * 4 + (y + b) % 4
        remote(grecv.at[chip], grecv.at[source], i_s.at[0], i_r.at[source], sibling).wait_recv()
    dgain_ref[...] = sum(grecv[n] for n in range(16))
    for n in range(16):
        theirs = late_piece(late_ref, 1 - c, n)
        remote(late_piece(half_sum, 0, 0), theirs, f_s.at[0], f_r.at[n], sibling).wait_recv()
    early_done()
    for h in range(2):
        for half in range(2):
            keep(h, half).wait()
            for n in range(4):
                piece_to_sibling(h, n, half).wait_recv()
    for ring in [dos, kvs, dqs, zg, draws, wqs] + zrings + reduces + gathers + pieces:
        ring.drain()
    for copy in copies:
        copy.wait_send()


def backward_attention(doc_starts, *operands):
    width = operands[2].shape[1]
    streamed = operands[8:]
    return pl.pallas_call(
        attn_backward,
        name="attn_backward",
        out_shape=[
            shape(LOW, 32 * LATE, HD),
            shape(LOW, 2 * EARLY, width),
            shape(FULL, BLK, width),
            shape(FULL, 8, width),
            shape(LOW, 2 * ROWS + 64, width),
        ],
        in_specs=[SMEM] + [VMEM] * 8 + [ANY] * 13,
        out_specs=[VMEM] * 4 + [ANY],
        scratch_shapes=[
            vmem(LOW, 8, HALF, HD),
            vmem(FULL, 8, 8, HALF),
            vmem(FULL, 8, HD, HALF),
            vmem(FULL, 8, BLK, HD),
            vmem(FULL, 8, BLK, HD),
            vmem(LOW, 8, HD, BLK),
            vmem(LOW, 4, 2, BLK, HD),
            vmem(LOW, 4, 2, BLK, HD),
            vmem(LOW, 3, 2, BLK // 4, HD),
            vmem(LOW, 2, BLK // 4, HD),
            vmem(LOW, 2, 2, BLK // 4, HD),
            vmem(LOW, 8, HALF, HD),
            vmem(LOW, 2, HALF, HD),
            vmem(LOW, 2, 2, HALF, HD),
            vmem(LOW, HALF, HD),
            vmem(LOW, HALF, HD),
            vmem(LOW, 4, 4, 2, BLK // 4, HD),
            vmem(LOW, 4, 2, BLK // 4, HD),
            vmem(LOW, 4, 2, 2, BLK // 4, HD),
            vmem(FULL, 2, BLK // 4, HD),
            vmem(FULL, 4, 8, HD),
            vmem(LOW, 2, WINDOW, width),
            vmem(LOW, 2, 2, WINDOW, width),
            vmem(LOW, PIECE, width),
            vmem(LOW, PIECE, width),
            vmem(LOW, BLK, 4 * HD),
            vmem(LOW, 4, 2, BLK // 4, HD),
            vmem(LOW, BLK, HD),
            vmem(LOW, BLK, HD),
            vmem(LOW, 32 * LATE, HD),
            vmem(LOW, 16 * LATE, HD),
            vmem(LOW, 16 * LATE, HD),
            vmem(LOW, 16, LATE, HD),
            vmem(FULL, 2, 8, width),
            vmem(FULL, 16, 8, width),
            vmem(LOW, EARLY, width),
            vmem(LOW, EARLY, width),
            vmem(LOW, 16, 16, width),
            *[vmem(operand.dtype, *operand.shape) for operand in streamed[:10]],
            vmem(LOW, width, 4 * HD),
            vmem(LOW, *streamed[11].shape),
            dma(16, 6), dma(16, 6), dma(2, 3), dma(8), dma(3), dma(3), dma(4), dma(4), dma(3), dma(4),
            dma(2, 4, 2), dma(2, 4, 2), dma(2, 2),
            dma(13), dma(2), dma(2), dma(15), dma(16), dma(15), dma(16), dma(16), dma(16), dma(16), dma(17),
            dma(KEEPERS), dma(16), dma(15), dma(16), dma(KEEPERS), dma(KEEPERS),
        ],
        compiler_params=params(2, 60),
        cost_estimate=cost(15),
    )(doc_starts, *operands)


def per_device(
    tokens,
    cotangent,
    doc_starts,
    query_weight,
    key_weight,
    value_weight,
    out_weight,
    gate_weight,
    up_weight,
    down_weight,
    input_gain,
    attn_gain,
    prenorm_gain,
    post_gain,
    query_gain,
    key_gain,
):
    row_count = tokens.shape[0]
    first_row = lax.axis_index("seq") * row_count
    own_index = first_row + jnp.arange(row_count, dtype=jnp.int32)
    own_position = doc_layout(doc_starts, own_index)[1]
    cos_table, sine_table = rope_tables(own_position, HD)
    query_scale = HD ** (-0.5)
    inputs = tokens.astype(jnp.float32)
    normed = rms_norm(inputs, input_gain)
    normed_low = normed.astype(jnp.bfloat16)
    query_raw = jnp.dot(normed_low, query_weight, preferred_element_type=jnp.float32)
    key_raw = jnp.dot(normed_low, key_weight, preferred_element_type=jnp.float32)
    value_low = jnp.dot(normed_low, value_weight, preferred_element_type=jnp.float32).astype(
        jnp.bfloat16
    )

    def query_piece(source, scaling):
        return rotate(rms_norm(source, scaling), cos_table, sine_table) * query_scale

    def key_piece(source, scaling):
        return rotate(rms_norm(source, scaling), cos_table, sine_table)

    query_rows = query_piece(query_raw, query_gain)
    query_low = query_rows.astype(jnp.bfloat16)
    key_rows = key_piece(key_raw, key_gain)
    key_low = key_rows.astype(jnp.bfloat16)
    mix_all, lse_rows, q_all, k_all, v_all, out_weight_all = forward_attention(
        doc_starts, query_low, key_low, value_low, out_weight
    )
    width = tokens.shape[1]
    mix_grad, stats, early, piece_a, piece_b, mixed, resid = middle(
        attn_gain,
        prenorm_gain,
        post_gain,
        lse_rows,
        mix_all,
        out_weight_all,
        tokens,
        cotangent,
        jnp.transpose(gate_weight),
        jnp.transpose(up_weight),
        down_weight,
    )
    late, early, tokens_grad, input_gain_rows, big = backward_attention(
        doc_starts,
        mix_grad,
        stats,
        piece_a,
        piece_b,
        query_gain,
        key_gain,
        input_gain,
        early,
        q_all,
        k_all,
        v_all,
        query_raw,
        key_raw,
        cos_table,
        sine_table,
        key_weight,
        value_weight,
        jnp.transpose(normed_low),
        query_weight,
        tokens,
        resid,
    )
    input_gain_grad = input_gain_rows[0]
    query_weight_grad = late[:width].astype(jnp.float32)
    key_weight_grad = late[width : 2 * width].astype(jnp.float32)
    value_weight_grad = late[2 * width : 3 * width].astype(jnp.float32)
    query_gain_grad = late[3 * width].astype(jnp.float32)
    key_gain_grad = late[3 * width + 1].astype(jnp.float32)
    out_weight_grad = early[:HD].astype(jnp.float32)
    rest = early[HD : HD + 64]
    gains = early[HD + 64 : HD + 67].astype(jnp.float32)
    attn_gain_grad, prenorm_gain_grad, post_gain_grad = gains[0], gains[1], gains[2]
    hidden = gate_weight.shape[1]
    gate_weight_grad = jnp.transpose(big[:hidden].astype(jnp.float32))
    up_weight_grad = jnp.transpose(big[hidden : 2 * hidden].astype(jnp.float32))
    down_weight_grad = big[2 * hidden :].astype(jnp.float32)
    down_weight_grad = lax.dynamic_update_slice(
        down_weight_grad, rest.astype(jnp.float32), (hidden - rest.shape[0], 0)
    )
    return (
        mixed,
        tokens_grad,
        query_weight_grad,
        key_weight_grad,
        value_weight_grad,
        out_weight_grad,
        gate_weight_grad,
        up_weight_grad,
        down_weight_grad,
        input_gain_grad,
        attn_gain_grad,
        prenorm_gain_grad,
        post_gain_grad,
        query_gain_grad,
        key_gain_grad,
    )


def solution(mesh):
    placed = (
        P("seq", None),
        P("seq", None),
        P(),
        P(None, "head"),
        P(),
        P(),
        P("head", None),
        P(None, "head"),
        P(None, "head"),
        P("head", None),
        P(),
        P(),
        P(),
        P(),
        P(),
        P(),
    )
    return jax.shard_map(
        per_device,
        mesh=mesh,
        in_specs=placed,
        out_specs=(
            P("seq", None),
            P("seq", None),
            P(None, "head"),
            P(),
            P(),
            P("head", None),
            P(None, "head"),
            P(None, "head"),
            P("head", None),
            P(),
            P(),
            P(),
            P(),
            P(),
            P(),
        ),
        check_vma=False,
    )
```

```python
import functools
import math

import jax
import jax.numpy as jnp
from jax import lax
from jax.experimental import pallas as pl
from jax.experimental.pallas import tpu as pltpu
from jax.sharding import PartitionSpec as P

HD = 256


EPS = 1e-06
THETA = 1000000.0
NEG = -1e30


def rms_norm(values, scaling):
    return values * lax.rsqrt(jnp.mean(values * values, axis=-1, keepdims=True) + EPS) * scaling


def doc_layout(doc_starts, token_index):
    before = doc_starts[None, :] <= token_index[:, None]
    segment = jnp.sum(before.astype(jnp.int32), axis=1)
    doc_begin = jnp.max(jnp.where(before, doc_starts[None, :], 0), axis=1)
    return (segment, token_index - doc_begin)


def rope_tables(position, head_width):
    half_width = head_width // 2
    inverse = jnp.exp(
        -math.log(THETA) * 2.0 * jnp.arange(half_width, dtype=jnp.float32) / head_width
    )
    angles = position.astype(jnp.float32)[:, None] * inverse[None, :]
    return (jnp.cos(angles), jnp.sin(angles))


def rotate(values, cos_table, sine_table):
    half_width = values.shape[-1] // 2
    first, second = values[..., :half_width], values[..., half_width:]
    return jnp.concatenate(
        [first * cos_table - second * sine_table, second * cos_table + first * sine_table], axis=-1
    )


MESH_ID = pl.DeviceIdType.MESH
HALF = 256
BLK = 512
LOW = jnp.bfloat16
FULL = jnp.float32
NT = (((1,), (1,)), ((), ()))


def place():
    s = lax.axis_index("seq")
    return s // 8, (s // 2) % 4, s % 2, lax.axis_index("head")


def at(x, y, c, z):
    return ((x % 4) * 8 + (y % 4) * 2 + c, z % 4)


def greet(peers):
    barrier = pltpu.get_barrier_semaphore()
    for peer in peers:
        pl.semaphore_signal(barrier, inc=1, device_id=peer, device_id_type=MESH_ID)
    pl.semaphore_wait(barrier, len(peers))


def remote(src, dst, send_sem, recv_sem, peer):
    return pltpu.make_async_remote_copy(
        src_ref=src,
        dst_ref=dst,
        send_sem=send_sem,
        recv_sem=recv_sem,
        device_id=peer,
        device_id_type=MESH_ID,
    )


def rows_at(ref, start, size):
    return ref.at[pl.ds(pl.multiple_of(start, 16), size)]


class RingGather:
    def __init__(self, view, me, plus, minus, sems, ring, source=None):
        send, recv = sems

        def near(rel, half):
            return view((me + rel) % 4, half)

        own = source or (lambda half: near(0, half))
        plan = (
            (own(0), near(0, 0), plus),
            (own(1), near(0, 1), plus),
            (near(3, 0), near(3, 0), plus),
            (own(0), near(0, 0), minus),
            (own(1), near(0, 1), minus),
            (near(1, 1), near(1, 1), minus),
        )
        self.copies = [
            remote(src, dst, send.at[ring, k], recv.at[ring, k], peer) for k, (src, dst, peer) in enumerate(plan)
        ]

    def own(self, half):
        self.copies[half].start()
        self.copies[3 + half].start()

    def whole(self):
        for k in (0, 4, 1, 3):
            self.copies[k].start()

    def forward(self):
        self.copies[0].wait_recv()
        self.copies[2].start()
        self.copies[4].wait_recv()
        self.copies[5].start()

    def near(self):
        self.copies[1].wait_recv()
        self.copies[3].wait_recv()

    def far(self):
        self.copies[2].wait_recv()
        self.copies[5].wait_recv()

    def drain(self):
        for copy in self.copies:
            copy.wait_send()


class RingReduce:
    def __init__(self, view, passing, got, plus, minus, sems, ring):
        send, recv = sems
        self.view, self.passing, self.got = view, passing, got
        plan = (
            (view(2, 0), passing(0), minus),
            (view(2, 1), passing(1), plus),
            (view(3, 1), got(0, 1), minus),
            (view(1, 0), got(1, 0), plus),
            (passing(0), got(0, 0), minus),
            (passing(1), got(1, 1), plus),
        )
        self.copies = [
            remote(src, dst, send.at[ring, k], recv.at[ring, k], peer) for k, (src, dst, peer) in enumerate(plan)
        ]

    def start(self, *numbers):
        for k in numbers or (0, 1, 2, 3):
            self.copies[k].start()

    def relay(self):
        for half, rel in ((0, 3), (1, 1)):
            self.copies[half].wait_recv()
            land, term = self.passing(half), self.view(rel, half)
            land[...] = (land[...].astype(FULL) + term[...].astype(FULL)).astype(LOW)
            self.copies[4 + half].start()

    def finish(self):
        for k in (2, 3, 4, 5):
            self.copies[k].wait_recv()

    def arrived(self, half):
        return self.got(0, half)[...].astype(FULL) + self.got(1, half)[...].astype(FULL)

    def drain(self):
        for copy in self.copies:
            copy.wait_send()


def tile_first(i, x, c):
    column = jnp.where(i % 2 == 1, 3 - x, x)
    return BLK * (8 * column + 2 * (i // 2) + c) + HALF * (i % 2)


def begin_of(token, starts_ref):
    begin = jnp.zeros_like(token)
    for n in range(starts_ref.shape[0]):
        start = starts_ref[n]
        begin = jnp.where(start <= token, start, begin)
    return begin


def attn_forward(
    starts_ref, q_ref, k_ref, v_ref, wout_hbm,
    mix_ref, lse_ref, q_out, k_out, v_out, wout_all,
    qg_ref, kg_ref, vg_ref, acc, lacc, osend, opass, ogot, lsend, lrecv, hsend, lhsend,
    rs, rr, sib_s, sib_r, l_s, l_r, sw_s, sw_r, keep_sem,
):
    x, y, c, z = place()
    xp, xm, yp, ym = at(x + 1, y, c, z), at(x + 3, y, c, z), at(x, y + 1, c, z), at(x, y + 3, c, z)
    zp, zm, y2 = at(x, y, c, z + 1), at(x, y, c, z + 3), at(x, y + 2, c, z)
    sibling, partner = at(x, y, 1 - c, z), at(3 - x, y, c, z)
    greet([partner, sibling, xp, xm, yp, ym, y2, zp, zm])
    copies = []

    def go(copy):
        copy.start()
        copies.append(copy)

    q_low, q_high = q_ref.at[pl.ds(0, HALF)], q_ref.at[pl.ds(HALF, HALF)]
    swap = remote(q_high, qg_ref.at[2 * y + 1], sw_s.at[0], sw_r.at[0], partner)
    go(swap)

    def kv_view(index, half):
        return (kg_ref, vg_ref)[half].at[2 * index + c]

    kv = RingGather(kv_view, x, xp, xm, (rs, rr), 0, lambda half: (k_ref, v_ref)[half])
    kv.whole()
    qs = RingGather(
        lambda index, half: qg_ref.at[2 * index + half], y, yp, ym, (rs, rr), 1,
        lambda half: q_low if half == 0 else qg_ref.at[2 * y + 1],
    )
    qs.own(0)

    def pass_on(index, half, source=None):
        block = kv_view(index, half)
        return remote(block if source is None else source, block, sib_s.at[index, half], sib_r.at[index, half], sibling)

    for half, source in enumerate((k_ref, v_ref)):
        go(pass_on(x, half, source))
    wide = wout_hbm.shape[0]

    def wout_view(index, half):
        return rows_at(wout_all, wide * index + half * (wide // 2), wide // 2)

    wouts = RingGather(
        wout_view, z, zp, zm, (rs, rr), 4, lambda half: wout_hbm.at[pl.ds(half * (wide // 2), wide // 2)]
    )
    wouts.whole()
    wout_keep = pltpu.make_async_copy(wout_hbm, rows_at(wout_all, wide * z, wide), keep_sem.at[3])
    wout_keep.start()
    qg_ref[2 * y] = q_ref[0:HALF, :]
    kg_ref[2 * x + c] = k_ref[...]
    vg_ref[2 * x + c] = v_ref[...]
    acc[...] = jnp.zeros_like(acc)
    lacc[...] = jnp.zeros_like(lacc)
    swap.wait_recv()
    qs.own(1)
    kv.forward()
    qs.forward()
    kv.near()
    for rel in (1, 3):
        for half in range(2):
            go(pass_on((x + rel) % 4, half))
    qs.near()
    qs.far()
    wouts.forward()

    def chunk(i, first_q, pair, first_k, masked):
        queries = qg_ref[i]
        if masked:
            token = first_q + lax.broadcasted_iota(jnp.int32, (HALF, 1), 0)
            begin = begin_of(token, starts_ref)
        total = None
        sums = None
        for cc in range(2):
            keys, values = kg_ref[pair * 2 + cc], vg_ref[pair * 2 + cc]
            scores = lax.dot_general(queries, keys, NT, preferred_element_type=FULL)
            exps = jnp.exp(scores)
            if masked:
                key_index = first_k + cc * BLK + lax.broadcasted_iota(jnp.int32, (1, BLK), 1)
                exps = jnp.where((key_index <= token) & (key_index >= begin), exps, 0.0)
            part = jnp.dot(exps.astype(LOW), values, preferred_element_type=FULL)
            total = part if total is None else total + part
            for n in range(BLK // 128):
                piece = exps[:, n * 128 : (n + 1) * 128]
                sums = piece if sums is None else sums + piece
        acc[i] = acc[i] + total
        lacc[i] = lacc[i] + sums

    def visit(i, pair):
        first_q, first_k = tile_first(i, x, c), 4096 * pair + 1024 * y
        some = first_k <= first_q + (HALF - 1)
        full = (first_k + 1023 <= first_q) & (first_k > 0) & (first_q < 31 * BLK)

        @pl.when(full)
        def _():
            chunk(i, first_q, pair, first_k, False)

        @pl.when(some & jnp.logical_not(full))
        def _():
            chunk(i, first_q, pair, first_k, True)

    numer = RingReduce(
        lambda rel, half: osend.at[2 * ((y + rel) % 4) + half],
        lambda half: opass.at[half],
        lambda side, half: ogot.at[side, half],
        yp, ym, (rs, rr), 2,
    )

    def sums_to(rel, peer):
        index = (y + rel) % 4
        return remote(lsend.at[pl.ds(2 * index, 2)], lrecv.at[y], l_s.at[rel - 1], l_r.at[y], peer)

    keeps = [
        pltpu.make_async_copy(src, dst, keep_sem.at[n])
        for n, (src, dst) in enumerate(((qg_ref, q_out), (kg_ref, k_out), (vg_ref, v_out)))
    ]
    for rel, peer in ((2, y2), (1, yp), (3, ym), (0, None)):
        first = 2 * ((y + rel) % 4)
        if rel == 2:
            for turn in (0, 1, 3, 2):
                pair = (x + turn) % 4
                if turn == 2:
                    kv.far()
                    for half in range(2):
                        go(pass_on(pair, half))
                for half in range(2):
                    pass_on(pair, half).wait_recv()
                for upper in range(2):
                    visit(first + upper, pair)
            for keep in keeps:
                keep.start()
        else:

            def one(n, carry):
                visit(first + n // 4, n % 4)
                return carry

            lax.fori_loop(0, 8, one, 0)

        for upper in range(2):
            i = first + upper
            osend[i] = acc[i].astype(LOW)
            row = jnp.sum(jnp.transpose(lacc[i]), axis=0, keepdims=True)
            lsend[i] = jnp.broadcast_to(row, (8, HALF))
        if rel == 2:
            numer.start(0, 1)
        elif rel == 1:
            numer.start(3)
        elif rel == 3:
            numer.start(2)
            numer.relay()
        if rel > 0:
            go(sums_to(rel, peer))
    lrecv[y] = lsend[pl.ds(2 * y, 2)]
    for rel in (1, 3, 2):
        remote(lsend.at[pl.ds(0, 2)], lrecv.at[(y + rel) % 4], l_s.at[0], l_r.at[(y + rel) % 4], sibling).wait_recv()
    numer.finish()

    def mix_view(index, half):
        return mix_ref.at[pl.ds(half * HALF, HALF), pl.ds(pl.multiple_of(index * HD, HD), HD)]

    mixes = RingGather(mix_view, z, zp, zm, (rs, rr), 3)
    returns = (
        remote(hsend, mix_view(z, 1), sw_s.at[1], sw_r.at[1], partner),
        remote(lhsend, lse_ref.at[1], sw_s.at[2], sw_r.at[2], partner),
    )
    for half in (1, 0):
        denom = sum(lrecv[n, half] for n in range(4))
        total = osend[2 * y + half].astype(FULL) + numer.arrived(half)
        inverse = jnp.transpose(jnp.broadcast_to(1.0 / denom[0:1, :], (128, HALF)))
        scaled = (total * jnp.concatenate([inverse, inverse], axis=1)).astype(LOW)
        if half == 1:
            hsend[...] = scaled
            lhsend[...] = jnp.log(denom)
            for copy in returns:
                go(copy)
        else:
            mix_view(z, 0)[...] = scaled
            lse_ref[0] = jnp.log(denom)
    mixes.own(0)
    for copy in returns:
        copy.wait_recv()
    mixes.own(1)
    wouts.near()
    wouts.far()
    wout_keep.wait()
    mixes.forward()
    mixes.near()
    mixes.far()
    for ring in (kv, qs, numer, mixes, wouts):
        ring.drain()
    for keep in keeps:
        keep.wait()
    for copy in copies:
        copy.wait_send()


VMEM = pl.BlockSpec(memory_space=pltpu.VMEM)
SMEM = pl.BlockSpec(memory_space=pltpu.SMEM)
ANY = pl.BlockSpec(memory_space=pl.ANY)


def dma(*shape):
    return pltpu.SemaphoreType.DMA(shape)


def shape(dtype, *dims):
    return jax.ShapeDtypeStruct(dims, dtype)


def vmem(dtype, *dims):
    return pltpu.VMEM(dims, dtype)


def params(number, mebibytes):
    return pltpu.CompilerParams(collective_id=number, has_side_effects=True, vmem_limit_bytes=mebibytes << 20)


def cost(gflops):
    return pl.CostEstimate(flops=gflops * 10**9, bytes_accessed=20 * 2**20, transcendentals=0)


def forward_attention(doc_starts, query, key, value, wout):
    return pl.pallas_call(
        attn_forward,
        name="attn_forward",
        out_shape=[
            shape(LOW, BLK, 4 * HD),
            shape(FULL, 2, 8, HALF),
            shape(LOW, 8, HALF, HD),
            shape(LOW, 8, BLK, HD),
            shape(LOW, 8, BLK, HD),
            shape(LOW, 4 * HD, wout.shape[1]),
        ],
        in_specs=[SMEM] + [VMEM] * 3 + [ANY],
        out_specs=[VMEM] * 2 + [ANY] * 4,
        scratch_shapes=[
            vmem(LOW, 8, HALF, HD),
            vmem(LOW, 8, BLK, HD),
            vmem(LOW, 8, BLK, HD),
            vmem(FULL, 8, HALF, HD),
            vmem(FULL, 8, HALF, 128),
            vmem(LOW, 8, HALF, HD),
            vmem(LOW, 2, HALF, HD),
            vmem(LOW, 2, 2, HALF, HD),
            vmem(FULL, 8, 8, HALF),
            vmem(FULL, 4, 2, 8, HALF),
            vmem(LOW, HALF, HD),
            vmem(FULL, 8, HALF),
            dma(5, 6), dma(5, 6), dma(4, 2), dma(4, 2), dma(3), dma(4), dma(3), dma(3), dma(4),
        ],
        compiler_params=params(1, 60),
        cost_estimate=cost(6),
    )(doc_starts, query, key, value, wout)


ROWS = 2560
SIDE = ROWS // 2
PIECE = SIDE // 4
WINDOW = PIECE // 4
CUTS = (0, 448, 896, 1280, 1728, 2144, 2560)


BLOCKS = ((0, 384), (384, 384), (768, 384), (1152, 384), (1536, 192))
PARTS = ((0, 512), (512, 640))
CORNER = 0.7978845608028654


def unit_of(values):
    inverse = lax.rsqrt(jnp.mean(values * values, axis=1, keepdims=True) + EPS)
    return inverse, values * inverse


def norm_back(inverse, unit, scaled):
    return inverse * (scaled - unit * jnp.mean(unit * scaled, axis=1, keepdims=True))


def middle_kernel(
    again_ref, pgain_ref, fgain_ref, lse_ref,
    mix_hbm, wout_hbm, tokens_hbm, cot_hbm, gate_hbm, up_hbm, down_hbm,
    mgrad_ref, stat_ref, early_ref, piece_a_ref, piece_b_ref, mixed_hbm, resid_hbm,
    mixed_ref, resid_ref, weights, wout, mix, tokens, cot, attn_out, left, right, turned, turned_up, aol,
    part_f, part_b, sum_f, sum_b, z_pass, z_got, sib_recv, pass_ab, got_ab, grows,
    in_sem, sib_s, sib_r, rs, rr, out_sem,
):
    x, y, c, z = place()
    xp, xm, yp, ym = at(x + 1, y, c, z), at(x + 3, y, c, z), at(x, y + 1, c, z), at(x, y + 3, c, z)
    zp, zm, sibling = at(x, y, c, z + 1), at(x, y, c, z + 3), at(x, y, 1 - c, z)
    hidden = gate_hbm.shape[0]
    width = weights.shape[1]
    loads = [
        pltpu.make_async_copy(src, dst, in_sem.at[n])
        for n, (src, dst) in enumerate(
            (
                (mix_hbm, mix),
                (wout_hbm, wout),
                (tokens_hbm, tokens),
                (gate_hbm, weights.at[pl.ds(0, hidden)]),
                (up_hbm, weights.at[pl.ds(hidden, hidden)]),
                (down_hbm, weights.at[pl.ds(2 * hidden, hidden)]),
                (cot_hbm, cot),
            )
        )
    ]
    for load in loads:
        load.start()
    greet([xp, xm, yp, ym, zp, zm, sibling])
    sems = (rs, rr)
    thirds = [pl.ds(start, size) for start, size in PARTS]

    def rows_of(r):
        return pl.ds(r * HALF, HALF)

    def head_sum(r, number, part, whole):
        quarter = HALF // 4
        first = r * HALF

        def span(ref, index, half):
            return rows_at(ref, first + quarter * index + half * (quarter // 2), quarter // 2)

        reduce = RingReduce(
            lambda rel, half: span(part, (z + rel) % 4, half),
            lambda half: z_pass.at[number, half],
            lambda side, half: z_got.at[number, side, half],
            zp, zm, sems, 2 * number,
        )
        gather = RingGather(lambda index, half: span(whole, index, half), z, zp, zm, sems, 2 * number + 1)

        def summed():
            reduce.finish()
            for half in range(2):
                own = span(part, z, half)[...].astype(FULL) + reduce.arrived(half)
                span(whole, z, half)[...] = own.astype(LOW)
            gather.whole()

        def gathered():
            gather.near()
            gather.far()

        return reduce, gather, summed, gathered

    sums = [head_sum(0, 0, part_f, sum_f), head_sum(1, 1, part_f, sum_f)]
    sums += [head_sum(0, 2, part_b, sum_b), head_sum(1, 3, part_b, sum_b)]

    def forward(r, hooks):
        rows, columns = rows_of(r), pl.ds(r * HALF, HALF)
        if r == 0:
            for load in loads[:3]:
                load.wait()
        for third in thirds:
            attn_out[rows, third] = jnp.dot(mix[rows, :], wout[:, third], preferred_element_type=FULL)
        _, unit = unit_of(attn_out[rows, :])
        state = tokens[rows, :].astype(FULL) + unit * again_ref[...][None, :]
        resid_ref[rows, :] = state
        _, unit = unit_of(state)
        right[0, rows, :] = (unit * pgain_ref[...][None, :]).astype(LOW)
        if r == 0:
            for load in loads[3:5]:
                load.wait()
        for n, (start, size) in enumerate(BLOCKS):
            low = right[0, rows, :]
            gate = lax.dot_general(weights[pl.ds(start, size), :], low, NT, preferred_element_type=FULL)
            up = lax.dot_general(weights[pl.ds(hidden + start, size), :], low, NT, preferred_element_type=FULL)
            square = gate * gate
            bend = jnp.tanh(CORNER * gate * (1.0 + 0.044715 * square))
            share = 0.5 * (1.0 + bend)
            gelu = gate * share
            slope = share + 0.5 * gate * (1.0 - bend * bend) * (CORNER * (1.0 + 3.0 * 0.044715 * square))
            act = (gelu * up).astype(LOW)
            left[pl.ds(start, size), columns] = (up * slope).astype(LOW)
            left[pl.ds(hidden + start, size), columns] = gelu.astype(LOW)
            left[pl.ds(2 * hidden + start, size), columns] = act
            turned[:, start : start + size] = jnp.transpose(act)
            if n in hooks:
                hooks[n]()
        if r == 0:
            loads[5].wait()
        for third in thirds:
            part = jnp.dot(
                turned[:, :hidden], weights[pl.ds(2 * hidden, hidden), third], preferred_element_type=FULL
            )
            part_f[rows, third] = part.astype(LOW)

    def backward(r, hooks):
        rows, columns = rows_of(r), pl.ds(r * HALF, HALF)
        if r == 0:
            loads[6].wait()
        inverse, unit = unit_of(sum_f[rows, :].astype(FULL))
        mixed_ref[rows, :] = (resid_ref[rows, :] + unit * fgain_ref[...][None, :]).astype(LOW)
        grad = cot[rows, :].astype(FULL)
        grows[2, r : r + 1, :] = jnp.sum(unit * grad, axis=0, keepdims=True)
        right[1, rows, :] = norm_back(inverse, unit, fgain_ref[...][None, :] * grad).astype(LOW)
        for n, (start, size) in enumerate(BLOCKS):
            act_grad = lax.dot_general(
                weights[pl.ds(2 * hidden + start, size), :], right[1, rows, :], NT, preferred_element_type=FULL
            )
            for first, turn in ((start, turned), (hidden + start, turned_up)):
                span = pl.ds(first, size)
                grads = (act_grad * left[span, columns].astype(FULL)).astype(LOW)
                left[span, columns] = grads
                turn[:, start : start + size] = jnp.transpose(grads)
            if n in hooks:
                hooks[n]()
        for third in thirds:
            part = jnp.dot(turned[:, :hidden], weights[pl.ds(0, hidden), third], preferred_element_type=FULL)
            part = part + jnp.dot(
                turned_up[:, :hidden], weights[pl.ds(hidden, hidden), third], preferred_element_type=FULL
            )
            part_b[rows, third] = part.astype(LOW)

    own_head = pl.ds(pl.multiple_of(z * HD, HD), HD)

    def finish(r):
        rows = rows_of(r)
        grad = sum_b[rows, :].astype(FULL)
        inverse, unit = unit_of(resid_ref[rows, :])
        grows[1, r : r + 1, :] = jnp.sum(unit * grad, axis=0, keepdims=True)
        grad = cot[rows, :].astype(FULL) + norm_back(inverse, unit, pgain_ref[...][None, :] * grad)
        resid_ref[rows, :] = grad
        inverse, unit = unit_of(attn_out[rows, :])
        grows[0, r : r + 1, :] = jnp.sum(unit * grad, axis=0, keepdims=True)
        aol[rows, :] = norm_back(inverse, unit, again_ref[...][None, :] * grad).astype(LOW)
        grads = lax.dot_general(aol[rows, :], wout[own_head, :], NT, preferred_element_type=FULL).astype(LOW)
        mgrad_ref[rows, :] = grads
        products = grads.astype(FULL) * mix[rows, own_head].astype(FULL)
        delta = jnp.sum(jnp.transpose(products), axis=0, keepdims=True)
        number = lax.broadcasted_iota(jnp.int32, (8, HALF), 0)
        stat_ref[r] = jnp.where(number == 1, delta, lse_ref[r])

    sib_send, mine = weights.at[pl.ds(0, ROWS)], weights.at[pl.ds(ROWS, ROWS)]

    def product(core, n, target, added):
        first, size = CUTS[n], CUTS[n + 1] - CUTS[n]
        lhs = left[pl.ds(pl.multiple_of(ROWS * core + first, 16), size), :]
        which = jnp.where(n >= 2, core, 0)
        for third in thirds:
            tile = jnp.dot(lhs, right[which, :, third], preferred_element_type=FULL)
            if added is not None:
                tile = tile + added[pl.ds(first, size), third].astype(FULL)
            target[pl.ds(first, size), third] = tile.astype(LOW)

    def to_sibling(n):
        span = pl.ds(CUTS[n], CUTS[n + 1] - CUTS[n])
        return remote(sib_send.at[span], sib_recv.at[span], sib_s.at[n], sib_r.at[n], sibling)

    def side_ring(h, me, plus, minus):
        return RingReduce(
            lambda rel, half: rows_at(
                weights, ROWS + SIDE * h + PIECE * ((me + rel) % 4) + half * (PIECE // 2), PIECE // 2
            ),
            lambda half: pass_ab.at[h, half],
            lambda side, half: got_ab.at[h, side, half],
            plus, minus, sems, 8 + h,
        )

    rings = (side_ring(0, x, xp, xm), side_ring(1, y, yp, ym))
    outs = [
        pltpu.make_async_copy(src, dst, out_sem.at[n])
        for n, (src, dst) in enumerate(
            ((mixed_ref, mixed_hbm), (resid_ref, resid_hbm))
        )
    ]
    forward(0, {})
    sums[0][0].start()
    forward(1, {3: sums[0][0].relay})
    sums[1][0].start()
    sums[0][2]()
    sums[1][0].relay()
    sums[0][1].forward()
    sums[0][3]()
    sums[1][2]()
    backward(0, {2: sums[1][1].forward})
    sums[2][0].start()
    sums[1][3]()
    backward(1, {2: sums[2][0].relay, 4: sums[2][2]})
    sums[3][0].start()
    outs[0].start()
    count = len(CUTS) - 1

    def for_sibling(chunks):
        for n in chunks:
            product(1 - c, n, sib_send, None)
            to_sibling(n).start()

    def for_self(chunks):
        for n in chunks:
            to_sibling(n).wait_recv()
            product(c, n, mine, sib_recv)

    side_a, side_b = range(count // 2), range(count // 2, count)
    for_sibling(side_a)
    sums[2][1].forward()
    sums[3][0].relay()
    for_self(side_a)
    rings[0].start(0, 1)
    sums[3][2]()
    for_sibling(side_b)
    rings[0].start(2, 3)
    sums[3][1].forward()
    for_self(side_b)
    rings[1].start(0, 1)
    sums[2][3]()
    finish(0)
    rings[1].start(2, 3)
    rings[0].relay()
    sums[3][3]()
    finish(1)
    rest = jnp.dot(left[2 * ROWS :, :], right[1], preferred_element_type=FULL)
    early_ref[pl.ds(HD, 64), :] = rest.astype(LOW)
    outs[1].start()
    lhs = jnp.transpose(mix[:, own_head])
    for third in thirds:
        early_ref[0:HD, third] = jnp.dot(lhs, aol[:, third], preferred_element_type=FULL).astype(LOW)
    number = lax.broadcasted_iota(jnp.int32, (32, width), 0)
    gains = jnp.zeros((32, width), FULL)
    for n in range(3):
        gains = jnp.where(number == n, grows[n, 0:1, :] + grows[n, 1:2, :], gains)
    early_ref[pl.ds(HD + 64, 32), :] = gains.astype(LOW)
    rings[1].relay()
    for h, (ring, me, out) in enumerate(((rings[0], x, piece_a_ref), (rings[1], y, piece_b_ref))):
        ring.finish()
        for half in range(2):
            size = PIECE // 2
            own = rows_at(weights, ROWS + SIDE * h + PIECE * me + half * size, size)[...]
            out[pl.ds(half * size, size), :] = (own.astype(FULL) + ring.arrived(half)).astype(LOW)
    for out in outs:
        out.wait()
    for reduce, gather, _, _ in sums:
        reduce.drain()
        gather.drain()
    for ring in rings:
        ring.drain()
    for n in range(count):
        to_sibling(n).wait_send()


def middle(again, pgain, fgain, lse, mix, wout, tokens, cot, gate_t, up_t, down):
    rows, width = tokens.shape
    hidden = gate_t.shape[0]
    stacked = 3 * hidden
    return pl.pallas_call(
        middle_kernel,
        name="middle",
        out_shape=[
            shape(LOW, rows, HD),
            shape(FULL, 2, 8, HALF),
            shape(LOW, HD + 96, width),
            shape(LOW, PIECE, width),
            shape(LOW, PIECE, width),
            shape(LOW, rows, width),
            shape(FULL, rows, width),
        ],
        in_specs=[VMEM] * 4 + [ANY] * 7,
        out_specs=[VMEM] * 5 + [ANY] * 2,
        scratch_shapes=[
            vmem(LOW, rows, width),
            vmem(FULL, rows, width),
            vmem(LOW, stacked, width),
            vmem(LOW, 4 * HD, width),
            vmem(LOW, rows, 4 * HD),
            vmem(LOW, rows, width),
            vmem(LOW, rows, width),
            vmem(FULL, rows, width),
            vmem(LOW, stacked, rows),
            vmem(LOW, 2, rows, width),
            vmem(LOW, HALF, 1792),
            vmem(LOW, HALF, 1792),
            vmem(LOW, rows, width),
            *[vmem(LOW, rows, width)] * 4,
            vmem(LOW, 4, 2, HALF // 8, width),
            vmem(LOW, 4, 2, 2, HALF // 8, width),
            vmem(LOW, ROWS, width),
            vmem(LOW, 2, 2, PIECE // 2, width),
            vmem(LOW, 2, 2, 2, PIECE // 2, width),
            vmem(FULL, 3, 8, width),
            dma(7), dma(6), dma(6), dma(10, 6), dma(10, 6), dma(2),
        ],
        compiler_params=params(4, 60),
        cost_estimate=cost(20),
    )(again, pgain, fgain, lse, mix, wout, tokens, cot, gate_t, up_t, down)


LATE = 112
EARLY = 176
KEEPERS = 11


def attn_backward(
    starts_ref, do_ref, stat_ref, piece_a_ref, piece_b_ref, qgain_ref, kgain_ref, igain_ref, early_ref,
    q_hbm, k_hbm, v_hbm, raw_hbm, kraw_hbm, cos_hbm, sin_hbm, wk_hbm, wv_hbm, normed_hbm, wq_hbm, tokens_hbm, resid_hbm,
    late_ref, esum_ref, tgrad_ref, dgain_ref, big_ref,
    dog, statg, dqacc, dkall, dvall, ktall, sibsend, sibrecv, kvsrc, kvpass, kvgot,
    dqsend, dqpass, dqgot, dqback, dqhigh, zpart, zpass, zgot, own_sum, gaing, winpass, wingot, full_a, full_b,
    draw_ref, dkv_ref, dkraw, dvrow, part, core_recv, half_sum, plane_recv, grow, grecv,
    e_core, e_half, e_plane,
    q_in, k_in, v_in, raw_ref, kraw_ref, cos_ref, sin_ref, wk_ref, wv_ref, normed_t, wq_ref, tok_ref,
    rs, rr, st_s, st_r, sw_s, sw_r, sib_s, sib_r, gn_s, gn_r, sf_s, sf_r, own_sem,
    load_sem, c_s, c_r, p_s, p_r, g_s, g_r, f_s, f_r, i_s, i_r,
    ep_s, ep_r, eg_s, eg_r, ef_s, ef_r,
):
    x, y, c, z = place()
    xp, xm, yp, ym = at(x + 1, y, c, z), at(x + 3, y, c, z), at(x, y + 1, c, z), at(x, y + 3, c, z)
    zp, zm, y2, z2 = at(x, y, c, z + 1), at(x, y, c, z + 3), at(x, y + 2, c, z), at(x, y, c, z + 2)
    sibling, partner = at(x, y, 1 - c, z), at(3 - x, y, c, z)
    shifts = [(a, b) for a in range(4) for b in range(4) if (a, b) != (0, 0)]
    plane = [at(x + a, y + b, c, z) for a, b in shifts]
    loads = [
        pltpu.make_async_copy(src, dst, load_sem.at[n])
        for n, (src, dst) in enumerate(
            (
                (q_hbm, q_in), (k_hbm, k_in), (v_hbm, v_in), (raw_hbm, raw_ref), (kraw_hbm, kraw_ref),
                (cos_hbm, cos_ref), (sin_hbm, sin_ref), (wk_hbm, wk_ref), (wv_hbm, wv_ref),
                (normed_hbm, normed_t), (wq_hbm, wq_ref.at[:, pl.ds(pl.multiple_of(z * HD, HD), HD)]), (tokens_hbm, tok_ref), (resid_hbm, tgrad_ref),
            )
        )
    ]
    for load in loads:
        load.start()
    greet(plane + [sibling, zp, zm, z2])
    copies = []

    def go(copy):
        copy.start()
        copies.append(copy)

    sems = (rs, rr)
    do_low, do_high = do_ref.at[pl.ds(0, HALF)], do_ref.at[pl.ds(HALF, HALF)]
    swaps = (
        remote(do_high, dog.at[2 * y + 1], sw_s.at[0], sw_r.at[0], partner),
        remote(stat_ref.at[1], statg.at[2 * y + 1], sw_s.at[1], sw_r.at[1], partner),
    )
    for copy in swaps:
        go(copy)
    dos = RingGather(
        lambda index, half: dog.at[2 * index + half], y, yp, ym, sems, 0,
        lambda half: do_low if half == 0 else dog.at[2 * y + 1],
    )
    dos.own(0)
    tall = wq_hbm.shape[0] // 2

    def wq_view(index, half):
        return wq_ref.at[pl.ds(half * tall, tall), pl.ds(pl.multiple_of(index * HD, HD), HD)]

    wqs = RingGather(
        wq_view, z, zp, zm, sems, 12, lambda half: wq_hbm.at[pl.ds(half * tall, tall)]
    )
    wqs.whole()
    chip = x * 4 + y
    e_cross = remote(rows_at(early_ref, EARLY * (1 - c), EARLY), e_core, c_s.at[1], c_r.at[1], sibling)
    go(e_cross)

    def early_part(owner):
        return remote(
            rows_at(e_half, 16 * owner, 16), e_plane.at[chip], ep_s.at[owner], ep_r.at[chip],
            at(owner // 4, owner % 4, c, z),
        )

    def early_spread():
        e_cross.wait_recv()
        own = early_ref[pl.ds(pl.multiple_of(EARLY * c, 16), EARLY), :]
        e_half[...] = (own.astype(FULL) + e_core[...].astype(FULL)).astype(LOW)
        for owner in range(KEEPERS):
            pl.when(chip != owner)(early_part(owner).start)

    def early_piece(core, owner):
        return rows_at(esum_ref, EARLY * core + 16 * owner, 16)

    def early_out(n):
        return remote(early_piece(c, chip), early_piece(c, chip), eg_s.at[n], eg_r.at[chip], plane[n])

    def early_across(owner):
        block = early_piece(c, owner)
        return remote(block, block, ef_s.at[owner], ef_r.at[owner], sibling)

    def early_summed():
        @pl.when(chip < KEEPERS)
        def _():
            total = rows_at(e_half, 16 * chip, 16)[...].astype(FULL)
            for a, b in shifts:
                source = ((x + a) % 4) * 4 + (y + b) % 4
                block = rows_at(e_half, 0, 16)
                remote(block, e_plane.at[source], ep_s.at[0], ep_r.at[source], sibling).wait_recv()
                total = total + e_plane[source].astype(FULL)
            early_piece(c, chip)[...] = total.astype(LOW)
            for n in range(15):
                early_out(n).start()
            early_across(chip).start()

    def early_passed():
        for owner in range(KEEPERS):

            @pl.when(chip != owner)
            def _():
                block = early_piece(c, owner)
                remote(rows_at(e_half, 0, 16), block, eg_s.at[0], eg_r.at[owner], sibling).wait_recv()
                early_across(owner).start()

    def early_done():
        for owner in range(KEEPERS):
            block = early_piece(1 - c, owner)
            remote(rows_at(e_half, 0, 16), block, ef_s.at[0], ef_r.at[owner], sibling).wait_recv()
            early_across(owner).wait_send()
            pl.when(chip != owner)(early_part(owner).wait_send)

        @pl.when(chip < KEEPERS)
        def _():
            for n in range(15):
                early_out(n).wait_send()

    def stats_to(upper, rel, peer):
        slot = 2 * y + upper
        source = statg.at[slot] if upper else stat_ref.at[0]
        return remote(source, statg.at[slot], st_s.at[upper, rel - 1], st_r.at[slot], peer)

    y_peers = ((1, yp), (3, ym), (2, y2))
    for rel, peer in y_peers:
        go(stats_to(0, rel, peer))

    cut = (48, WINDOW - 48)

    def window(ref, index, half):
        return rows_at(ref, WINDOW * index + 48 * half, cut[half])

    sides = ((piece_a_ref, full_a, y, yp, ym), (piece_b_ref, full_b, x, xp, xm))
    reduces, gathers = [], []
    for h, (piece, full, me, plus, minus) in enumerate(sides):
        reduces.append(
            RingReduce(
                lambda rel, half, piece=piece, me=me: window(piece, (me + rel) % 4, half),
                lambda half, h=h: winpass.at[h, pl.ds(48 * half, cut[half])],
                lambda side, half, h=h: wingot.at[h, side, pl.ds(48 * half, cut[half])],
                plus, minus, sems, 1 + h,
            )
        )
        gathers.append(
            RingGather(lambda index, half, full=full: window(full, index, half), me, plus, minus, sems, 3 + h)
        )
        reduces[h].start()

    def big_view(core, h, index, half):
        return rows_at(big_ref, ROWS * core + SIDE * h + PIECE * index + half * (PIECE // 2), PIECE // 2)

    owners = ((x, xp, xm), (y, yp, ym))
    pieces = [
        RingGather(
            lambda index, half, h=h: big_view(c, h, index, half), me, plus, minus, sems, 5 + h,
            lambda half, h=h: sides[h][1].at[pl.ds(half * (PIECE // 2), PIECE // 2)],
        )
        for h, (me, plus, minus) in enumerate(owners)
    ]

    def piece_to_sibling(h, index, half, source=None):
        block = big_view(c, h, index, half)
        return remote(block if source is None else source, block, sf_s.at[h, index, half], sf_r.at[h, index, half], sibling)

    def keep(h, half):
        source = sides[h][1].at[pl.ds(half * (PIECE // 2), PIECE // 2)]
        return pltpu.make_async_copy(source, big_view(c, h, owners[h][0], half), own_sem.at[h, half])

    def window_summed(h):
        ring, gather = reduces[h], gathers[h]
        piece, full, me, _, _ = sides[h]
        ring.finish()
        for half in range(2):
            total = window(piece, me, half)[...].astype(FULL) + ring.arrived(half)
            window(full, me, half)[...] = total.astype(LOW)
        gather.whole()

    def window_gathered(h):
        gathers[h].near()
        gathers[h].far()

    def pieces_sent(h):
        pieces[h].whole()
        for half in range(2):
            source = sides[h][1].at[pl.ds(half * (PIECE // 2), PIECE // 2)]
            go(piece_to_sibling(h, owners[h][0], half, source))
            keep(h, half).start()

    def pieces_near(h):
        pieces[h].near()
        for rel in (1, 3):
            for half in range(2):
                go(piece_to_sibling(h, (owners[h][0] + rel) % 4, half))

    def pieces_far(h):
        pieces[h].far()
        for half in range(2):
            go(piece_to_sibling(h, (owners[h][0] + 2) % 4, half))

    def tile(i, first_q, slot, first_k, masked):
        queries, out_grads = q_in[i], dog[i]
        lse, delta = statg[i, 0:1, :], statg[i, 1:2, :]
        if masked:
            token = first_q + lax.broadcasted_iota(jnp.int32, (1, HALF), 1)
            begin = begin_of(token, starts_ref)
        dq_part = None
        for n in range(2):
            rows = pl.ds(n * 256, 256)
            keys, values = k_in[slot, rows], v_in[slot, rows]
            scores = lax.dot_general(keys, queries, NT, preferred_element_type=FULL)
            prob_grad = lax.dot_general(values, out_grads, NT, preferred_element_type=FULL)
            soft = jnp.exp(scores - lse)
            if masked:
                key_index = first_k + n * 256 + lax.broadcasted_iota(jnp.int32, (256, 1), 0)
                soft = jnp.where((key_index <= token) & (key_index >= begin), soft, 0.0)
            score_grad = (soft * (prob_grad - delta)).astype(LOW)
            dvall[slot, rows, :] += jnp.dot(soft.astype(LOW), out_grads, preferred_element_type=FULL)
            dkall[slot, rows, :] += jnp.dot(score_grad, queries, preferred_element_type=FULL)
            part = jnp.dot(ktall[slot, :, n * 256 : (n + 1) * 256], score_grad, preferred_element_type=FULL)
            dq_part = part if dq_part is None else dq_part + part
        dqacc[i] = dqacc[i] + dq_part

    def visit(i, slot):
        first_q = tile_first(i, x, c)
        first_k = 4096 * (slot // 2) + 1024 * y + BLK * (slot % 2)
        some = first_k <= first_q + (HALF - 1)
        full = (first_k + BLK - 1 <= first_q) & (first_k > 0) & (first_q < 31 * BLK)

        @pl.when(full)
        def _():
            tile(i, first_q, slot, first_k, False)

        @pl.when(some & jnp.logical_not(full))
        def _():
            tile(i, first_q, slot, first_k, True)

    def own_tile(upper):
        def one(slot, carry):
            visit(2 * y + upper, slot)
            return carry

        lax.fori_loop(0, 8, one, 0)

    dog[2 * y] = do_ref[0:HALF, :]
    statg[2 * y] = stat_ref[0]
    dqacc[...] = jnp.zeros_like(dqacc)
    dkall[...] = jnp.zeros_like(dkall)
    dvall[...] = jnp.zeros_like(dvall)
    for load in loads[:3]:
        load.wait()

    def turn_keys(slot, carry):
        ktall[slot] = jnp.transpose(k_in[slot])
        return carry

    lax.fori_loop(0, 8, turn_keys, 0)
    for copy in swaps:
        copy.wait_recv()
    dos.own(1)
    for rel, peer in y_peers:
        go(stats_to(1, rel, peer))
    own_tile(0)
    dos.forward()
    for ring in reduces:
        ring.relay()
    own_tile(1)
    dos.near()
    dos.far()
    for upper in range(2):
        for rel, peer in y_peers:
            slot = 2 * ((y + rel) % 4) + upper
            remote(stat_ref.at[0], statg.at[slot], st_s.at[0, 0], st_r.at[slot], sibling).wait_recv()

    window_summed(0)
    window_summed(1)

    zrows = BLK // 4
    place_of = {2: 0, 1: 1, 3: 2, 0: 3}
    kvs = RingReduce(
        lambda rel, half: kvsrc.at[place_of[rel], half],
        lambda half: kvpass.at[half],
        lambda side, half: kvgot.at[side, half],
        xp, xm, sems, 7,
    )
    zrings = [
        RingReduce(
            lambda rel, half, step=step: zpart.at[step, (z + rel) % 4, half],
            lambda half, step=step: zpass.at[step, half],
            lambda side, half, step=step: zgot.at[step, side, half],
            zp, zm, sems, number,
        )
        for step, number in enumerate((9, 13, 14, 15))
    ]

    def cores_summed(step, rel):
        slot = ((x + rel) % 4) * 2 + c
        remote(sibsend.at[step], sibrecv.at[step], sib_s.at[step], sib_r.at[step], sibling).wait_recv()
        for half, ref in enumerate((dkall, dvall)):
            for n in range(4):
                rows = pl.ds(n * zrows, zrows)
                both = ref[slot, rows, :] + sibrecv[step, half, rows, :].astype(FULL)
                zpart[step, n, half] = both.astype(LOW)
        zrings[step].start()

    def heads_summed(step):
        zrings[step].finish()
        for half in range(2):
            total = zpart[step, z, half].astype(FULL) + zrings[step].arrived(half)
            if step == 3:
                own_sum[half] = total
            else:
                kvsrc[step, half] = total.astype(LOW)
        if step < 3:
            kvs.start(*((0, 1), (3,), (2,))[step])

    def pieces_start():
        for h in range(2):
            window_gathered(h)
            pieces_sent(h)

    def each_side(method):
        for h in range(2):
            method(h)

    between = {
        (0, 0): (early_spread,),
        (0, 1): (gathers[0].forward, gathers[1].forward),
        (1, 0): (pieces_start,),
        (1, 1): (lambda: cores_summed(0, 2),),
        (2, 0): (zrings[0].relay, early_summed, wqs.forward),
        (2, 1): (lambda: cores_summed(1, 1), lambda: heads_summed(0), pieces[0].forward, pieces[1].forward),
        (3, 0): (zrings[1].relay, wqs.near, wqs.far),
        (3, 1): (lambda: cores_summed(2, 3), lambda: heads_summed(1), lambda: each_side(pieces_near)),
    }
    for step, rel in enumerate((2, 1, 3, 0)):
        pair = (x + rel) % 4
        for turn in range(2):
            if (step, turn) in between:
                for hook in between[step, turn]:
                    hook()
            cc = 1 - c if turn == 0 else c
            slot = pair * 2 + cc

            def one(n, carry):
                visit((2 * y + 2 + n) % 8, slot)
                return carry

            lax.fori_loop(0, 6, one, 0)
            if turn == 0:
                sibsend[step, 0] = dkall[slot].astype(LOW)
                sibsend[step, 1] = dvall[slot].astype(LOW)
                go(remote(sibsend.at[step], sibrecv.at[step], sib_s.at[step], sib_r.at[step], sibling))

    zrings[2].relay()
    cores_summed(3, 0)
    zg = RingGather(lambda index, half: dkv_ref.at[index, half], z, zp, zm, sems, 10)

    def cast(i, carry):
        dqsend[i] = jnp.transpose(dqacc[i]).astype(LOW)
        return carry

    lax.fori_loop(0, 8, cast, 0)
    dqs = RingReduce(
        lambda rel, half: dqsend.at[2 * ((y + rel) % 4) + half],
        lambda half: dqpass.at[half],
        lambda side, half: dqgot.at[side, half],
        yp, ym, sems, 8,
    )
    dqs.start()
    heads_summed(2)
    zrings[3].relay()
    kvs.relay()
    dqs.relay()
    heads_summed(3)
    kvs.finish()
    for half in range(2):
        dkv_ref[z, half] = (own_sum[half] + kvs.arrived(half)).astype(LOW)
    zg.whole()
    early_passed()
    each_side(pieces_far)
    for load in loads[3:]:
        load.wait()
    dqs.finish()
    back = remote(dqback, dqhigh, sw_s.at[2], sw_r.at[2], partner)
    dqback[...] = (dqsend[2 * y + 1].astype(FULL) + dqs.arrived(1)).astype(LOW)
    go(back)

    draws = RingGather(
        lambda index, half: draw_ref.at[pl.ds(half * HALF, HALF), pl.ds(pl.multiple_of(index * HD, HD), HD)],
        z, zp, zm, sems, 11,
    )

    def unrotated(grad, raw, gain, rows):
        cosine, sine = cos_ref[rows, :], sin_ref[rows, :]
        first, second = grad[:, : HD // 2], grad[:, HD // 2 :]
        turned = jnp.concatenate([first * cosine + second * sine, second * cosine - first * sine], axis=1)
        inverse = lax.rsqrt(jnp.mean(raw * raw, axis=1, keepdims=True) + EPS)
        unit = raw * inverse
        scaled = gain * turned
        raw_grad = inverse * (scaled - unit * jnp.mean(unit * scaled, axis=1, keepdims=True))
        return raw_grad.astype(LOW), jnp.sum(unit * turned, axis=0, keepdims=True)

    gain_grad = None
    for half in range(2):
        if half == 0:
            grad = dqsend[2 * y].astype(FULL) + dqs.arrived(0)
        else:
            back.wait_recv()
            grad = dqhigh[...].astype(FULL)
        rows = pl.ds(half * HALF, HALF)
        raw_grad, piece = unrotated(grad * (HD**-0.5), raw_ref[rows, :], qgain_ref[...][None, :], rows)
        draw_ref[rows, pl.ds(pl.multiple_of(z * HD, HD), HD)] = raw_grad
        draws.own(half)
        gain_grad = piece if gain_grad is None else gain_grad + piece
    gaing[z] = jnp.broadcast_to(gain_grad, (8, HD))
    for n, peer in enumerate((zp, zm, z2)):
        go(remote(gaing.at[z], gaing.at[z], gn_s.at[n], gn_r.at[z], peer))

    chunk_rows = normed_t.shape[0] // 4

    def weight_grad(m, rhs):
        def block(r, carry):
            lhs = normed_t[pl.ds(pl.multiple_of(r * chunk_rows, 16), chunk_rows), :]
            tile = jnp.dot(lhs, rhs[...], preferred_element_type=FULL).astype(LOW)
            part[pl.ds(pl.multiple_of((4 * m + r) * chunk_rows, 16), chunk_rows), :] = tile
            return carry

        lax.fori_loop(0, 4, block, 0)

    zg.forward()
    weight_grad(0, draw_ref.at[:, pl.ds(pl.multiple_of(z * HD, HD), HD)])
    draws.forward()
    zg.near()
    zg.far()
    key_gain_grad = None
    for n in range(4):
        rows = pl.ds(n * zrows, zrows)
        raw_grad, piece = unrotated(dkv_ref[n, 0].astype(FULL), kraw_ref[rows, :], kgain_ref[...][None, :], rows)
        dkraw[rows, :] = raw_grad
        dvrow[rows, :] = dkv_ref[n, 1]
        key_gain_grad = piece if key_gain_grad is None else key_gain_grad + piece
    for rel in (1, 3, 2):
        other = (z + rel) % 4
        remote(gaing.at[z], gaing.at[other], gn_s.at[0], gn_r.at[other], sibling).wait_recv()
    query_gain_grad = sum(gaing[n, 0:1, :] for n in range(4))
    number = lax.broadcasted_iota(jnp.int32, (16, HD), 0)
    both = jnp.where(number == 0, query_gain_grad, jnp.where(number == 1, key_gain_grad, 0.0))
    part[pl.ds(12 * chunk_rows, 16), :] = both.astype(LOW)
    part[pl.ds(12 * chunk_rows + 16, LATE), :] = jnp.zeros((LATE, HD), LOW)
    weight_grad(1, dkraw)
    weight_grad(2, dvrow)

    side = 16 * LATE

    def late_piece(ref, core, owner):
        return rows_at(ref, side * core + LATE * owner, LATE)

    cross = remote(rows_at(part, side * (1 - c), side), core_recv, c_s.at[0], c_r.at[0], sibling)
    go(cross)
    cross.wait_recv()

    def add(r, carry):
        both = part[pl.ds(pl.multiple_of(side * c + 2 * LATE * r, 16), 2 * LATE), :].astype(FULL)
        rows = pl.ds(pl.multiple_of(2 * LATE * r, 16), 2 * LATE)
        half_sum[rows, :] = (both + core_recv[rows, :].astype(FULL)).astype(LOW)
        return carry

    lax.fori_loop(0, 8, add, 0)
    for n, (a, b) in enumerate(shifts):
        target = ((x + a) % 4) * 4 + (y + b) % 4
        go(remote(late_piece(half_sum, 0, target), plane_recv.at[chip], p_s.at[n], p_r.at[chip], plane[n]))

    draws.near()
    draws.far()
    gain_row = None
    for half in range(2):
        rows = pl.ds(half * HALF, HALF)
        grad = lax.dot_general(draw_ref[rows, :], wq_ref[...], NT, preferred_element_type=FULL)
        grad = grad + lax.dot_general(dkraw[rows, :], wk_ref[...], NT, preferred_element_type=FULL)
        grad = grad + lax.dot_general(dvrow[rows, :], wv_ref[...], NT, preferred_element_type=FULL)
        value = tok_ref[rows, :].astype(FULL)
        inverse = lax.rsqrt(jnp.mean(value * value, axis=1, keepdims=True) + EPS)
        unit = value * inverse
        scaled = igain_ref[...][None, :] * grad
        back_grad = inverse * (scaled - unit * jnp.mean(unit * scaled, axis=1, keepdims=True))
        tgrad_ref[rows, :] = tgrad_ref[rows, :] + back_grad
        piece = jnp.sum(unit * grad, axis=0, keepdims=True)
        gain_row = piece if gain_row is None else gain_row + piece
    grow[0] = jnp.broadcast_to(gain_row, grow.shape[1:])
    to_core = remote(grow.at[0], grow.at[1], i_s.at[15], i_r.at[16], sibling)
    go(to_core)

    total = late_piece(half_sum, 0, chip)[...].astype(FULL)
    for a, b in shifts:
        source = ((x + a) % 4) * 4 + (y + b) % 4
        remote(late_piece(half_sum, 0, 0), plane_recv.at[source], p_s.at[0], p_r.at[source], sibling).wait_recv()
        total = total + plane_recv[source].astype(FULL)

    def piece_of(owner):
        return late_piece(late_ref, c, owner)

    piece_of(chip)[...] = total.astype(LOW)
    for n in range(15):
        go(remote(piece_of(chip), piece_of(chip), g_s.at[n], g_r.at[chip], plane[n]))
    go(remote(piece_of(chip), piece_of(chip), f_s.at[chip], f_r.at[chip], sibling))
    to_core.wait_recv()
    grecv[chip] = grow[0] + grow[1]
    for n in range(15):
        go(remote(grecv.at[chip], grecv.at[chip], i_s.at[n], i_r.at[chip], plane[n]))
    for a, b in shifts:
        source = ((x + a) % 4) * 4 + (y + b) % 4
        remote(late_piece(half_sum, 0, 0), piece_of(source), g_s.at[0], g_r.at[source], sibling).wait_recv()
        go(remote(piece_of(source), piece_of(source), f_s.at[source], f_r.at[source], sibling))
    for a, b in shifts:
        source = ((x + a) % 4) * 4 + (y + b) % 4
        remote(grecv.at[chip], grecv.at[source], i_s.at[0], i_r.at[source], sibling).wait_recv()
    dgain_ref[...] = sum(grecv[n] for n in range(16))
    for n in range(16):
        theirs = late_piece(late_ref, 1 - c, n)
        remote(late_piece(half_sum, 0, 0), theirs, f_s.at[0], f_r.at[n], sibling).wait_recv()
    early_done()
    for h in range(2):
        for half in range(2):
            keep(h, half).wait()
            for n in range(4):
                piece_to_sibling(h, n, half).wait_recv()
    for ring in [dos, kvs, dqs, zg, draws, wqs] + zrings + reduces + gathers + pieces:
        ring.drain()
    for copy in copies:
        copy.wait_send()


def backward_attention(doc_starts, *operands):
    width = operands[2].shape[1]
    streamed = operands[8:]
    return pl.pallas_call(
        attn_backward,
        name="attn_backward",
        out_shape=[
            shape(LOW, 32 * LATE, HD),
            shape(LOW, 2 * EARLY, width),
            shape(FULL, BLK, width),
            shape(FULL, 8, width),
            shape(LOW, 2 * ROWS + 64, width),
        ],
        in_specs=[SMEM] + [VMEM] * 8 + [ANY] * 13,
        out_specs=[VMEM] * 4 + [ANY],
        scratch_shapes=[
            vmem(LOW, 8, HALF, HD),
            vmem(FULL, 8, 8, HALF),
            vmem(FULL, 8, HD, HALF),
            vmem(FULL, 8, BLK, HD),
            vmem(FULL, 8, BLK, HD),
            vmem(LOW, 8, HD, BLK),
            vmem(LOW, 4, 2, BLK, HD),
            vmem(LOW, 4, 2, BLK, HD),
            vmem(LOW, 3, 2, BLK // 4, HD),
            vmem(LOW, 2, BLK // 4, HD),
            vmem(LOW, 2, 2, BLK // 4, HD),
            vmem(LOW, 8, HALF, HD),
            vmem(LOW, 2, HALF, HD),
            vmem(LOW, 2, 2, HALF, HD),
            vmem(LOW, HALF, HD),
            vmem(LOW, HALF, HD),
            vmem(LOW, 4, 4, 2, BLK // 4, HD),
            vmem(LOW, 4, 2, BLK // 4, HD),
            vmem(LOW, 4, 2, 2, BLK // 4, HD),
            vmem(FULL, 2, BLK // 4, HD),
            vmem(FULL, 4, 8, HD),
            vmem(LOW, 2, WINDOW, width),
            vmem(LOW, 2, 2, WINDOW, width),
            vmem(LOW, PIECE, width),
            vmem(LOW, PIECE, width),
            vmem(LOW, BLK, 4 * HD),
            vmem(LOW, 4, 2, BLK // 4, HD),
            vmem(LOW, BLK, HD),
            vmem(LOW, BLK, HD),
            vmem(LOW, 32 * LATE, HD),
            vmem(LOW, 16 * LATE, HD),
            vmem(LOW, 16 * LATE, HD),
            vmem(LOW, 16, LATE, HD),
            vmem(FULL, 2, 8, width),
            vmem(FULL, 16, 8, width),
            vmem(LOW, EARLY, width),
            vmem(LOW, EARLY, width),
            vmem(LOW, 16, 16, width),
            *[vmem(operand.dtype, *operand.shape) for operand in streamed[:10]],
            vmem(LOW, width, 4 * HD),
            vmem(LOW, *streamed[11].shape),
            dma(16, 6), dma(16, 6), dma(2, 3), dma(8), dma(3), dma(3), dma(4), dma(4), dma(3), dma(4),
            dma(2, 4, 2), dma(2, 4, 2), dma(2, 2),
            dma(13), dma(2), dma(2), dma(15), dma(16), dma(15), dma(16), dma(16), dma(16), dma(16), dma(17),
            dma(KEEPERS), dma(16), dma(15), dma(16), dma(KEEPERS), dma(KEEPERS),
        ],
        compiler_params=params(2, 60),
        cost_estimate=cost(15),
    )(doc_starts, *operands)


def per_device(
    tokens,
    cotangent,
    doc_starts,
    query_weight,
    key_weight,
    value_weight,
    out_weight,
    gate_weight,
    up_weight,
    down_weight,
    input_gain,
    attn_gain,
    prenorm_gain,
    post_gain,
    query_gain,
    key_gain,
):
    row_count = tokens.shape[0]
    first_row = lax.axis_index("seq") * row_count
    own_index = first_row + jnp.arange(row_count, dtype=jnp.int32)
    own_position = doc_layout(doc_starts, own_index)[1]
    cos_table, sine_table = rope_tables(own_position, HD)
    query_scale = HD ** (-0.5)
    inputs = tokens.astype(jnp.float32)
    normed = rms_norm(inputs, input_gain)
    normed_low = normed.astype(jnp.bfloat16)
    query_raw = jnp.dot(normed_low, query_weight, preferred_element_type=jnp.float32)
    key_raw = jnp.dot(normed_low, key_weight, preferred_element_type=jnp.float32)
    value_low = jnp.dot(normed_low, value_weight, preferred_element_type=jnp.float32).astype(
        jnp.bfloat16
    )

    def query_piece(source, scaling):
        return rotate(rms_norm(source, scaling), cos_table, sine_table) * query_scale

    def key_piece(source, scaling):
        return rotate(rms_norm(source, scaling), cos_table, sine_table)

    query_rows = query_piece(query_raw, query_gain)
    query_low = query_rows.astype(jnp.bfloat16)
    key_rows = key_piece(key_raw, key_gain)
    key_low = key_rows.astype(jnp.bfloat16)
    mix_all, lse_rows, q_all, k_all, v_all, out_weight_all = forward_attention(
        doc_starts, query_low, key_low, value_low, out_weight
    )
    width = tokens.shape[1]
    mix_grad, stats, early, piece_a, piece_b, mixed, resid = middle(
        attn_gain,
        prenorm_gain,
        post_gain,
        lse_rows,
        mix_all,
        out_weight_all,
        tokens,
        cotangent,
        jnp.transpose(gate_weight),
        jnp.transpose(up_weight),
        down_weight,
    )
    late, early, tokens_grad, input_gain_rows, big = backward_attention(
        doc_starts,
        mix_grad,
        stats,
        piece_a,
        piece_b,
        query_gain,
        key_gain,
        input_gain,
        early,
        q_all,
        k_all,
        v_all,
        query_raw,
        key_raw,
        cos_table,
        sine_table,
        key_weight,
        value_weight,
        jnp.transpose(normed_low),
        query_weight,
        tokens,
        resid,
    )
    input_gain_grad = input_gain_rows[0]
    query_weight_grad = late[:width].astype(jnp.float32)
    key_weight_grad = late[width : 2 * width].astype(jnp.float32)
    value_weight_grad = late[2 * width : 3 * width].astype(jnp.float32)
    query_gain_grad = late[3 * width].astype(jnp.float32)
    key_gain_grad = late[3 * width + 1].astype(jnp.float32)
    out_weight_grad = early[:HD].astype(jnp.float32)
    rest = early[HD : HD + 64]
    gains = early[HD + 64 : HD + 67].astype(jnp.float32)
    attn_gain_grad, prenorm_gain_grad, post_gain_grad = gains[0], gains[1], gains[2]
    hidden = gate_weight.shape[1]
    gate_weight_grad = jnp.transpose(big[:hidden].astype(jnp.float32))
    up_weight_grad = jnp.transpose(big[hidden : 2 * hidden].astype(jnp.float32))
    down_weight_grad = big[2 * hidden :].astype(jnp.float32)
    down_weight_grad = lax.dynamic_update_slice(
        down_weight_grad, rest.astype(jnp.float32), (hidden - rest.shape[0], 0)
    )
    return (
        mixed,
        tokens_grad,
        query_weight_grad,
        key_weight_grad,
        value_weight_grad,
        out_weight_grad,
        gate_weight_grad,
        up_weight_grad,
        down_weight_grad,
        input_gain_grad,
        attn_gain_grad,
        prenorm_gain_grad,
        post_gain_grad,
        query_gain_grad,
        key_gain_grad,
    )


def solution(mesh):
    placed = (
        P("seq", None),
        P("seq", None),
        P(),
        P(None, "head"),
        P(),
        P(),
        P("head", None),
        P(None, "head"),
        P(None, "head"),
        P("head", None),
        P(),
        P(),
        P(),
        P(),
        P(),
        P(),
    )
    return jax.shard_map(
        per_device,
        mesh=mesh,
        in_specs=placed,
        out_specs=(
            P("seq", None),
            P("seq", None),
            P(None, "head"),
            P(),
            P(),
            P("head", None),
            P(None, "head"),
            P(None, "head"),
            P("head", None),
            P(),
            P(),
            P(),
            P(),
            P(),
            P(),
        ),
        check_vma=False,
    )
```
